32 devices in a mesh: dp: 8 (over y, x, core), state: 4 (over z).
Axes of the slice: x: 2, y: 2, z: 4, core: 2. Of those that a mesh axis runs over, the one named last changes fastest.
Arguments:
- tokens: bfloat16 [8, 2, 512, 1024], P('dp', None, 'state'), may hold values from -32 to 32
- carried_state: float32 [8, 512, 1024], P('dp', 'state'), may hold values from -6 to 6
- past_keys: bfloat16 [8, 512, 2, 1024], P('dp', None, None, 'state'), may hold values from -6 to 6
- fresh_start: int32 [8], P('dp'), may hold values 0 or 1
- valid_count: int32 [8], P('dp'), may hold values from 128 to 1024, as said below
- bucket_ids: int32 [512], replicated, may hold values from 0 to 31
- grad_output: bfloat16 [8, 2, 512, 1024], P('dp', None, 'state'), may hold values from -6 to 6
- grad_state: float32 [8, 512, 1024], P('dp', 'state'), may hold values from -6 to 6
- norm_gains: float32 [3, 1024], replicated, may hold values from 0.5 to 1.5
- token_qkv: bfloat16 [1024, 3, 1024], P('dp', None, 'state'), may hold values from -0.1875 to 0.1875
- token_out: bfloat16 [1024, 1024], P('dp', 'state'), may hold values from -3 to 3
- bias_table: float32 [32, 8], P(None, 'state'), may hold values from -4 to 4
- mlp_up: bfloat16 [1024, 4096], P('dp', 'state'), may hold values from -0.1875 to 0.1875
- mlp_down: bfloat16 [1024, 4096], P('dp', 'state'), may hold values from -0.09375 to 0.09375
- state_qkv: bfloat16 [1024, 3, 1024], P('dp', None, 'state'), may hold values from -0.1875 to 0.1875
- state_gates: bfloat16 [1024, 3, 1024], P('dp'), may hold values from -3 to 3
- initial_state: bfloat16 [512, 1024], P('state', 'dp'), may hold values from -6 to 6
Outputs:
- block_out: bfloat16 [8, 2, 512, 1024], P('dp', None, 'state')
- state_out: float32 [8, 512, 1024], P('dp', 'state')
- rms_stats: float32 [3], replicated
- tokens_grad: bfloat16 [8, 2, 512, 1024], P('dp', None, 'state')
- carried_grad: float32 [8, 512, 1024], P('dp', 'state')
- past_grad: float32 [8, 512, 2, 1024], P('dp', None, None, 'state')
- gains_grad: float32 [3, 1024], P(None, ('dp', 'state'))
- token_qkv_grad: float32 [1024, 3, 1024], P('dp', None, 'state')
- token_out_grad: float32 [1024, 1024], P('dp', 'state')
- table_grad: float32 [32, 8], P('dp', 'state')
- mlp_up_grad: float32 [1024, 4096], P('dp', 'state')
- mlp_down_grad: float32 [1024, 4096], P('dp', 'state')
- state_qkv_grad: float32 [1024, 3, 1024], P('dp', None, 'state')
- state_gates_grad: float32 [1024, 3, 1024], P(('dp', 'state'))
- initial_grad: float32 [512, 1024], P('state', 'dp')
The draws below stay inside these ranges and needn't reach their ends.
Inputs may be any that keep to these rules, and one draw needn't show every extreme that they name: `fresh_start`: 1 marks an item that begins a segment: it starts from initial_state and has no valid previous keys. `valid_count`: some item is wholly valid and some item has 128 valid tokens. `bucket_ids`: bucket of each distance from 0 to 511.
All inputs are finite; a program needn't handle non-finite values. No bound on the sum of `fresh_start` on one device may be relied on, other than what follows from the above.
Results may differ from the reference program's by a relative error of at most 0.04.
Values may be sent and summed in bfloat16 or wider, within the bound.
A program may use at most 576 MiB of HBM per device.

```python
import math
import jax
import jax.numpy as jnp
from jax import lax

D = 1024
H = 8
DH = 128
FF = 4096
W = 512
NS = 512
NB = 32
BLOCKS = 2
HD = 1024
ITEMS = 8


def draw_valid_count(key, part):
    key = jax.random.fold_in(key, 11)
    first_key, second_key = jax.random.split(key)
    counts = jax.random.randint(first_key, (ITEMS,), W // 4, BLOCKS * W + 1)
    shuffled = jax.random.permutation(second_key, ITEMS)
    counts = jnp.where(shuffled == 0, BLOCKS * W, counts)
    counts = jnp.where(shuffled == 1, W // 4, counts)
    return counts.astype(jnp.int32)


def item_scales(low_end, high_end):
    place = jnp.arange(ITEMS).astype(jnp.float32) / max(ITEMS - 1, 1)
    return (low_end + (high_end - low_end) * place)[:, None, None, None]


def draw_tokens(key, part):
    key = jax.random.fold_in(key, 23)
    shape = (ITEMS, BLOCKS, W, D)
    values = jnp.clip(jax.random.normal(key, shape, jnp.float32), -6.0, 6.0) * item_scales(0.4, 4.0)
    return values.astype(jnp.bfloat16)


def touch_ends(values, stream_key, low, top_value):
    longest = values.shape.index(max(values.shape))
    spots = []
    for shift in (0, 1):
        where = [jax.random.randint(jax.random.fold_in(stream_key, axis), (), 0, length) for axis, length in enumerate(values.shape)]
        where[longest] = (where[longest] + shift) % values.shape[longest]
        spots.append(tuple(where))
    return values.at[spots[0]].set(low).at[spots[1]].set(top_value)


def levels(key, dims, cuts, least, high):
    loudness = 1.0
    for axis_at, parts in cuts:
        heights = jax.random.uniform(jax.random.fold_in(jax.random.fold_in(key, 6), axis_at), (parts,), jnp.float32, least / len(cuts), high / len(cuts))
        loudness = loudness * jnp.repeat(jnp.exp(heights), dims[axis_at] // parts).reshape((-1,) + (1,) * (len(dims) - 1 - axis_at))
    return loudness


def gaussian(rng, shape, deviation, limit, cuts=(), held_as=jnp.bfloat16):
    values = deviation * jax.random.normal(rng, shape, jnp.float32)
    if cuts:
        values = values * levels(rng, shape, cuts, -0.22, 0.18)
    return jnp.clip(values, -limit, limit).astype(held_as)


def setup_inputs(seed: int = 0) -> dict:
    keys = jax.random.split(jax.random.key(seed), 18)
    tokens = draw_tokens(jax.random.fold_in(keys[17], 71), 0)
    carried_state = gaussian(keys[1], (ITEMS, NS, D), 1.0, 6.0, ((0, 8), (1, 4)), jnp.float32)
    past_keys = gaussian(keys[2], (ITEMS, W, 2, HD), 1.0, 6.0, ((0, 8), (3, 4)))
    fresh_start = touch_ends((jax.random.randint(keys[3], (ITEMS,), 0, 4) < 1).astype(jnp.int32), jax.random.fold_in(keys[3], 1), 0, 1)
    valid_count = draw_valid_count(jax.random.fold_in(keys[17], 71), 0)
    bucket_ids = touch_ends(jax.random.randint(keys[5], (W,), 0, NB), jax.random.fold_in(keys[5], 1), 0, NB - 1).astype(jnp.int32)
    grad_output = gaussian(keys[6], (ITEMS, BLOCKS, W, D), 1.0, 6.0, ((0, 8), (2, 4)))
    grad_state = gaussian(keys[7], (ITEMS, NS, D), 1.0, 6.0, ((0, 8), (1, 4)), jnp.float32)
    norm_gains = jnp.clip(1.0 + 0.1 * jax.random.normal(keys[8], (3, D), jnp.float32), 0.5, 1.5)
    token_qkv = gaussian(keys[9], (D, 3, HD), D ** -0.5, 0.1875, ((0, 8), (2, 4)))
    token_out = gaussian(keys[10], (D, HD), (max(HD // 256, 1)) ** -0.5, 3.0, ((0, 8), (1, 4)))
    bias_table = gaussian(keys[11], (NB, H), 1.0, 4.0, ((1, 4),), jnp.float32)
    mlp_up = gaussian(keys[12], (D, FF), D ** -0.5, 0.1875, ((0, 8), (1, 4)))
    mlp_down = gaussian(keys[13], (D, FF), FF ** -0.5, 0.09375, ((0, 8), (1, 4)))
    state_qkv = gaussian(keys[14], (D, 3, HD), D ** -0.5, 0.1875, ((0, 8), (2, 4)))
    state_gates = gaussian(keys[15], (D, 3, HD), (max(HD // 256, 1)) ** -0.5, 3.0, ((0, 8),))
    initial_state = gaussian(keys[16], (NS, D), 1.0, 6.0, ((0, 4), (1, 8)))
    return dict(tokens=tokens, carried_state=carried_state, past_keys=past_keys, fresh_start=fresh_start, valid_count=valid_count, bucket_ids=bucket_ids, grad_output=grad_output, grad_state=grad_state, norm_gains=norm_gains, token_qkv=token_qkv, token_out=token_out, bias_table=bias_table, mlp_up=mlp_up, mlp_down=mlp_down, state_qkv=state_qkv, state_gates=state_gates, initial_state=initial_state)


@jax.custom_vjp
def low(v):
    return lax.optimization_barrier(v.astype(jnp.bfloat16)).astype(jnp.float32)

@jax.custom_vjp
def low_back(v):
    return v

def low_keep(v):
    return (low(v), None)

def low_pass(kept, grad):
    return (grad,)

def back_keep(v):
    return (v, None)

def back_low(kept, grad):
    return (low(grad),)
low.defvjp(low_keep, low_pass)
low_back.defvjp(back_keep, back_low)
EPS = 1e-06
NEGATIVE = -1e+30
HIGHEST = lax.Precision.HIGHEST

def round_both(tensor):
    return low(low_back(tensor))

def rms_norm(tensor, gains_row):
    return tensor * lax.rsqrt(lax.optimization_barrier(jnp.mean(tensor * tensor, axis=-1, keepdims=True)) + EPS) * gains_row

def split_heads(tensor):
    return tensor.reshape(tensor.shape[0], H, DH)

def attend(queries, key_rows, values, bias_add, allowed):
    scores = jnp.einsum('qhd,khd->hqk', queries, key_rows, precision=HIGHEST) / math.sqrt(DH)
    if bias_add is not None:
        scores = scores + bias_add
    scores = jnp.where(allowed[None], low_back(scores), NEGATIVE)
    row_max = lax.optimization_barrier(jnp.max(scores, axis=-1, keepdims=True))
    weights = jnp.exp(scores - row_max)
    attn_probs = low(weights / lax.optimization_barrier(jnp.sum(weights, axis=-1, keepdims=True)))
    mixed_heads = jnp.einsum('hqk,khd->qhd', attn_probs, values, precision=HIGHEST)
    return round_both(mixed_heads.reshape(mixed_heads.shape[0], H * DH))

def one_block(inputs, state_now, past_key, past_value, past_ok, token_ok, bias_grid, inside, params):
    gains, qkv_weights, out_weights, up_weights, down_weights, sqkv_weights, gate_weights = params
    normed = low(rms_norm(inputs, gains[0]))
    project = jnp.einsum('wd,dch->cwh', normed, qkv_weights, precision=HIGHEST)
    token_query, token_key, token_value = (round_both(project[0]), round_both(project[1]), round_both(project[2]))
    state_normed = low(rms_norm(state_now, gains[2]))
    state_project = jnp.einsum('nd,dch->cnh', state_normed, sqkv_weights, precision=HIGHEST)
    state_query, state_key, state_value = (round_both(state_project[0]), round_both(state_project[1]), round_both(state_project[2]))
    window_ok = inside & jnp.concatenate([past_ok, token_ok])[None, :]
    token_allowed = jnp.concatenate([window_ok, jnp.ones((W, NS), jnp.bool_)], axis=1)
    token_bias = jnp.concatenate([bias_grid, jnp.zeros((H, W, NS), jnp.float32)], axis=2)
    mixed_heads = attend(split_heads(token_query), split_heads(jnp.concatenate([past_key, token_key, state_key], axis=0)), split_heads(jnp.concatenate([past_value, token_value, state_value], axis=0)), token_bias, token_allowed)
    branch = low_back(jnp.einsum('wh,dh->wd', mixed_heads, out_weights, precision=HIGHEST))
    middle = inputs + branch
    middle_normed = low(rms_norm(middle, gains[1]))
    up_values = low_back(jnp.dot(middle_normed, up_weights, precision=HIGHEST))
    hidden = low(jax.nn.gelu(up_values, approximate=True))
    feed_out = jnp.einsum('wf,df->wd', hidden, down_weights, precision=HIGHEST)
    result = middle + feed_out
    state_allowed = jnp.concatenate([jnp.ones((NS, NS), jnp.bool_), jnp.broadcast_to(token_ok[None, :], (NS, W))], axis=1)
    state_mixed = attend(split_heads(state_query), split_heads(jnp.concatenate([state_key, token_key], axis=0)), split_heads(jnp.concatenate([state_value, token_value], axis=0)), None, state_allowed)
    gate_values = low_back(jnp.einsum('nh,dch->cnd', state_mixed, gate_weights, precision=HIGHEST))
    new_state = state_now * jax.nn.sigmoid(gate_values[2] + 1.0) + jnp.tanh(gate_values[0]) * jax.nn.sigmoid(gate_values[1] - 1.0)
    return (result, new_state, token_key, token_value, branch, feed_out)

def reference(tokens, carried_state, past_keys, fresh_start, valid_count, bucket_ids, grad_output, grad_state, norm_gains, token_qkv, token_out, bias_table, mlp_up, mlp_down, state_qkv, state_gates, initial_state):
    query_pos = jnp.arange(W)[:, None]
    key_pos = jnp.arange(2 * W)[None, :]
    offset = W + query_pos - key_pos
    inside = (offset >= 0) & (offset < W)
    pick_index = jnp.clip(offset, 0, W - 1)
    one_hot = (bucket_ids[:, None] == jnp.arange(NB)[None, :]).astype(jnp.float32)

    def forward(inputs, carried, past_pairs, gains, qkv_weights, out_weights, table_values, up_weights, down_weights, sqkv_weights, gate_weights, initial):
        per_offset = jnp.dot(one_hot, table_values, precision=HIGHEST)
        bias_grid = jnp.transpose(jnp.take(per_offset, pick_index, axis=0), (2, 0, 1))
        params = (gains, qkv_weights, out_weights, up_weights, down_weights, sqkv_weights, gate_weights)

        def item_step(pieces):
            item_in, item_state, item_past, item_fresh, item_count = pieces
            state_now = jnp.where(item_fresh == 1, initial, item_state)
            past_key = item_past[:, 0]
            past_value = item_past[:, 1]
            past_ok = jnp.broadcast_to(item_fresh == 0, (W,))
            results, branches, feeds = ([], [], [])
            for block_at in range(BLOCKS):
                token_ok = block_at * W + jnp.arange(W) < item_count
                result, state_now, past_key, past_value, branch, feed_out = one_block(item_in[block_at], state_now, past_key, past_value, past_ok, token_ok, bias_grid, inside, params)
                past_ok = token_ok
                results.append(result)
                branches.append(branch)
                feeds.append(feed_out)
            return (jnp.stack(results), state_now, jnp.stack(branches), jnp.stack(feeds))
        outputs = lax.map(jax.checkpoint(item_step), (inputs, carried, past_pairs, fresh_start, valid_count))
        return ((outputs[0], outputs[1]), (outputs[2], outputs[3]))
    primals = (tokens.astype(jnp.float32), carried_state, past_keys.astype(jnp.float32), norm_gains, token_qkv.astype(jnp.float32), token_out.astype(jnp.float32), bias_table, mlp_up.astype(jnp.float32), mlp_down.astype(jnp.float32), state_qkv.astype(jnp.float32), state_gates.astype(jnp.float32), initial_state.astype(jnp.float32))
    (result, final_state), pullback, (branch, feed_out) = jax.vjp(forward, *primals, has_aux=True)
    gradients = pullback((grad_output.astype(jnp.float32), grad_state))
    valid_mask = (jnp.arange(BLOCKS * W)[None, :] < valid_count[:, None]).reshape(ITEMS, BLOCKS, W, 1)
    valid_total = jnp.sum(valid_mask.astype(jnp.float32))

    def root_mean(tensor):
        return jnp.sqrt(jnp.sum(jnp.where(valid_mask, tensor * tensor, 0.0)) / valid_total)
    rms_stats = jnp.stack([root_mean(result), root_mean(branch), root_mean(feed_out)])
    return (result.astype(jnp.bfloat16), final_state, rms_stats, gradients[0].astype(jnp.bfloat16), gradients[1], gradients[2], gradients[3], gradients[4], gradients[5], gradients[6], gradients[7], gradients[8], gradients[9], gradients[10], gradients[11])
```

```python
import math

import jax
import jax.numpy as jnp
from jax import lax
from jax.sharding import PartitionSpec as P

DH = 128


EPS = 1e-06
NEGATIVE = -1e30
HIGHEST = lax.Precision.HIGHEST


def rms_norm(tensor, gains_row):
    return tensor * lax.rsqrt(jnp.mean(tensor * tensor, axis=-1, keepdims=True) + EPS) * gains_row


def norm_back(tensor, gains_row, cotangent):
    return jax.vjp(rms_norm, tensor, gains_row)[1](cotangent)


def smooth_gelu(tensor):
    return jax.nn.gelu(tensor, approximate=True)


def renew_state(state_now, gate_values):
    return state_now * jax.nn.sigmoid(gate_values[2] + 1.0) + jnp.tanh(
        gate_values[0]
    ) * jax.nn.sigmoid(gate_values[1] - 1.0)


def split_heads(tensor):
    return tensor.reshape(tensor.shape[0], tensor.shape[1], tensor.shape[2] // DH, DH)


def merge_heads(tensor):
    return tensor.reshape(tensor.shape[0], tensor.shape[1], tensor.shape[2] * DH)


def score_grid(queries, key_rows, bias_add, allowed):
    scores = jnp.einsum(
        "iqhd,ikhd->ihqk", queries, key_rows, preferred_element_type=jnp.float32
    ) / math.sqrt(DH)
    if bias_add is not None:
        scores = scores + bias_add[None]
    return jnp.where(allowed[:, None], scores, NEGATIVE)


def attend_forward(queries, key_rows, values, bias_add, allowed):
    scores = score_grid(queries, key_rows, bias_add, allowed)
    row_max = jnp.max(scores, axis=-1, keepdims=True)
    weights = jnp.exp(scores - row_max)
    row_total = jnp.sum(weights, axis=-1, keepdims=True)
    attn_probs = (weights / row_total).astype(jnp.bfloat16)
    mixed_heads = jnp.einsum(
        "ihqk,ikhd->iqhd", attn_probs, values, preferred_element_type=jnp.float32
    )
    return (merge_heads(mixed_heads.astype(jnp.bfloat16)), row_max + jnp.log(row_total))


def attention_backward_pass(queries, key_rows, values, bias_add, allowed, log_total, grad_mixed):
    scores = score_grid(queries, key_rows, bias_add, allowed)
    attn_probs = jnp.exp(scores - log_total)
    probs_grad = jnp.einsum(
        "iqhd,ikhd->ihqk", grad_mixed, values, preferred_element_type=jnp.float32
    )
    scores_grad = attn_probs * (
        probs_grad - jnp.sum(attn_probs * probs_grad, axis=-1, keepdims=True)
    )
    scores_grad = scores_grad.astype(jnp.bfloat16)
    values_grad = jnp.einsum(
        "ihqk,iqhd->ikhd",
        attn_probs.astype(jnp.bfloat16),
        grad_mixed,
        preferred_element_type=jnp.float32,
    )
    queries_grad = jnp.einsum(
        "ihqk,ikhd->iqhd", scores_grad, key_rows, preferred_element_type=jnp.float32
    ) / math.sqrt(DH)
    keys_grad = jnp.einsum(
        "ihqk,iqhd->ikhd", scores_grad, queries, preferred_element_type=jnp.float32
    ) / math.sqrt(DH)
    return (
        merge_heads(queries_grad),
        merge_heads(keys_grad),
        merge_heads(values_grad),
        scores_grad,
    )


def diagonal_sums(grid_values):
    num_heads, num_rows, num_cols = grid_values.shape
    flat = grid_values.reshape(num_heads, num_rows * num_cols)
    flat = jnp.pad(flat, ((0, 0), (0, num_rows)))
    sums = jnp.sum(flat.reshape(num_heads, num_rows, num_cols + 1), axis=1)
    return sums[:, num_rows:0:-1]


def toeplitz_grid(per_offset, num_rows):
    num_cols = 2 * num_rows
    line = jnp.pad(per_offset[::-1].T, ((0, 0), (1, num_cols - num_rows)))
    flat = jnp.tile(line, (1, num_rows))[:, : num_rows * num_cols]
    return flat.reshape(-1, num_rows, num_cols)


def sum_rows(partial_value):
    return lax.psum_scatter(
        partial_value.astype(jnp.bfloat16), "state", scatter_dimension=1, tiled=True
    ).astype(jnp.float32)


def whole_rows(partial_value):
    return lax.all_gather(partial_value, "state", axis=1, tiled=True)


def shards(
    tokens,
    carried_state,
    past_keys,
    fresh_start,
    valid_count,
    bucket_ids,
    grad_output,
    grad_state,
    norm_gains,
    token_qkv,
    token_out,
    bias_table,
    mlp_up,
    mlp_down,
    state_qkv,
    state_gates,
    initial_state,
):
    item_count, blocks, share_rows, model_width = tokens.shape
    groups = lax.axis_size("state")
    state_rank = lax.axis_index("state")
    window_width = share_rows * groups
    vector_rows = carried_state.shape[1] * groups
    local_width = token_qkv.shape[2]
    qkv_full, out_full, up_full, down_full, sqkv_full, gates_full, initial_full = (
        lax.all_gather(token_qkv, "dp", axis=0, tiled=True),
        lax.all_gather(token_out, "dp", axis=0, tiled=True),
        lax.all_gather(mlp_up, "dp", axis=0, tiled=True),
        lax.all_gather(mlp_down, "dp", axis=0, tiled=True),
        lax.all_gather(state_qkv, "dp", axis=0, tiled=True),
        lax.all_gather(state_gates, "dp", axis=0, tiled=True),
        lax.all_gather(initial_state, "dp", axis=1, tiled=True),
    )
    gates_used = lax.dynamic_slice_in_dim(gates_full, state_rank * local_width, local_width, 2)
    one_hot = (bucket_ids[:, None] == jnp.arange(bias_table.shape[0])[None, :]).astype(jnp.float32)
    per_offset = jnp.dot(one_hot, bias_table, precision=HIGHEST)
    query_pos = jnp.arange(window_width)[:, None]
    key_pos = jnp.arange(2 * window_width)[None, :]
    offset = window_width + query_pos - key_pos
    inside = (offset >= 0) & (offset < window_width)
    bias_grid = toeplitz_grid(per_offset, window_width)
    token_bias = jnp.pad(bias_grid, ((0, 0), (0, 0), (0, vector_rows)))
    is_fresh = fresh_start == 1
    state_now = jnp.where(
        is_fresh[:, None, None], initial_full.astype(jnp.float32)[None], carried_state
    )
    past_key = past_keys[:, :, 0]
    past_value = past_keys[:, :, 1]
    past_ok = jnp.broadcast_to(~is_fresh[:, None], (item_count, window_width))
    gains_token, gains_middle, gains_state = (norm_gains[0], norm_gains[1], norm_gains[2])
    share_pos = state_rank * share_rows + jnp.arange(share_rows)
    square_sums = jnp.zeros((3,), jnp.float32)
    valid_total = jnp.zeros((), jnp.float32)
    kept_values = []
    results = []
    for block_at in range(blocks):
        token_ok = (
            block_at * window_width + jnp.arange(window_width)[None, :] < valid_count[:, None]
        )
        inputs = tokens[:, block_at].astype(jnp.float32)
        normed, state_normed = (
            lax.all_gather(
                rms_norm(inputs, gains_token).astype(jnp.bfloat16), "state", axis=1, tiled=True
            ),
            lax.all_gather(
                rms_norm(state_now, gains_state).astype(jnp.bfloat16), "state", axis=1, tiled=True
            ),
        )
        project = jnp.einsum(
            "iwd,dch->ciwh", normed, qkv_full, preferred_element_type=jnp.float32
        ).astype(jnp.bfloat16)
        state_project = jnp.einsum(
            "ind,dch->cinh", state_normed, sqkv_full, preferred_element_type=jnp.float32
        ).astype(jnp.bfloat16)
        token_keys = jnp.concatenate([past_key, project[1], state_project[1]], axis=1)
        token_values = jnp.concatenate([past_value, project[2], state_project[2]], axis=1)
        window_ok = inside[None] & jnp.concatenate([past_ok, token_ok], axis=1)[:, None, :]
        token_allowed = jnp.concatenate(
            [window_ok, jnp.ones((item_count, window_width, vector_rows), jnp.bool_)], axis=2
        )
        mixed_heads, token_total = attend_forward(
            split_heads(project[0]),
            split_heads(token_keys),
            split_heads(token_values),
            token_bias,
            token_allowed,
        )
        branch = sum_rows(
            jnp.einsum("iwh,dh->iwd", mixed_heads, out_full, preferred_element_type=jnp.float32)
        )
        middle = inputs + branch
        middle_normed = lax.all_gather(
            rms_norm(middle, gains_middle).astype(jnp.bfloat16), "state", axis=1, tiled=True
        )
        up_values = jnp.einsum(
            "iwd,df->iwf", middle_normed, up_full, preferred_element_type=jnp.float32
        )
        hidden = smooth_gelu(up_values).astype(jnp.bfloat16)
        feed_out = sum_rows(
            jnp.einsum("iwf,df->iwd", hidden, down_full, preferred_element_type=jnp.float32)
        )
        result = middle + feed_out
        results.append(result.astype(jnp.bfloat16))
        share_ok = (block_at * window_width + share_pos[None, :] < valid_count[:, None]).astype(
            jnp.float32
        )[:, :, None]
        square_sums = square_sums + jnp.stack(
            [
                jnp.sum(share_ok * result * result),
                jnp.sum(share_ok * branch * branch),
                jnp.sum(share_ok * feed_out * feed_out),
            ]
        )
        valid_total = valid_total + jnp.sum(share_ok)
        state_keys = jnp.concatenate([state_project[1], project[1]], axis=1)
        state_values = jnp.concatenate([state_project[2], project[2]], axis=1)
        state_allowed = jnp.concatenate(
            [
                jnp.ones((item_count, vector_rows, vector_rows), jnp.bool_),
                jnp.broadcast_to(token_ok[:, None, :], (item_count, vector_rows, window_width)),
            ],
            axis=2,
        )
        state_mixed, state_total = attend_forward(
            split_heads(state_project[0]),
            split_heads(state_keys),
            split_heads(state_values),
            None,
            state_allowed,
        )
        gate_source = state_mixed
        gate_values = lax.psum_scatter(
            jnp.einsum(
                "inh,dch->cind", state_mixed, gates_used, preferred_element_type=jnp.float32
            ).astype(jnp.bfloat16),
            "state",
            scatter_dimension=2,
            tiled=True,
        ).astype(jnp.float32)
        kept_values.append(
            (
                inputs,
                normed,
                state_normed,
                project,
                state_project,
                token_keys,
                token_values,
                token_allowed,
                mixed_heads,
                token_total,
                middle,
                middle_normed,
                up_values,
                hidden,
                state_keys,
                state_values,
                state_allowed,
                state_total,
                gate_source,
                gate_values,
                state_now,
            )
        )
        state_now = renew_state(state_now, gate_values)
        past_key, past_value, past_ok = (project[1], project[2], token_ok)
    square_sums, valid_total = lax.psum((square_sums, valid_total), ("dp", "state"))
    rms_stats = jnp.sqrt(square_sums / valid_total)
    qkv_grad = jnp.zeros(qkv_full.shape, jnp.float32)
    out_grad = jnp.zeros(out_full.shape, jnp.float32)
    up_grad = jnp.zeros(up_full.shape, jnp.float32)
    down_grad = jnp.zeros(down_full.shape, jnp.float32)
    sqkv_grad = jnp.zeros(sqkv_full.shape, jnp.float32)
    gate_grad = jnp.zeros(gates_used.shape, jnp.float32)
    bias_grad = jnp.zeros(bias_grid.shape, jnp.float32)
    gain_token_grad = jnp.zeros((model_width,), jnp.float32)
    gain_middle_grad = jnp.zeros((model_width,), jnp.float32)
    gain_state_grad = jnp.zeros((model_width,), jnp.float32)
    state_grad = grad_state
    carried_key_rows = jnp.zeros(past_keys[:, :, 0].shape, jnp.float32)
    carry_value = jnp.zeros(past_keys[:, :, 0].shape, jnp.float32)
    token_grads = [None] * blocks
    for block_at in reversed(range(blocks)):
        (
            inputs,
            normed,
            state_normed,
            project,
            state_project,
            token_keys,
            token_values,
            token_allowed,
            mixed_heads,
            token_total,
            middle,
            middle_normed,
            up_values,
            hidden,
            state_keys,
            state_values,
            state_allowed,
            state_total,
            gate_source,
            gate_values,
            state_before,
        ) = kept_values[block_at]
        direct_grad, gates_grad = jax.vjp(renew_state, state_before, gate_values)[1](state_grad)
        gates_low = gates_grad.astype(jnp.bfloat16)
        gates_rows = lax.all_gather(gates_low, "state", axis=2, tiled=True)
        state_mixed_grad = jnp.einsum(
            "cind,dch->inh", gates_rows, gates_used, preferred_element_type=jnp.float32
        ).astype(jnp.bfloat16)
        gate_grad = gate_grad + jnp.einsum(
            "inh,cind->dch", gate_source, gates_rows, preferred_element_type=jnp.float32
        )
        state_query_gradient, state_keys_gradient, state_values_gradient, discarded_output = (
            attention_backward_pass(
                split_heads(state_project[0]),
                split_heads(state_keys),
                split_heads(state_values),
                None,
                state_allowed,
                state_total,
                split_heads(state_mixed_grad),
            )
        )
        out_share = grad_output[:, block_at]
        out_whole = whole_rows(out_share)
        down_grad = down_grad + jnp.einsum(
            "iwf,iwd->df", hidden, out_whole, preferred_element_type=jnp.float32
        )
        hidden_grad = jnp.einsum(
            "iwd,df->iwf", out_whole, down_full, preferred_element_type=jnp.float32
        )
        up_values_grad = jax.vjp(smooth_gelu, up_values)[1](hidden_grad)[0].astype(jnp.bfloat16)
        up_grad = up_grad + jnp.einsum(
            "iwd,iwf->df", middle_normed, up_values_grad, preferred_element_type=jnp.float32
        )
        middle_normed_grad = lax.psum_scatter(
            jnp.einsum(
                "iwf,df->iwd", up_values_grad, up_full, preferred_element_type=jnp.float32
            ).astype(jnp.bfloat16),
            "state",
            scatter_dimension=1,
            tiled=True,
        ).astype(jnp.float32)
        middle_grad, gain_part = norm_back(middle, gains_middle, middle_normed_grad)
        middle_grad = out_share.astype(jnp.float32) + middle_grad
        gain_middle_grad = gain_middle_grad + gain_part
        branch_whole = whole_rows(middle_grad.astype(jnp.bfloat16))
        out_grad = out_grad + jnp.einsum(
            "iwh,iwd->dh", mixed_heads, branch_whole, preferred_element_type=jnp.float32
        )
        mixed_grad = jnp.einsum(
            "iwd,dh->iwh", branch_whole, out_full, preferred_element_type=jnp.float32
        ).astype(jnp.bfloat16)
        query_grad, token_keys_gradient, tvalues_grad, scores_grad = attention_backward_pass(
            split_heads(project[0]),
            split_heads(token_keys),
            split_heads(token_values),
            token_bias,
            token_allowed,
            token_total,
            split_heads(mixed_grad),
        )
        bias_grad = bias_grad + jnp.sum(
            scores_grad[:, :, :, : 2 * window_width].astype(jnp.float32), axis=0
        )
        key_gradient_rows = (
            token_keys_gradient[:, window_width : 2 * window_width]
            + state_keys_gradient[:, vector_rows:]
            + carried_key_rows
        )
        value_grad = (
            tvalues_grad[:, window_width : 2 * window_width]
            + state_values_gradient[:, vector_rows:]
            + carry_value
        )
        state_key_gradient = (
            token_keys_gradient[:, 2 * window_width :] + state_keys_gradient[:, :vector_rows]
        )
        state_value_gradient = (
            tvalues_grad[:, 2 * window_width :] + state_values_gradient[:, :vector_rows]
        )
        project_grad = jnp.stack([query_grad, key_gradient_rows, value_grad]).astype(jnp.bfloat16)
        state_projection_gradient = jnp.stack(
            [state_query_gradient, state_key_gradient, state_value_gradient]
        ).astype(jnp.bfloat16)
        qkv_grad = qkv_grad + jnp.einsum(
            "iwd,ciwh->dch", normed, project_grad, preferred_element_type=jnp.float32
        )
        sqkv_grad = sqkv_grad + jnp.einsum(
            "ind,cinh->dch",
            state_normed,
            state_projection_gradient,
            preferred_element_type=jnp.float32,
        )
        normed_grad, state_normed_grad = (
            lax.psum_scatter(
                jnp.einsum(
                    "ciwh,dch->iwd", project_grad, qkv_full, preferred_element_type=jnp.float32
                ).astype(jnp.bfloat16),
                "state",
                scatter_dimension=1,
                tiled=True,
            ).astype(jnp.float32),
            lax.psum_scatter(
                jnp.einsum(
                    "cinh,dch->ind",
                    state_projection_gradient,
                    sqkv_full,
                    preferred_element_type=jnp.float32,
                ).astype(jnp.bfloat16),
                "state",
                scatter_dimension=1,
                tiled=True,
            ).astype(jnp.float32),
        )
        input_grad, gain_part = norm_back(inputs, gains_token, normed_grad)
        gain_token_grad = gain_token_grad + gain_part
        token_grads[block_at] = (middle_grad + input_grad).astype(jnp.bfloat16)
        state_norm_grad, gain_part = norm_back(state_before, gains_state, state_normed_grad)
        gain_state_grad = gain_state_grad + gain_part
        state_grad = direct_grad + state_norm_grad
        carried_key_rows = token_keys_gradient[:, :window_width]
        carry_value = tvalues_grad[:, :window_width]
    carried_grad = jnp.where(is_fresh[:, None, None], 0.0, state_grad)
    initial_part = jnp.sum(jnp.where(is_fresh[:, None, None], state_grad, 0.0), axis=0)
    past_grad = jnp.stack([carried_key_rows, carry_value], axis=2)
    table_part = jnp.dot(one_hot.T, diagonal_sums(bias_grad).T, precision=HIGHEST)
    gain_columns = jnp.stack([gain_token_grad, gain_middle_grad, gain_state_grad], axis=1)
    summed = (
        lax.psum_scatter(
            qkv_grad.astype(jnp.bfloat16), "dp", scatter_dimension=0, tiled=True
        ).astype(jnp.float32),
        lax.psum_scatter(
            out_grad.astype(jnp.bfloat16), "dp", scatter_dimension=0, tiled=True
        ).astype(jnp.float32),
        lax.psum_scatter(
            table_part.astype(jnp.bfloat16), "dp", scatter_dimension=0, tiled=True
        ).astype(jnp.float32),
        lax.psum_scatter(
            up_grad.astype(jnp.bfloat16), "dp", scatter_dimension=0, tiled=True
        ).astype(jnp.float32),
        lax.psum_scatter(
            down_grad.astype(jnp.bfloat16), "dp", scatter_dimension=0, tiled=True
        ).astype(jnp.float32),
        lax.psum_scatter(
            sqkv_grad.astype(jnp.bfloat16), "dp", scatter_dimension=0, tiled=True
        ).astype(jnp.float32),
        lax.psum_scatter(
            initial_part.astype(jnp.bfloat16), "dp", scatter_dimension=1, tiled=True
        ).astype(jnp.float32),
        lax.psum_scatter(
            gate_grad.astype(jnp.bfloat16), "dp", scatter_dimension=0, tiled=True
        ).astype(jnp.float32),
        lax.psum_scatter(
            gain_columns.astype(jnp.bfloat16), "dp", scatter_dimension=0, tiled=True
        ).astype(jnp.float32),
    )
    gate_pieces, gain_pieces = (
        lax.all_to_all(
            summed[7][:, :, None, :].astype(jnp.bfloat16),
            "state",
            split_axis=0,
            concat_axis=2,
            tiled=True,
        ).astype(jnp.float32),
        lax.all_to_all(
            summed[8][:, :, None, None].astype(jnp.bfloat16),
            "state",
            split_axis=0,
            concat_axis=2,
            tiled=True,
        ).astype(jnp.float32),
    )
    gains_grad = jnp.sum(gain_pieces, axis=(2, 3)).T
    gates_grad_out = gate_pieces.reshape(
        gate_pieces.shape[0], gate_pieces.shape[1], gate_pieces.shape[2] * gate_pieces.shape[3]
    )
    return (
        jnp.stack(results, axis=1),
        state_now,
        rms_stats,
        jnp.stack(token_grads, axis=1),
        carried_grad,
        past_grad,
        gains_grad,
        summed[0],
        summed[1],
        summed[2],
        summed[3],
        summed[4],
        summed[5],
        gates_grad_out,
        summed[6],
    )


def solution(mesh):
    in_specs = (
        P("dp", None, "state", None),
        P("dp", "state", None),
        P("dp", None, None, "state"),
        P("dp"),
        P("dp"),
        P(),
        P("dp", None, "state", None),
        P("dp", "state", None),
        P(),
        P("dp", None, "state"),
        P("dp", "state"),
        P(None, "state"),
        P("dp", "state"),
        P("dp", "state"),
        P("dp", None, "state"),
        P("dp", None, None),
        P("state", "dp"),
    )
    out_specs = (
        P("dp", None, "state", None),
        P("dp", "state", None),
        P(),
        P("dp", None, "state", None),
        P("dp", "state", None),
        P("dp", None, None, "state"),
        P(None, ("dp", "state")),
        P("dp", None, "state"),
        P("dp", "state"),
        P("dp", "state"),
        P("dp", "state"),
        P("dp", "state"),
        P("dp", None, "state"),
        P(("dp", "state"), None, None),
        P("state", "dp"),
    )
    return jax.shard_map(shards, mesh=mesh, in_specs=in_specs, out_specs=out_specs, check_vma=False)
```

```python
import math

import jax
import jax.numpy as jnp
from jax import lax
from jax.experimental import pallas as pl
from jax.experimental.pallas import tpu as pltpu
from jax.sharding import PartitionSpec as P

DH = 128


EPS = 1e-06
NEGATIVE = -1e30
HIGHEST = lax.Precision.HIGHEST


def rms_norm(tensor, gains_row):
    return tensor * lax.rsqrt(jnp.mean(tensor * tensor, axis=-1, keepdims=True) + EPS) * gains_row


def norm_back(tensor, gains_row, cotangent):
    return jax.vjp(rms_norm, tensor, gains_row)[1](cotangent)


def smooth_gelu(tensor):
    return jax.nn.gelu(tensor, approximate=True)


def renew_state(state_now, gate_values):
    return state_now * jax.nn.sigmoid(gate_values[2] + 1.0) + jnp.tanh(
        gate_values[0]
    ) * jax.nn.sigmoid(gate_values[1] - 1.0)


def split_heads(tensor):
    return tensor.reshape(tensor.shape[0], tensor.shape[1], tensor.shape[2] // DH, DH)


def merge_heads(tensor):
    return tensor.reshape(tensor.shape[0], tensor.shape[1], tensor.shape[2] * DH)


def score_grid(queries, key_rows, bias_add, allowed):
    scores = jnp.einsum(
        "iqhd,ikhd->ihqk", queries, key_rows, preferred_element_type=jnp.float32
    ) / math.sqrt(DH)
    if bias_add is not None:
        scores = scores + bias_add[None]
    return jnp.where(allowed[:, None], scores, NEGATIVE)


def attend_forward(queries, key_rows, values, bias_add, allowed):
    scores = score_grid(queries, key_rows, bias_add, allowed)
    row_max = jnp.max(scores, axis=-1, keepdims=True)
    weights = jnp.exp(scores - row_max)
    row_total = jnp.sum(weights, axis=-1, keepdims=True)
    attn_probs = (weights / row_total).astype(jnp.bfloat16)
    mixed_heads = jnp.einsum(
        "ihqk,ikhd->iqhd", attn_probs, values, preferred_element_type=jnp.float32
    )
    return (merge_heads(mixed_heads.astype(jnp.bfloat16)), row_max + jnp.log(row_total))


def attention_backward_pass(queries, key_rows, values, bias_add, allowed, log_total, grad_mixed):
    scores = score_grid(queries, key_rows, bias_add, allowed)
    attn_probs = jnp.exp(scores - log_total)
    probs_grad = jnp.einsum(
        "iqhd,ikhd->ihqk", grad_mixed, values, preferred_element_type=jnp.float32
    )
    scores_grad = attn_probs * (
        probs_grad - jnp.sum(attn_probs * probs_grad, axis=-1, keepdims=True)
    )
    scores_grad = scores_grad.astype(jnp.bfloat16)
    values_grad = jnp.einsum(
        "ihqk,iqhd->ikhd",
        attn_probs.astype(jnp.bfloat16),
        grad_mixed,
        preferred_element_type=jnp.float32,
    )
    queries_grad = jnp.einsum(
        "ihqk,ikhd->iqhd", scores_grad, key_rows, preferred_element_type=jnp.float32
    ) / math.sqrt(DH)
    keys_grad = jnp.einsum(
        "ihqk,iqhd->ikhd", scores_grad, queries, preferred_element_type=jnp.float32
    ) / math.sqrt(DH)
    return (
        merge_heads(queries_grad),
        merge_heads(keys_grad),
        merge_heads(values_grad),
        scores_grad,
    )


def diagonal_sums(grid_values):
    num_heads, num_rows, num_cols = grid_values.shape
    flat = grid_values.reshape(num_heads, num_rows * num_cols)
    flat = jnp.pad(flat, ((0, 0), (0, num_rows)))
    sums = jnp.sum(flat.reshape(num_heads, num_rows, num_cols + 1), axis=1)
    return sums[:, num_rows:0:-1]


def toeplitz_grid(per_offset, num_rows):
    num_cols = 2 * num_rows
    line = jnp.pad(per_offset[::-1].T, ((0, 0), (1, num_cols - num_rows)))
    flat = jnp.tile(line, (1, num_rows))[:, : num_rows * num_cols]
    return flat.reshape(-1, num_rows, num_cols)


def sum_rows(partial_value):
    return lax.psum_scatter(
        partial_value.astype(jnp.bfloat16), "state", scatter_dimension=1, tiled=True
    ).astype(jnp.float32)


def whole_rows(partial_value):
    return lax.all_gather(partial_value, "state", axis=1, tiled=True)


def shards(
    tokens,
    carried_state,
    past_keys,
    fresh_start,
    valid_count,
    bucket_ids,
    grad_output,
    grad_state,
    norm_gains,
    token_qkv,
    token_out,
    bias_table,
    mlp_up,
    mlp_down,
    state_qkv,
    state_gates,
    initial_state,
):
    item_count, blocks, share_rows, model_width = tokens.shape
    groups = lax.axis_size("state")
    state_rank = lax.axis_index("state")
    window_width = share_rows * groups
    vector_rows = carried_state.shape[1] * groups
    local_width = token_qkv.shape[2]
    qkv_full, out_full, up_full, down_full, sqkv_full, gates_full, initial_full = (
        lax.all_gather(token_qkv, "dp", axis=0, tiled=True),
        lax.all_gather(token_out, "dp", axis=0, tiled=True),
        lax.all_gather(mlp_up, "dp", axis=0, tiled=True),
        lax.all_gather(mlp_down, "dp", axis=0, tiled=True),
        lax.all_gather(state_qkv, "dp", axis=0, tiled=True),
        lax.all_gather(state_gates, "dp", axis=0, tiled=True),
        lax.all_gather(initial_state, "dp", axis=1, tiled=True),
    )
    gates_used = lax.dynamic_slice_in_dim(gates_full, state_rank * local_width, local_width, 2)
    one_hot = (bucket_ids[:, None] == jnp.arange(bias_table.shape[0])[None, :]).astype(jnp.float32)
    per_offset = jnp.dot(one_hot, bias_table, precision=HIGHEST)
    query_pos = jnp.arange(window_width)[:, None]
    key_pos = jnp.arange(2 * window_width)[None, :]
    offset = window_width + query_pos - key_pos
    inside = (offset >= 0) & (offset < window_width)
    bias_grid = toeplitz_grid(per_offset, window_width)
    token_bias = jnp.pad(bias_grid, ((0, 0), (0, 0), (0, vector_rows)))
    is_fresh = fresh_start == 1
    state_now = jnp.where(
        is_fresh[:, None, None], initial_full.astype(jnp.float32)[None], carried_state
    )
    past_key = past_keys[:, :, 0]
    past_value = past_keys[:, :, 1]
    past_ok = jnp.broadcast_to(~is_fresh[:, None], (item_count, window_width))
    gains_token, gains_middle, gains_state = (norm_gains[0], norm_gains[1], norm_gains[2])
    share_pos = state_rank * share_rows + jnp.arange(share_rows)
    square_sums = jnp.zeros((3,), jnp.float32)
    valid_total = jnp.zeros((), jnp.float32)
    kept_values = []
    results = []
    for block_at in range(blocks):
        token_ok = (
            block_at * window_width + jnp.arange(window_width)[None, :] < valid_count[:, None]
        )
        inputs = tokens[:, block_at].astype(jnp.float32)
        normed, state_normed = (
            lax.all_gather(
                rms_norm(inputs, gains_token).astype(jnp.bfloat16), "state", axis=1, tiled=True
            ),
            lax.all_gather(
                rms_norm(state_now, gains_state).astype(jnp.bfloat16), "state", axis=1, tiled=True
            ),
        )
        project = jnp.einsum(
            "iwd,dch->ciwh", normed, qkv_full, preferred_element_type=jnp.float32
        ).astype(jnp.bfloat16)
        state_project = jnp.einsum(
            "ind,dch->cinh", state_normed, sqkv_full, preferred_element_type=jnp.float32
        ).astype(jnp.bfloat16)
        token_keys = jnp.concatenate([past_key, project[1], state_project[1]], axis=1)
        token_values = jnp.concatenate([past_value, project[2], state_project[2]], axis=1)
        window_ok = inside[None] & jnp.concatenate([past_ok, token_ok], axis=1)[:, None, :]
        token_allowed = jnp.concatenate(
            [window_ok, jnp.ones((item_count, window_width, vector_rows), jnp.bool_)], axis=2
        )
        mixed_heads, token_total = attend_forward(
            split_heads(project[0]),
            split_heads(token_keys),
            split_heads(token_values),
            token_bias,
            token_allowed,
        )
        branch = sum_rows(
            jnp.einsum("iwh,dh->iwd", mixed_heads, out_full, preferred_element_type=jnp.float32)
        )
        middle = inputs + branch
        middle_normed = lax.all_gather(
            rms_norm(middle, gains_middle).astype(jnp.bfloat16), "state", axis=1, tiled=True
        )
        up_values = jnp.einsum(
            "iwd,df->iwf", middle_normed, up_full, preferred_element_type=jnp.float32
        )
        hidden = smooth_gelu(up_values).astype(jnp.bfloat16)
        feed_out = sum_rows(
            jnp.einsum("iwf,df->iwd", hidden, down_full, preferred_element_type=jnp.float32)
        )
        result = middle + feed_out
        results.append(result.astype(jnp.bfloat16))
        share_ok = (block_at * window_width + share_pos[None, :] < valid_count[:, None]).astype(
            jnp.float32
        )[:, :, None]
        square_sums = square_sums + jnp.stack(
            [
                jnp.sum(share_ok * result * result),
                jnp.sum(share_ok * branch * branch),
                jnp.sum(share_ok * feed_out * feed_out),
            ]
        )
        valid_total = valid_total + jnp.sum(share_ok)
        state_keys = jnp.concatenate([state_project[1], project[1]], axis=1)
        state_values = jnp.concatenate([state_project[2], project[2]], axis=1)
        state_allowed = jnp.concatenate(
            [
                jnp.ones((item_count, vector_rows, vector_rows), jnp.bool_),
                jnp.broadcast_to(token_ok[:, None, :], (item_count, vector_rows, window_width)),
            ],
            axis=2,
        )
        state_mixed, state_total = attend_forward(
            split_heads(state_project[0]),
            split_heads(state_keys),
            split_heads(state_values),
            None,
            state_allowed,
        )
        gate_source = state_mixed
        gate_values = lax.psum_scatter(
            jnp.einsum(
                "inh,dch->cind", state_mixed, gates_used, preferred_element_type=jnp.float32
            ).astype(jnp.bfloat16),
            "state",
            scatter_dimension=2,
            tiled=True,
        ).astype(jnp.float32)
        kept_values.append(
            (
                inputs,
                normed,
                state_normed,
                project,
                state_project,
                token_keys,
                token_values,
                token_allowed,
                mixed_heads,
                token_total,
                middle,
                middle_normed,
                up_values,
                hidden,
                state_keys,
                state_values,
                state_allowed,
                state_total,
                gate_source,
                gate_values,
                state_now,
            )
        )
        state_now = renew_state(state_now, gate_values)
        past_key, past_value, past_ok = (project[1], project[2], token_ok)
    square_sums, valid_total = lax.psum((square_sums, valid_total), ("dp", "state"))
    rms_stats = jnp.sqrt(square_sums / valid_total)
    qkv_grad = jnp.zeros(qkv_full.shape, jnp.float32)
    out_grad = jnp.zeros(out_full.shape, jnp.float32)
    up_grad = jnp.zeros(up_full.shape, jnp.float32)
    down_grad = jnp.zeros(down_full.shape, jnp.float32)
    sqkv_grad = jnp.zeros(sqkv_full.shape, jnp.float32)
    gate_grad = jnp.zeros(gates_used.shape, jnp.float32)
    bias_grad = jnp.zeros(bias_grid.shape, jnp.float32)
    gain_token_grad = jnp.zeros((model_width,), jnp.float32)
    gain_middle_grad = jnp.zeros((model_width,), jnp.float32)
    gain_state_grad = jnp.zeros((model_width,), jnp.float32)
    state_grad = grad_state
    carried_key_rows = jnp.zeros(past_keys[:, :, 0].shape, jnp.float32)
    carry_value = jnp.zeros(past_keys[:, :, 0].shape, jnp.float32)
    token_grads = [None] * blocks
    for block_at in reversed(range(blocks)):
        (
            inputs,
            normed,
            state_normed,
            project,
            state_project,
            token_keys,
            token_values,
            token_allowed,
            mixed_heads,
            token_total,
            middle,
            middle_normed,
            up_values,
            hidden,
            state_keys,
            state_values,
            state_allowed,
            state_total,
            gate_source,
            gate_values,
            state_before,
        ) = kept_values[block_at]
        direct_grad, gates_grad = jax.vjp(renew_state, state_before, gate_values)[1](state_grad)
        gates_low = gates_grad.astype(jnp.bfloat16)
        gates_rows = lax.all_gather(gates_low, "state", axis=2, tiled=True)
        state_mixed_grad = jnp.einsum(
            "cind,dch->inh", gates_rows, gates_used, preferred_element_type=jnp.float32
        ).astype(jnp.bfloat16)
        gate_grad = gate_grad + jnp.einsum(
            "inh,cind->dch", gate_source, gates_rows, preferred_element_type=jnp.float32
        )
        state_query_gradient, state_keys_gradient, state_values_gradient, discarded_output = (
            attention_backward_pass(
                split_heads(state_project[0]),
                split_heads(state_keys),
                split_heads(state_values),
                None,
                state_allowed,
                state_total,
                split_heads(state_mixed_grad),
            )
        )
        out_share = grad_output[:, block_at]
        out_whole = whole_rows(out_share)
        down_grad = down_grad + jnp.einsum(
            "iwf,iwd->df", hidden, out_whole, preferred_element_type=jnp.float32
        )
        hidden_grad = jnp.einsum(
            "iwd,df->iwf", out_whole, down_full, preferred_element_type=jnp.float32
        )
        up_values_grad = jax.vjp(smooth_gelu, up_values)[1](hidden_grad)[0].astype(jnp.bfloat16)
        up_grad = up_grad + jnp.einsum(
            "iwd,iwf->df", middle_normed, up_values_grad, preferred_element_type=jnp.float32
        )
        middle_normed_grad = lax.psum_scatter(
            jnp.einsum(
                "iwf,df->iwd", up_values_grad, up_full, preferred_element_type=jnp.float32
            ).astype(jnp.bfloat16),
            "state",
            scatter_dimension=1,
            tiled=True,
        ).astype(jnp.float32)
        middle_grad, gain_part = norm_back(middle, gains_middle, middle_normed_grad)
        middle_grad = out_share.astype(jnp.float32) + middle_grad
        gain_middle_grad = gain_middle_grad + gain_part
        branch_whole = whole_rows(middle_grad.astype(jnp.bfloat16))
        out_grad = out_grad + jnp.einsum(
            "iwh,iwd->dh", mixed_heads, branch_whole, preferred_element_type=jnp.float32
        )
        mixed_grad = jnp.einsum(
            "iwd,dh->iwh", branch_whole, out_full, preferred_element_type=jnp.float32
        ).astype(jnp.bfloat16)
        query_grad, token_keys_gradient, tvalues_grad, scores_grad = attention_backward_pass(
            split_heads(project[0]),
            split_heads(token_keys),
            split_heads(token_values),
            token_bias,
            token_allowed,
            token_total,
            split_heads(mixed_grad),
        )
        bias_grad = bias_grad + jnp.sum(
            scores_grad[:, :, :, : 2 * window_width].astype(jnp.float32), axis=0
        )
        key_gradient_rows = (
            token_keys_gradient[:, window_width : 2 * window_width]
            + state_keys_gradient[:, vector_rows:]
            + carried_key_rows
        )
        value_grad = (
            tvalues_grad[:, window_width : 2 * window_width]
            + state_values_gradient[:, vector_rows:]
            + carry_value
        )
        state_key_gradient = (
            token_keys_gradient[:, 2 * window_width :] + state_keys_gradient[:, :vector_rows]
        )
        state_value_gradient = (
            tvalues_grad[:, 2 * window_width :] + state_values_gradient[:, :vector_rows]
        )
        project_grad = jnp.stack([query_grad, key_gradient_rows, value_grad]).astype(jnp.bfloat16)
        state_projection_gradient = jnp.stack(
            [state_query_gradient, state_key_gradient, state_value_gradient]
        ).astype(jnp.bfloat16)
        qkv_grad = qkv_grad + jnp.einsum(
            "iwd,ciwh->dch", normed, project_grad, preferred_element_type=jnp.float32
        )
        sqkv_grad = sqkv_grad + jnp.einsum(
            "ind,cinh->dch",
            state_normed,
            state_projection_gradient,
            preferred_element_type=jnp.float32,
        )
        normed_grad, state_normed_grad = (
            lax.psum_scatter(
                jnp.einsum(
                    "ciwh,dch->iwd", project_grad, qkv_full, preferred_element_type=jnp.float32
                ).astype(jnp.bfloat16),
                "state",
                scatter_dimension=1,
                tiled=True,
            ).astype(jnp.float32),
            lax.psum_scatter(
                jnp.einsum(
                    "cinh,dch->ind",
                    state_projection_gradient,
                    sqkv_full,
                    preferred_element_type=jnp.float32,
                ).astype(jnp.bfloat16),
                "state",
                scatter_dimension=1,
                tiled=True,
            ).astype(jnp.float32),
        )
        input_grad, gain_part = norm_back(inputs, gains_token, normed_grad)
        gain_token_grad = gain_token_grad + gain_part
        token_grads[block_at] = (middle_grad + input_grad).astype(jnp.bfloat16)
        state_norm_grad, gain_part = norm_back(state_before, gains_state, state_normed_grad)
        gain_state_grad = gain_state_grad + gain_part
        state_grad = direct_grad + state_norm_grad
        carried_key_rows = token_keys_gradient[:, :window_width]
        carry_value = tvalues_grad[:, :window_width]
    carried_grad = jnp.where(is_fresh[:, None, None], 0.0, state_grad)
    initial_part = jnp.sum(jnp.where(is_fresh[:, None, None], state_grad, 0.0), axis=0)
    past_grad = jnp.stack([carried_key_rows, carry_value], axis=2)
    table_part = jnp.dot(one_hot.T, diagonal_sums(bias_grad).T, precision=HIGHEST)
    gain_columns = jnp.stack([gain_token_grad, gain_middle_grad, gain_state_grad], axis=1)
    summed = (
        lax.psum_scatter(
            qkv_grad.astype(jnp.bfloat16), "dp", scatter_dimension=0, tiled=True
        ).astype(jnp.float32),
        lax.psum_scatter(
            out_grad.astype(jnp.bfloat16), "dp", scatter_dimension=0, tiled=True
        ).astype(jnp.float32),
        lax.psum_scatter(
            table_part.astype(jnp.bfloat16), "dp", scatter_dimension=0, tiled=True
        ).astype(jnp.float32),
        lax.psum_scatter(
            up_grad.astype(jnp.bfloat16), "dp", scatter_dimension=0, tiled=True
        ).astype(jnp.float32),
        lax.psum_scatter(
            down_grad.astype(jnp.bfloat16), "dp", scatter_dimension=0, tiled=True
        ).astype(jnp.float32),
        lax.psum_scatter(
            sqkv_grad.astype(jnp.bfloat16), "dp", scatter_dimension=0, tiled=True
        ).astype(jnp.float32),
        lax.psum_scatter(
            initial_part.astype(jnp.bfloat16), "dp", scatter_dimension=1, tiled=True
        ).astype(jnp.float32),
        lax.psum_scatter(
            gate_grad.astype(jnp.bfloat16), "dp", scatter_dimension=0, tiled=True
        ).astype(jnp.float32),
        lax.psum_scatter(
            gain_columns.astype(jnp.bfloat16), "dp", scatter_dimension=0, tiled=True
        ).astype(jnp.float32),
    )
    gate_pieces, gain_pieces = (
        lax.all_to_all(
            summed[7][:, :, None, :].astype(jnp.bfloat16),
            "state",
            split_axis=0,
            concat_axis=2,
            tiled=True,
        ).astype(jnp.float32),
        lax.all_to_all(
            summed[8][:, :, None, None].astype(jnp.bfloat16),
            "state",
            split_axis=0,
            concat_axis=2,
            tiled=True,
        ).astype(jnp.float32),
    )
    gains_grad = jnp.sum(gain_pieces, axis=(2, 3)).T
    gates_grad_out = gate_pieces.reshape(
        gate_pieces.shape[0], gate_pieces.shape[1], gate_pieces.shape[2] * gate_pieces.shape[3]
    )
    return (
        jnp.stack(results, axis=1),
        state_now,
        rms_stats,
        jnp.stack(token_grads, axis=1),
        carried_grad,
        past_grad,
        gains_grad,
        summed[0],
        summed[1],
        summed[2],
        summed[3],
        summed[4],
        summed[5],
        gates_grad_out,
        summed[6],
    )


MESH = pl.DeviceIdType.MESH
NN = (((1,), (0,)), ((), ()))
NT = (((1,), (1,)), ((), ()))
TN = (((0,), (0,)), ((), ()))
VMEM_BYTES = 62 * 2**20


def place():
    chip_core = lax.axis_index("dp")
    level = lax.axis_index("state")
    core, low = lax.rem(chip_core, 2), lax.rem(level, 2)
    x, y = lax.rem(chip_core // 2, 2), chip_core // 4
    flip = lambda bit: 1 - 2 * bit
    return {
        "rank": 2 * low + core,
        "ranks": [2 * low + core, 2 * low + 1 - core, 2 * (1 - low) + core, 2 * (1 - low) + 1 - core],
        "mates": [
            None,
            (chip_core + flip(core), level),
            (chip_core, level + flip(low)),
            (chip_core + flip(core), level + flip(low)),
        ],
        "plane": 2 * y + x,
        "planes": [2 * y + x, 2 * y + 1 - x, 2 * (1 - y) + x, 2 * (1 - y) + 1 - x],
        "plane_mates": [
            None,
            (chip_core + 2 * flip(x), level),
            (chip_core + 4 * flip(y), level),
            (chip_core + 2 * flip(x) + 4 * flip(y), level),
        ],
        "core": core,
        "dp": chip_core,
    }


def rows_at(start, size, step=128):
    return pl.ds(pl.multiple_of(start, step), size)


class Links:
    def __init__(self, send_sems, recv_sems):
        self.send_sems, self.recv_sems = send_sems, recv_sems
        self.used = 0
        self.open_sends = []

    def copy(self, source, target, device):
        at = self.used
        self.used += 1
        moved = pltpu.make_async_remote_copy(
            src_ref=source,
            dst_ref=target,
            send_sem=self.send_sems.at[at],
            recv_sem=self.recv_sems.at[at],
            device_id=device,
            device_id_type=MESH,
        )
        moved.start()
        self.open_sends.append(moved)
        return moved

    def close(self):
        for moved in self.open_sends:
            moved.wait_send()
        self.open_sends = []


def greet(devices):
    barrier = pltpu.get_barrier_semaphore()
    for device in devices:
        pl.semaphore_signal(barrier, inc=1, device_id=device, device_id_type=MESH)
    pl.semaphore_wait(barrier, len(devices))


class RowGather:
    def __init__(self, links, here, ref, base, rows):
        self.links, self.here, self.ref, self.base, self.rows = links, here, ref, base, rows

    def part(self, k):
        return self.ref.at[rows_at(self.base + self.here["ranks"][k] * self.rows, self.rows)]

    def start(self):
        own, mates = self.part(0), self.here["mates"]
        self.far = self.links.copy(own, own, mates[2])
        self.near = self.links.copy(own, own, mates[1])
        return self

    def ready(self, k):
        if k == 1:
            self.near.wait_recv()
        elif k == 2:
            self.far.wait_recv()
            block = self.part(2)
            self.last = self.links.copy(block, block, self.here["mates"][1])
        elif k == 3:
            self.last.wait_recv()


class RowSum:
    def __init__(self, links, here, stage, near_in, far_out, far_in, rows):
        self.links, self.here, self.rows = links, here, rows
        self.stage, self.near_in, self.far_out, self.far_in = stage, near_in, far_out, far_in

    def part(self, k):
        return self.stage.at[rows_at(self.here["ranks"][k] * self.rows, self.rows)]

    def fill(self, make_rows):
        sibling = self.here["mates"][1]
        for k, slot in ((3, 0), (1, 1)):
            self.part(k)[...] = make_rows(self.here["ranks"][k]).astype(jnp.bfloat16)
            moved = self.links.copy(self.part(k), self.near_in.at[slot], sibling)
            if slot == 0:
                self.near_far = moved
            else:
                self.near_own = moved
        for k in (2, 0):
            self.part(k)[...] = make_rows(self.here["ranks"][k]).astype(jnp.bfloat16)
        return self

    def forward(self):
        self.near_far.wait_recv()
        summed = self.part(2)[...].astype(jnp.float32) + self.near_in[0].astype(jnp.float32)
        self.far_out[...] = summed.astype(jnp.bfloat16)
        self.far = self.links.copy(self.far_out, self.far_in, self.here["mates"][2])
        return self

    def finish(self):
        self.near_own.wait_recv()
        self.far.wait_recv()
        return (
            self.part(0)[...].astype(jnp.float32)
            + self.near_in[1].astype(jnp.float32)
            + self.far_in[...].astype(jnp.float32)
        )


def row_sum_scratch(rows, width):
    return [
        pltpu.VMEM((4 * rows, width), jnp.bfloat16),
        pltpu.VMEM((2, rows, width), jnp.bfloat16),
        pltpu.VMEM((rows, width), jnp.bfloat16),
        pltpu.VMEM((rows, width), jnp.bfloat16),
    ]


def dot(left, right, dims):
    return lax.dot_general(left, right, dims, preferred_element_type=jnp.float32)


def scale_of(tensor):
    return lax.rsqrt(jnp.mean(tensor * tensor, axis=-1, keepdims=True) + EPS)


def rms_back(tensor, gains_row, cotangent):
    scale = scale_of(tensor)
    weighted = cotangent * gains_row
    inner = jnp.mean(tensor * weighted, axis=-1, keepdims=True)
    straight = scale * weighted - tensor * (scale * scale * scale * inner)
    return straight, jnp.sum(cotangent * tensor * scale, axis=0, keepdims=True)


def column_heads(head):
    return pl.ds(head * DH, DH)


def bias_tiles(lines_ref, tiles_ref, heads, width):
    for head in range(heads):
        line = lines_ref[head : head + 1, :]
        spread = jnp.broadcast_to(line, (tiles_ref.shape[1], line.shape[1]))
        tiles_ref[head] = pltpu.roll(spread, 0, 1, stride=1, stride_axis=0)[:, :width]


def softmax_pair(first, second):
    top = jnp.maximum(
        jnp.max(first, axis=-1, keepdims=True), jnp.max(second, axis=-1, keepdims=True)
    )
    first, second = jnp.exp(first - top), jnp.exp(second - top)
    total = jnp.sum(first, axis=-1, keepdims=True) + jnp.sum(second, axis=-1, keepdims=True)
    share = 1.0 / total
    return (
        (first * share).astype(jnp.bfloat16),
        (second * share).astype(jnp.bfloat16),
        top + jnp.log(total),
    )


TILE = 256
ROOT = 1.0 / math.sqrt(DH)


def attention_kernel(
    x_ref, s0_ref, past_ref, mask_ref, rowmask_ref, lines_ref, gains_ref,
    wst_in, wtok_in, wout_in, gates_in, wup_in, wdn_in,
    normed, snormed, queries, keys, values, state_qkv, lse_token, lse_state, mixed, smixed,
    middle, gate_values, s1_ref, s2_ref, branch_sum, wst, wtok, wout, gates, wup, wdn,
    tiles, a2a_0, a2a_1, *rest,
):
    rs = [rest[0:4], rest[4:8]]
    links = Links(rest[8], rest[9])
    here = place()
    rank, ranks, mates = here["rank"], here["ranks"], here["mates"]
    planes, plane_mates = here["planes"], here["plane_mates"]
    rows = s0_ref.shape[0]
    window = 4 * rows
    width = queries.shape[1]
    heads = width // DH
    greet(mates[1:] + plane_mates[1:])

    def spread(local, full):
        size = local.shape[0]
        target = full.at[rows_at(planes[0] * size, size)]
        return [links.copy(local, target, plane_mates[k]) for k in (1, 2, 3)]

    def own_rows(local, full):
        size = local.shape[0]
        full[rows_at(planes[0] * size, size), :] = local[...]

    def arrived(copies):
        for moved in copies:
            moved.wait_recv()

    s0 = s0_ref[...]
    snormed[rows_at(rank * rows, rows), :] = (s0 * scale_of(s0) * gains_ref[2:3, :]).astype(jnp.bfloat16)
    gather_s0 = RowGather(links, here, snormed, 0, rows).start()
    wst_moves = spread(wst_in, wst)
    gather_x = []
    for block in range(2):
        x = x_ref[block * rows : (block + 1) * rows, :].astype(jnp.float32)
        normed[rows_at(block * window + rank * rows, rows), :] = (
            x * scale_of(x) * gains_ref[0:1, :]
        ).astype(jnp.bfloat16)
        gather_x.append(RowGather(links, here, normed, block * window, rows).start())
        if block == 0:
            wtok_moves = spread(wtok_in, wtok)
    wout_moves = spread(wout_in, wout)
    gate_rows = gates_in.shape[0]
    gate_target = gates.at[rows_at(here["dp"] * gate_rows, gate_rows)]
    gate_moves = [links.copy(gates_in, gate_target, plane_mates[k]) for k in (1, 2, 3)]
    gate_near = links.copy(gates_in, gate_target, mates[1])
    wup_moves = spread(wup_in, wup)
    wdn_moves = spread(wdn_in, wdn)
    own_rows(wst_in, wst)
    own_rows(wtok_in, wtok)
    own_rows(wout_in, wout)
    own_rows(wup_in, wup)
    own_rows(wdn_in, wdn)
    gates[rows_at(here["dp"] * gate_rows, gate_rows), :] = gates_in[...]
    keys[0:window, :] = past_ref[0]
    values[0:window, :] = past_ref[1]
    bias_tiles(lines_ref, tiles, heads, 3 * TILE)

    def project_state(block, gather):
        for k in range(4):
            gather.ready(k)
            at = rows_at(block * window + ranks[k] * rows, rows)
            state_qkv[at, :] = dot(snormed[at, :], wst[...], NN).astype(jnp.bfloat16)

    def project_token(block, gather):
        for k in range(4):
            gather.ready(k)
            at = rows_at(block * window + ranks[k] * rows, rows)
            later = rows_at((block + 1) * window + ranks[k] * rows, rows)
            out = dot(normed[at, :], wtok[...], NN).astype(jnp.bfloat16)
            queries[at, :] = out[:, :width]
            keys[later, :] = out[:, width : 2 * width]
            values[later, :] = out[:, 2 * width :]

    def state_attention(block):
        base = block * window
        own = pl.ds((block + 1) * window, window)
        whole = pl.ds(base, window)
        own_mask = mask_ref[0:1, (block + 1) * window : (block + 2) * window]
        for head in range(heads):
            at = head * DH
            for tile in range(window // TILE):
                here_rows = pl.ds(base + tile * TILE, TILE)
                query = state_qkv[here_rows, at : at + DH]
                first = dot(query, state_qkv[whole, width + at : width + at + DH], NT) * ROOT
                second = dot(query, keys[own, at : at + DH], NT) * ROOT + own_mask
                first, second, lse = softmax_pair(first, second)
                out = dot(first, state_qkv[whole, 2 * width + at : 2 * width + at + DH], NN)
                out = out + dot(second, values[own, at : at + DH], NN)
                smixed[here_rows, at : at + DH] = out.astype(jnp.bfloat16)
                lse_state[here_rows, head : head + 1] = lse

    def token_attention(block):
        base = block * window
        whole = pl.ds(base, window)
        for head in range(heads):
            at = head * DH
            for tile in range(window // TILE):
                here_rows = pl.ds(base + tile * TILE, TILE)
                near = pl.ds(base + tile * TILE, 3 * TILE)
                query = queries[here_rows, at : at + DH]
                first = dot(query, keys[near, at : at + DH], NT) * ROOT + tiles[head]
                first = first + mask_ref[0:1, base + tile * TILE : base + tile * TILE + 3 * TILE]
                second = dot(query, state_qkv[whole, width + at : width + at + DH], NT) * ROOT
                first, second, lse = softmax_pair(first, second)
                out = dot(first, values[near, at : at + DH], NN)
                out = out + dot(second, state_qkv[whole, 2 * width + at : 2 * width + at + DH], NN)
                mixed[here_rows, at : at + DH] = out.astype(jnp.bfloat16)
                lse_token[here_rows, head : head + 1] = lse

    def spread_state(block, buffer):
        moves = []
        columns = pl.ds(pl.multiple_of(rank * width, width), width)
        for k in (2, 3, 1):
            source = smixed.at[rows_at(block * window + ranks[k] * rows, rows)]
            moves.append(links.copy(source, buffer.at[:, columns], mates[k]))
        buffer[:, columns] = smixed[rows_at(block * window + rank * rows, rows), :]
        return moves

    def renew(block, buffer, state_now):
        size = state_now.shape[1]
        source = buffer[...]
        parts = []
        for c in range(3):
            part = dot(source, gates[:, c * size : (c + 1) * size], NT)
            gate_values[block * rows : (block + 1) * rows, c * size : (c + 1) * size] = part
            parts.append(part)
        return state_now * jax.nn.sigmoid(parts[2] + 1.0) + jnp.tanh(parts[0]) * jax.nn.sigmoid(
            parts[1] - 1.0
        )

    def branch_rows(block):
        def make(which):
            return dot(mixed[rows_at(block * window + which * rows, rows), :], wout[...], NT)

        return make

    sums = [RowSum(links, here, *rs[block], rows) for block in range(2)]

    def finish_branch(block):
        branch = sums[block].finish()
        at = slice(block * rows, (block + 1) * rows)
        middle[at, :] = x_ref[at, :].astype(jnp.float32) + branch
        return jnp.sum(branch * branch * rowmask_ref[at, :], axis=0, keepdims=True)

    arrived(wst_moves)
    project_state(0, gather_s0)
    arrived(wtok_moves)
    project_token(0, gather_x[0])
    state_attention(0)
    moves_0 = spread_state(0, a2a_0)
    project_token(1, gather_x[1])
    arrived(gate_moves)
    gate_forward = []
    for k in (1, 2, 3):
        block_at = gates.at[rows_at((2 * planes[k] + here["core"]) * gate_rows, gate_rows)]
        gate_forward.append(links.copy(block_at, block_at, mates[1]))
    token_attention(0)
    arrived(wout_moves)
    sums[0].fill(branch_rows(0))
    arrived(moves_0)
    gate_near.wait_recv()
    arrived(gate_forward)
    s1 = renew(0, a2a_0, s0_ref[...])
    s1_ref[...] = s1
    snormed[rows_at(window + rank * rows, rows), :] = (s1 * scale_of(s1) * gains_ref[2:3, :]).astype(
        jnp.bfloat16
    )
    gather_s1 = RowGather(links, here, snormed, window, rows).start()
    sums[0].forward()
    project_state(1, gather_s1)
    state_attention(1)
    moves_1 = spread_state(1, a2a_1)
    token_attention(1)
    sums[1].fill(branch_rows(1))
    total = finish_branch(0)
    arrived(moves_1)
    sums[1].forward()
    s2_ref[...] = renew(1, a2a_1, s1_ref[...])
    total = total + finish_branch(1)
    branch_sum[...] = jnp.broadcast_to(total, branch_sum.shape)
    arrived(wup_moves)
    arrived(wdn_moves)
    links.close()


def feed_kernel(
    middle_ref, gout_ref, gains_ref, rowmask_ref, wup, wdn,
    block_out, middle_grad, wup_grad, wdn_grad, gain_grad, sums_out,
    normed, gout, up, hidden, up_grad, *rest,
):
    rs = [rest[4 * k : 4 * k + 4] for k in range(4)]
    links = Links(rest[16], rest[17])
    here = place()
    rank, ranks, mates = here["rank"], here["ranks"], here["mates"]
    rows = middle_ref.shape[0] // 2
    window = 4 * rows
    greet(mates[1:])
    gathers, gout_gathers = [], []
    for block in range(2):
        at = slice(block * rows, (block + 1) * rows)
        middle = middle_ref[at, :]
        spot = rows_at(block * window + rank * rows, rows)
        normed[spot, :] = (middle * scale_of(middle) * gains_ref[1:2, :]).astype(jnp.bfloat16)
        gathers.append(RowGather(links, here, normed, block * window, rows).start())
    for block in range(2):
        at = slice(block * rows, (block + 1) * rows)
        gout[rows_at(block * window + rank * rows, rows), :] = gout_ref[at, :]
        gout_gathers.append(RowGather(links, here, gout, block * window, rows).start())
    feeds = [RowSum(links, here, *rs[k], rows) for k in range(2)]
    backs = [RowSum(links, here, *rs[2 + k], rows) for k in range(2)]

    def rise(block):
        for k in range(4):
            gathers[block].ready(k)
            at = rows_at(block * window + ranks[k] * rows, rows)
            value = dot(normed[at, :], wup[...], NN)
            up[at, :] = value
            hidden[at, :] = jax.nn.gelu(value, approximate=True).astype(jnp.bfloat16)
        feeds[block].fill(
            lambda which: dot(hidden[rows_at(block * window + which * rows, rows), :], wdn[...], NT)
        )

    def back(block):
        for k in range(4):
            gout_gathers[block].ready(k)
            at = rows_at(block * window + ranks[k] * rows, rows)
            hidden_grad = dot(gout[at, :], wdn[...], NN)
            value = up[at, :]
            square = value * value
            root = math.sqrt(2.0 / math.pi)
            bend = jnp.tanh(root * value * (1.0 + 0.044715 * square))
            slope = 0.5 * (1.0 + bend) + 0.5 * value * (1.0 - bend * bend) * (
                root * (1.0 + 3.0 * 0.044715 * square)
            )
            up_grad[at, :] = (hidden_grad * slope).astype(jnp.bfloat16)
        backs[block].fill(
            lambda which: dot(up_grad[rows_at(block * window + which * rows, rows), :], wup[...], NT)
        )

    rise(0)
    rise(1)
    feeds[0].forward()
    back(0)
    feeds[1].forward()
    back(1)
    backs[0].forward()
    tile = 256
    size = wdn_grad.shape[0]
    for part in range(size // tile):
        at = slice(part * tile, (part + 1) * tile)
        wdn_grad[at, :] = dot(gout[:, at], hidden[...], TN).astype(jnp.bfloat16)
    backs[1].forward()
    for part in range(size // tile):
        at = slice(part * tile, (part + 1) * tile)
        wup_grad[at, :] = dot(normed[:, at], up_grad[...], TN).astype(jnp.bfloat16)
    feed_total, result_total, gain_total = 0.0, 0.0, 0.0
    for block in range(2):
        at = slice(block * rows, (block + 1) * rows)
        feed = feeds[block].finish()
        result = middle_ref[at, :] + feed
        block_out[at, :] = result.astype(jnp.bfloat16)
        share = rowmask_ref[at, :]
        feed_total = feed_total + jnp.sum(feed * feed * share, axis=0, keepdims=True)
        result_total = result_total + jnp.sum(result * result * share, axis=0, keepdims=True)
    sums_out[...] = jnp.concatenate(
        [result_total, feed_total, jnp.zeros((6, result_total.shape[1]), jnp.float32)], axis=0
    )
    for block in range(2):
        at = slice(block * rows, (block + 1) * rows)
        straight, gain = rms_back(middle_ref[at, :], gains_ref[1:2, :], backs[block].finish())
        middle_grad[at, :] = gout_ref[at, :].astype(jnp.float32) + straight
        gain_total = gain_total + gain
    gain_grad[...] = jnp.broadcast_to(gain_total, gain_grad.shape)
    links.close()


def cotangent_kernel(
    middle_grad, gstate_ref, x_ref, s0_ref, s1_ref, gate_values, gains_ref, mask_ref, lines_ref,
    normed, snormed, queries, keys, values, state_qkv, lse_token, lse_state, mixed, smixed,
    wst, wtok, wout, gates,
    tokens_grad, carried, past_grad, gain_grad, line_grad, wst_grad, wtok_grad, wout_grad, gates_grad,
    tiles, tile_grads, branch_grad, mixed_grad, gate_rows, state_mixed_grad, key_grad, value_grad,
    skey_grad, svalue_grad, query_grad, squery_grad, token_cot, state_cot, *rest,
):
    rs = [rest[4 * k : 4 * k + 4] for k in range(4)]
    links = Links(rest[16], rest[17])
    here = place()
    rank, ranks, mates = here["rank"], here["ranks"], here["mates"]
    rows = s0_ref.shape[0]
    window = 4 * rows
    width = queries.shape[1]
    heads = width // DH
    size = s0_ref.shape[1]
    greet(mates[1:])
    branch_gathers = []
    for block in (1, 0):
        at = slice(block * rows, (block + 1) * rows)
        branch_grad[rows_at(block * window + rank * rows, rows), :] = middle_grad[at, :].astype(
            jnp.bfloat16
        )

    def gates_back(block, state, state_grad):
        at = slice(block * rows, (block + 1) * rows)
        spot = rows_at(block * window + rank * rows, rows)
        keep = jax.nn.sigmoid(gate_values[at, 2 * size : 3 * size] + 1.0)
        fresh = jnp.tanh(gate_values[at, 0:size])
        let_in = jax.nn.sigmoid(gate_values[at, size : 2 * size] - 1.0)
        gate_rows[spot, 0:size] = (state_grad * let_in * (1.0 - fresh * fresh)).astype(jnp.bfloat16)
        gate_rows[spot, size : 2 * size] = (
            state_grad * fresh * let_in * (1.0 - let_in)
        ).astype(jnp.bfloat16)
        gate_rows[spot, 2 * size : 3 * size] = (
            state_grad * state * keep * (1.0 - keep)
        ).astype(jnp.bfloat16)
        out = dot(gate_rows[spot, 0:size], gates[:, 0:size], NN)
        out = out + dot(gate_rows[spot, size : 2 * size], gates[:, size : 2 * size], NN)
        out = out + dot(gate_rows[spot, 2 * size : 3 * size], gates[:, 2 * size : 3 * size], NN)
        sending = rest[18 + block]
        sending[...] = out.astype(jnp.bfloat16)
        moves = []
        for k in (2, 3, 1):
            columns = pl.ds(pl.multiple_of(ranks[k] * width, width), width)
            moves.append(links.copy(sending.at[:, columns], state_mixed_grad.at[spot], mates[k]))
        columns = pl.ds(pl.multiple_of(rank * width, width), width)
        state_mixed_grad[spot, :] = sending[:, columns]
        return state_grad * keep, moves

    def pair_back(first, second, lse, first_grad, second_grad):
        first, second = jnp.exp(first - lse), jnp.exp(second - lse)
        inner = jnp.sum(first * first_grad, axis=-1, keepdims=True) + jnp.sum(
            second * second_grad, axis=-1, keepdims=True
        )
        return (
            first.astype(jnp.bfloat16),
            second.astype(jnp.bfloat16),
            (first * (first_grad - inner)).astype(jnp.bfloat16),
            (second * (second_grad - inner)).astype(jnp.bfloat16),
        )

    def token_back(block):
        base = block * window
        whole = pl.ds(base, window)
        for head in range(heads):
            at = head * DH
            lanes = slice(at, at + DH)
            skey_lanes = slice(width + at, width + at + DH)
            svalue_lanes = slice(2 * width + at, 2 * width + at + DH)
            for tile in range(window // TILE):
                here_rows = pl.ds(base + tile * TILE, TILE)
                near = pl.ds(base + tile * TILE, 3 * TILE)
                query = queries[here_rows, lanes]
                out_grad = mixed_grad[here_rows, lanes]
                first = dot(query, keys[near, lanes], NT) * ROOT + tiles[head]
                first = first + mask_ref[0:1, base + tile * TILE : base + tile * TILE + 3 * TILE]
                second = dot(query, state_qkv[whole, skey_lanes], NT) * ROOT
                first, second, first_grad, second_grad = pair_back(
                    first,
                    second,
                    lse_token[here_rows, head : head + 1],
                    dot(out_grad, values[near, lanes], NT),
                    dot(out_grad, state_qkv[whole, svalue_lanes], NT),
                )
                value_grad[near, lanes] += dot(first, out_grad, TN)
                svalue_grad[whole, lanes] += dot(second, out_grad, TN)
                part = dot(first_grad, keys[near, lanes], NN) + dot(
                    second_grad, state_qkv[whole, skey_lanes], NN
                )
                query_grad[pl.ds(tile * TILE, TILE), lanes] = part * ROOT
                key_grad[near, lanes] += dot(first_grad, query, TN) * ROOT
                skey_grad[whole, lanes] += dot(second_grad, query, TN) * ROOT
                tile_grads[head, :, 0 : 3 * TILE] += first_grad.astype(jnp.float32)
        token_cot[whole, 0:width] = query_grad[...].astype(jnp.bfloat16)

    def state_back(block):
        base = block * window
        whole = pl.ds(base, window)
        own = pl.ds(base + window, window)
        own_mask = mask_ref[0:1, base + window : base + 2 * window]
        for head in range(heads):
            at = head * DH
            lanes = slice(at, at + DH)
            skey_lanes = slice(width + at, width + at + DH)
            svalue_lanes = slice(2 * width + at, 2 * width + at + DH)
            for tile in range(window // TILE):
                here_rows = pl.ds(base + tile * TILE, TILE)
                query = state_qkv[here_rows, lanes]
                out_grad = state_mixed_grad[here_rows, lanes]
                first = dot(query, state_qkv[whole, skey_lanes], NT) * ROOT
                second = dot(query, keys[own, lanes], NT) * ROOT + own_mask
                first, second, first_grad, second_grad = pair_back(
                    first,
                    second,
                    lse_state[here_rows, head : head + 1],
                    dot(out_grad, state_qkv[whole, svalue_lanes], NT),
                    dot(out_grad, values[own, lanes], NT),
                )
                svalue_grad[whole, lanes] += dot(first, out_grad, TN)
                value_grad[own, lanes] += dot(second, out_grad, TN)
                part = dot(first_grad, state_qkv[whole, skey_lanes], NN) + dot(
                    second_grad, keys[own, lanes], NN
                )
                squery_grad[pl.ds(tile * TILE, TILE), lanes] = part * ROOT
                skey_grad[whole, lanes] += dot(first_grad, query, TN) * ROOT
                key_grad[own, lanes] += dot(second_grad, query, TN) * ROOT

    def gather_cot(block):
        whole = pl.ds(block * window, window)
        own = pl.ds(block * window + window, window)
        token_cot[whole, width : 2 * width] = key_grad[own, :].astype(jnp.bfloat16)
        token_cot[whole, 2 * width : 3 * width] = value_grad[own, :].astype(jnp.bfloat16)
        state_cot[whole, 0:width] = squery_grad[...].astype(jnp.bfloat16)
        state_cot[whole, width : 2 * width] = skey_grad[whole, :].astype(jnp.bfloat16)
        state_cot[whole, 2 * width : 3 * width] = svalue_grad[whole, :].astype(jnp.bfloat16)

    sums = [RowSum(links, here, *rs[k], rows) for k in range(4)]

    def send_state(block):
        sums[block].fill(
            lambda which: dot(state_cot[rows_at(block * window + which * rows, rows), :], wst[...], NT)
        )

    def send_token(block):
        sums[2 + block].fill(
            lambda which: dot(token_cot[rows_at(block * window + which * rows, rows), :], wtok[...], NT)
        )

    def mix_back(block):
        for k in range(4):
            branch_gathers[1 - block].ready(k)
            at = rows_at(block * window + ranks[k] * rows, rows)
            mixed_grad[at, :] = dot(branch_grad[at, :], wout[...], NN).astype(jnp.bfloat16)

    direct_1, moves_1 = gates_back(1, s1_ref[...], gstate_ref[...])
    for block in (1, 0):
        branch_gathers.append(RowGather(links, here, branch_grad, block * window, rows).start())
    gate_gather_1 = RowGather(links, here, gate_rows, window, rows).start()
    for ref in (tile_grads, key_grad, value_grad, skey_grad, svalue_grad):
        ref[...] = jnp.zeros(ref.shape, ref.dtype)
    bias_tiles(lines_ref, tiles, heads, 3 * TILE)
    mix_back(1)
    token_back(1)
    for moved in moves_1:
        moved.wait_recv()
    state_back(1)
    gather_cot(1)
    send_state(1)
    send_token(1)
    sums[1].forward()
    mix_back(0)
    state_norm_grad, gain_2 = rms_back(s1_ref[...], gains_ref[2:3, :], sums[1].finish())
    direct_0, moves_0 = gates_back(0, s0_ref[...], direct_1 + state_norm_grad)
    sums[3].forward()
    for k in range(1, 4):
        gate_gather_1.ready(k)
    gate_gather_0 = RowGather(links, here, gate_rows, 0, rows).start()
    token_back(0)
    for moved in moves_0:
        moved.wait_recv()
    state_back(0)
    gather_cot(0)
    send_state(0)
    send_token(0)
    past_grad[0] = key_grad[0:window, :].astype(past_grad.dtype)
    past_grad[1] = value_grad[0:window, :].astype(past_grad.dtype)
    sums[0].forward()
    sums[2].forward()
    wst_grad[...] = dot(snormed[...], state_cot[...], TN).astype(jnp.bfloat16)
    wtok_grad[...] = dot(normed[...], token_cot[...], TN).astype(jnp.bfloat16)
    wout_grad[...] = dot(branch_grad[...], mixed[...], TN).astype(jnp.bfloat16)
    for k in range(1, 4):
        gate_gather_0.ready(k)
    for c in range(3):
        gates_grad[:, c * width : (c + 1) * width] = dot(
            gate_rows[:, c * size : (c + 1) * size], smixed[...], TN
        ).astype(jnp.bfloat16)
    for head in range(heads):
        lines = tile_grads[head, 0:8, :]
        span = lines.shape[1]
        for group in range(1, TILE // 8):
            lines = lines + pltpu.roll(tile_grads[head, 8 * group : 8 * group + 8, :], span - 8 * group, 1)
        total = lines[0:1]
        for line in range(1, 8):
            total = total + pltpu.roll(lines[line : line + 1], span - line, 1)
        line_grad[head : head + 1, :] = total
    state_norm_grad, gain = rms_back(s0_ref[...], gains_ref[2:3, :], sums[0].finish())
    carried[...] = direct_0 + state_norm_grad
    gain_2 = gain_2 + gain
    gain_0 = 0.0
    for block in (1, 0):
        at = slice(block * rows, (block + 1) * rows)
        straight, gain = rms_back(
            x_ref[at, :].astype(jnp.float32), gains_ref[0:1, :], sums[2 + block].finish()
        )
        tokens_grad[at, :] = (middle_grad[at, :] + straight).astype(jnp.bfloat16)
        gain_0 = gain_0 + gain
    gain_grad[...] = jnp.concatenate(
        [gain_0, gain_2, jnp.zeros((6, gain_0.shape[1]), jnp.float32)], axis=0
    )
    links.close()


def run_kernel(body, outs, scratch, copies, collective, name, *operands):
    vmem = pl.BlockSpec(memory_space=pltpu.VMEM)
    return pl.pallas_call(
        body,
        out_shape=outs,
        in_specs=[vmem] * len(operands),
        out_specs=[vmem] * len(outs),
        scratch_shapes=scratch,
        compiler_params=pltpu.CompilerParams(
            collective_id=collective, has_side_effects=True, vmem_limit_bytes=VMEM_BYTES
        ),
        name=name,
    )(*operands)


def plane_kernel(*refs):
    count = (len(refs) - 2) // 3
    locals_, outs, inbox = refs[:count], refs[count : 2 * count], refs[2 * count : 3 * count]
    links = Links(refs[-2], refs[-1])
    here = place()
    planes, mates = here["planes"], here["plane_mates"]
    greet(mates[1:])
    moves = []
    for local, slots in zip(locals_, inbox):
        size = slots.shape[1]
        moves.append(
            [
                links.copy(local.at[rows_at(planes[k] * size, size)], slots.at[k - 1], mates[k])
                for k in (3, 1, 2)
            ]
        )
    for local, out, slots, copies in zip(locals_, outs, inbox, moves):
        for moved in copies:
            moved.wait_recv()
        size = slots.shape[1]
        total = local[rows_at(planes[0] * size, size), :].astype(jnp.float32)
        for k in range(3):
            total = total + slots[k].astype(jnp.float32)
        out[...] = total.astype(out.dtype)
    links.close()


def sems(count):
    return [pltpu.SemaphoreType.DMA((count,)), pltpu.SemaphoreType.DMA((count,))]


def turned(dp_size, levels, other):
    pairs = []
    for dp in range(dp_size):
        for level in range(levels):
            core = dp % 2
            half = 1 - core if other else core
            target = (dp - core + level % 2) * levels + 2 * half + level // 2
            pairs.append((dp * levels + level, target))
    return pairs


def grouped(
    tokens, carried_state, past_keys, fresh_start, valid_count, bucket_ids, grad_output, grad_state,
    norm_gains, token_qkv, token_out, bias_table, mlp_up, mlp_down, state_qkv, state_gates, initial_state,
):
    axes = ("dp", "state")
    dp_size, levels = lax.axis_size("dp"), lax.axis_size("state")
    there, across = turned(dp_size, levels, False), turned(dp_size, levels, True)
    back, back_across = [(b, a) for a, b in there], [(b, a) for a, b in across]
    go = lambda tensor: lax.ppermute(tensor, axes, there)
    go_across = lambda tensor: lax.ppermute(tensor, axes, across)
    home = lambda tensor: lax.ppermute(tensor, axes, back)
    home_across = lambda tensor: lax.ppermute(tensor, axes, back_across)
    core, level = lax.rem(lax.axis_index("dp"), 2), lax.axis_index("state")
    half = level // 2
    rank = 2 * lax.rem(level, 2) + core
    _, blocks, rows, size = tokens.shape
    window = rows * levels
    width = token_qkv.shape[2]
    heads = width // DH
    units = mlp_up.shape[1]
    model_rows = token_qkv.shape[0]
    low, full = jnp.bfloat16, jnp.float32

    initial_rows = lax.all_gather(initial_state, "dp", axis=1, tiled=True).astype(full)
    is_fresh = fresh_start[0] == 1
    s0 = go(jnp.where(is_fresh, initial_rows, carried_state[0]))
    facts = go(jnp.concatenate([fresh_start, valid_count]))
    item_fresh, item_valid = facts[0] == 1, facts[1]

    def column(weight):
        first, second = go(weight), go_across(weight)
        return jnp.where(
            half == 0, jnp.concatenate([first, second]), jnp.concatenate([second, first])
        )

    wst = column(state_qkv.reshape(model_rows, 3 * width))
    x = go(tokens[0].reshape(blocks * rows, size))
    wtok = column(token_qkv.reshape(model_rows, 3 * width))
    past = go(jnp.swapaxes(past_keys[0], 0, 1))
    table = go(bias_table)
    wout = column(token_out)
    wup = column(mlp_up)
    wdn = column(mlp_down)
    gates = state_gates.reshape(model_rows, 3 * size)
    gout = go(grad_output[0].reshape(blocks * rows, size))
    gstate = go(grad_state[0])

    one_hot = (bucket_ids[:, None] == jnp.arange(table.shape[0])[None, :]).astype(full)
    per_offset = jnp.dot(one_hot, table, precision=HIGHEST)
    lines = jnp.pad(
        per_offset[::-1].T, ((0, 0), (1, window - 1)), constant_values=NEGATIVE
    )
    places = jnp.arange(window)
    valid = jnp.concatenate(
        [jnp.broadcast_to(~item_fresh, (window,)), places < item_valid, window + places < item_valid]
    )
    mask = jnp.where(valid, 0.0, NEGATIVE).astype(full)[None, :]
    own_places = rank * rows + jnp.arange(rows)
    rowmask = jnp.concatenate([own_places < item_valid, window + own_places < item_valid])
    rowmask = rowmask.astype(full)[:, None]

    shape = jax.ShapeDtypeStruct
    vmem = pltpu.VMEM
    rs = row_sum_scratch(rows, size)
    lanes = 4 * window // 2
    (
        normed, snormed, queries, keys, values, sqkv, lse_token, lse_state, mixed, smixed,
        middle, gate_values, s1, s2, branch_sum, wst_all, wtok_all, wout_all, gates_all, wup_all, wdn_all,
    ) = run_kernel(
        attention_kernel,
        [
            shape((2 * window, size), low),
            shape((2 * window, size), low),
            shape((2 * window, width), low),
            shape((3 * window, width), low),
            shape((3 * window, width), low),
            shape((2 * window, 3 * width), low),
            shape((2 * window, heads), full),
            shape((2 * window, heads), full),
            shape((2 * window, width), low),
            shape((2 * window, width), low),
            shape((2 * rows, size), full),
            shape((2 * rows, 3 * size), full),
            shape((rows, size), full),
            shape((rows, size), full),
            shape((8, size), full),
            shape((size, 3 * width), low),
            shape((size, 3 * width), low),
            shape((size, width), low),
            shape((size, 3 * size), low),
            shape((size, units), low),
            shape((size, units), low),
        ],
        [vmem((heads, TILE, 3 * TILE), full), vmem((rows, size), low), vmem((rows, size), low)]
        + rs * 2
        + sems(64),
        0,
        0,
        "attention",
        x, s0, past, mask, rowmask, lines, norm_gains, wst, wtok, wout, gates, wup, wdn,
    )
    block_out, middle_grad, wup_grad, wdn_grad, gain_middle, feed_sums = run_kernel(
        feed_kernel,
        [
            shape((2 * rows, size), low),
            shape((2 * rows, size), full),
            shape((size, units), low),
            shape((size, units), low),
            shape((8, size), full),
            shape((8, size), full),
        ],
        [
            vmem((2 * window, size), low),
            vmem((2 * window, size), low),
            vmem((2 * window, units), full),
            vmem((2 * window, units), low),
            vmem((2 * window, units), low),
        ]
        + rs * 4
        + sems(32),
        0,
        1,
        "feed",
        middle, gout, norm_gains, rowmask, wup_all, wdn_all,
    )
    (
        tokens_grad, carried, past_grad, gain_ends, line_grad, wst_grad, wtok_grad, wout_grad, gates_grad,
    ) = run_kernel(
        cotangent_kernel,
        [
            shape((2 * rows, size), low),
            shape((rows, size), full),
            shape((2, window, width), low),
            shape((8, size), full),
            shape((heads, 4 * TILE), full),
            shape((size, 3 * width), low),
            shape((size, 3 * width), low),
            shape((size, width), low),
            shape((size, 3 * width), low),
        ],
        [
            vmem((heads, TILE, 3 * TILE), full),
            vmem((heads, TILE, 4 * TILE), full),
            vmem((2 * window, size), low),
            vmem((2 * window, width), low),
            vmem((2 * window, 3 * size), low),
            vmem((2 * window, width), low),
            vmem((3 * window, width), full),
            vmem((3 * window, width), full),
            vmem((2 * window, width), full),
            vmem((2 * window, width), full),
            vmem((window, width), full),
            vmem((window, width), full),
            vmem((2 * window, 3 * width), low),
            vmem((2 * window, 3 * width), low),
        ]
        + rs * 4
        + sems(48)
        + [vmem((rows, size), low), vmem((rows, size), low)],
        0,
        2,
        "cotangent",
        middle_grad, gstate, x, s0, s1, gate_values, norm_gains, mask, lines,
        normed, snormed, queries, keys, values, sqkv, lse_token, lse_state, mixed, smixed,
        wst_all, wtok_all, wout_all, gates_all,
    )
    partials = [wup_grad, wdn_grad, wtok_grad, wst_grad, gates_grad, wout_grad]
    quarter = size // 4
    plane_sums = run_kernel(
        plane_kernel,
        [shape((quarter, part.shape[1]), low) for part in partials],
        [vmem((3, quarter, part.shape[1]), low) for part in partials] + sems(3 * len(partials)),
        0,
        3,
        "plane",
        *partials,
    )

    def settle(part):
        first, second = part[:model_rows], part[model_rows:]
        straight = home(jnp.where(half == 0, first, second))
        crossed = home_across(jnp.where(half == 0, second, first))
        return straight.astype(full) + crossed.astype(full)

    up_out, down_out, qkv_out, sqkv_out, gates_out, out_out = [settle(part) for part in plane_sums]
    gates_out = lax.all_to_all(
        gates_out.reshape(model_rows, 3, 1, width).astype(low), "state", split_axis=0, concat_axis=2, tiled=True
    ).astype(full)
    gates_out = gates_out.reshape(model_rows // levels, 3, size)

    table_part = jnp.dot(one_hot.T, line_grad[:, 1 : window + 1][:, ::-1].T, precision=HIGHEST)
    in_place = (jnp.arange(levels) == rank).astype(full)
    table_wide = (table_part[:, None, :] * in_place[None, :, None]).reshape(-1)
    sums = jnp.stack(
        [jnp.sum(feed_sums[0]), jnp.sum(branch_sum[0]), jnp.sum(feed_sums[1]), jnp.sum(rowmask)]
    )
    packed = jnp.concatenate(
        [gain_ends[0], gain_middle[0], gain_ends[1], table_wide, sums, jnp.zeros((124,), full)]
    )
    packed = lax.psum(packed, axes)
    gains_all = packed[: 3 * size].reshape(3, size)
    share = size // (dp_size * levels)
    dp_at = lax.axis_index("dp")
    gains_out = lax.dynamic_slice_in_dim(gains_all, (dp_at * levels + level) * share, share, 1)
    table_all = packed[3 * size : 3 * size + table_wide.shape[0]].reshape(-1, levels * heads)
    table_rows = table_all.shape[0] // dp_size
    table_out = lax.dynamic_slice(table_all, (dp_at * table_rows, level * heads), (table_rows, heads))
    sums = packed[3 * size + table_wide.shape[0] :][:4]
    rms_stats = jnp.sqrt(sums[:3] / sums[3])

    state_out = home(s2.astype(low)).astype(full)
    carried_home = home(carried.astype(low)).astype(full)
    block_home = home(block_out).reshape(1, blocks, rows, size)
    tokens_home = home(tokens_grad).reshape(1, blocks, rows, size)
    past_home = jnp.swapaxes(home(past_grad).astype(full), 0, 1)
    carried_grad = jnp.where(is_fresh, 0.0, carried_home)
    initial_part = jnp.where(is_fresh, carried_home, 0.0).astype(low)
    initial_grad = lax.psum_scatter(initial_part, "dp", scatter_dimension=1, tiled=True).astype(full)
    return (
        block_home,
        state_out[None],
        rms_stats,
        tokens_home,
        carried_grad[None],
        past_home[None],
        gains_out,
        qkv_out.reshape(model_rows, 3, width),
        out_out,
        table_out,
        up_out,
        down_out,
        sqkv_out.reshape(model_rows, 3, width),
        gates_out,
        initial_grad,
    )


def solution(mesh):
    in_specs = (
        P("dp", None, "state", None),
        P("dp", "state", None),
        P("dp", None, None, "state"),
        P("dp"),
        P("dp"),
        P(),
        P("dp", None, "state", None),
        P("dp", "state", None),
        P(),
        P("dp", None, "state"),
        P("dp", "state"),
        P(None, "state"),
        P("dp", "state"),
        P("dp", "state"),
        P("dp", None, "state"),
        P("dp", None, None),
        P("state", "dp"),
    )
    out_specs = (
        P("dp", None, "state", None),
        P("dp", "state", None),
        P(),
        P("dp", None, "state", None),
        P("dp", "state", None),
        P("dp", None, None, "state"),
        P(None, ("dp", "state")),
        P("dp", None, "state"),
        P("dp", "state"),
        P("dp", "state"),
        P("dp", "state"),
        P("dp", "state"),
        P("dp", None, "state"),
        P(("dp", "state"), None, None),
        P("state", "dp"),
    )
    body = grouped if dict(mesh.shape) == {"dp": 8, "state": 4} else shards
    return jax.shard_map(body, mesh=mesh, in_specs=in_specs, out_specs=out_specs, check_vma=False)
```

```python
import math

import jax
import jax.numpy as jnp
from jax import lax
from jax.experimental import pallas as pl
from jax.experimental.pallas import tpu as pltpu
from jax.sharding import PartitionSpec as P

DH = 128


EPS = 1e-06
NEGATIVE = -1e30
HIGHEST = lax.Precision.HIGHEST


def rms_norm(tensor, gains_row):
    return tensor * lax.rsqrt(jnp.mean(tensor * tensor, axis=-1, keepdims=True) + EPS) * gains_row


def norm_back(tensor, gains_row, cotangent):
    return jax.vjp(rms_norm, tensor, gains_row)[1](cotangent)


def smooth_gelu(tensor):
    return jax.nn.gelu(tensor, approximate=True)


def renew_state(state_now, gate_values):
    return state_now * jax.nn.sigmoid(gate_values[2] + 1.0) + jnp.tanh(
        gate_values[0]
    ) * jax.nn.sigmoid(gate_values[1] - 1.0)


def split_heads(tensor):
    return tensor.reshape(tensor.shape[0], tensor.shape[1], tensor.shape[2] // DH, DH)


def merge_heads(tensor):
    return tensor.reshape(tensor.shape[0], tensor.shape[1], tensor.shape[2] * DH)


def score_grid(queries, key_rows, bias_add, allowed):
    scores = jnp.einsum(
        "iqhd,ikhd->ihqk", queries, key_rows, preferred_element_type=jnp.float32
    ) / math.sqrt(DH)
    if bias_add is not None:
        scores = scores + bias_add[None]
    return jnp.where(allowed[:, None], scores, NEGATIVE)


def attend_forward(queries, key_rows, values, bias_add, allowed):
    scores = score_grid(queries, key_rows, bias_add, allowed)
    row_max = jnp.max(scores, axis=-1, keepdims=True)
    weights = jnp.exp(scores - row_max)
    row_total = jnp.sum(weights, axis=-1, keepdims=True)
    attn_probs = (weights / row_total).astype(jnp.bfloat16)
    mixed_heads = jnp.einsum(
        "ihqk,ikhd->iqhd", attn_probs, values, preferred_element_type=jnp.float32
    )
    return (merge_heads(mixed_heads.astype(jnp.bfloat16)), row_max + jnp.log(row_total))


def attention_backward_pass(queries, key_rows, values, bias_add, allowed, log_total, grad_mixed):
    scores = score_grid(queries, key_rows, bias_add, allowed)
    attn_probs = jnp.exp(scores - log_total)
    probs_grad = jnp.einsum(
        "iqhd,ikhd->ihqk", grad_mixed, values, preferred_element_type=jnp.float32
    )
    scores_grad = attn_probs * (
        probs_grad - jnp.sum(attn_probs * probs_grad, axis=-1, keepdims=True)
    )
    scores_grad = scores_grad.astype(jnp.bfloat16)
    values_grad = jnp.einsum(
        "ihqk,iqhd->ikhd",
        attn_probs.astype(jnp.bfloat16),
        grad_mixed,
        preferred_element_type=jnp.float32,
    )
    queries_grad = jnp.einsum(
        "ihqk,ikhd->iqhd", scores_grad, key_rows, preferred_element_type=jnp.float32
    ) / math.sqrt(DH)
    keys_grad = jnp.einsum(
        "ihqk,iqhd->ikhd", scores_grad, queries, preferred_element_type=jnp.float32
    ) / math.sqrt(DH)
    return (
        merge_heads(queries_grad),
        merge_heads(keys_grad),
        merge_heads(values_grad),
        scores_grad,
    )


def diagonal_sums(grid_values):
    num_heads, num_rows, num_cols = grid_values.shape
    flat = grid_values.reshape(num_heads, num_rows * num_cols)
    flat = jnp.pad(flat, ((0, 0), (0, num_rows)))
    sums = jnp.sum(flat.reshape(num_heads, num_rows, num_cols + 1), axis=1)
    return sums[:, num_rows:0:-1]


def toeplitz_grid(per_offset, num_rows):
    num_cols = 2 * num_rows
    line = jnp.pad(per_offset[::-1].T, ((0, 0), (1, num_cols - num_rows)))
    flat = jnp.tile(line, (1, num_rows))[:, : num_rows * num_cols]
    return flat.reshape(-1, num_rows, num_cols)


def sum_rows(partial_value):
    return lax.psum_scatter(
        partial_value.astype(jnp.bfloat16), "state", scatter_dimension=1, tiled=True
    ).astype(jnp.float32)


def whole_rows(partial_value):
    return lax.all_gather(partial_value, "state", axis=1, tiled=True)


def shards(
    tokens,
    carried_state,
    past_keys,
    fresh_start,
    valid_count,
    bucket_ids,
    grad_output,
    grad_state,
    norm_gains,
    token_qkv,
    token_out,
    bias_table,
    mlp_up,
    mlp_down,
    state_qkv,
    state_gates,
    initial_state,
):
    item_count, blocks, share_rows, model_width = tokens.shape
    groups = lax.axis_size("state")
    state_rank = lax.axis_index("state")
    window_width = share_rows * groups
    vector_rows = carried_state.shape[1] * groups
    local_width = token_qkv.shape[2]
    qkv_full, out_full, up_full, down_full, sqkv_full, gates_full, initial_full = (
        lax.all_gather(token_qkv, "dp", axis=0, tiled=True),
        lax.all_gather(token_out, "dp", axis=0, tiled=True),
        lax.all_gather(mlp_up, "dp", axis=0, tiled=True),
        lax.all_gather(mlp_down, "dp", axis=0, tiled=True),
        lax.all_gather(state_qkv, "dp", axis=0, tiled=True),
        lax.all_gather(state_gates, "dp", axis=0, tiled=True),
        lax.all_gather(initial_state, "dp", axis=1, tiled=True),
    )
    gates_used = lax.dynamic_slice_in_dim(gates_full, state_rank * local_width, local_width, 2)
    one_hot = (bucket_ids[:, None] == jnp.arange(bias_table.shape[0])[None, :]).astype(jnp.float32)
    per_offset = jnp.dot(one_hot, bias_table, precision=HIGHEST)
    query_pos = jnp.arange(window_width)[:, None]
    key_pos = jnp.arange(2 * window_width)[None, :]
    offset = window_width + query_pos - key_pos
    inside = (offset >= 0) & (offset < window_width)
    bias_grid = toeplitz_grid(per_offset, window_width)
    token_bias = jnp.pad(bias_grid, ((0, 0), (0, 0), (0, vector_rows)))
    is_fresh = fresh_start == 1
    state_now = jnp.where(
        is_fresh[:, None, None], initial_full.astype(jnp.float32)[None], carried_state
    )
    past_key = past_keys[:, :, 0]
    past_value = past_keys[:, :, 1]
    past_ok = jnp.broadcast_to(~is_fresh[:, None], (item_count, window_width))
    gains_token, gains_middle, gains_state = (norm_gains[0], norm_gains[1], norm_gains[2])
    share_pos = state_rank * share_rows + jnp.arange(share_rows)
    square_sums = jnp.zeros((3,), jnp.float32)
    valid_total = jnp.zeros((), jnp.float32)
    kept_values = []
    results = []
    for block_at in range(blocks):
        token_ok = (
            block_at * window_width + jnp.arange(window_width)[None, :] < valid_count[:, None]
        )
        inputs = tokens[:, block_at].astype(jnp.float32)
        normed, state_normed = (
            lax.all_gather(
                rms_norm(inputs, gains_token).astype(jnp.bfloat16), "state", axis=1, tiled=True
            ),
            lax.all_gather(
                rms_norm(state_now, gains_state).astype(jnp.bfloat16), "state", axis=1, tiled=True
            ),
        )
        project = jnp.einsum(
            "iwd,dch->ciwh", normed, qkv_full, preferred_element_type=jnp.float32
        ).astype(jnp.bfloat16)
        state_project = jnp.einsum(
            "ind,dch->cinh", state_normed, sqkv_full, preferred_element_type=jnp.float32
        ).astype(jnp.bfloat16)
        token_keys = jnp.concatenate([past_key, project[1], state_project[1]], axis=1)
        token_values = jnp.concatenate([past_value, project[2], state_project[2]], axis=1)
        window_ok = inside[None] & jnp.concatenate([past_ok, token_ok], axis=1)[:, None, :]
        token_allowed = jnp.concatenate(
            [window_ok, jnp.ones((item_count, window_width, vector_rows), jnp.bool_)], axis=2
        )
        mixed_heads, token_total = attend_forward(
            split_heads(project[0]),
            split_heads(token_keys),
            split_heads(token_values),
            token_bias,
            token_allowed,
        )
        branch = sum_rows(
            jnp.einsum("iwh,dh->iwd", mixed_heads, out_full, preferred_element_type=jnp.float32)
        )
        middle = inputs + branch
        middle_normed = lax.all_gather(
            rms_norm(middle, gains_middle).astype(jnp.bfloat16), "state", axis=1, tiled=True
        )
        up_values = jnp.einsum(
            "iwd,df->iwf", middle_normed, up_full, preferred_element_type=jnp.float32
        )
        hidden = smooth_gelu(up_values).astype(jnp.bfloat16)
        feed_out = sum_rows(
            jnp.einsum("iwf,df->iwd", hidden, down_full, preferred_element_type=jnp.float32)
        )
        result = middle + feed_out
        results.append(result.astype(jnp.bfloat16))
        share_ok = (block_at * window_width + share_pos[None, :] < valid_count[:, None]).astype(
            jnp.float32
        )[:, :, None]
        square_sums = square_sums + jnp.stack(
            [
                jnp.sum(share_ok * result * result),
                jnp.sum(share_ok * branch * branch),
                jnp.sum(share_ok * feed_out * feed_out),
            ]
        )
        valid_total = valid_total + jnp.sum(share_ok)
        state_keys = jnp.concatenate([state_project[1], project[1]], axis=1)
        state_values = jnp.concatenate([state_project[2], project[2]], axis=1)
        state_allowed = jnp.concatenate(
            [
                jnp.ones((item_count, vector_rows, vector_rows), jnp.bool_),
                jnp.broadcast_to(token_ok[:, None, :], (item_count, vector_rows, window_width)),
            ],
            axis=2,
        )
        state_mixed, state_total = attend_forward(
            split_heads(state_project[0]),
            split_heads(state_keys),
            split_heads(state_values),
            None,
            state_allowed,
        )
        gate_source = state_mixed
        gate_values = lax.psum_scatter(
            jnp.einsum(
                "inh,dch->cind", state_mixed, gates_used, preferred_element_type=jnp.float32
            ).astype(jnp.bfloat16),
            "state",
            scatter_dimension=2,
            tiled=True,
        ).astype(jnp.float32)
        kept_values.append(
            (
                inputs,
                normed,
                state_normed,
                project,
                state_project,
                token_keys,
                token_values,
                token_allowed,
                mixed_heads,
                token_total,
                middle,
                middle_normed,
                up_values,
                hidden,
                state_keys,
                state_values,
                state_allowed,
                state_total,
                gate_source,
                gate_values,
                state_now,
            )
        )
        state_now = renew_state(state_now, gate_values)
        past_key, past_value, past_ok = (project[1], project[2], token_ok)
    square_sums, valid_total = lax.psum((square_sums, valid_total), ("dp", "state"))
    rms_stats = jnp.sqrt(square_sums / valid_total)
    qkv_grad = jnp.zeros(qkv_full.shape, jnp.float32)
    out_grad = jnp.zeros(out_full.shape, jnp.float32)
    up_grad = jnp.zeros(up_full.shape, jnp.float32)
    down_grad = jnp.zeros(down_full.shape, jnp.float32)
    sqkv_grad = jnp.zeros(sqkv_full.shape, jnp.float32)
    gate_grad = jnp.zeros(gates_used.shape, jnp.float32)
    bias_grad = jnp.zeros(bias_grid.shape, jnp.float32)
    gain_token_grad = jnp.zeros((model_width,), jnp.float32)
    gain_middle_grad = jnp.zeros((model_width,), jnp.float32)
    gain_state_grad = jnp.zeros((model_width,), jnp.float32)
    state_grad = grad_state
    carried_key_rows = jnp.zeros(past_keys[:, :, 0].shape, jnp.float32)
    carry_value = jnp.zeros(past_keys[:, :, 0].shape, jnp.float32)
    token_grads = [None] * blocks
    for block_at in reversed(range(blocks)):
        (
            inputs,
            normed,
            state_normed,
            project,
            state_project,
            token_keys,
            token_values,
            token_allowed,
            mixed_heads,
            token_total,
            middle,
            middle_normed,
            up_values,
            hidden,
            state_keys,
            state_values,
            state_allowed,
            state_total,
            gate_source,
            gate_values,
            state_before,
        ) = kept_values[block_at]
        direct_grad, gates_grad = jax.vjp(renew_state, state_before, gate_values)[1](state_grad)
        gates_low = gates_grad.astype(jnp.bfloat16)
        gates_rows = lax.all_gather(gates_low, "state", axis=2, tiled=True)
        state_mixed_grad = jnp.einsum(
            "cind,dch->inh", gates_rows, gates_used, preferred_element_type=jnp.float32
        ).astype(jnp.bfloat16)
        gate_grad = gate_grad + jnp.einsum(
            "inh,cind->dch", gate_source, gates_rows, preferred_element_type=jnp.float32
        )
        state_query_gradient, state_keys_gradient, state_values_gradient, discarded_output = (
            attention_backward_pass(
                split_heads(state_project[0]),
                split_heads(state_keys),
                split_heads(state_values),
                None,
                state_allowed,
                state_total,
                split_heads(state_mixed_grad),
            )
        )
        out_share = grad_output[:, block_at]
        out_whole = whole_rows(out_share)
        down_grad = down_grad + jnp.einsum(
            "iwf,iwd->df", hidden, out_whole, preferred_element_type=jnp.float32
        )
        hidden_grad = jnp.einsum(
            "iwd,df->iwf", out_whole, down_full, preferred_element_type=jnp.float32
        )
        up_values_grad = jax.vjp(smooth_gelu, up_values)[1](hidden_grad)[0].astype(jnp.bfloat16)
        up_grad = up_grad + jnp.einsum(
            "iwd,iwf->df", middle_normed, up_values_grad, preferred_element_type=jnp.float32
        )
        middle_normed_grad = lax.psum_scatter(
            jnp.einsum(
                "iwf,df->iwd", up_values_grad, up_full, preferred_element_type=jnp.float32
            ).astype(jnp.bfloat16),
            "state",
            scatter_dimension=1,
            tiled=True,
        ).astype(jnp.float32)
        middle_grad, gain_part = norm_back(middle, gains_middle, middle_normed_grad)
        middle_grad = out_share.astype(jnp.float32) + middle_grad
        gain_middle_grad = gain_middle_grad + gain_part
        branch_whole = whole_rows(middle_grad.astype(jnp.bfloat16))
        out_grad = out_grad + jnp.einsum(
            "iwh,iwd->dh", mixed_heads, branch_whole, preferred_element_type=jnp.float32
        )
        mixed_grad = jnp.einsum(
            "iwd,dh->iwh", branch_whole, out_full, preferred_element_type=jnp.float32
        ).astype(jnp.bfloat16)
        query_grad, token_keys_gradient, tvalues_grad, scores_grad = attention_backward_pass(
            split_heads(project[0]),
            split_heads(token_keys),
            split_heads(token_values),
            token_bias,
            token_allowed,
            token_total,
            split_heads(mixed_grad),
        )
        bias_grad = bias_grad + jnp.sum(
            scores_grad[:, :, :, : 2 * window_width].astype(jnp.float32), axis=0
        )
        key_gradient_rows = (
            token_keys_gradient[:, window_width : 2 * window_width]
            + state_keys_gradient[:, vector_rows:]
            + carried_key_rows
        )
        value_grad = (
            tvalues_grad[:, window_width : 2 * window_width]
            + state_values_gradient[:, vector_rows:]
            + carry_value
        )
        state_key_gradient = (
            token_keys_gradient[:, 2 * window_width :] + state_keys_gradient[:, :vector_rows]
        )
        state_value_gradient = (
            tvalues_grad[:, 2 * window_width :] + state_values_gradient[:, :vector_rows]
        )
        project_grad = jnp.stack([query_grad, key_gradient_rows, value_grad]).astype(jnp.bfloat16)
        state_projection_gradient = jnp.stack(
            [state_query_gradient, state_key_gradient, state_value_gradient]
        ).astype(jnp.bfloat16)
        qkv_grad = qkv_grad + jnp.einsum(
            "iwd,ciwh->dch", normed, project_grad, preferred_element_type=jnp.float32
        )
        sqkv_grad = sqkv_grad + jnp.einsum(
            "ind,cinh->dch",
            state_normed,
            state_projection_gradient,
            preferred_element_type=jnp.float32,
        )
        normed_grad, state_normed_grad = (
            lax.psum_scatter(
                jnp.einsum(
                    "ciwh,dch->iwd", project_grad, qkv_full, preferred_element_type=jnp.float32
                ).astype(jnp.bfloat16),
                "state",
                scatter_dimension=1,
                tiled=True,
            ).astype(jnp.float32),
            lax.psum_scatter(
                jnp.einsum(
                    "cinh,dch->ind",
                    state_projection_gradient,
                    sqkv_full,
                    preferred_element_type=jnp.float32,
                ).astype(jnp.bfloat16),
                "state",
                scatter_dimension=1,
                tiled=True,
            ).astype(jnp.float32),
        )
        input_grad, gain_part = norm_back(inputs, gains_token, normed_grad)
        gain_token_grad = gain_token_grad + gain_part
        token_grads[block_at] = (middle_grad + input_grad).astype(jnp.bfloat16)
        state_norm_grad, gain_part = norm_back(state_before, gains_state, state_normed_grad)
        gain_state_grad = gain_state_grad + gain_part
        state_grad = direct_grad + state_norm_grad
        carried_key_rows = token_keys_gradient[:, :window_width]
        carry_value = tvalues_grad[:, :window_width]
    carried_grad = jnp.where(is_fresh[:, None, None], 0.0, state_grad)
    initial_part = jnp.sum(jnp.where(is_fresh[:, None, None], state_grad, 0.0), axis=0)
    past_grad = jnp.stack([carried_key_rows, carry_value], axis=2)
    table_part = jnp.dot(one_hot.T, diagonal_sums(bias_grad).T, precision=HIGHEST)
    gain_columns = jnp.stack([gain_token_grad, gain_middle_grad, gain_state_grad], axis=1)
    summed = (
        lax.psum_scatter(
            qkv_grad.astype(jnp.bfloat16), "dp", scatter_dimension=0, tiled=True
        ).astype(jnp.float32),
        lax.psum_scatter(
            out_grad.astype(jnp.bfloat16), "dp", scatter_dimension=0, tiled=True
        ).astype(jnp.float32),
        lax.psum_scatter(
            table_part.astype(jnp.bfloat16), "dp", scatter_dimension=0, tiled=True
        ).astype(jnp.float32),
        lax.psum_scatter(
            up_grad.astype(jnp.bfloat16), "dp", scatter_dimension=0, tiled=True
        ).astype(jnp.float32),
        lax.psum_scatter(
            down_grad.astype(jnp.bfloat16), "dp", scatter_dimension=0, tiled=True
        ).astype(jnp.float32),
        lax.psum_scatter(
            sqkv_grad.astype(jnp.bfloat16), "dp", scatter_dimension=0, tiled=True
        ).astype(jnp.float32),
        lax.psum_scatter(
            initial_part.astype(jnp.bfloat16), "dp", scatter_dimension=1, tiled=True
        ).astype(jnp.float32),
        lax.psum_scatter(
            gate_grad.astype(jnp.bfloat16), "dp", scatter_dimension=0, tiled=True
        ).astype(jnp.float32),
        lax.psum_scatter(
            gain_columns.astype(jnp.bfloat16), "dp", scatter_dimension=0, tiled=True
        ).astype(jnp.float32),
    )
    gate_pieces, gain_pieces = (
        lax.all_to_all(
            summed[7][:, :, None, :].astype(jnp.bfloat16),
            "state",
            split_axis=0,
            concat_axis=2,
            tiled=True,
        ).astype(jnp.float32),
        lax.all_to_all(
            summed[8][:, :, None, None].astype(jnp.bfloat16),
            "state",
            split_axis=0,
            concat_axis=2,
            tiled=True,
        ).astype(jnp.float32),
    )
    gains_grad = jnp.sum(gain_pieces, axis=(2, 3)).T
    gates_grad_out = gate_pieces.reshape(
        gate_pieces.shape[0], gate_pieces.shape[1], gate_pieces.shape[2] * gate_pieces.shape[3]
    )
    return (
        jnp.stack(results, axis=1),
        state_now,
        rms_stats,
        jnp.stack(token_grads, axis=1),
        carried_grad,
        past_grad,
        gains_grad,
        summed[0],
        summed[1],
        summed[2],
        summed[3],
        summed[4],
        summed[5],
        gates_grad_out,
        summed[6],
    )


MESH = pl.DeviceIdType.MESH
NN = (((1,), (0,)), ((), ()))
NT = (((1,), (1,)), ((), ()))
TN = (((0,), (0,)), ((), ()))
VMEM_BYTES = 63 * 2**20


class Place:
    def __init__(self):
        chip_core, level = lax.axis_index("dp"), lax.axis_index("state")
        core, low = lax.rem(chip_core, 2), lax.rem(level, 2)
        x, y = lax.rem(chip_core // 2, 2), chip_core // 4
        flip = lambda bit: 1 - 2 * bit
        self.dp, self.core, self.level, self.half = chip_core, core, level, level // 2
        self.rank = 2 * low + core
        self.ranks = [self.rank, 2 * low + 1 - core, 2 * (1 - low) + core, 2 * (1 - low) + 1 - core]
        self.mates = [
            None,
            (chip_core + flip(core), level),
            (chip_core, level + flip(low)),
            (chip_core + flip(core), level + flip(low)),
        ]
        self.planes = [2 * y + x, 2 * y + 1 - x, 2 * (1 - y) + x, 2 * (1 - y) + 1 - x]
        self.plane_mates = [
            None,
            (chip_core + 2 * flip(x), level),
            (chip_core + 4 * flip(y), level),
            (chip_core + 2 * flip(x) + 4 * flip(y), level),
        ]
        first = chip_core - core
        self.there = (first + low, 2 * core + self.half)
        self.across = (first + low, 2 * (1 - core) + self.half)
        self.from_there = (first + self.half, 2 * low + core)
        self.from_across = (first + 1 - self.half, 2 * low + core)
        self.stays = (core == low) & (self.half == core)


def rows_at(start, size, step=128):
    return pl.ds(pl.multiple_of(start, step), size)


class Links:
    def __init__(self, send_sems, recv_sems):
        self.send_sems, self.recv_sems = send_sems, recv_sems
        self.used = 0
        self.open_sends = []
        self.open_turns = []

    def plan(self, source, target, device):
        at = self.used
        self.used += 1
        return pltpu.make_async_remote_copy(
            src_ref=source,
            dst_ref=target,
            send_sem=self.send_sems.at[at],
            recv_sem=self.recv_sems.at[at],
            device_id=device,
            device_id_type=MESH,
        )

    def copy(self, source, target, device):
        moved = self.plan(source, target, device)
        moved.start()
        self.open_sends.append(moved)
        return moved

    def sent(self, moved):
        self.open_sends = [other for other in self.open_sends if other is not moved]
        moved.wait_send()

    def close(self):
        for moved in self.open_sends:
            moved.wait_send()
        for turn in self.open_turns:
            turn.sent()
        self.open_sends, self.open_turns = [], []


def greet(devices, turned=None):
    barrier = pltpu.get_barrier_semaphore()
    for device in devices:
        pl.semaphore_signal(barrier, inc=1, device_id=device, device_id_type=MESH)
    if turned is None:
        pl.semaphore_wait(barrier, len(devices))
    else:
        moves = jnp.logical_not(turned.stays)

        @pl.when(moves)
        def _():
            pl.semaphore_signal(barrier, inc=1, device_id=turned.from_there, device_id_type=MESH)

        pl.semaphore_wait(barrier, len(devices) + moves.astype(jnp.int32))


class Turn:
    def __init__(self, links, here, source, target, device):
        self.stays = here.stays
        self.moved = links.plan(source, target, device)
        self.kept = pltpu.make_async_copy(source, target, links.recv_sems.at[links.used - 1])
        links.open_turns.append(self)

        @pl.when(jnp.logical_not(self.stays))
        def _():
            self.moved.start()

        @pl.when(self.stays)
        def _():
            self.kept.start()

    def arrived(self):
        @pl.when(jnp.logical_not(self.stays))
        def _():
            self.moved.wait_recv()

        @pl.when(self.stays)
        def _():
            self.kept.wait()

    def sent(self):
        @pl.when(jnp.logical_not(self.stays))
        def _():
            self.moved.wait_send()


class WeightGather:
    def __init__(self, links, here, local, full):
        self.links, self.here, self.local, self.full = links, here, local, full
        self.rows = local.shape[0]

    def enter(self):
        target = self.full.at[rows_at(self.here.dp * self.rows, self.rows)]
        self.turn = Turn(self.links, self.here, self.local, target, self.here.there)
        self.cross = self.links.copy(self.local, target, self.here.across)
        return self

    def block(self, k):
        return self.full.at[rows_at(self.here.planes[k] * 2 * self.rows, 2 * self.rows)]

    def half(self, k, which):
        start = self.here.planes[k] * 2 * self.rows + which * self.rows
        return self.full.at[rows_at(start, self.rows)]

    def spread(self):
        self.turn.arrived()
        self.cross.wait_recv()
        mates = self.here.plane_mates
        self.over_x = self.links.copy(self.block(0), self.block(0), mates[1])
        self.over_y = self.links.copy(self.block(0), self.block(0), mates[2])

    def forward(self):
        mates = self.here.plane_mates
        self.over_x.wait_recv()
        self.corner_0 = self.links.copy(self.half(1, 0), self.half(1, 0), mates[2])
        self.over_y.wait_recv()
        self.corner_1 = self.links.copy(self.half(2, 1), self.half(2, 1), mates[1])

    def finish(self):
        self.corner_0.wait_recv()
        self.corner_1.wait_recv()


class GateGather:
    def __init__(self, links, here, local, full, sem):
        self.links, self.here, self.local, self.full, self.sem = links, here, local, full, sem
        self.rows = local.shape[0]

    def block(self, k):
        start = (2 * self.here.planes[k] + self.here.core) * self.rows
        return self.full.at[rows_at(start, self.rows)]

    def part(self, k, which):
        size = self.rows // 2
        start = (2 * self.here.planes[k] + self.here.core) * self.rows + which * size
        return self.full.at[rows_at(start, size, 64)]

    def spread(self):
        mates, sibling = self.here.plane_mates, self.here.mates[1]
        self.over_x = self.links.copy(self.local, self.block(0), mates[1])
        self.over_y = self.links.copy(self.local, self.block(0), mates[2])
        self.near = [self.links.copy(self.local, self.block(0), sibling)]
        self.kept = pltpu.make_async_copy(self.local, self.block(0), self.sem)
        self.kept.start()

    def forward(self):
        mates, sibling = self.here.plane_mates, self.here.mates[1]
        self.over_x.wait_recv()
        self.corner_0 = self.links.copy(self.part(1, 0), self.part(1, 0), mates[2])
        self.near.append(self.links.copy(self.block(1), self.block(1), sibling))
        self.over_y.wait_recv()
        self.corner_1 = self.links.copy(self.part(2, 1), self.part(2, 1), mates[1])
        self.near.append(self.links.copy(self.block(2), self.block(2), sibling))

    def last(self):
        self.corner_0.wait_recv()
        self.corner_1.wait_recv()
        self.near.append(self.links.copy(self.block(3), self.block(3), self.here.mates[1]))

    def finish(self):
        self.kept.wait()
        for moved in self.near:
            moved.wait_recv()


class RowGather:
    def __init__(self, links, here, ref, base, rows):
        self.links, self.here, self.ref, self.base, self.rows = links, here, ref, base, rows

    def part(self, k):
        return self.ref.at[rows_at(self.base + self.here.ranks[k] * self.rows, self.rows)]

    def start(self):
        own, mates = self.part(0), self.here.mates
        self.far = self.links.copy(own, own, mates[2])
        self.near = self.links.copy(own, own, mates[1])
        return self

    def ready(self, k):
        if k == 1:
            self.near.wait_recv()
        elif k == 2:
            self.far.wait_recv()
            block = self.part(2)
            self.last = self.links.copy(block, block, self.here.mates[1])
        elif k == 3:
            self.last.wait_recv()

    def sent(self):
        for moved in (self.far, self.near, self.last):
            self.links.sent(moved)


class RowSum:
    def __init__(self, links, here, stage, near_in, far_out, far_in, rows):
        self.links, self.here, self.rows = links, here, rows
        self.stage, self.near_in, self.far_out, self.far_in = stage, near_in, far_out, far_in

    def part(self, k):
        return self.stage.at[rows_at(self.here.ranks[k] * self.rows, self.rows)]

    def fill(self, make_rows):
        sibling = self.here.mates[1]
        for k, slot in ((3, 0), (1, 1)):
            self.part(k)[...] = make_rows(self.here.ranks[k]).astype(jnp.bfloat16)
            moved = self.links.copy(self.part(k), self.near_in.at[slot], sibling)
            if slot == 0:
                self.near_far = moved
            else:
                self.near_own = moved
        for k in (2, 0):
            self.part(k)[...] = make_rows(self.here.ranks[k]).astype(jnp.bfloat16)
        return self

    def forward(self):
        self.near_far.wait_recv()
        summed = self.part(2)[...].astype(jnp.float32) + self.near_in[0].astype(jnp.float32)
        self.far_out[...] = summed.astype(jnp.bfloat16)
        self.far = self.links.copy(self.far_out, self.far_in, self.here.mates[2])
        return self

    def sent(self):
        for moved in (self.near_far, self.near_own, self.far):
            self.links.sent(moved)

    def finish(self):
        self.near_own.wait_recv()
        self.far.wait_recv()
        return (
            self.part(0)[...].astype(jnp.float32)
            + self.near_in[1].astype(jnp.float32)
            + self.far_in[...].astype(jnp.float32)
        )


def row_sum_scratch(rows, width):
    return [
        pltpu.VMEM((4 * rows, width), jnp.bfloat16),
        pltpu.VMEM((2, rows, width), jnp.bfloat16),
        pltpu.VMEM((rows, width), jnp.bfloat16),
        pltpu.VMEM((rows, width), jnp.bfloat16),
    ]


def dot(left, right, dims):
    return lax.dot_general(left, right, dims, preferred_element_type=jnp.float32)


def scale_of(tensor):
    return lax.rsqrt(jnp.mean(tensor * tensor, axis=-1, keepdims=True) + EPS)


def rms_back(tensor, gains_row, cotangent):
    scale = scale_of(tensor)
    weighted = cotangent * gains_row
    inner = jnp.mean(tensor * weighted, axis=-1, keepdims=True)
    straight = scale * weighted - tensor * (scale * scale * scale * inner)
    return straight, jnp.sum(cotangent * tensor * scale, axis=0, keepdims=True)


def row_mask(facts, start, rows):
    place_of = lax.broadcasted_iota(jnp.int32, (rows, 1), 0) + start
    return jnp.where(place_of.astype(jnp.float32) < facts[2:3, 0:1], 1.0, 0.0)


def bias_tiles(lines_ref, tiles_ref, heads, width):
    for head in range(heads):
        line = lines_ref[head : head + 1, :]
        spread = jnp.broadcast_to(line, (tiles_ref.shape[1], line.shape[1]))
        tiles_ref[head] = pltpu.roll(spread, 0, 1, stride=1, stride_axis=0)[:, :width]


def softmax_pair(first, second):
    top = jnp.maximum(
        jnp.max(first, axis=-1, keepdims=True), jnp.max(second, axis=-1, keepdims=True)
    )
    first, second = jnp.exp(first - top), jnp.exp(second - top)
    total = jnp.sum(first, axis=-1, keepdims=True) + jnp.sum(second, axis=-1, keepdims=True)
    share = 1.0 / total
    return (
        (first * share).astype(jnp.bfloat16),
        (second * share).astype(jnp.bfloat16),
        top + jnp.log(total),
    )


TILE = 256
ROOT = 1.0 / math.sqrt(DH)


def forward_kernel(
    x_in, carried_in, initial_in, far_past, facts_in, far_gout, far_gstate, gains_ref,
    wst_in, wtok_in, wout_in, gates_in, far_wup, far_wdn,
    normed, snormed, queries, keys, values, state_qkv, lse_ref, mixed, smixed,
    far_gate_values, s1_ref, s2_ref, wst, wtok, wout, gates, x_ref, s0_ref, facts, far_gstate_here,
    block_out, middle_grad, far_wup_grad, far_wdn_grad, small_sums,
    tiles, a2a_0, a2a_1, initial_all, normed_send, s0_send, gate_values, wup, wdn, middle,
    middle_normed, gout_rows, gout, slope, hidden, up_grad, grad_stage, *rest,
):
    rs = [rest[4 * k : 4 * k + 4] for k in range(4)]
    links = Links(rest[16], rest[17])
    local_sems = rest[18]
    here = Place()
    rank, ranks, mates = here.rank, here.ranks, here.mates
    rows = s0_ref.shape[0]
    window = 4 * rows
    width = queries.shape[1]
    heads = width // DH
    ring = [(lax.rem(here.dp + step, 8), here.level) for step in range(1, 8)]
    greet(ring + mates[2:] + [here.from_across], here)

    def turn(source, target):
        return Turn(links, here, source, target, here.there)

    part = initial_in.shape[1]
    own_columns = pl.ds(pl.multiple_of(here.dp * part, part), part)
    initial_moves = [links.copy(initial_in, initial_all.at[:, own_columns], mate) for mate in ring]
    facts_turn = turn(facts_in, facts)
    gather_wst = WeightGather(links, here, wst_in, wst).enter()
    initial_all[:, own_columns] = initial_in[...]
    for moved in initial_moves:
        moved.wait_recv()
    is_fresh = facts_in[3:4, :] > 0.5
    start = jnp.where(is_fresh, initial_all[...].astype(jnp.float32), carried_in[...])
    s0_send[...] = start
    normed_send[...] = (start * scale_of(start) * gains_ref[2:3, :]).astype(jnp.bfloat16)
    normed_turn = turn(normed_send, snormed.at[rows_at(here.level * rows, rows)])
    x_turn = turn(x_in, x_ref)
    gather_wtok = WeightGather(links, here, wtok_in, wtok).enter()
    facts_turn.arrived()
    bias_tiles(facts, tiles, heads, 3 * TILE)
    normed_turn.arrived()
    gather_s0 = RowGather(links, here, snormed, 0, rows).start()
    gather_wst.spread()
    past_turns = [
        turn(far_past.at[0], keys.at[pl.ds(0, window)]),
        turn(far_past.at[1], values.at[pl.ds(0, window)]),
    ]
    gather_wout = WeightGather(links, here, wout_in, wout).enter()
    x_turn.arrived()
    gather_x = []
    for block in range(2):
        x = x_ref[block * rows : (block + 1) * rows, :].astype(jnp.float32)
        normed[rows_at(block * window + rank * rows, rows), :] = (
            x * scale_of(x) * gains_ref[0:1, :]
        ).astype(jnp.bfloat16)
        gather_x.append(RowGather(links, here, normed, block * window, rows).start())
    gather_wst.forward()
    gather_wtok.spread()
    s0_turn = turn(s0_send, s0_ref)

    def key_mask(start, size):
        place_of = lax.broadcasted_iota(jnp.int32, (1, size), 1).astype(jnp.float32)
        place_of = place_of + float(start - window)
        own = jnp.where(place_of < facts[2:3, 0:size], 0.0, NEGATIVE)
        return jnp.where(place_of < 0.0, facts[3:4, 0:size] * NEGATIVE, own)

    def project_state(block, gather):
        for k in range(4):
            gather.ready(k)
            at = rows_at(block * window + ranks[k] * rows, rows)
            state_qkv[at, :] = dot(snormed[at, :], wst[...], NN).astype(jnp.bfloat16)

    def project_token(block, gather):
        for k in range(4):
            gather.ready(k)
            at = rows_at(block * window + ranks[k] * rows, rows)
            later = rows_at((block + 1) * window + ranks[k] * rows, rows)
            out = dot(normed[at, :], wtok[...], NN).astype(jnp.bfloat16)
            queries[at, :] = out[:, :width]
            keys[later, :] = out[:, width : 2 * width]
            values[later, :] = out[:, 2 * width :]

    def state_attention(block):
        base = block * window
        own = pl.ds((block + 1) * window, window)
        whole = pl.ds(base, window)
        own_mask = key_mask(base + window, window)
        for head in range(heads):
            at = head * DH
            for tile in range(window // TILE):
                here_rows = pl.ds(base + tile * TILE, TILE)
                query = state_qkv[here_rows, at : at + DH]
                first = dot(query, state_qkv[whole, width + at : width + at + DH], NT) * ROOT
                second = dot(query, keys[own, at : at + DH], NT) * ROOT + own_mask
                first, second, lse = softmax_pair(first, second)
                out = dot(first, state_qkv[whole, 2 * width + at : 2 * width + at + DH], NN)
                out = out + dot(second, values[own, at : at + DH], NN)
                smixed[here_rows, at : at + DH] = out.astype(jnp.bfloat16)
                lse_ref[here_rows, heads + head : heads + head + 1] = lse

    def token_attention(block):
        base = block * window
        whole = pl.ds(base, window)
        for tile in range(window // TILE):
            near_mask = key_mask(base + tile * TILE, 3 * TILE)
            for head in range(heads):
                at = head * DH
                here_rows = pl.ds(base + tile * TILE, TILE)
                near = pl.ds(base + tile * TILE, 3 * TILE)
                query = queries[here_rows, at : at + DH]
                first = dot(query, keys[near, at : at + DH], NT) * ROOT + tiles[head] + near_mask
                second = dot(query, state_qkv[whole, width + at : width + at + DH], NT) * ROOT
                first, second, lse = softmax_pair(first, second)
                out = dot(first, values[near, at : at + DH], NN)
                out = out + dot(second, state_qkv[whole, 2 * width + at : 2 * width + at + DH], NN)
                mixed[here_rows, at : at + DH] = out.astype(jnp.bfloat16)
                lse_ref[here_rows, head : head + 1] = lse

    def spread_state(block, buffer):
        moves = []
        columns = pl.ds(pl.multiple_of(rank * width, width), width)
        for k in (2, 3, 1):
            source = smixed.at[rows_at(block * window + ranks[k] * rows, rows)]
            moves.append(links.copy(source, buffer.at[:, columns], mates[k]))
        buffer[:, columns] = smixed[rows_at(block * window + rank * rows, rows), :]
        return moves

    def renew(block, buffer, state_now):
        size = state_now.shape[1]
        source = buffer[...]
        parts = []
        for c in range(3):
            part = dot(source, gates[:, c * size : (c + 1) * size], NT)
            gate_values[:, c * size : (c + 1) * size] = part
            parts.append(part)
        keep = pltpu.make_async_copy(
            gate_values, far_gate_values.at[pl.ds(block * rows, rows)], local_sems.at[0]
        )
        keep.start()
        new_state = state_now * jax.nn.sigmoid(parts[2] + 1.0) + jnp.tanh(parts[0]) * jax.nn.sigmoid(
            parts[1] - 1.0
        )
        return new_state, keep

    def branch_rows(block):
        def make(which):
            return dot(mixed[rows_at(block * window + which * rows, rows), :], wout[...], NT)

        return make

    sums = [RowSum(links, here, *rs[block], rows) for block in range(2)]

    def finish_branch(block):
        branch = sums[block].finish()
        at = slice(block * rows, (block + 1) * rows)
        total = x_ref[at, :].astype(jnp.float32) + branch
        middle[at, :] = total
        middle_normed[rows_at(block * window + rank * rows, rows), :] = (
            total * scale_of(total) * gains_ref[1:2, :]
        ).astype(jnp.bfloat16)
        gather = RowGather(links, here, middle_normed, block * window, rows).start()
        share = row_mask(facts, block * window + rank * rows, rows)
        return jnp.sum(branch * branch * share, axis=0, keepdims=True), gather

    def rise(block, gather):
        root = math.sqrt(2.0 / math.pi)
        for k in range(4):
            gather.ready(k)
            at = rows_at(block * window + ranks[k] * rows, rows)
            value = dot(middle_normed[at, :], wup[...], NN)
            square = value * value
            bend = jnp.tanh(root * value * (1.0 + 0.044715 * square))
            half = 0.5 * (1.0 + bend)
            hidden[at, :] = (value * half).astype(jnp.bfloat16)
            slope[at, :] = half + 0.5 * value * (1.0 - bend * bend) * (
                root * (1.0 + 3.0 * 0.044715 * square)
            )

    def feed_sum(block):
        return RowSum(links, here, *rs[block], rows).fill(
            lambda which: dot(hidden[rows_at(block * window + which * rows, rows), :], wdn[...], NT)
        )

    def start_gout(block):
        at = slice(block * rows, (block + 1) * rows)
        gout[rows_at(block * window + rank * rows, rows), :] = gout_rows[at, :]
        return RowGather(links, here, gout, block * window, rows).start()

    def feed_back(block, gather):
        for k in range(4):
            gather.ready(k)
            at = rows_at(block * window + ranks[k] * rows, rows)
            up_grad[at, :] = (dot(gout[at, :], wdn[...], NN) * slope[at, :]).astype(jnp.bfloat16)
        return RowSum(links, here, *rs[2 + block], rows).fill(
            lambda which: dot(up_grad[rows_at(block * window + which * rows, rows), :], wup[...], NT)
        )

    def weight_grad(stage, left, right, target, sem):
        step = 256
        for part in range(stage.shape[0] // step):
            at = slice(part * step, (part + 1) * step)
            stage[at, :] = dot(left[:, at], right[...], TN).astype(jnp.bfloat16)
        keep = pltpu.make_async_copy(stage, target, sem)
        keep.start()
        return keep

    gather_wst.finish()
    project_state(0, gather_s0)
    gather_wtok.forward()
    gather_gates = GateGather(links, here, gates_in, gates, local_sems.at[3])
    gather_gates.spread()
    gather_wup = WeightGather(links, here, far_wup, wup).enter()
    gather_wtok.finish()
    project_token(0, gather_x[0])
    project_token(1, gather_x[1])
    for moved in past_turns:
        moved.arrived()
    state_attention(0)
    moves_0 = spread_state(0, a2a_0)
    gather_wout.spread()
    gather_gates.forward()
    gout_turn = turn(far_gout, gout_rows)
    token_attention(0)
    gather_wout.forward()
    gather_gates.last()
    gather_wdn = WeightGather(links, here, far_wdn, wdn).enter()
    gather_wup.spread()
    gather_wout.finish()
    sums[0].fill(branch_rows(0))
    for moved in moves_0:
        moved.wait_recv()
    gather_gates.finish()
    s0_turn.arrived()
    s1, keep_gates = renew(0, a2a_0, s0_ref[...])
    s1_ref[...] = s1
    snormed[rows_at(window + rank * rows, rows), :] = (s1 * scale_of(s1) * gains_ref[2:3, :]).astype(
        jnp.bfloat16
    )
    gather_s1 = RowGather(links, here, snormed, window, rows).start()
    sums[0].forward()
    gather_wup.forward()
    gather_wdn.spread()
    gstate_turn = turn(far_gstate, far_gstate_here)
    project_state(1, gather_s1)
    state_attention(1)
    moves_1 = spread_state(1, a2a_1)
    branch_total, gather_m0 = finish_branch(0)
    token_attention(1)
    gather_wdn.forward()
    sums[1].fill(branch_rows(1))
    gather_wup.finish()
    gout_turn.arrived()
    gather_g0 = start_gout(0)
    rise(0, gather_m0)
    sums[1].forward()
    for moved in moves_1:
        moved.wait_recv()
    keep_gates.wait()
    s2, keep_gates = renew(1, a2a_1, s1_ref[...])
    s2_ref[...] = s2.astype(jnp.bfloat16)
    gather_wdn.finish()
    sums[0].sent()
    feed_0 = feed_sum(0)
    more, gather_m1 = finish_branch(1)
    branch_total = branch_total + more
    gather_g1 = start_gout(1)
    feed_0.forward()
    back_0 = feed_back(0, gather_g0)
    rise(1, gather_m1)
    sums[1].sent()
    feed_1 = feed_sum(1)
    back_0.forward()
    back_1 = feed_back(1, gather_g1)
    feed_1.forward()
    keep_down = weight_grad(grad_stage, gout, hidden, far_wdn_grad, local_sems.at[1])
    back_1.forward()
    keep_up = weight_grad(hidden, middle_normed, up_grad, far_wup_grad, local_sems.at[2])
    feed_total, result_total, gain_total = 0.0, 0.0, 0.0
    for block, feed_here in ((0, feed_0), (1, feed_1)):
        at = slice(block * rows, (block + 1) * rows)
        feed = feed_here.finish()
        result = middle[at, :] + feed
        block_out[at, :] = result.astype(jnp.bfloat16)
        share = row_mask(facts, block * window + rank * rows, rows)
        feed_total = feed_total + jnp.sum(feed * feed * share, axis=0, keepdims=True)
        result_total = result_total + jnp.sum(result * result * share, axis=0, keepdims=True)
    for block, back_here in ((1, back_1), (0, back_0)):
        at = slice(block * rows, (block + 1) * rows)
        straight, gain = rms_back(middle[at, :], gains_ref[1:2, :], back_here.finish())
        middle_grad[at, :] = gout_rows[at, :].astype(jnp.float32) + straight
        gain_total = gain_total + gain
    small_sums[...] = jnp.concatenate(
        [gain_total, result_total, branch_total, feed_total]
        + [jnp.zeros((4, gain_total.shape[1]), jnp.float32)],
        axis=0,
    )
    gstate_turn.arrived()
    keep_gates.wait()
    keep_down.wait()
    keep_up.wait()
    links.close()


class PlaneSum:
    def __init__(self, links, here, grad, first_in, last_in):
        self.links, self.here, self.grad = links, here, grad
        self.first_in, self.last_in = first_in, last_in
        self.rows = first_in.shape[1]

    def part(self, k, which):
        start = self.here.planes[k] * 2 * self.rows + which * self.rows
        return self.grad.at[rows_at(start, self.rows)]

    def start(self):
        mates = self.here.plane_mates
        self.firsts = [
            self.links.copy(self.part(k, which), self.first_in.at[slot], mates[mate])
            for slot, (k, which, mate) in enumerate(((1, 0, 1), (3, 0, 1), (2, 1, 2), (3, 1, 2)))
        ]
        return self

    def add(self, k, which, arrived):
        part = self.part(k, which)
        part[...] = (part[...].astype(jnp.float32) + arrived[...].astype(jnp.float32)).astype(part.dtype)

    def forward(self):
        mates = self.here.plane_mates
        self.firsts[1].wait_recv()
        self.add(2, 0, self.first_in.at[1])
        self.last_0 = self.links.copy(self.part(2, 0), self.last_in.at[0], mates[2])
        self.firsts[3].wait_recv()
        self.add(1, 1, self.first_in.at[3])
        self.last_1 = self.links.copy(self.part(1, 1), self.last_in.at[1], mates[1])

    def finish(self):
        self.firsts[0].wait_recv()
        self.add(0, 0, self.first_in.at[0])
        self.firsts[2].wait_recv()
        self.add(0, 1, self.first_in.at[2])
        self.last_0.wait_recv()
        self.add(0, 0, self.last_in.at[0])
        self.last_1.wait_recv()
        self.add(0, 1, self.last_in.at[1])

    def result(self, which):
        return self.grad.at[
            rows_at(self.here.planes[0] * 2 * self.rows + which * self.rows, self.rows)
        ]


class FarPlaneSum(PlaneSum):
    def __init__(self, links, here, grad, first_in, last_in, forwards, brought, brought_sems):
        super().__init__(links, here, grad, first_in, last_in)
        self.forwards = forwards
        self.brought, self.brought_sems = brought, brought_sems

    def total(self, *pieces):
        brings = [
            pltpu.make_async_copy(piece, self.brought.at[slot], self.brought_sems.at[slot])
            for slot, piece in enumerate(pieces)
        ]
        for bring in brings:
            bring.start()
        for bring in brings:
            bring.wait()
        out = self.brought[0].astype(jnp.float32)
        for slot in range(1, len(pieces)):
            out = out + self.brought[slot].astype(jnp.float32)
        return out.astype(jnp.bfloat16)

    def forward(self):
        mates = self.here.plane_mates
        self.firsts[1].wait_recv()
        self.forwards[0] = self.total(self.part(2, 0), self.first_in.at[1])
        self.last_0 = self.links.copy(self.forwards.at[0], self.last_in.at[0], mates[2])
        self.firsts[3].wait_recv()
        self.forwards[1] = self.total(self.part(1, 1), self.first_in.at[3])
        self.last_1 = self.links.copy(self.forwards.at[1], self.last_in.at[1], mates[1])

    def finish(self):
        self.firsts[0].wait_recv()
        self.last_0.wait_recv()
        self.links.sent(self.last_0)
        self.forwards[0] = self.total(self.part(0, 0), self.first_in.at[0], self.last_in.at[0])
        self.firsts[2].wait_recv()
        self.last_1.wait_recv()
        self.links.sent(self.last_1)
        self.forwards[1] = self.total(self.part(0, 1), self.first_in.at[2], self.last_in.at[1])

    def result(self, which):
        return self.forwards.at[which]


class Settle:
    def __init__(self, links, here, summed, target):
        half = here.half
        self.straight = Turn(links, here, summed.result(half), target.at[0], here.from_there)
        self.crossed = links.copy(summed.result(1 - half), target.at[1], here.from_across)

    def arrived(self):
        self.straight.arrived()
        self.crossed.wait_recv()


def cotangent_kernel(
    middle_grad, gstate_ref, x_ref, s0_ref, s1_ref, far_gate_values, gains_ref, facts, facts_home,
    small_sums,
    far_normed, far_snormed, queries, keys, values, state_qkv, lse_ref, mixed, smixed,
    wst, wtok, wout, gates, far_wup_grad, far_wdn_grad, far_block_out, far_state_out,
    block_home, state_home, tokens_home, past_home, carried_grad, initial_grad, totals,
    up_home, down_home, wst_home, wtok_home, wout_home, gates_home,
    up_first, down_first, up_last, down_last,
    tiles, tile_grads, branch_grad, mixed_grad, gate_rows, state_mixed_grad, key_grad, value_grad,
    skey_grad, svalue_grad, token_cot, state_cot, gate_values, sending,
    tokens_send, carried_send, carried_in, past_send, initial_send, initial_in,
    wst_grad, wtok_grad, wout_grad, gates_grad,
    wst_first, wtok_first, wout_first, gates_first, wst_last, wtok_last, wout_last, gates_last,
    up_forwards, down_forwards, brought, ring_in, level_in, ring_send, level_send,
    *rest,
):
    rs = [rest[0:4], rest[4:8], rest[8:12]]
    links = Links(rest[12], rest[13])
    local_sems, brought_sems = rest[14], rest[15]
    here = Place()
    rank, ranks, mates = here.rank, here.ranks, here.mates
    rows = s0_ref.shape[0]
    window = 4 * rows
    width = queries.shape[1]
    heads = width // DH
    size = s0_ref.shape[1]
    ring = [(lax.rem(here.dp + step, 8), here.level) for step in range(1, 8)]
    other = here.dp + 1 - 2 * here.core
    column = [
        (chip, lax.rem(here.level + step, 4)) for step in range(1, 4) for chip in (here.dp, other)
    ]
    greet(ring + column)
    bring_gates = pltpu.make_async_copy(
        far_gate_values.at[pl.ds(rows, rows)], gate_values, local_sems.at[0]
    )
    bring_gates.start()
    branch_gathers = []
    for block in (1, 0):
        at = slice(block * rows, (block + 1) * rows)
        branch_grad[rows_at(block * window + rank * rows, rows), :] = middle_grad[at, :].astype(
            jnp.bfloat16
        )

    def home(source, target):
        return Turn(links, here, source, target, here.from_there)

    def gates_back(block, state, state_grad):
        spot = rows_at(block * window + rank * rows, rows)
        keep = jax.nn.sigmoid(gate_values[:, 2 * size : 3 * size] + 1.0)
        fresh = jnp.tanh(gate_values[:, 0:size])
        let_in = jax.nn.sigmoid(gate_values[:, size : 2 * size] - 1.0)
        gate_rows[spot, 0:size] = (state_grad * let_in * (1.0 - fresh * fresh)).astype(jnp.bfloat16)
        gate_rows[spot, size : 2 * size] = (
            state_grad * fresh * let_in * (1.0 - let_in)
        ).astype(jnp.bfloat16)
        gate_rows[spot, 2 * size : 3 * size] = (
            state_grad * state * keep * (1.0 - keep)
        ).astype(jnp.bfloat16)
        out = dot(gate_rows[spot, 0:size], gates[:, 0:size], NN)
        out = out + dot(gate_rows[spot, size : 2 * size], gates[:, size : 2 * size], NN)
        out = out + dot(gate_rows[spot, 2 * size : 3 * size], gates[:, 2 * size : 3 * size], NN)
        sending[block] = out.astype(jnp.bfloat16)
        moves = []
        for k in (2, 3, 1):
            columns = pl.ds(pl.multiple_of(ranks[k] * width, width), width)
            moves.append(
                links.copy(sending.at[block, :, columns], state_mixed_grad.at[spot], mates[k])
            )
        columns = pl.ds(pl.multiple_of(rank * width, width), width)
        state_mixed_grad[spot, :] = sending[block, :, columns]
        return state_grad * keep, moves

    def key_mask(start, size):
        place_of = lax.broadcasted_iota(jnp.int32, (1, size), 1).astype(jnp.float32)
        place_of = place_of + float(start - window)
        own = jnp.where(place_of < facts[2:3, 0:size], 0.0, NEGATIVE)
        return jnp.where(place_of < 0.0, facts[3:4, 0:size] * NEGATIVE, own)

    def pair_back(first, second, lse, first_grad, second_grad):
        first, second = jnp.exp(first - lse), jnp.exp(second - lse)
        inner = jnp.sum(first * first_grad, axis=-1, keepdims=True) + jnp.sum(
            second * second_grad, axis=-1, keepdims=True
        )
        return (
            first.astype(jnp.bfloat16),
            second.astype(jnp.bfloat16),
            (first * (first_grad - inner)).astype(jnp.bfloat16),
            (second * (second_grad - inner)).astype(jnp.bfloat16),
        )

    def token_back(block):
        base = block * window
        whole = pl.ds(base, window)
        for tile in range(window // TILE):
            near_mask = key_mask(base + tile * TILE, 3 * TILE)
            for head in range(heads):
                at = head * DH
                lanes = slice(at, at + DH)
                skey_lanes = slice(width + at, width + at + DH)
                svalue_lanes = slice(2 * width + at, 2 * width + at + DH)
                here_rows = pl.ds(base + tile * TILE, TILE)
                near = pl.ds(base + tile * TILE, 3 * TILE)
                query = queries[here_rows, lanes]
                out_grad = mixed_grad[here_rows, lanes]
                first = dot(query, keys[near, lanes], NT) * ROOT + tiles[head] + near_mask
                second = dot(query, state_qkv[whole, skey_lanes], NT) * ROOT
                first, second, first_grad, second_grad = pair_back(
                    first,
                    second,
                    lse_ref[here_rows, head : head + 1],
                    dot(out_grad, values[near, lanes], NT),
                    dot(out_grad, state_qkv[whole, svalue_lanes], NT),
                )
                value_grad[near, lanes] += dot(first, out_grad, TN)
                svalue_grad[:, lanes] += dot(second, out_grad, TN)
                part = dot(first_grad, keys[near, lanes], NN) + dot(
                    second_grad, state_qkv[whole, skey_lanes], NN
                )
                token_cot[here_rows, lanes] = (part * ROOT).astype(jnp.bfloat16)
                key_grad[near, lanes] += dot(first_grad, query, TN) * ROOT
                skey_grad[:, lanes] += dot(second_grad, query, TN) * ROOT
                tile_grads[head, :, 0 : 3 * TILE] += first_grad.astype(jnp.float32)

    def state_back(block):
        base = block * window
        whole = pl.ds(base, window)
        own = pl.ds(base + window, window)
        own_mask = key_mask(base + window, window)
        for head in range(heads):
            at = head * DH
            lanes = slice(at, at + DH)
            skey_lanes = slice(width + at, width + at + DH)
            svalue_lanes = slice(2 * width + at, 2 * width + at + DH)
            for tile in range(window // TILE):
                here_rows = pl.ds(base + tile * TILE, TILE)
                query = state_qkv[here_rows, lanes]
                out_grad = state_mixed_grad[here_rows, lanes]
                first = dot(query, state_qkv[whole, skey_lanes], NT) * ROOT
                second = dot(query, keys[own, lanes], NT) * ROOT + own_mask
                first, second, first_grad, second_grad = pair_back(
                    first,
                    second,
                    lse_ref[here_rows, heads + head : heads + head + 1],
                    dot(out_grad, state_qkv[whole, svalue_lanes], NT),
                    dot(out_grad, values[own, lanes], NT),
                )
                svalue_grad[:, lanes] += dot(first, out_grad, TN)
                value_grad[own, lanes] += dot(second, out_grad, TN)
                part = dot(first_grad, state_qkv[whole, skey_lanes], NN) + dot(
                    second_grad, keys[own, lanes], NN
                )
                state_cot[here_rows, lanes] = (part * ROOT).astype(jnp.bfloat16)
                skey_grad[:, lanes] += dot(first_grad, query, TN) * ROOT
                key_grad[own, lanes] += dot(second_grad, query, TN) * ROOT

    def gather_cot(block):
        whole = pl.ds(block * window, window)
        own = pl.ds(block * window + window, window)
        token_cot[whole, width : 2 * width] = key_grad[own, :].astype(jnp.bfloat16)
        token_cot[whole, 2 * width : 3 * width] = value_grad[own, :].astype(jnp.bfloat16)
        state_cot[whole, width : 2 * width] = skey_grad[...].astype(jnp.bfloat16)
        state_cot[whole, 2 * width : 3 * width] = svalue_grad[...].astype(jnp.bfloat16)

    def state_sum(block):
        return RowSum(links, here, *rs[0], rows).fill(
            lambda which: dot(state_cot[rows_at(block * window + which * rows, rows), :], wst[...], NT)
        )

    def token_sum(block):
        return RowSum(links, here, *rs[1 + block], rows).fill(
            lambda which: dot(token_cot[rows_at(block * window + which * rows, rows), :], wtok[...], NT)
        )

    def mix_back(block):
        for k in range(4):
            branch_gathers[1 - block].ready(k)
            at = rows_at(block * window + ranks[k] * rows, rows)
            mixed_grad[at, :] = dot(branch_grad[at, :], wout[...], NN).astype(jnp.bfloat16)

    def weight_grad(target, left, right, lanes):
        step = 256
        for part in range(size // step):
            at = slice(part * step, (part + 1) * step)
            target[at, lanes] = dot(left[:, at], right, TN).astype(jnp.bfloat16)

    def finish_tokens(block, summed):
        at = slice(block * rows, (block + 1) * rows)
        straight, gain = rms_back(x_ref[at, :].astype(jnp.float32), gains_ref[0:1, :], summed.finish())
        tokens_send[at, :] = (middle_grad[at, :] + straight).astype(jnp.bfloat16)
        return gain, home(tokens_send.at[pl.ds(block * rows, rows)], tokens_home.at[pl.ds(block * rows, rows)])

    bring_gates.wait()
    direct_1, moves_1 = gates_back(1, s1_ref[...], gstate_ref[...])
    for block in (1, 0):
        branch_gathers.append(RowGather(links, here, branch_grad, block * window, rows).start())
    up_sum = FarPlaneSum(
        links, here, far_wup_grad, up_first, up_last, up_forwards, brought, brought_sems
    ).start()
    down_sum = FarPlaneSum(
        links, here, far_wdn_grad, down_first, down_last, down_forwards, brought, brought_sems
    ).start()
    gate_gather_1 = RowGather(links, here, gate_rows, window, rows).start()
    bring_gates = pltpu.make_async_copy(far_gate_values.at[pl.ds(0, rows)], gate_values, local_sems.at[0])
    bring_gates.start()
    for ref in (tile_grads, key_grad, value_grad, skey_grad, svalue_grad):
        ref[...] = jnp.zeros(ref.shape, ref.dtype)
    bias_tiles(facts, tiles, heads, 3 * TILE)
    mix_back(1)
    token_back(1)
    for moved in moves_1:
        moved.wait_recv()
    block_turn = home(far_block_out, block_home)
    state_turn = home(far_state_out, state_home)
    state_back(1)
    gather_cot(1)
    state_sum_1 = state_sum(1)
    token_sum_1 = token_sum(1)
    state_sum_1.forward()
    mix_back(0)
    up_sum.forward()
    bring_gates.wait()
    state_norm_grad, gain_2 = rms_back(s1_ref[...], gains_ref[2:3, :], state_sum_1.finish())
    direct_0, moves_0 = gates_back(0, s0_ref[...], direct_1 + state_norm_grad)
    token_sum_1.forward()
    down_sum.forward()
    weight_grad(wout_grad, branch_grad, mixed[...], slice(0, width))
    wout_sum = PlaneSum(links, here, wout_grad, wout_first, wout_last).start()
    for k in range(1, 4):
        gate_gather_1.ready(k)
    gate_gather_0 = RowGather(links, here, gate_rows, 0, rows).start()
    bring_snormed = pltpu.make_async_copy(far_snormed, branch_grad, local_sems.at[2])
    for ref in (skey_grad, svalue_grad):
        ref[...] = jnp.zeros(ref.shape, ref.dtype)
    token_back(0)
    past_send[0] = key_grad[0:window, :].astype(jnp.bfloat16)
    past_send[1] = value_grad[0:window, :].astype(jnp.bfloat16)
    up_sum.finish()
    up_settle = Settle(links, here, up_sum, up_home)
    gain_1, turn_1 = finish_tokens(1, token_sum_1)
    for k in range(1, 4):
        gate_gather_0.ready(k)
    for c in range(3):
        weight_grad(
            gates_grad,
            gate_rows.at[:, c * size : (c + 1) * size],
            smixed[...],
            slice(c * width, (c + 1) * width),
        )
    gates_sum = PlaneSum(links, here, gates_grad, gates_first, gates_last).start()
    down_sum.finish()
    down_settle = Settle(links, here, down_sum, down_home)
    wout_sum.forward()
    for moved in moves_0:
        moved.wait_recv()
    for gather in branch_gathers:
        gather.sent()
    bring_snormed.start()
    state_back(0)
    gather_cot(0)
    state_sum_1.sent()
    state_sum_0 = state_sum(0)
    token_sum_0 = token_sum(0)
    past_turn = home(past_send, past_home)
    bring_snormed.wait()
    weight_grad(wst_grad, branch_grad, state_cot[...], slice(0, 3 * width))
    wst_sum = PlaneSum(links, here, wst_grad, wst_first, wst_last).start()
    for gather in (gate_gather_1, gate_gather_0):
        gather.sent()
    normed = gate_rows.at[:, 0:size]
    bring_normed = pltpu.make_async_copy(far_normed, normed, local_sems.at[2])
    bring_normed.start()
    state_sum_0.forward()
    gates_sum.forward()
    bring_normed.wait()
    weight_grad(wtok_grad, normed, token_cot[...], slice(0, 3 * width))
    wtok_sum = PlaneSum(links, here, wtok_grad, wtok_first, wtok_last).start()
    token_sum_0.forward()
    state_norm_grad, gain = rms_back(s0_ref[...], gains_ref[2:3, :], state_sum_0.finish())
    carried_send[...] = (direct_0 + state_norm_grad).astype(jnp.bfloat16)
    carried_turn = home(carried_send, carried_in)
    gain_2 = gain_2 + gain
    wout_sum.finish()
    wout_settle = Settle(links, here, wout_sum, wout_home)
    gain_0, turn_0 = finish_tokens(0, token_sum_0)

    for head in range(heads):
        lines = tile_grads[head, 0:8, :]
        span = lines.shape[1]
        for group in range(1, TILE // 8):
            lines = lines + pltpu.roll(tile_grads[head, 8 * group : 8 * group + 8, :], span - 8 * group, 1)
        total = lines[0:1]
        for line in range(1, 8):
            total = total + pltpu.roll(lines[line : line + 1], span - line, 1)
        for owner in range(4):
            at = 8 + heads * owner + head
            ring_send[at : at + 1, :] = jnp.where(rank == owner, total, 0.0)
    ring_send[0:1, :] = gain_0 + gain_1
    ring_send[1:2, :] = small_sums[0:1, :]
    ring_send[2:3, :] = gain_2
    ring_send[3:6, :] = small_sums[1:4, :]
    counted = jnp.zeros((1, 1), jnp.float32)
    for block in range(2):
        valid_rows = row_mask(facts, block * window + rank * rows, rows)
        counted = counted + jnp.sum(valid_rows, axis=0, keepdims=True)
    ring_send[6:7, :] = jnp.broadcast_to(counted, (1, size))
    ring_send[7:8, :] = jnp.zeros((1, size), jnp.float32)
    ring_moves = [
        links.copy(ring_send, ring_in.at[step - 1], ring[step - 1]) for step in range(1, 8)
    ]
    wst_sum.forward()
    wtok_sum.forward()
    carried_turn.arrived()
    is_fresh = facts_home[3:4, :] > 0.5
    came = carried_in[...]
    carried_grad[...] = jnp.where(is_fresh, 0.0, came.astype(jnp.float32))
    initial_send[...] = jnp.where(is_fresh, came, jnp.zeros_like(came))
    part = initial_grad.shape[1]
    initial_moves = []
    for step in range(1, 8):
        to = lax.rem(here.dp + step, 8)
        columns = pl.ds(pl.multiple_of(to * part, part), part)
        initial_moves.append(
            links.copy(initial_send.at[:, columns], initial_in.at[step - 1], ring[step - 1])
        )
    for moved in ring_moves:
        moved.wait_recv()
    total = ring_send[...]
    for step in range(7):
        total = total + ring_in[step]
    level_send[...] = total
    level_moves = [
        links.copy(level_send, level_in.at[step - 1], (here.dp, lax.rem(here.level + step, 4)))
        for step in range(1, 4)
    ]
    gates_sum.finish()
    slot = here.half * 4 + rank
    piece = rows // 4
    gate_moves = []
    for step in range(4):
        to_level = lax.rem(here.level + step, 4)
        for to_core, chip in ((here.core, here.dp), (1 - here.core, other)):
            start = here.planes[0] * 2 * rows + to_core * rows + to_level * piece
            source = gates_grad.at[rows_at(start, piece, piece)]
            if step == 0 and chip is here.dp:
                kept = pltpu.make_async_copy(source, gates_home.at[slot], local_sems.at[3])
                kept.start()
            else:
                gate_moves.append(links.copy(source, gates_home.at[slot], (chip, to_level)))
    wst_sum.finish()
    wst_settle = Settle(links, here, wst_sum, wst_home)
    wtok_sum.finish()
    wtok_settle = Settle(links, here, wtok_sum, wtok_home)
    for moved in initial_moves:
        moved.wait_recv()
    own_columns = pl.ds(pl.multiple_of(here.dp * part, part), part)
    initial = initial_send[:, own_columns].astype(jnp.float32)
    for step in range(7):
        initial = initial + initial_in[step].astype(jnp.float32)
    initial_grad[...] = initial
    for moved in level_moves:
        moved.wait_recv()
    total = level_send[...]
    for step in range(3):
        total = total + level_in[step]
    totals[...] = total
    kept.wait()
    for moved in gate_moves:
        moved.wait_recv()
    for turn in (block_turn, state_turn, past_turn, turn_1, turn_0):
        turn.arrived()
    for settle in (up_settle, down_settle, wout_settle, wst_settle, wtok_settle):
        settle.arrived()
    links.close()


def run_kernel(body, outs, scratch, collective, name, operands, far_in=(), far_out=()):
    vmem = pl.BlockSpec(memory_space=pltpu.VMEM)
    far = pl.BlockSpec(memory_space=pl.ANY)
    return pl.pallas_call(
        body,
        out_shape=outs,
        in_specs=[far if at in far_in else vmem for at in range(len(operands))],
        out_specs=[far if at in far_out else vmem for at in range(len(outs))],
        scratch_shapes=scratch,
        compiler_params=pltpu.CompilerParams(
            collective_id=collective, has_side_effects=True, vmem_limit_bytes=VMEM_BYTES
        ),
        name=name,
    )(*operands)


def sems(count):
    return [pltpu.SemaphoreType.DMA((count,)), pltpu.SemaphoreType.DMA((count,))]


def grouped(
    tokens, carried_state, past_keys, fresh_start, valid_count, bucket_ids, grad_output, grad_state,
    norm_gains, token_qkv, token_out, bias_table, mlp_up, mlp_down, state_qkv, state_gates, initial_state,
):
    dp_size, levels = lax.axis_size("dp"), lax.axis_size("state")
    dp_at, level = lax.axis_index("dp"), lax.axis_index("state")
    _, blocks, rows, size = tokens.shape
    window = rows * levels
    width = token_qkv.shape[2]
    heads = width // DH
    units = mlp_up.shape[1]
    model_rows = token_qkv.shape[0]
    low, full = jnp.bfloat16, jnp.float32

    one_hot = (bucket_ids[:, None] == jnp.arange(bias_table.shape[0])[None, :]).astype(full)
    per_offset = jnp.dot(one_hot, bias_table, precision=HIGHEST)
    lines = jnp.pad(per_offset[::-1].T, ((0, 0), (1, window - 1)), constant_values=NEGATIVE)
    numbers = jnp.stack([valid_count[0], fresh_start[0]]).astype(full)
    facts_in = jnp.concatenate(
        [
            lines,
            jnp.broadcast_to(numbers[:, None], (2, lines.shape[1])),
            jnp.zeros((4, lines.shape[1]), full),
        ]
    )

    shape = jax.ShapeDtypeStruct
    vmem = pltpu.VMEM
    rs = row_sum_scratch(rows, size)
    (
        normed, snormed, queries, keys, values, sqkv, lse, mixed, smixed,
        gate_values, s1, s2, wst_all, wtok_all, wout_all, gates_all, x, s0, facts, gstate,
        block_out, middle_grad, wup_grad, wdn_grad, small_sums,
    ) = run_kernel(
        forward_kernel,
        [
            shape((2 * window, size), low),
            shape((2 * window, size), low),
            shape((2 * window, width), low),
            shape((3 * window, width), low),
            shape((3 * window, width), low),
            shape((2 * window, 3 * width), low),
            shape((2 * window, 2 * heads), full),
            shape((2 * window, width), low),
            shape((2 * window, width), low),
            shape((2 * rows, 3 * size), full),
            shape((rows, size), full),
            shape((rows, size), low),
            shape((size, 3 * width), low),
            shape((size, 3 * width), low),
            shape((size, width), low),
            shape((size, 3 * size), low),
            shape((2 * rows, size), low),
            shape((rows, size), full),
            shape((8, 2 * window), full),
            shape((rows, size), full),
            shape((2 * rows, size), low),
            shape((2 * rows, size), full),
            shape((size, units), low),
            shape((size, units), low),
            shape((8, size), full),
        ],
        [
            vmem((heads, TILE, 3 * TILE), full),
            vmem((rows, size), low),
            vmem((rows, size), low),
            vmem((rows, size), low),
            vmem((rows, size), low),
            vmem((rows, size), full),
            vmem((rows, 3 * size), full),
            vmem((size, units), low),
            vmem((size, units), low),
            vmem((2 * rows, size), full),
            vmem((2 * window, size), low),
            vmem((2 * rows, size), low),
            vmem((2 * window, size), low),
            vmem((2 * window, units), full),
            vmem((2 * window, units), low),
            vmem((2 * window, units), low),
            vmem((size, units), low),
        ]
        + rs * 4
        + sems(128)
        + [pltpu.SemaphoreType.DMA((4,))],
        0,
        "forward",
        [
            tokens[0].reshape(blocks * rows, size),
            carried_state[0],
            initial_state,
            jnp.swapaxes(past_keys[0], 0, 1),
            facts_in,
            grad_output[0].reshape(blocks * rows, size),
            grad_state[0],
            norm_gains,
            state_qkv.reshape(model_rows, 3 * width),
            token_qkv.reshape(model_rows, 3 * width),
            token_out,
            state_gates.reshape(model_rows, 3 * size),
            mlp_up,
            mlp_down,
        ],
        far_in=(3, 5, 6, 12, 13),
        far_out=(9, 19, 22, 23),
    )
    grads = [("wst", 3 * width), ("wtok", 3 * width), ("wout", width), ("gates", 3 * width)]
    (
        block_home, state_home, tokens_home, past_home, carried_grad, initial_grad, totals,
        up_home, down_home, wst_home, wtok_home, wout_home, gates_home, *_,
    ) = run_kernel(
        cotangent_kernel,
        [
            shape((2 * rows, size), low),
            shape((rows, size), low),
            shape((2 * rows, size), low),
            shape((2, window, width), low),
            shape((rows, size), full),
            shape((rows, size // dp_size), full),
            shape((16, size), full),
            shape((2, rows, units), low),
            shape((2, rows, units), low),
            shape((2, rows, 3 * width), low),
            shape((2, rows, 3 * width), low),
            shape((2, rows, width), low),
            shape((8, rows // 4, 3 * width), low),
            shape((4, rows, units), low),
            shape((4, rows, units), low),
            shape((2, rows, units), low),
            shape((2, rows, units), low),
        ],
        [
            vmem((heads, TILE, 3 * TILE), full),
            vmem((heads, TILE, 4 * TILE), full),
            vmem((2 * window, size), low),
            vmem((2 * window, width), low),
            vmem((2 * window, 3 * size), low),
            vmem((2 * window, width), low),
            vmem((3 * window, width), full),
            vmem((3 * window, width), full),
            vmem((window, width), full),
            vmem((window, width), full),
            vmem((2 * window, 3 * width), low),
            vmem((2 * window, 3 * width), low),
            vmem((rows, 3 * size), full),
            vmem((2, rows, size), low),
            vmem((2 * rows, size), low),
            vmem((rows, size), low),
            vmem((rows, size), low),
            vmem((2, window, width), low),
            vmem((rows, size), low),
            vmem((dp_size - 1, rows, size // dp_size), low),
        ]
        + [vmem((size, columns), low) for _, columns in grads]
        + [vmem((4, rows, columns), low) for _, columns in grads]
        + [vmem((2, rows, columns), low) for _, columns in grads]
        + [vmem((2, rows, units), low)] * 2
        + [
            vmem((3, rows, units), low),
            vmem((dp_size - 1, 16, size), full),
            vmem((levels - 1, 16, size), full),
            vmem((16, size), full),
            vmem((16, size), full),
        ]
        + rs * 3
        + sems(128)
        + [pltpu.SemaphoreType.DMA((4,)), pltpu.SemaphoreType.DMA((3,))],
        1,
        "cotangent",
        [
            middle_grad, gstate, x, s0, s1, gate_values, norm_gains, facts, facts_in,
            small_sums,
            normed, snormed, queries, keys, values, sqkv, lse, mixed, smixed,
            wst_all, wtok_all, wout_all, gates_all, wup_grad, wdn_grad, block_out, s2,
        ],
        far_in=(5, 10, 11, 23, 24, 25, 26),
        far_out=(0, 1, 2, 3, 7, 8, 9, 10, 11, 12, 13, 14, 15, 16),
    )
    both = lambda pair: pair[0].astype(full) + pair[1].astype(full)
    gates_out = gates_home.astype(full).reshape(2, levels, rows // 4, 3, width)
    gates_out = jnp.transpose(both(gates_out), (1, 2, 0, 3)).reshape(rows // 4, 3, size)
    line_sums = totals[8 : 8 + levels * heads, 1 : window + 1][:, ::-1]
    table_all = jnp.dot(one_hot.T, line_sums.T, precision=HIGHEST)
    table_rows = table_all.shape[0] // dp_size
    table_out = lax.dynamic_slice(table_all, (dp_at * table_rows, level * heads), (table_rows, heads))
    share = size // (dp_size * levels)
    gains_out = lax.dynamic_slice(totals, (0, (dp_at * levels + level) * share), (3, share))
    rms_stats = jnp.sqrt(jnp.sum(totals[3:6], axis=1) / totals[6, 0])
    return (
        block_home.reshape(1, blocks, rows, size),
        state_home.astype(full)[None],
        rms_stats,
        tokens_home.reshape(1, blocks, rows, size),
        carried_grad[None],
        jnp.swapaxes(past_home.astype(full), 0, 1)[None],
        gains_out,
        both(wtok_home).reshape(model_rows, 3, width),
        both(wout_home),
        table_out,
        both(up_home),
        both(down_home),
        both(wst_home).reshape(model_rows, 3, width),
        gates_out,
        initial_grad,
    )


def solution(mesh):
    in_specs = (
        P("dp", None, "state", None),
        P("dp", "state", None),
        P("dp", None, None, "state"),
        P("dp"),
        P("dp"),
        P(),
        P("dp", None, "state", None),
        P("dp", "state", None),
        P(),
        P("dp", None, "state"),
        P("dp", "state"),
        P(None, "state"),
        P("dp", "state"),
        P("dp", "state"),
        P("dp", None, "state"),
        P("dp", None, None),
        P("state", "dp"),
    )
    out_specs = (
        P("dp", None, "state", None),
        P("dp", "state", None),
        P(),
        P("dp", None, "state", None),
        P("dp", "state", None),
        P("dp", None, None, "state"),
        P(None, ("dp", "state")),
        P("dp", None, "state"),
        P("dp", "state"),
        P("dp", "state"),
        P("dp", "state"),
        P("dp", "state"),
        P("dp", None, "state"),
        P(("dp", "state"), None, None),
        P("state", "dp"),
    )
    body = grouped if dict(mesh.shape) == {"dp": 8, "state": 4} else shards
    return jax.shard_map(body, mesh=mesh, in_specs=in_specs, out_specs=out_specs, check_vma=False)
```

```python
import math

import jax
import jax.numpy as jnp
from jax import lax
from jax.experimental import pallas as pl
from jax.experimental.pallas import tpu as pltpu
from jax.sharding import PartitionSpec as P

DH = 128


EPS = 1e-06
NEGATIVE = -1e30
HIGHEST = lax.Precision.HIGHEST


def rms_norm(tensor, gains_row):
    return tensor * lax.rsqrt(jnp.mean(tensor * tensor, axis=-1, keepdims=True) + EPS) * gains_row


def norm_back(tensor, gains_row, cotangent):
    return jax.vjp(rms_norm, tensor, gains_row)[1](cotangent)


def smooth_gelu(tensor):
    return jax.nn.gelu(tensor, approximate=True)


def renew_state(state_now, gate_values):
    return state_now * jax.nn.sigmoid(gate_values[2] + 1.0) + jnp.tanh(
        gate_values[0]
    ) * jax.nn.sigmoid(gate_values[1] - 1.0)


def split_heads(tensor):
    return tensor.reshape(tensor.shape[0], tensor.shape[1], tensor.shape[2] // DH, DH)


def merge_heads(tensor):
    return tensor.reshape(tensor.shape[0], tensor.shape[1], tensor.shape[2] * DH)


def score_grid(queries, key_rows, bias_add, allowed):
    scores = jnp.einsum(
        "iqhd,ikhd->ihqk", queries, key_rows, preferred_element_type=jnp.float32
    ) / math.sqrt(DH)
    if bias_add is not None:
        scores = scores + bias_add[None]
    return jnp.where(allowed[:, None], scores, NEGATIVE)


def attend_forward(queries, key_rows, values, bias_add, allowed):
    scores = score_grid(queries, key_rows, bias_add, allowed)
    row_max = jnp.max(scores, axis=-1, keepdims=True)
    weights = jnp.exp(scores - row_max)
    row_total = jnp.sum(weights, axis=-1, keepdims=True)
    attn_probs = (weights / row_total).astype(jnp.bfloat16)
    mixed_heads = jnp.einsum(
        "ihqk,ikhd->iqhd", attn_probs, values, preferred_element_type=jnp.float32
    )
    return (merge_heads(mixed_heads.astype(jnp.bfloat16)), row_max + jnp.log(row_total))


def attention_backward_pass(queries, key_rows, values, bias_add, allowed, log_total, grad_mixed):
    scores = score_grid(queries, key_rows, bias_add, allowed)
    attn_probs = jnp.exp(scores - log_total)
    probs_grad = jnp.einsum(
        "iqhd,ikhd->ihqk", grad_mixed, values, preferred_element_type=jnp.float32
    )
    scores_grad = attn_probs * (
        probs_grad - jnp.sum(attn_probs * probs_grad, axis=-1, keepdims=True)
    )
    scores_grad = scores_grad.astype(jnp.bfloat16)
    values_grad = jnp.einsum(
        "ihqk,iqhd->ikhd",
        attn_probs.astype(jnp.bfloat16),
        grad_mixed,
        preferred_element_type=jnp.float32,
    )
    queries_grad = jnp.einsum(
        "ihqk,ikhd->iqhd", scores_grad, key_rows, preferred_element_type=jnp.float32
    ) / math.sqrt(DH)
    keys_grad = jnp.einsum(
        "ihqk,iqhd->ikhd", scores_grad, queries, preferred_element_type=jnp.float32
    ) / math.sqrt(DH)
    return (
        merge_heads(queries_grad),
        merge_heads(keys_grad),
        merge_heads(values_grad),
        scores_grad,
    )


def diagonal_sums(grid_values):
    num_heads, num_rows, num_cols = grid_values.shape
    flat = grid_values.reshape(num_heads, num_rows * num_cols)
    flat = jnp.pad(flat, ((0, 0), (0, num_rows)))
    sums = jnp.sum(flat.reshape(num_heads, num_rows, num_cols + 1), axis=1)
    return sums[:, num_rows:0:-1]


def toeplitz_grid(per_offset, num_rows):
    num_cols = 2 * num_rows
    line = jnp.pad(per_offset[::-1].T, ((0, 0), (1, num_cols - num_rows)))
    flat = jnp.tile(line, (1, num_rows))[:, : num_rows * num_cols]
    return flat.reshape(-1, num_rows, num_cols)


def sum_rows(partial_value):
    return lax.psum_scatter(
        partial_value.astype(jnp.bfloat16), "state", scatter_dimension=1, tiled=True
    ).astype(jnp.float32)


def whole_rows(partial_value):
    return lax.all_gather(partial_value, "state", axis=1, tiled=True)


def shards(
    tokens,
    carried_state,
    past_keys,
    fresh_start,
    valid_count,
    bucket_ids,
    grad_output,
    grad_state,
    norm_gains,
    token_qkv,
    token_out,
    bias_table,
    mlp_up,
    mlp_down,
    state_qkv,
    state_gates,
    initial_state,
):
    item_count, blocks, share_rows, model_width = tokens.shape
    groups = lax.axis_size("state")
    state_rank = lax.axis_index("state")
    window_width = share_rows * groups
    vector_rows = carried_state.shape[1] * groups
    local_width = token_qkv.shape[2]
    qkv_full, out_full, up_full, down_full, sqkv_full, gates_full, initial_full = (
        lax.all_gather(token_qkv, "dp", axis=0, tiled=True),
        lax.all_gather(token_out, "dp", axis=0, tiled=True),
        lax.all_gather(mlp_up, "dp", axis=0, tiled=True),
        lax.all_gather(mlp_down, "dp", axis=0, tiled=True),
        lax.all_gather(state_qkv, "dp", axis=0, tiled=True),
        lax.all_gather(state_gates, "dp", axis=0, tiled=True),
        lax.all_gather(initial_state, "dp", axis=1, tiled=True),
    )
    gates_used = lax.dynamic_slice_in_dim(gates_full, state_rank * local_width, local_width, 2)
    one_hot = (bucket_ids[:, None] == jnp.arange(bias_table.shape[0])[None, :]).astype(jnp.float32)
    per_offset = jnp.dot(one_hot, bias_table, precision=HIGHEST)
    query_pos = jnp.arange(window_width)[:, None]
    key_pos = jnp.arange(2 * window_width)[None, :]
    offset = window_width + query_pos - key_pos
    inside = (offset >= 0) & (offset < window_width)
    bias_grid = toeplitz_grid(per_offset, window_width)
    token_bias = jnp.pad(bias_grid, ((0, 0), (0, 0), (0, vector_rows)))
    is_fresh = fresh_start == 1
    state_now = jnp.where(
        is_fresh[:, None, None], initial_full.astype(jnp.float32)[None], carried_state
    )
    past_key = past_keys[:, :, 0]
    past_value = past_keys[:, :, 1]
    past_ok = jnp.broadcast_to(~is_fresh[:, None], (item_count, window_width))
    gains_token, gains_middle, gains_state = (norm_gains[0], norm_gains[1], norm_gains[2])
    share_pos = state_rank * share_rows + jnp.arange(share_rows)
    square_sums = jnp.zeros((3,), jnp.float32)
    valid_total = jnp.zeros((), jnp.float32)
    kept_values = []
    results = []
    for block_at in range(blocks):
        token_ok = (
            block_at * window_width + jnp.arange(window_width)[None, :] < valid_count[:, None]
        )
        inputs = tokens[:, block_at].astype(jnp.float32)
        normed, state_normed = (
            lax.all_gather(
                rms_norm(inputs, gains_token).astype(jnp.bfloat16), "state", axis=1, tiled=True
            ),
            lax.all_gather(
                rms_norm(state_now, gains_state).astype(jnp.bfloat16), "state", axis=1, tiled=True
            ),
        )
        project = jnp.einsum(
            "iwd,dch->ciwh", normed, qkv_full, preferred_element_type=jnp.float32
        ).astype(jnp.bfloat16)
        state_project = jnp.einsum(
            "ind,dch->cinh", state_normed, sqkv_full, preferred_element_type=jnp.float32
        ).astype(jnp.bfloat16)
        token_keys = jnp.concatenate([past_key, project[1], state_project[1]], axis=1)
        token_values = jnp.concatenate([past_value, project[2], state_project[2]], axis=1)
        window_ok = inside[None] & jnp.concatenate([past_ok, token_ok], axis=1)[:, None, :]
        token_allowed = jnp.concatenate(
            [window_ok, jnp.ones((item_count, window_width, vector_rows), jnp.bool_)], axis=2
        )
        mixed_heads, token_total = attend_forward(
            split_heads(project[0]),
            split_heads(token_keys),
            split_heads(token_values),
            token_bias,
            token_allowed,
        )
        branch = sum_rows(
            jnp.einsum("iwh,dh->iwd", mixed_heads, out_full, preferred_element_type=jnp.float32)
        )
        middle = inputs + branch
        middle_normed = lax.all_gather(
            rms_norm(middle, gains_middle).astype(jnp.bfloat16), "state", axis=1, tiled=True
        )
        up_values = jnp.einsum(
            "iwd,df->iwf", middle_normed, up_full, preferred_element_type=jnp.float32
        )
        hidden = smooth_gelu(up_values).astype(jnp.bfloat16)
        feed_out = sum_rows(
            jnp.einsum("iwf,df->iwd", hidden, down_full, preferred_element_type=jnp.float32)
        )
        result = middle + feed_out
        results.append(result.astype(jnp.bfloat16))
        share_ok = (block_at * window_width + share_pos[None, :] < valid_count[:, None]).astype(
            jnp.float32
        )[:, :, None]
        square_sums = square_sums + jnp.stack(
            [
                jnp.sum(share_ok * result * result),
                jnp.sum(share_ok * branch * branch),
                jnp.sum(share_ok * feed_out * feed_out),
            ]
        )
        valid_total = valid_total + jnp.sum(share_ok)
        state_keys = jnp.concatenate([state_project[1], project[1]], axis=1)
        state_values = jnp.concatenate([state_project[2], project[2]], axis=1)
        state_allowed = jnp.concatenate(
            [
                jnp.ones((item_count, vector_rows, vector_rows), jnp.bool_),
                jnp.broadcast_to(token_ok[:, None, :], (item_count, vector_rows, window_width)),
            ],
            axis=2,
        )
        state_mixed, state_total = attend_forward(
            split_heads(state_project[0]),
            split_heads(state_keys),
            split_heads(state_values),
            None,
            state_allowed,
        )
        gate_source = state_mixed
        gate_values = lax.psum_scatter(
            jnp.einsum(
                "inh,dch->cind", state_mixed, gates_used, preferred_element_type=jnp.float32
            ).astype(jnp.bfloat16),
            "state",
            scatter_dimension=2,
            tiled=True,
        ).astype(jnp.float32)
        kept_values.append(
            (
                inputs,
                normed,
                state_normed,
                project,
                state_project,
                token_keys,
                token_values,
                token_allowed,
                mixed_heads,
                token_total,
                middle,
                middle_normed,
                up_values,
                hidden,
                state_keys,
                state_values,
                state_allowed,
                state_total,
                gate_source,
                gate_values,
                state_now,
            )
        )
        state_now = renew_state(state_now, gate_values)
        past_key, past_value, past_ok = (project[1], project[2], token_ok)
    square_sums, valid_total = lax.psum((square_sums, valid_total), ("dp", "state"))
    rms_stats = jnp.sqrt(square_sums / valid_total)
    qkv_grad = jnp.zeros(qkv_full.shape, jnp.float32)
    out_grad = jnp.zeros(out_full.shape, jnp.float32)
    up_grad = jnp.zeros(up_full.shape, jnp.float32)
    down_grad = jnp.zeros(down_full.shape, jnp.float32)
    sqkv_grad = jnp.zeros(sqkv_full.shape, jnp.float32)
    gate_grad = jnp.zeros(gates_used.shape, jnp.float32)
    bias_grad = jnp.zeros(bias_grid.shape, jnp.float32)
    gain_token_grad = jnp.zeros((model_width,), jnp.float32)
    gain_middle_grad = jnp.zeros((model_width,), jnp.float32)
    gain_state_grad = jnp.zeros((model_width,), jnp.float32)
    state_grad = grad_state
    carried_key_rows = jnp.zeros(past_keys[:, :, 0].shape, jnp.float32)
    carry_value = jnp.zeros(past_keys[:, :, 0].shape, jnp.float32)
    token_grads = [None] * blocks
    for block_at in reversed(range(blocks)):
        (
            inputs,
            normed,
            state_normed,
            project,
            state_project,
            token_keys,
            token_values,
            token_allowed,
            mixed_heads,
            token_total,
            middle,
            middle_normed,
            up_values,
            hidden,
            state_keys,
            state_values,
            state_allowed,
            state_total,
            gate_source,
            gate_values,
            state_before,
        ) = kept_values[block_at]
        direct_grad, gates_grad = jax.vjp(renew_state, state_before, gate_values)[1](state_grad)
        gates_low = gates_grad.astype(jnp.bfloat16)
        gates_rows = lax.all_gather(gates_low, "state", axis=2, tiled=True)
        state_mixed_grad = jnp.einsum(
            "cind,dch->inh", gates_rows, gates_used, preferred_element_type=jnp.float32
        ).astype(jnp.bfloat16)
        gate_grad = gate_grad + jnp.einsum(
            "inh,cind->dch", gate_source, gates_rows, preferred_element_type=jnp.float32
        )
        state_query_gradient, state_keys_gradient, state_values_gradient, discarded_output = (
            attention_backward_pass(
                split_heads(state_project[0]),
                split_heads(state_keys),
                split_heads(state_values),
                None,
                state_allowed,
                state_total,
                split_heads(state_mixed_grad),
            )
        )
        out_share = grad_output[:, block_at]
        out_whole = whole_rows(out_share)
        down_grad = down_grad + jnp.einsum(
            "iwf,iwd->df", hidden, out_whole, preferred_element_type=jnp.float32
        )
        hidden_grad = jnp.einsum(
            "iwd,df->iwf", out_whole, down_full, preferred_element_type=jnp.float32
        )
        up_values_grad = jax.vjp(smooth_gelu, up_values)[1](hidden_grad)[0].astype(jnp.bfloat16)
        up_grad = up_grad + jnp.einsum(
            "iwd,iwf->df", middle_normed, up_values_grad, preferred_element_type=jnp.float32
        )
        middle_normed_grad = lax.psum_scatter(
            jnp.einsum(
                "iwf,df->iwd", up_values_grad, up_full, preferred_element_type=jnp.float32
            ).astype(jnp.bfloat16),
            "state",
            scatter_dimension=1,
            tiled=True,
        ).astype(jnp.float32)
        middle_grad, gain_part = norm_back(middle, gains_middle, middle_normed_grad)
        middle_grad = out_share.astype(jnp.float32) + middle_grad
        gain_middle_grad = gain_middle_grad + gain_part
        branch_whole = whole_rows(middle_grad.astype(jnp.bfloat16))
        out_grad = out_grad + jnp.einsum(
            "iwh,iwd->dh", mixed_heads, branch_whole, preferred_element_type=jnp.float32
        )
        mixed_grad = jnp.einsum(
            "iwd,dh->iwh", branch_whole, out_full, preferred_element_type=jnp.float32
        ).astype(jnp.bfloat16)
        query_grad, token_keys_gradient, tvalues_grad, scores_grad = attention_backward_pass(
            split_heads(project[0]),
            split_heads(token_keys),
            split_heads(token_values),
            token_bias,
            token_allowed,
            token_total,
            split_heads(mixed_grad),
        )
        bias_grad = bias_grad + jnp.sum(
            scores_grad[:, :, :, : 2 * window_width].astype(jnp.float32), axis=0
        )
        key_gradient_rows = (
            token_keys_gradient[:, window_width : 2 * window_width]
            + state_keys_gradient[:, vector_rows:]
            + carried_key_rows
        )
        value_grad = (
            tvalues_grad[:, window_width : 2 * window_width]
            + state_values_gradient[:, vector_rows:]
            + carry_value
        )
        state_key_gradient = (
            token_keys_gradient[:, 2 * window_width :] + state_keys_gradient[:, :vector_rows]
        )
        state_value_gradient = (
            tvalues_grad[:, 2 * window_width :] + state_values_gradient[:, :vector_rows]
        )
        project_grad = jnp.stack([query_grad, key_gradient_rows, value_grad]).astype(jnp.bfloat16)
        state_projection_gradient = jnp.stack(
            [state_query_gradient, state_key_gradient, state_value_gradient]
        ).astype(jnp.bfloat16)
        qkv_grad = qkv_grad + jnp.einsum(
            "iwd,ciwh->dch", normed, project_grad, preferred_element_type=jnp.float32
        )
        sqkv_grad = sqkv_grad + jnp.einsum(
            "ind,cinh->dch",
            state_normed,
            state_projection_gradient,
            preferred_element_type=jnp.float32,
        )
        normed_grad, state_normed_grad = (
            lax.psum_scatter(
                jnp.einsum(
                    "ciwh,dch->iwd", project_grad, qkv_full, preferred_element_type=jnp.float32
                ).astype(jnp.bfloat16),
                "state",
                scatter_dimension=1,
                tiled=True,
            ).astype(jnp.float32),
            lax.psum_scatter(
                jnp.einsum(
                    "cinh,dch->ind",
                    state_projection_gradient,
                    sqkv_full,
                    preferred_element_type=jnp.float32,
                ).astype(jnp.bfloat16),
                "state",
                scatter_dimension=1,
                tiled=True,
            ).astype(jnp.float32),
        )
        input_grad, gain_part = norm_back(inputs, gains_token, normed_grad)
        gain_token_grad = gain_token_grad + gain_part
        token_grads[block_at] = (middle_grad + input_grad).astype(jnp.bfloat16)
        state_norm_grad, gain_part = norm_back(state_before, gains_state, state_normed_grad)
        gain_state_grad = gain_state_grad + gain_part
        state_grad = direct_grad + state_norm_grad
        carried_key_rows = token_keys_gradient[:, :window_width]
        carry_value = tvalues_grad[:, :window_width]
    carried_grad = jnp.where(is_fresh[:, None, None], 0.0, state_grad)
    initial_part = jnp.sum(jnp.where(is_fresh[:, None, None], state_grad, 0.0), axis=0)
    past_grad = jnp.stack([carried_key_rows, carry_value], axis=2)
    table_part = jnp.dot(one_hot.T, diagonal_sums(bias_grad).T, precision=HIGHEST)
    gain_columns = jnp.stack([gain_token_grad, gain_middle_grad, gain_state_grad], axis=1)
    summed = (
        lax.psum_scatter(
            qkv_grad.astype(jnp.bfloat16), "dp", scatter_dimension=0, tiled=True
        ).astype(jnp.float32),
        lax.psum_scatter(
            out_grad.astype(jnp.bfloat16), "dp", scatter_dimension=0, tiled=True
        ).astype(jnp.float32),
        lax.psum_scatter(
            table_part.astype(jnp.bfloat16), "dp", scatter_dimension=0, tiled=True
        ).astype(jnp.float32),
        lax.psum_scatter(
            up_grad.astype(jnp.bfloat16), "dp", scatter_dimension=0, tiled=True
        ).astype(jnp.float32),
        lax.psum_scatter(
            down_grad.astype(jnp.bfloat16), "dp", scatter_dimension=0, tiled=True
        ).astype(jnp.float32),
        lax.psum_scatter(
            sqkv_grad.astype(jnp.bfloat16), "dp", scatter_dimension=0, tiled=True
        ).astype(jnp.float32),
        lax.psum_scatter(
            initial_part.astype(jnp.bfloat16), "dp", scatter_dimension=1, tiled=True
        ).astype(jnp.float32),
        lax.psum_scatter(
            gate_grad.astype(jnp.bfloat16), "dp", scatter_dimension=0, tiled=True
        ).astype(jnp.float32),
        lax.psum_scatter(
            gain_columns.astype(jnp.bfloat16), "dp", scatter_dimension=0, tiled=True
        ).astype(jnp.float32),
    )
    gate_pieces, gain_pieces = (
        lax.all_to_all(
            summed[7][:, :, None, :].astype(jnp.bfloat16),
            "state",
            split_axis=0,
            concat_axis=2,
            tiled=True,
        ).astype(jnp.float32),
        lax.all_to_all(
            summed[8][:, :, None, None].astype(jnp.bfloat16),
            "state",
            split_axis=0,
            concat_axis=2,
            tiled=True,
        ).astype(jnp.float32),
    )
    gains_grad = jnp.sum(gain_pieces, axis=(2, 3)).T
    gates_grad_out = gate_pieces.reshape(
        gate_pieces.shape[0], gate_pieces.shape[1], gate_pieces.shape[2] * gate_pieces.shape[3]
    )
    return (
        jnp.stack(results, axis=1),
        state_now,
        rms_stats,
        jnp.stack(token_grads, axis=1),
        carried_grad,
        past_grad,
        gains_grad,
        summed[0],
        summed[1],
        summed[2],
        summed[3],
        summed[4],
        summed[5],
        gates_grad_out,
        summed[6],
    )


MESH = pl.DeviceIdType.MESH
NN = (((1,), (0,)), ((), ()))
NT = (((1,), (1,)), ((), ()))
TN = (((0,), (0,)), ((), ()))
VMEM_BYTES = 63 * 2**20


class Place:
    def __init__(self):
        chip_core, level = lax.axis_index("dp"), lax.axis_index("state")
        core, low = lax.rem(chip_core, 2), lax.rem(level, 2)
        x, y = lax.rem(chip_core // 2, 2), chip_core // 4
        flip = lambda bit: 1 - 2 * bit
        self.dp, self.core, self.level, self.half = chip_core, core, level, level // 2
        self.rank = 2 * low + core
        self.ranks = [self.rank, 2 * low + 1 - core, 2 * (1 - low) + core, 2 * (1 - low) + 1 - core]
        self.mates = [
            None,
            (chip_core + flip(core), level),
            (chip_core, level + flip(low)),
            (chip_core + flip(core), level + flip(low)),
        ]
        self.planes = [2 * y + x, 2 * y + 1 - x, 2 * (1 - y) + x, 2 * (1 - y) + 1 - x]
        self.plane_mates = [
            None,
            (chip_core + 2 * flip(x), level),
            (chip_core + 4 * flip(y), level),
            (chip_core + 2 * flip(x) + 4 * flip(y), level),
        ]
        first = chip_core - core
        self.there = (first + low, 2 * core + self.half)
        self.across = (first + low, 2 * (1 - core) + self.half)
        self.from_there = (first + self.half, 2 * low + core)
        self.from_across = (first + 1 - self.half, 2 * low + core)
        self.stays = (core == low) & (self.half == core)


def rows_at(start, size, step=128):
    return pl.ds(pl.multiple_of(start, step), size)


class Links:
    def __init__(self, send_sems, recv_sems):
        self.send_sems, self.recv_sems = send_sems, recv_sems
        self.used = 0
        self.open_sends = []
        self.open_turns = []

    def plan(self, source, target, device):
        at = self.used
        self.used += 1
        return pltpu.make_async_remote_copy(
            src_ref=source,
            dst_ref=target,
            send_sem=self.send_sems.at[at],
            recv_sem=self.recv_sems.at[at],
            device_id=device,
            device_id_type=MESH,
        )

    def copy(self, source, target, device):
        moved = self.plan(source, target, device)
        moved.start()
        self.open_sends.append(moved)
        return moved

    def sent(self, moved):
        self.open_sends = [other for other in self.open_sends if other is not moved]
        moved.wait_send()

    def close(self):
        for moved in self.open_sends:
            moved.wait_send()
        for turn in self.open_turns:
            turn.sent()
        self.open_sends, self.open_turns = [], []


def greet(devices, turned=None):
    barrier = pltpu.get_barrier_semaphore()
    for device in devices:
        pl.semaphore_signal(barrier, inc=1, device_id=device, device_id_type=MESH)
    if turned is None:
        pl.semaphore_wait(barrier, len(devices))
    else:
        moves = jnp.logical_not(turned.stays)

        @pl.when(moves)
        def _():
            pl.semaphore_signal(barrier, inc=1, device_id=turned.from_there, device_id_type=MESH)

        pl.semaphore_wait(barrier, len(devices) + moves.astype(jnp.int32))


class Turn:
    def __init__(self, links, here, source, target, device):
        self.stays = here.stays
        self.moved = links.plan(source, target, device)
        self.kept = pltpu.make_async_copy(source, target, links.recv_sems.at[links.used - 1])
        links.open_turns.append(self)

        @pl.when(jnp.logical_not(self.stays))
        def _():
            self.moved.start()

        @pl.when(self.stays)
        def _():
            self.kept.start()

    def arrived(self):
        @pl.when(jnp.logical_not(self.stays))
        def _():
            self.moved.wait_recv()

        @pl.when(self.stays)
        def _():
            self.kept.wait()

    def sent(self):
        @pl.when(jnp.logical_not(self.stays))
        def _():
            self.moved.wait_send()


class WeightGather:
    def __init__(self, links, here, local, full):
        self.links, self.here, self.local, self.full = links, here, local, full
        self.rows = local.shape[0]

    def enter(self):
        target = self.full.at[rows_at(self.here.dp * self.rows, self.rows)]
        self.turn = Turn(self.links, self.here, self.local, target, self.here.there)
        self.cross = self.links.copy(self.local, target, self.here.across)
        return self

    def block(self, k):
        return self.full.at[rows_at(self.here.planes[k] * 2 * self.rows, 2 * self.rows)]

    def half(self, k, which):
        start = self.here.planes[k] * 2 * self.rows + which * self.rows
        return self.full.at[rows_at(start, self.rows)]

    def spread(self):
        self.turn.arrived()
        self.cross.wait_recv()
        mates = self.here.plane_mates
        self.over_x = self.links.copy(self.block(0), self.block(0), mates[1])
        self.over_y = self.links.copy(self.block(0), self.block(0), mates[2])

    def forward(self):
        mates = self.here.plane_mates
        self.over_x.wait_recv()
        self.corner_0 = self.links.copy(self.half(1, 0), self.half(1, 0), mates[2])
        self.over_y.wait_recv()
        self.corner_1 = self.links.copy(self.half(2, 1), self.half(2, 1), mates[1])

    def finish(self):
        self.corner_0.wait_recv()
        self.corner_1.wait_recv()


class GateGather:
    def __init__(self, links, here, local, full, sem):
        self.links, self.here, self.local, self.full, self.sem = links, here, local, full, sem
        self.rows = local.shape[0]

    def block(self, k):
        start = (2 * self.here.planes[k] + self.here.core) * self.rows
        return self.full.at[rows_at(start, self.rows)]

    def part(self, k, which):
        size = self.rows // 2
        start = (2 * self.here.planes[k] + self.here.core) * self.rows + which * size
        return self.full.at[rows_at(start, size, 64)]

    def spread(self):
        mates, sibling = self.here.plane_mates, self.here.mates[1]
        self.over_x = self.links.copy(self.local, self.block(0), mates[1])
        self.over_y = self.links.copy(self.local, self.block(0), mates[2])
        self.near = [self.links.copy(self.local, self.block(0), sibling)]
        self.kept = pltpu.make_async_copy(self.local, self.block(0), self.sem)
        self.kept.start()

    def forward(self):
        mates, sibling = self.here.plane_mates, self.here.mates[1]
        self.over_x.wait_recv()
        self.corner_0 = self.links.copy(self.part(1, 0), self.part(1, 0), mates[2])
        self.near.append(self.links.copy(self.block(1), self.block(1), sibling))
        self.over_y.wait_recv()
        self.corner_1 = self.links.copy(self.part(2, 1), self.part(2, 1), mates[1])
        self.near.append(self.links.copy(self.block(2), self.block(2), sibling))

    def last(self):
        self.corner_0.wait_recv()
        self.corner_1.wait_recv()
        self.near.append(self.links.copy(self.block(3), self.block(3), self.here.mates[1]))

    def finish(self):
        self.kept.wait()
        for moved in self.near:
            moved.wait_recv()


class RowGather:
    def __init__(self, links, here, ref, base, rows):
        self.links, self.here, self.ref, self.base, self.rows = links, here, ref, base, rows

    def part(self, k):
        return self.ref.at[rows_at(self.base + self.here.ranks[k] * self.rows, self.rows)]

    def start(self):
        own, mates = self.part(0), self.here.mates
        self.far = self.links.copy(own, own, mates[2])
        self.near = self.links.copy(own, own, mates[1])
        return self

    def ready(self, k):
        if k == 1:
            self.near.wait_recv()
        elif k == 2:
            self.far.wait_recv()
            block = self.part(2)
            self.last = self.links.copy(block, block, self.here.mates[1])
        elif k == 3:
            self.last.wait_recv()

    def sent(self):
        for moved in (self.far, self.near, self.last):
            self.links.sent(moved)


class RowSum:
    def __init__(self, links, here, stage, near_in, far_out, far_in, rows):
        self.links, self.here, self.rows = links, here, rows
        self.stage, self.near_in, self.far_out, self.far_in = stage, near_in, far_out, far_in

    def part(self, k):
        return self.stage.at[rows_at(self.here.ranks[k] * self.rows, self.rows)]

    def fill(self, make_rows):
        sibling = self.here.mates[1]
        for k, slot in ((3, 0), (1, 1)):
            self.part(k)[...] = make_rows(self.here.ranks[k]).astype(jnp.bfloat16)
            moved = self.links.copy(self.part(k), self.near_in.at[slot], sibling)
            if slot == 0:
                self.near_far = moved
            else:
                self.near_own = moved
        for k in (2, 0):
            self.part(k)[...] = make_rows(self.here.ranks[k]).astype(jnp.bfloat16)
        return self

    def forward(self):
        self.near_far.wait_recv()
        summed = self.part(2)[...].astype(jnp.float32) + self.near_in[0].astype(jnp.float32)
        self.far_out[...] = summed.astype(jnp.bfloat16)
        self.far = self.links.copy(self.far_out, self.far_in, self.here.mates[2])
        return self

    def sent(self):
        for moved in (self.near_far, self.near_own, self.far):
            self.links.sent(moved)

    def finish(self):
        self.near_own.wait_recv()
        self.far.wait_recv()
        return (
            self.part(0)[...].astype(jnp.float32)
            + self.near_in[1].astype(jnp.float32)
            + self.far_in[...].astype(jnp.float32)
        )


def row_sum_scratch(rows, width):
    return [
        pltpu.VMEM((4 * rows, width), jnp.bfloat16),
        pltpu.VMEM((2, rows, width), jnp.bfloat16),
        pltpu.VMEM((rows, width), jnp.bfloat16),
        pltpu.VMEM((rows, width), jnp.bfloat16),
    ]


def dot(left, right, dims):
    return lax.dot_general(left, right, dims, preferred_element_type=jnp.float32)


def scale_of(tensor):
    return lax.rsqrt(jnp.mean(tensor * tensor, axis=-1, keepdims=True) + EPS)


def rms_back(tensor, gains_row, cotangent):
    scale = scale_of(tensor)
    weighted = cotangent * gains_row
    inner = jnp.mean(tensor * weighted, axis=-1, keepdims=True)
    straight = scale * weighted - tensor * (scale * scale * scale * inner)
    return straight, jnp.sum(cotangent * tensor * scale, axis=0, keepdims=True)


def row_mask(facts, start, rows):
    place_of = lax.broadcasted_iota(jnp.int32, (rows, 1), 0) + start
    return jnp.where(place_of.astype(jnp.float32) < facts[2:3, 0:1], 1.0, 0.0)


def bias_tiles(lines_ref, tiles_ref, heads, width):
    for head in range(heads):
        line = lines_ref[head : head + 1, :]
        spread = jnp.broadcast_to(line, (tiles_ref.shape[1], line.shape[1]))
        tiles_ref[head] = pltpu.roll(spread, 0, 1, stride=1, stride_axis=0)[:, :width]


def softmax_pair(first, second):
    top = jnp.maximum(
        jnp.max(first, axis=-1, keepdims=True), jnp.max(second, axis=-1, keepdims=True)
    )
    first, second = jnp.exp(first - top), jnp.exp(second - top)
    total = jnp.sum(first, axis=-1, keepdims=True) + jnp.sum(second, axis=-1, keepdims=True)
    share = 1.0 / total
    return (
        (first * share).astype(jnp.bfloat16),
        (second * share).astype(jnp.bfloat16),
        top + jnp.log(total),
    )


TILE = 256
ROOT = 1.0 / math.sqrt(DH)


def forward_kernel(
    x_in, carried_in, initial_in, far_past, facts_in, far_gout, far_gstate, gains_ref,
    wst_in, wtok_in, wout_in, gates_in, far_wup, far_wdn,
    far_normed, far_snormed, far_queries, far_keys, far_values, far_state_qkv, far_lse, far_mixed,
    far_wst, far_wtok, far_wout, far_gates, far_x, far_s0, far_s1,
    far_gate_values, far_gstate_here, far_wup_grad, far_wdn_grad,
    smixed_rows, s2_ref, facts, block_out, middle_grad, small_sums,
    normed, snormed, queries, keys, values, state_qkv, lse_ref, mixed,
    wst, wtok, wout, gates, x_ref, s0_ref, s1_ref,
    smixed, tiles, initial_all, normed_send, s0_send, gate_values, wup, wdn, middle,
    middle_normed, gout_rows, gout, slope, hidden, up_grad, grad_stage, *rest,
):
    rs = [rest[4 * k : 4 * k + 4] for k in range(4)]
    links = Links(rest[16], rest[17])
    local_sems, keep_sems = rest[18], rest[19]
    kept = []

    def keep(source, target):
        moved = pltpu.make_async_copy(source, target, keep_sems.at[len(kept)])
        moved.start()
        kept.append(moved)

    here = Place()
    rank, ranks, mates = here.rank, here.ranks, here.mates
    rows = s0_ref.shape[0]
    window = 4 * rows
    width = queries.shape[1]
    heads = width // DH
    ring = [(lax.rem(here.dp + step, 8), here.level) for step in range(1, 8)]
    greet(ring + mates[2:] + [here.from_across], here)

    def turn(source, target):
        return Turn(links, here, source, target, here.there)

    part = initial_in.shape[1]
    own_columns = pl.ds(pl.multiple_of(here.dp * part, part), part)
    initial_moves = [links.copy(initial_in, initial_all.at[:, own_columns], mate) for mate in ring]
    facts_turn = turn(facts_in, facts)
    gather_wst = WeightGather(links, here, wst_in, wst).enter()
    initial_all[:, own_columns] = initial_in[...]
    for moved in initial_moves:
        moved.wait_recv()
    is_fresh = facts_in[3:4, :] > 0.5
    start = jnp.where(is_fresh, initial_all[...].astype(jnp.float32), carried_in[...])
    s0_send[...] = start
    normed_send[...] = (start * scale_of(start) * gains_ref[2:3, :]).astype(jnp.bfloat16)
    normed_turn = turn(normed_send, snormed.at[rows_at(here.level * rows, rows)])
    facts_turn.arrived()
    bias_tiles(facts, tiles, heads, 3 * TILE)
    gather_wst.spread()
    gather_wtok = WeightGather(links, here, wtok_in, wtok).enter()
    normed_turn.arrived()
    gather_s0 = RowGather(links, here, snormed, 0, rows).start()

    def enter_x(block):
        at = pl.ds(block * rows, rows)
        return turn(x_in.at[at], x_ref.at[at])

    def norm_x(block, moved):
        moved.arrived()
        x = x_ref[block * rows : (block + 1) * rows, :].astype(jnp.float32)
        normed[rows_at(block * window + rank * rows, rows), :] = (
            x * scale_of(x) * gains_ref[0:1, :]
        ).astype(jnp.bfloat16)
        return RowGather(links, here, normed, block * window, rows).start()

    x_turn_0 = enter_x(0)
    gather_wst.forward()
    gather_wtok.spread()
    x_turn_1 = enter_x(1)

    def key_mask(start, size):
        place_of = lax.broadcasted_iota(jnp.int32, (1, size), 1).astype(jnp.float32)
        place_of = place_of + float(start - window)
        own = jnp.where(place_of < facts[2:3, 0:size], 0.0, NEGATIVE)
        return jnp.where(place_of < 0.0, facts[3:4, 0:size] * NEGATIVE, own)

    def project_state(block, gather):
        for k in range(4):
            gather.ready(k)
            at = rows_at(block * window + ranks[k] * rows, rows)
            state_qkv[at, :] = dot(snormed[at, :], wst[...], NN).astype(jnp.bfloat16)

    def project_token(block, gather):
        for k in range(4):
            gather.ready(k)
            at = rows_at(block * window + ranks[k] * rows, rows)
            later = rows_at((block + 1) * window + ranks[k] * rows, rows)
            out = dot(normed[at, :], wtok[...], NN).astype(jnp.bfloat16)
            queries[at, :] = out[:, :width]
            keys[later, :] = out[:, width : 2 * width]
            values[later, :] = out[:, 2 * width :]

    def state_attention(block):
        base = block * window
        own = pl.ds((block + 1) * window, window)
        whole = pl.ds(base, window)
        own_mask = key_mask(base + window, window)
        for head in range(heads):
            at = head * DH
            for tile in range(window // TILE):
                here_rows = pl.ds(base + tile * TILE, TILE)
                query = state_qkv[here_rows, at : at + DH]
                first = dot(query, state_qkv[whole, width + at : width + at + DH], NT) * ROOT
                second = dot(query, keys[own, at : at + DH], NT) * ROOT + own_mask
                first, second, lse = softmax_pair(first, second)
                out = dot(first, state_qkv[whole, 2 * width + at : 2 * width + at + DH], NN)
                out = out + dot(second, values[own, at : at + DH], NN)
                smixed[here_rows, at : at + DH] = out.astype(jnp.bfloat16)
                lse_ref[here_rows, heads + head : heads + head + 1] = lse

    def token_attention(block):
        base = block * window
        whole = pl.ds(base, window)
        for tile in range(window // TILE):
            near_mask = key_mask(base + tile * TILE, 3 * TILE)
            for head in range(heads):
                at = head * DH
                here_rows = pl.ds(base + tile * TILE, TILE)
                near = pl.ds(base + tile * TILE, 3 * TILE)
                query = queries[here_rows, at : at + DH]
                first = dot(query, keys[near, at : at + DH], NT) * ROOT + tiles[head] + near_mask
                second = dot(query, state_qkv[whole, width + at : width + at + DH], NT) * ROOT
                first, second, lse = softmax_pair(first, second)
                out = dot(first, values[near, at : at + DH], NN)
                out = out + dot(second, state_qkv[whole, 2 * width + at : 2 * width + at + DH], NN)
                mixed[here_rows, at : at + DH] = out.astype(jnp.bfloat16)
                lse_ref[here_rows, head : head + 1] = lse

    def spread_state(block, buffer):
        moves = []
        columns = pl.ds(pl.multiple_of(rank * width, width), width)
        for k in (2, 3, 1):
            source = smixed.at[rows_at(block * window + ranks[k] * rows, rows)]
            moves.append(links.copy(source, buffer.at[:, columns], mates[k]))
        buffer[:, columns] = smixed[rows_at(block * window + rank * rows, rows), :]
        return moves

    def renew(block, buffer, state_now):
        size = state_now.shape[1]
        source = buffer[...]
        parts = []
        for c in range(3):
            part = dot(source, gates[:, c * size : (c + 1) * size], NT)
            gate_values[:, c * size : (c + 1) * size] = part
            parts.append(part)
        stored = pltpu.make_async_copy(
            gate_values, far_gate_values.at[pl.ds(block * rows, rows)], local_sems.at[0]
        )
        stored.start()
        new_state = state_now * jax.nn.sigmoid(parts[2] + 1.0) + jnp.tanh(parts[0]) * jax.nn.sigmoid(
            parts[1] - 1.0
        )
        return new_state, stored

    def branch_rows(block):
        def make(which):
            return dot(mixed[rows_at(block * window + which * rows, rows), :], wout[...], NT)

        return make

    sums = [RowSum(links, here, *rs[block], rows) for block in range(2)]

    def finish_branch(block):
        branch = sums[block].finish()
        at = slice(block * rows, (block + 1) * rows)
        total = x_ref[at, :].astype(jnp.float32) + branch
        middle[at, :] = total
        middle_normed[rows_at(block * window + rank * rows, rows), :] = (
            total * scale_of(total) * gains_ref[1:2, :]
        ).astype(jnp.bfloat16)
        gather = RowGather(links, here, middle_normed, block * window, rows).start()
        share = row_mask(facts, block * window + rank * rows, rows)
        return jnp.sum(branch * branch * share, axis=0, keepdims=True), gather

    def rise(block, gather):
        root = math.sqrt(2.0 / math.pi)
        for k in range(4):
            gather.ready(k)
            at = rows_at(block * window + ranks[k] * rows, rows)
            value = dot(middle_normed[at, :], wup[...], NN)
            square = value * value
            bend = jnp.tanh(root * value * (1.0 + 0.044715 * square))
            half = 0.5 * (1.0 + bend)
            hidden[at, :] = (value * half).astype(jnp.bfloat16)
            slope[at, :] = half + 0.5 * value * (1.0 - bend * bend) * (
                root * (1.0 + 3.0 * 0.044715 * square)
            )

    def feed_sum(block):
        return RowSum(links, here, *rs[block], rows).fill(
            lambda which: dot(hidden[rows_at(block * window + which * rows, rows), :], wdn[...], NT)
        )

    def start_gout(block):
        at = slice(block * rows, (block + 1) * rows)
        gout[rows_at(block * window + rank * rows, rows), :] = gout_rows[at, :]
        return RowGather(links, here, gout, block * window, rows).start()

    def feed_back(block, gather):
        for k in range(4):
            gather.ready(k)
            at = rows_at(block * window + ranks[k] * rows, rows)
            up_grad[at, :] = (dot(gout[at, :], wdn[...], NN) * slope[at, :]).astype(jnp.bfloat16)
        return RowSum(links, here, *rs[2 + block], rows).fill(
            lambda which: dot(up_grad[rows_at(block * window + which * rows, rows), :], wup[...], NT)
        )

    def weight_grad(stage, left, right, target, sem):
        step = 256
        for part in range(stage.shape[0] // step):
            at = slice(part * step, (part + 1) * step)
            stage[at, :] = dot(left[:, at], right[...], TN).astype(jnp.bfloat16)
        stored = pltpu.make_async_copy(stage, target, sem)
        stored.start()
        return stored

    gather_wst.finish()
    keep(wst, far_wst)
    project_state(0, gather_s0)
    gather_x0 = norm_x(0, x_turn_0)
    gather_wtok.forward()
    gather_gates = GateGather(links, here, gates_in, gates, local_sems.at[3])
    gather_gates.spread()
    gather_wout = WeightGather(links, here, wout_in, wout).enter()
    past_turns = [
        turn(far_past.at[0], keys.at[pl.ds(0, window)]),
        turn(far_past.at[1], values.at[pl.ds(0, window)]),
    ]
    gather_x1 = norm_x(1, x_turn_1)
    gather_wtok.finish()
    keep(wtok, far_wtok)
    keep(x_ref, far_x)
    project_token(0, gather_x0)
    state_attention(0)
    a2a_0 = smixed_rows.at[pl.ds(0, rows)]
    a2a_1 = smixed_rows.at[pl.ds(rows, rows)]
    moves_0 = spread_state(0, a2a_0)
    s0_turn = turn(s0_send, s0_ref)
    gather_wout.spread()
    gather_wup = WeightGather(links, here, far_wup, wup).enter()
    project_token(1, gather_x1)
    keep(normed, far_normed)
    keep(queries, far_queries)
    gather_gates.forward()
    for moved in past_turns:
        moved.arrived()
    keep(keys, far_keys)
    keep(values, far_values)
    token_attention(0)
    gather_wout.forward()
    gather_gates.last()
    gather_wdn = WeightGather(links, here, far_wdn, wdn).enter()
    gather_wup.spread()
    gather_wout.finish()
    keep(wout, far_wout)
    sums[0].fill(branch_rows(0))
    for moved in moves_0:
        moved.wait_recv()
    gather_gates.finish()
    keep(gates, far_gates)
    s0_turn.arrived()
    keep(s0_ref, far_s0)
    s1, keep_gates = renew(0, a2a_0, s0_ref[...])
    s1_ref[...] = s1
    keep(s1_ref, far_s1)
    snormed[rows_at(window + rank * rows, rows), :] = (s1 * scale_of(s1) * gains_ref[2:3, :]).astype(
        jnp.bfloat16
    )
    gather_s1 = RowGather(links, here, snormed, window, rows).start()
    sums[0].forward()
    gather_wup.forward()
    gather_wdn.spread()
    project_state(1, gather_s1)
    gout_turn = turn(far_gout, gout_rows)
    keep(snormed, far_snormed)
    keep(state_qkv, far_state_qkv)
    state_attention(1)
    moves_1 = spread_state(1, a2a_1)
    branch_total, gather_m0 = finish_branch(0)
    token_attention(1)
    keep(lse_ref, far_lse)
    keep(mixed, far_mixed)
    gather_wdn.forward()
    sums[1].fill(branch_rows(1))
    gather_wup.finish()
    gout_turn.arrived()
    gather_g0 = start_gout(0)
    rise(0, gather_m0)
    sums[1].forward()
    for moved in moves_1:
        moved.wait_recv()
    keep_gates.wait()
    s2, keep_gates = renew(1, a2a_1, s1_ref[...])
    gstate_turn = turn(far_gstate, far_gstate_here)
    s2_ref[...] = s2.astype(jnp.bfloat16)
    gather_wdn.finish()
    sums[0].sent()
    feed_0 = feed_sum(0)
    more, gather_m1 = finish_branch(1)
    branch_total = branch_total + more
    gather_g1 = start_gout(1)
    feed_0.forward()
    back_0 = feed_back(0, gather_g0)
    rise(1, gather_m1)
    sums[1].sent()
    feed_1 = feed_sum(1)
    back_0.forward()
    back_1 = feed_back(1, gather_g1)
    feed_1.forward()
    keep_down = weight_grad(grad_stage, gout, hidden, far_wdn_grad, local_sems.at[1])
    back_1.forward()
    keep_up = weight_grad(hidden, middle_normed, up_grad, far_wup_grad, local_sems.at[2])
    feed_total, result_total, gain_total = 0.0, 0.0, 0.0
    for block, feed_here in ((0, feed_0), (1, feed_1)):
        at = slice(block * rows, (block + 1) * rows)
        feed = feed_here.finish()
        result = middle[at, :] + feed
        block_out[at, :] = result.astype(jnp.bfloat16)
        share = row_mask(facts, block * window + rank * rows, rows)
        feed_total = feed_total + jnp.sum(feed * feed * share, axis=0, keepdims=True)
        result_total = result_total + jnp.sum(result * result * share, axis=0, keepdims=True)
    for block, back_here in ((1, back_1), (0, back_0)):
        at = slice(block * rows, (block + 1) * rows)
        straight, gain = rms_back(middle[at, :], gains_ref[1:2, :], back_here.finish())
        middle_grad[at, :] = gout_rows[at, :].astype(jnp.float32) + straight
        gain_total = gain_total + gain
    small_sums[...] = jnp.concatenate(
        [gain_total, result_total, branch_total, feed_total]
        + [jnp.zeros((4, gain_total.shape[1]), jnp.float32)],
        axis=0,
    )
    gstate_turn.arrived()
    keep_gates.wait()
    keep_down.wait()
    keep_up.wait()
    for moved in kept:
        moved.wait()
    links.close()


class PlaneSum:
    def __init__(self, links, here, grad, first_in, last_in):
        self.links, self.here, self.grad = links, here, grad
        self.first_in, self.last_in = first_in, last_in
        self.rows = first_in.shape[1]

    def part(self, k, which):
        start = self.here.planes[k] * 2 * self.rows + which * self.rows
        return self.grad.at[rows_at(start, self.rows)]

    def start(self):
        mates = self.here.plane_mates
        self.firsts = [
            self.links.copy(self.part(k, which), self.first_in.at[slot], mates[mate])
            for slot, (k, which, mate) in enumerate(((1, 0, 1), (3, 0, 1), (2, 1, 2), (3, 1, 2)))
        ]
        return self

    def add(self, k, which, arrived):
        part = self.part(k, which)
        part[...] = (part[...].astype(jnp.float32) + arrived[...].astype(jnp.float32)).astype(part.dtype)

    def forward(self):
        mates = self.here.plane_mates
        self.firsts[1].wait_recv()
        self.add(2, 0, self.first_in.at[1])
        self.last_0 = self.links.copy(self.part(2, 0), self.last_in.at[0], mates[2])
        self.firsts[3].wait_recv()
        self.add(1, 1, self.first_in.at[3])
        self.last_1 = self.links.copy(self.part(1, 1), self.last_in.at[1], mates[1])

    def finish(self):
        self.firsts[0].wait_recv()
        self.add(0, 0, self.first_in.at[0])
        self.firsts[2].wait_recv()
        self.add(0, 1, self.first_in.at[2])
        self.last_0.wait_recv()
        self.add(0, 0, self.last_in.at[0])
        self.last_1.wait_recv()
        self.add(0, 1, self.last_in.at[1])

    def result(self, which):
        return self.grad.at[
            rows_at(self.here.planes[0] * 2 * self.rows + which * self.rows, self.rows)
        ]


class FarPlaneSum(PlaneSum):
    def __init__(self, links, here, grad, first_in, last_in, forwards, brought, brought_sems):
        super().__init__(links, here, grad, first_in, last_in)
        self.forwards = forwards
        self.brought, self.brought_sems = brought, brought_sems

    def totals(self, *groups):
        brings, at, outs = [], 0, []
        for pieces in groups:
            for piece in pieces:
                brings.append(pltpu.make_async_copy(piece, self.brought.at[at], self.brought_sems.at[at]))
                brings[-1].start()
                at += 1
        for bring in brings:
            bring.wait()
        at = 0
        for slot, pieces in enumerate(groups):
            out = self.brought[at].astype(jnp.float32)
            for step in range(1, len(pieces)):
                out = out + self.brought[at + step].astype(jnp.float32)
            at += len(pieces)
            self.forwards[slot] = out.astype(jnp.bfloat16)

    def forward(self):
        mates = self.here.plane_mates
        self.firsts[1].wait_recv()
        self.firsts[3].wait_recv()
        self.totals(
            (self.part(2, 0), self.first_in.at[1]),
            (self.part(1, 1), self.first_in.at[3]),
        )
        self.last_0 = self.links.copy(self.forwards.at[0], self.last_in.at[0], mates[2])
        self.last_1 = self.links.copy(self.forwards.at[1], self.last_in.at[1], mates[1])

    def finish(self):
        self.firsts[0].wait_recv()
        self.firsts[2].wait_recv()
        self.last_0.wait_recv()
        self.last_1.wait_recv()
        self.links.sent(self.last_0)
        self.links.sent(self.last_1)
        self.totals(
            (self.part(0, 0), self.first_in.at[0], self.last_in.at[0]),
            (self.part(0, 1), self.first_in.at[2], self.last_in.at[1]),
        )

    def result(self, which):
        return self.forwards.at[which]


class Settle:
    def __init__(self, links, here, summed, target):
        half = here.half
        self.straight = Turn(links, here, summed.result(half), target.at[0], here.from_there)
        self.crossed = links.copy(summed.result(1 - half), target.at[1], here.from_across)

    def arrived(self):
        self.straight.arrived()
        self.crossed.wait_recv()


def cotangent_kernel(
    middle_grad, gstate_ref, x_ref, s0_ref, s1_ref, far_gate_values, gains_ref, facts, facts_home,
    small_sums,
    far_normed, far_snormed, queries, keys, values, state_qkv, lse_ref, mixed, smixed_rows,
    wst, wtok, wout, gates, far_wup_grad, far_wdn_grad, far_block_out, far_state_out,
    block_home, state_home, tokens_home, past_home, carried_grad, initial_grad, totals,
    up_home, down_home, wst_home, wtok_home, wout_home, gates_home,
    up_first, down_first, up_last, down_last,
    tiles, tile_grads, branch_grad, mixed_grad, gate_rows, state_mixed_grad, key_grad, value_grad,
    skey_grad, svalue_grad, token_cot, state_cot, gate_values, smixed_pair, sending,
    tokens_send, carried_send, carried_in, past_send, initial_send, initial_in,
    wst_grad, wtok_grad, wout_grad, gates_grad,
    wst_first, wtok_first, wout_first, gates_first, wst_last, wtok_last, wout_last, gates_last,
    up_forwards, down_forwards, brought, ring_in, level_in, ring_send, level_send,
    *rest,
):
    rs = [rest[0:4], rest[4:8], rest[8:12]]
    links = Links(rest[12], rest[13])
    local_sems, brought_sems = rest[14], rest[15]
    here = Place()
    rank, ranks, mates = here.rank, here.ranks, here.mates
    rows = s0_ref.shape[0]
    window = 4 * rows
    width = queries.shape[1]
    heads = width // DH
    size = s0_ref.shape[1]
    ring = [(lax.rem(here.dp + step, 8), here.level) for step in range(1, 8)]
    other = here.dp + 1 - 2 * here.core
    column = [
        (chip, lax.rem(here.level + step, 4)) for step in range(1, 4) for chip in (here.dp, other)
    ]
    greet(ring + column)
    bring_gates = pltpu.make_async_copy(
        far_gate_values.at[pl.ds(rows, rows)], gate_values, local_sems.at[0]
    )
    bring_gates.start()
    for block in (1, 0):
        at = slice(block * rows, (block + 1) * rows)
        branch_grad[rows_at(block * window + rank * rows, rows), :] = middle_grad[at, :].astype(
            jnp.bfloat16
        )

    def home(source, target):
        return Turn(links, here, source, target, here.from_there)

    def pair_rows(block):
        return rows_at((2 * block + here.core) * rows, rows)

    def gates_back(block, state, state_grad):
        spot = pair_rows(block)
        keep = jax.nn.sigmoid(gate_values[:, 2 * size : 3 * size] + 1.0)
        fresh = jnp.tanh(gate_values[:, 0:size])
        let_in = jax.nn.sigmoid(gate_values[:, size : 2 * size] - 1.0)
        gate_rows[spot, 0:size] = (state_grad * let_in * (1.0 - fresh * fresh)).astype(jnp.bfloat16)
        gate_rows[spot, size : 2 * size] = (
            state_grad * fresh * let_in * (1.0 - let_in)
        ).astype(jnp.bfloat16)
        gate_rows[spot, 2 * size : 3 * size] = (
            state_grad * state * keep * (1.0 - keep)
        ).astype(jnp.bfloat16)
        out = dot(gate_rows[spot, 0:size], gates[:, 0:size], NN)
        out = out + dot(gate_rows[spot, size : 2 * size], gates[:, size : 2 * size], NN)
        out = out + dot(gate_rows[spot, 2 * size : 3 * size], gates[:, 2 * size : 3 * size], NN)
        sending[block] = out.astype(jnp.bfloat16)
        spot = rows_at(block * window + rank * rows, rows)
        moves = []
        for k in (2, 3, 1):
            columns = pl.ds(pl.multiple_of(ranks[k] * width, width), width)
            moves.append(
                links.copy(sending.at[block, :, columns], state_mixed_grad.at[spot], mates[k])
            )
        columns = pl.ds(pl.multiple_of(rank * width, width), width)
        state_mixed_grad[spot, :] = sending[block, :, columns]
        pair = gate_rows.at[pair_rows(block)]
        return state_grad * keep, moves, links.copy(pair, pair, mates[1])

    def key_mask(start, size):
        place_of = lax.broadcasted_iota(jnp.int32, (1, size), 1).astype(jnp.float32)
        place_of = place_of + float(start - window)
        own = jnp.where(place_of < facts[2:3, 0:size], 0.0, NEGATIVE)
        return jnp.where(place_of < 0.0, facts[3:4, 0:size] * NEGATIVE, own)

    def pair_back(first, second, lse, first_grad, second_grad):
        first, second = jnp.exp(first - lse), jnp.exp(second - lse)
        inner = jnp.sum(first * first_grad, axis=-1, keepdims=True) + jnp.sum(
            second * second_grad, axis=-1, keepdims=True
        )
        return (
            first.astype(jnp.bfloat16),
            second.astype(jnp.bfloat16),
            (first * (first_grad - inner)).astype(jnp.bfloat16),
            (second * (second_grad - inner)).astype(jnp.bfloat16),
        )

    def token_back(block):
        base = block * window
        whole = pl.ds(base, window)
        for tile in range(window // TILE):
            near_mask = key_mask(base + tile * TILE, 3 * TILE)
            for head in range(heads):
                at = head * DH
                lanes = slice(at, at + DH)
                skey_lanes = slice(width + at, width + at + DH)
                svalue_lanes = slice(2 * width + at, 2 * width + at + DH)
                here_rows = pl.ds(base + tile * TILE, TILE)
                near = pl.ds(base + tile * TILE, 3 * TILE)
                query = queries[here_rows, lanes]
                out_grad = mixed_grad[here_rows, lanes]
                first = dot(query, keys[near, lanes], NT) * ROOT + tiles[head] + near_mask
                second = dot(query, state_qkv[whole, skey_lanes], NT) * ROOT
                first, second, first_grad, second_grad = pair_back(
                    first,
                    second,
                    lse_ref[here_rows, head : head + 1],
                    dot(out_grad, values[near, lanes], NT),
                    dot(out_grad, state_qkv[whole, svalue_lanes], NT),
                )
                value_grad[near, lanes] += dot(first, out_grad, TN)
                svalue_grad[:, lanes] += dot(second, out_grad, TN)
                part = dot(first_grad, keys[near, lanes], NN) + dot(
                    second_grad, state_qkv[whole, skey_lanes], NN
                )
                token_cot[here_rows, lanes] = (part * ROOT).astype(jnp.bfloat16)
                key_grad[near, lanes] += dot(first_grad, query, TN) * ROOT
                skey_grad[:, lanes] += dot(second_grad, query, TN) * ROOT
                tile_grads[head] += first_grad.astype(jnp.float32)

    def state_back(block):
        base = block * window
        whole = pl.ds(base, window)
        own = pl.ds(base + window, window)
        own_mask = key_mask(base + window, window)
        for head in range(heads):
            at = head * DH
            lanes = slice(at, at + DH)
            skey_lanes = slice(width + at, width + at + DH)
            svalue_lanes = slice(2 * width + at, 2 * width + at + DH)
            for tile in range(window // TILE):
                here_rows = pl.ds(base + tile * TILE, TILE)
                query = state_qkv[here_rows, lanes]
                out_grad = state_mixed_grad[here_rows, lanes]
                first = dot(query, state_qkv[whole, skey_lanes], NT) * ROOT
                second = dot(query, keys[own, lanes], NT) * ROOT + own_mask
                first, second, first_grad, second_grad = pair_back(
                    first,
                    second,
                    lse_ref[here_rows, heads + head : heads + head + 1],
                    dot(out_grad, state_qkv[whole, svalue_lanes], NT),
                    dot(out_grad, values[own, lanes], NT),
                )
                svalue_grad[:, lanes] += dot(first, out_grad, TN)
                value_grad[own, lanes] += dot(second, out_grad, TN)
                part = dot(first_grad, state_qkv[whole, skey_lanes], NN) + dot(
                    second_grad, keys[own, lanes], NN
                )
                state_cot[here_rows, lanes] = (part * ROOT).astype(jnp.bfloat16)
                skey_grad[:, lanes] += dot(first_grad, query, TN) * ROOT
                key_grad[own, lanes] += dot(second_grad, query, TN) * ROOT

    def gather_cot(block):
        whole = pl.ds(block * window, window)
        own = pl.ds(block * window + window, window)
        token_cot[whole, width : 2 * width] = key_grad[own, :].astype(jnp.bfloat16)
        token_cot[whole, 2 * width : 3 * width] = value_grad[own, :].astype(jnp.bfloat16)
        state_cot[whole, width : 2 * width] = skey_grad[...].astype(jnp.bfloat16)
        state_cot[whole, 2 * width : 3 * width] = svalue_grad[...].astype(jnp.bfloat16)

    def state_sum(block):
        return RowSum(links, here, *rs[0], rows).fill(
            lambda which: dot(state_cot[rows_at(block * window + which * rows, rows), :], wst[...], NT)
        )

    def token_sum(block):
        return RowSum(links, here, *rs[1 + block], rows).fill(
            lambda which: dot(token_cot[rows_at(block * window + which * rows, rows), :], wtok[...], NT)
        )

    def mix_back(block, gather):
        for k in range(4):
            gather.ready(k)
            at = rows_at(block * window + ranks[k] * rows, rows)
            mixed_grad[at, :] = dot(branch_grad[at, :], wout[...], NN).astype(jnp.bfloat16)

    def weight_grad(target, left, right, lanes):
        right = right[...]
        step = 256
        for part in range(size // step):
            at = slice(part * step, (part + 1) * step)
            target[at, lanes] = dot(left[:, at], right, TN).astype(jnp.bfloat16)

    def finish_tokens(block, summed):
        at = slice(block * rows, (block + 1) * rows)
        straight, gain = rms_back(x_ref[at, :].astype(jnp.float32), gains_ref[0:1, :], summed.finish())
        tokens_send[at, :] = (middle_grad[at, :] + straight).astype(jnp.bfloat16)
        return gain, home(tokens_send.at[pl.ds(block * rows, rows)], tokens_home.at[pl.ds(block * rows, rows)])

    reach = 2 * width
    other_half = pl.ds(pl.multiple_of((1 - here.core) * reach, reach), reach)
    own_half = pl.ds(pl.multiple_of(here.core * reach, reach), reach)
    smixed_moves = []
    for block in range(2):
        own_rows = pl.ds(block * rows, rows)
        smixed_pair[pair_rows(block), :] = smixed_rows[own_rows, own_half]
        smixed_moves.append(
            links.copy(
                smixed_rows.at[own_rows, other_half], smixed_pair.at[pair_rows(block)], mates[1]
            )
        )
    branch_1 = RowGather(links, here, branch_grad, window, rows).start()
    bring_gates.wait()
    direct_1, moves_1, pair_1 = gates_back(1, s1_ref[...], gstate_ref[...].astype(jnp.float32))
    up_sum = FarPlaneSum(
        links, here, far_wup_grad, up_first, up_last, up_forwards, brought, brought_sems
    ).start()
    down_sum = FarPlaneSum(
        links, here, far_wdn_grad, down_first, down_last, down_forwards, brought, brought_sems
    ).start()
    bring_gates = pltpu.make_async_copy(far_gate_values.at[pl.ds(0, rows)], gate_values, local_sems.at[0])
    bring_gates.start()
    for ref in (tile_grads, key_grad, value_grad, skey_grad, svalue_grad):
        ref[...] = jnp.zeros(ref.shape, ref.dtype)
    bias_tiles(facts, tiles, heads, 3 * TILE)
    mix_back(1, branch_1)
    branch_0 = RowGather(links, here, branch_grad, 0, rows).start()
    block_turn = home(far_block_out, block_home)
    state_turn = home(far_state_out, state_home)
    token_back(1)
    for moved in moves_1:
        moved.wait_recv()
    state_back(1)
    gather_cot(1)
    state_sum_1 = state_sum(1)
    token_sum_1 = token_sum(1)
    state_sum_1.forward()
    mix_back(0, branch_0)
    for ref in (skey_grad, svalue_grad):
        ref[...] = jnp.zeros(ref.shape, ref.dtype)
    up_sum.forward()
    down_sum.forward()
    token_back(0)
    token_sum_1.forward()
    bring_gates.wait()
    state_norm_grad, gain_2 = rms_back(s1_ref[...], gains_ref[2:3, :], state_sum_1.finish())
    direct_0, moves_0, pair_0 = gates_back(0, s0_ref[...], direct_1 + state_norm_grad)
    past_send[0] = key_grad[0:window, :].astype(jnp.bfloat16)
    past_send[1] = value_grad[0:window, :].astype(jnp.bfloat16)
    for moved in smixed_moves + [pair_1, pair_0]:
        moved.wait_recv()
    for c in range(3):
        weight_grad(
            gates_grad,
            gate_rows.at[:, c * size : (c + 1) * size],
            smixed_pair,
            slice(c * reach, (c + 1) * reach),
        )
    gates_sum = PlaneSum(links, here, gates_grad, gates_first, gates_last).start()
    weight_grad(wout_grad, branch_grad, mixed, slice(0, width))
    wout_sum = PlaneSum(links, here, wout_grad, wout_first, wout_last).start()
    up_sum.finish()
    up_settle = Settle(links, here, up_sum, up_home)
    for moved in moves_0:
        moved.wait_recv()
    past_turn = home(past_send, past_home)
    down_sum.finish()
    down_settle = Settle(links, here, down_sum, down_home)
    for gather in (branch_1, branch_0):
        gather.sent()
    bring_snormed = pltpu.make_async_copy(far_snormed, branch_grad, local_sems.at[2])
    bring_snormed.start()
    for moved in (pair_1, pair_0):
        links.sent(moved)
    bring_normed = []
    for block in range(2):
        bring_normed.append(
            pltpu.make_async_copy(
                far_normed.at[pl.ds(block * window, window)],
                gate_rows.at[:, block * size : (block + 1) * size],
                local_sems.at[4 + block],
            )
        )
        bring_normed[block].start()
    state_back(0)
    gather_cot(0)
    bring_snormed.wait()
    weight_grad(wst_grad, branch_grad, state_cot, slice(0, 3 * width))
    wst_sum = PlaneSum(links, here, wst_grad, wst_first, wst_last).start()
    for block in range(2):
        bring_normed[block].wait()
    for part in range(size // 256):
        at = slice(part * 256, (part + 1) * 256)
        later = slice(size + part * 256, size + (part + 1) * 256)
        summed = dot(gate_rows[:, at], token_cot[0:window, :], TN)
        summed = summed + dot(gate_rows[:, later], token_cot[window : 2 * window, :], TN)
        wtok_grad[at, :] = summed.astype(jnp.bfloat16)
    wtok_sum = PlaneSum(links, here, wtok_grad, wtok_first, wtok_last).start()
    state_sum_1.sent()
    state_sum_0 = state_sum(0)
    token_sum_0 = token_sum(0)
    gain_1, turn_1 = finish_tokens(1, token_sum_1)
    state_sum_0.forward()
    token_sum_0.forward()
    wst_sum.forward()
    gates_sum.forward()
    wtok_sum.forward()
    wout_sum.forward()
    state_norm_grad, gain = rms_back(s0_ref[...], gains_ref[2:3, :], state_sum_0.finish())
    carried_send[...] = (direct_0 + state_norm_grad).astype(jnp.bfloat16)
    carried_turn = home(carried_send, carried_in)
    gain_2 = gain_2 + gain
    wst_sum.finish()
    wst_settle = Settle(links, here, wst_sum, wst_home)
    gain_0, turn_0 = finish_tokens(0, token_sum_0)

    for head in range(heads):
        lines = tile_grads[head, 0:8, :]
        span = lines.shape[1]
        for group in range(1, TILE // 8):
            lines = lines + pltpu.roll(tile_grads[head, 8 * group : 8 * group + 8, :], span - 8 * group, 1)
        total = lines[0:1]
        for line in range(1, 8):
            total = total + pltpu.roll(lines[line : line + 1], span - line, 1)
        for owner in range(4):
            at = 8 + heads * owner + head
            ring_send[at : at + 1, :] = jnp.zeros((1, size), jnp.float32)
            ring_send[at : at + 1, 0:span] = jnp.where(rank == owner, total, 0.0)
    ring_send[0:1, :] = gain_0 + gain_1
    ring_send[1:2, :] = small_sums[0:1, :]
    ring_send[2:3, :] = gain_2
    ring_send[3:6, :] = small_sums[1:4, :]
    counted = jnp.zeros((1, 1), jnp.float32)
    for block in range(2):
        valid_rows = row_mask(facts, block * window + rank * rows, rows)
        counted = counted + jnp.sum(valid_rows, axis=0, keepdims=True)
    ring_send[6:7, :] = jnp.broadcast_to(counted, (1, size))
    ring_send[7:8, :] = jnp.zeros((1, size), jnp.float32)
    ring_moves = [
        links.copy(ring_send, ring_in.at[step - 1], ring[step - 1]) for step in range(1, 8)
    ]
    wtok_sum.finish()
    wtok_settle = Settle(links, here, wtok_sum, wtok_home)
    gates_sum.finish()
    slot = here.level * 2 + here.core
    piece = rows // 4
    gate_moves = []
    for step in range(4):
        to_level = lax.rem(here.level + step, 4)
        for to_core, chip in ((here.core, here.dp), (1 - here.core, other)):
            start = here.planes[0] * 2 * rows + to_core * rows + to_level * piece
            source = gates_grad.at[rows_at(start, piece, piece)]
            if step == 0 and chip is here.dp:
                kept = pltpu.make_async_copy(source, gates_home.at[slot], local_sems.at[3])
                kept.start()
            else:
                gate_moves.append(links.copy(source, gates_home.at[slot], (chip, to_level)))
    wout_sum.finish()
    wout_settle = Settle(links, here, wout_sum, wout_home)
    carried_turn.arrived()
    is_fresh = facts_home[3:4, :] > 0.5
    came = carried_in[...]
    carried_grad[...] = jnp.where(is_fresh, 0.0, came.astype(jnp.float32))
    initial_send[...] = jnp.where(is_fresh, came, jnp.zeros_like(came))
    part = initial_grad.shape[1]
    initial_moves = []
    for step in range(1, 8):
        to = lax.rem(here.dp + step, 8)
        columns = pl.ds(pl.multiple_of(to * part, part), part)
        initial_moves.append(
            links.copy(initial_send.at[:, columns], initial_in.at[step - 1], ring[step - 1])
        )
    for moved in ring_moves:
        moved.wait_recv()
    total = ring_send[...]
    for step in range(7):
        total = total + ring_in[step]
    level_send[...] = total
    level_moves = [
        links.copy(level_send, level_in.at[step - 1], (here.dp, lax.rem(here.level + step, 4)))
        for step in range(1, 4)
    ]
    for moved in initial_moves:
        moved.wait_recv()
    own_columns = pl.ds(pl.multiple_of(here.dp * part, part), part)
    initial = initial_send[:, own_columns].astype(jnp.float32)
    for step in range(7):
        initial = initial + initial_in[step].astype(jnp.float32)
    initial_grad[...] = initial
    for moved in level_moves:
        moved.wait_recv()
    total = level_send[...]
    for step in range(3):
        total = total + level_in[step]
    totals[...] = total
    kept.wait()
    for moved in gate_moves:
        moved.wait_recv()
    for turn in (block_turn, state_turn, past_turn, turn_1, turn_0):
        turn.arrived()
    for settle in (up_settle, down_settle, wout_settle, wst_settle, wtok_settle):
        settle.arrived()
    links.close()


def run_kernel(body, outs, scratch, collective, name, operands, far_in=(), far_out=()):
    vmem = pl.BlockSpec(memory_space=pltpu.VMEM)
    far = pl.BlockSpec(memory_space=pl.ANY)
    return pl.pallas_call(
        body,
        out_shape=outs,
        in_specs=[far if at in far_in else vmem for at in range(len(operands))],
        out_specs=[far if at in far_out else vmem for at in range(len(outs))],
        scratch_shapes=scratch,
        compiler_params=pltpu.CompilerParams(
            collective_id=collective, has_side_effects=True, vmem_limit_bytes=VMEM_BYTES
        ),
        name=name,
    )(*operands)


def sems(count):
    return [pltpu.SemaphoreType.DMA((count,)), pltpu.SemaphoreType.DMA((count,))]


def grouped(
    tokens, carried_state, past_keys, fresh_start, valid_count, bucket_ids, grad_output, grad_state,
    norm_gains, token_qkv, token_out, bias_table, mlp_up, mlp_down, state_qkv, state_gates, initial_state,
):
    dp_size, levels = lax.axis_size("dp"), lax.axis_size("state")
    dp_at, level = lax.axis_index("dp"), lax.axis_index("state")
    _, blocks, rows, size = tokens.shape
    window = rows * levels
    width = token_qkv.shape[2]
    heads = width // DH
    units = mlp_up.shape[1]
    model_rows = token_qkv.shape[0]
    low, full = jnp.bfloat16, jnp.float32

    one_hot = (bucket_ids[:, None] == jnp.arange(bias_table.shape[0])[None, :]).astype(full)
    per_offset = jnp.dot(one_hot, bias_table, precision=HIGHEST)
    lines = jnp.pad(per_offset[::-1].T, ((0, 0), (1, window - 1)), constant_values=NEGATIVE)
    numbers = jnp.stack([valid_count[0], fresh_start[0]]).astype(full)
    facts_in = jnp.concatenate(
        [
            lines,
            jnp.broadcast_to(numbers[:, None], (2, lines.shape[1])),
            jnp.zeros((4, lines.shape[1]), full),
        ]
    )

    shape = jax.ShapeDtypeStruct
    vmem = pltpu.VMEM
    rs = row_sum_scratch(rows, size)
    kept = [
        ((2 * window, size), low),
        ((2 * window, size), low),
        ((2 * window, width), low),
        ((3 * window, width), low),
        ((3 * window, width), low),
        ((2 * window, 3 * width), low),
        ((2 * window, 2 * heads), full),
        ((2 * window, width), low),
        ((size, 3 * width), low),
        ((size, 3 * width), low),
        ((size, width), low),
        ((size, 3 * size), low),
        ((2 * rows, size), low),
        ((rows, size), full),
        ((rows, size), full),
    ]
    (
        normed, snormed, queries, keys, values, sqkv, lse, mixed, wst_all, wtok_all, wout_all, gates_all,
        x, s0, s1, gate_values, gstate, wup_grad, wdn_grad, smixed_rows, s2, facts,
        block_out, middle_grad, small_sums,
    ) = run_kernel(
        forward_kernel,
        [shape(*of) for of in kept]
        + [
            shape((2 * rows, 3 * size), full),
            shape((rows, size), low),
            shape((size, units), low),
            shape((size, units), low),
            shape((2 * rows, size), low),
            shape((rows, size), low),
            shape((8, 2 * window), full),
            shape((2 * rows, size), low),
            shape((2 * rows, size), full),
            shape((8, size), full),
        ],
        [vmem(*of) for of in kept]
        + [
            vmem((2 * window, width), low),
            vmem((heads, TILE, 3 * TILE), full),
            vmem((rows, size), low),
            vmem((rows, size), low),
            vmem((rows, size), full),
            vmem((rows, 3 * size), full),
            vmem((size, units), low),
            vmem((size, units), low),
            vmem((2 * rows, size), full),
            vmem((2 * window, size), low),
            vmem((2 * rows, size), low),
            vmem((2 * window, size), low),
            vmem((2 * window, units), full),
            vmem((2 * window, units), low),
            vmem((2 * window, units), low),
            vmem((size, units), low),
        ]
        + rs * 4
        + sems(128)
        + [pltpu.SemaphoreType.DMA((4,)), pltpu.SemaphoreType.DMA((len(kept),))],
        0,
        "forward",
        [
            tokens[0].reshape(blocks * rows, size),
            carried_state[0],
            initial_state,
            jnp.swapaxes(past_keys[0], 0, 1),
            facts_in,
            grad_output[0].reshape(blocks * rows, size),
            grad_state[0].astype(low),
            norm_gains,
            state_qkv.reshape(model_rows, 3 * width),
            token_qkv.reshape(model_rows, 3 * width),
            token_out,
            state_gates.reshape(model_rows, 3 * size),
            mlp_up,
            mlp_down,
        ],
        far_in=(3, 5, 6, 12, 13),
        far_out=range(len(kept) + 4),
    )
    grads = [("wst", 3 * width), ("wtok", 3 * width), ("wout", width), ("gates", 6 * width)]
    (
        block_home, state_home, tokens_home, past_home, carried_grad, initial_grad, totals,
        up_home, down_home, wst_home, wtok_home, wout_home, gates_home, *_,
    ) = run_kernel(
        cotangent_kernel,
        [
            shape((2 * rows, size), low),
            shape((rows, size), low),
            shape((2 * rows, size), low),
            shape((2, window, width), low),
            shape((rows, size), full),
            shape((rows, size // dp_size), full),
            shape((16, size), full),
            shape((2, rows, units), low),
            shape((2, rows, units), low),
            shape((2, rows, 3 * width), low),
            shape((2, rows, 3 * width), low),
            shape((2, rows, width), low),
            shape((8, rows // 4, 6 * width), low),
            shape((4, rows, units), low),
            shape((4, rows, units), low),
            shape((2, rows, units), low),
            shape((2, rows, units), low),
        ],
        [
            vmem((heads, TILE, 3 * TILE), full),
            vmem((heads, TILE, 3 * TILE), full),
            vmem((2 * window, size), low),
            vmem((2 * window, width), low),
            vmem((4 * rows, 3 * size), low),
            vmem((2 * window, width), low),
            vmem((3 * window, width), full),
            vmem((3 * window, width), full),
            vmem((window, width), full),
            vmem((window, width), full),
            vmem((2 * window, 3 * width), low),
            vmem((2 * window, 3 * width), low),
            vmem((rows, 3 * size), full),
            vmem((4 * rows, 2 * width), low),
            vmem((2, rows, size), low),
            vmem((2 * rows, size), low),
            vmem((rows, size), low),
            vmem((rows, size), low),
            vmem((2, window, width), low),
            vmem((rows, size), low),
            vmem((dp_size - 1, rows, size // dp_size), low),
        ]
        + [vmem((size, columns), low) for _, columns in grads]
        + [vmem((4, rows, columns), low) for _, columns in grads]
        + [vmem((2, rows, columns), low) for _, columns in grads]
        + [vmem((2, rows, units), low)] * 2
        + [
            vmem((6, rows, units), low),
            vmem((dp_size - 1, 16, size), full),
            vmem((levels - 1, 16, size), full),
            vmem((16, size), full),
            vmem((16, size), full),
        ]
        + rs * 3
        + sems(128)
        + [pltpu.SemaphoreType.DMA((6,)), pltpu.SemaphoreType.DMA((6,))],
        1,
        "cotangent",
        [
            middle_grad, gstate, x, s0, s1, gate_values, norm_gains, facts, facts_in,
            small_sums,
            normed, snormed, queries, keys, values, sqkv, lse, mixed, smixed_rows,
            wst_all, wtok_all, wout_all, gates_all, wup_grad, wdn_grad, block_out, s2,
        ],
        far_in=(5, 10, 11, 23, 24, 25, 26),
        far_out=(0, 1, 2, 3, 7, 8, 9, 10, 11, 12, 13, 14, 15, 16),
    )
    both = lambda pair: pair[0].astype(full) + pair[1].astype(full)
    gates_out = jnp.sum(gates_home.astype(full).reshape(levels, 2, rows // 4, 3, 2 * width), axis=0)
    gates_out = jnp.transpose(gates_out, (1, 2, 0, 3)).reshape(rows // 4, 3, size)
    line_sums = totals[8 : 8 + levels * heads, 1 : window + 1][:, ::-1]
    table_all = jnp.dot(one_hot.T, line_sums.T, precision=HIGHEST)
    table_rows = table_all.shape[0] // dp_size
    table_out = lax.dynamic_slice(table_all, (dp_at * table_rows, level * heads), (table_rows, heads))
    share = size // (dp_size * levels)
    gains_out = lax.dynamic_slice(totals, (0, (dp_at * levels + level) * share), (3, share))
    rms_stats = jnp.sqrt(jnp.sum(totals[3:6], axis=1) / totals[6, 0])
    return (
        block_home.reshape(1, blocks, rows, size),
        state_home.astype(full)[None],
        rms_stats,
        tokens_home.reshape(1, blocks, rows, size),
        carried_grad[None],
        jnp.swapaxes(past_home.astype(full), 0, 1)[None],
        gains_out,
        both(wtok_home).reshape(model_rows, 3, width),
        both(wout_home),
        table_out,
        both(up_home),
        both(down_home),
        both(wst_home).reshape(model_rows, 3, width),
        gates_out,
        initial_grad,
    )


def solution(mesh):
    in_specs = (
        P("dp", None, "state", None),
        P("dp", "state", None),
        P("dp", None, None, "state"),
        P("dp"),
        P("dp"),
        P(),
        P("dp", None, "state", None),
        P("dp", "state", None),
        P(),
        P("dp", None, "state"),
        P("dp", "state"),
        P(None, "state"),
        P("dp", "state"),
        P("dp", "state"),
        P("dp", None, "state"),
        P("dp", None, None),
        P("state", "dp"),
    )
    out_specs = (
        P("dp", None, "state", None),
        P("dp", "state", None),
        P(),
        P("dp", None, "state", None),
        P("dp", "state", None),
        P("dp", None, None, "state"),
        P(None, ("dp", "state")),
        P("dp", None, "state"),
        P("dp", "state"),
        P("dp", "state"),
        P("dp", "state"),
        P("dp", "state"),
        P("dp", None, "state"),
        P(("dp", "state"), None, None),
        P("state", "dp"),
    )
    body = grouped if dict(mesh.shape) == {"dp": 8, "state": 4} else shards
    return jax.shard_map(body, mesh=mesh, in_specs=in_specs, out_specs=out_specs, check_vma=False)
```

```python
import math

import jax
import jax.numpy as jnp
from jax import lax
from jax.experimental import pallas as pl
from jax.experimental.pallas import tpu as pltpu
from jax.sharding import PartitionSpec as P

DH = 128


EPS = 1e-06
NEGATIVE = -1e30
HIGHEST = lax.Precision.HIGHEST


def rms_norm(tensor, gains_row):
    return tensor * lax.rsqrt(jnp.mean(tensor * tensor, axis=-1, keepdims=True) + EPS) * gains_row


def norm_back(tensor, gains_row, cotangent):
    return jax.vjp(rms_norm, tensor, gains_row)[1](cotangent)


def smooth_gelu(tensor):
    return jax.nn.gelu(tensor, approximate=True)


def renew_state(state_now, gate_values):
    return state_now * jax.nn.sigmoid(gate_values[2] + 1.0) + jnp.tanh(
        gate_values[0]
    ) * jax.nn.sigmoid(gate_values[1] - 1.0)


def split_heads(tensor):
    return tensor.reshape(tensor.shape[0], tensor.shape[1], tensor.shape[2] // DH, DH)


def merge_heads(tensor):
    return tensor.reshape(tensor.shape[0], tensor.shape[1], tensor.shape[2] * DH)


def score_grid(queries, key_rows, bias_add, allowed):
    scores = jnp.einsum(
        "iqhd,ikhd->ihqk", queries, key_rows, preferred_element_type=jnp.float32
    ) / math.sqrt(DH)
    if bias_add is not None:
        scores = scores + bias_add[None]
    return jnp.where(allowed[:, None], scores, NEGATIVE)


def attend_forward(queries, key_rows, values, bias_add, allowed):
    scores = score_grid(queries, key_rows, bias_add, allowed)
    row_max = jnp.max(scores, axis=-1, keepdims=True)
    weights = jnp.exp(scores - row_max)
    row_total = jnp.sum(weights, axis=-1, keepdims=True)
    attn_probs = (weights / row_total).astype(jnp.bfloat16)
    mixed_heads = jnp.einsum(
        "ihqk,ikhd->iqhd", attn_probs, values, preferred_element_type=jnp.float32
    )
    return (merge_heads(mixed_heads.astype(jnp.bfloat16)), row_max + jnp.log(row_total))


def attention_backward_pass(queries, key_rows, values, bias_add, allowed, log_total, grad_mixed):
    scores = score_grid(queries, key_rows, bias_add, allowed)
    attn_probs = jnp.exp(scores - log_total)
    probs_grad = jnp.einsum(
        "iqhd,ikhd->ihqk", grad_mixed, values, preferred_element_type=jnp.float32
    )
    scores_grad = attn_probs * (
        probs_grad - jnp.sum(attn_probs * probs_grad, axis=-1, keepdims=True)
    )
    scores_grad = scores_grad.astype(jnp.bfloat16)
    values_grad = jnp.einsum(
        "ihqk,iqhd->ikhd",
        attn_probs.astype(jnp.bfloat16),
        grad_mixed,
        preferred_element_type=jnp.float32,
    )
    queries_grad = jnp.einsum(
        "ihqk,ikhd->iqhd", scores_grad, key_rows, preferred_element_type=jnp.float32
    ) / math.sqrt(DH)
    keys_grad = jnp.einsum(
        "ihqk,iqhd->ikhd", scores_grad, queries, preferred_element_type=jnp.float32
    ) / math.sqrt(DH)
    return (
        merge_heads(queries_grad),
        merge_heads(keys_grad),
        merge_heads(values_grad),
        scores_grad,
    )


def diagonal_sums(grid_values):
    num_heads, num_rows, num_cols = grid_values.shape
    flat = grid_values.reshape(num_heads, num_rows * num_cols)
    flat = jnp.pad(flat, ((0, 0), (0, num_rows)))
    sums = jnp.sum(flat.reshape(num_heads, num_rows, num_cols + 1), axis=1)
    return sums[:, num_rows:0:-1]


def toeplitz_grid(per_offset, num_rows):
    num_cols = 2 * num_rows
    line = jnp.pad(per_offset[::-1].T, ((0, 0), (1, num_cols - num_rows)))
    flat = jnp.tile(line, (1, num_rows))[:, : num_rows * num_cols]
    return flat.reshape(-1, num_rows, num_cols)


def sum_rows(partial_value):
    return lax.psum_scatter(
        partial_value.astype(jnp.bfloat16), "state", scatter_dimension=1, tiled=True
    ).astype(jnp.float32)


def whole_rows(partial_value):
    return lax.all_gather(partial_value, "state", axis=1, tiled=True)


def shards(
    tokens,
    carried_state,
    past_keys,
    fresh_start,
    valid_count,
    bucket_ids,
    grad_output,
    grad_state,
    norm_gains,
    token_qkv,
    token_out,
    bias_table,
    mlp_up,
    mlp_down,
    state_qkv,
    state_gates,
    initial_state,
):
    item_count, blocks, share_rows, model_width = tokens.shape
    groups = lax.axis_size("state")
    state_rank = lax.axis_index("state")
    window_width = share_rows * groups
    vector_rows = carried_state.shape[1] * groups
    local_width = token_qkv.shape[2]
    qkv_full, out_full, up_full, down_full, sqkv_full, gates_full, initial_full = (
        lax.all_gather(token_qkv, "dp", axis=0, tiled=True),
        lax.all_gather(token_out, "dp", axis=0, tiled=True),
        lax.all_gather(mlp_up, "dp", axis=0, tiled=True),
        lax.all_gather(mlp_down, "dp", axis=0, tiled=True),
        lax.all_gather(state_qkv, "dp", axis=0, tiled=True),
        lax.all_gather(state_gates, "dp", axis=0, tiled=True),
        lax.all_gather(initial_state, "dp", axis=1, tiled=True),
    )
    gates_used = lax.dynamic_slice_in_dim(gates_full, state_rank * local_width, local_width, 2)
    one_hot = (bucket_ids[:, None] == jnp.arange(bias_table.shape[0])[None, :]).astype(jnp.float32)
    per_offset = jnp.dot(one_hot, bias_table, precision=HIGHEST)
    query_pos = jnp.arange(window_width)[:, None]
    key_pos = jnp.arange(2 * window_width)[None, :]
    offset = window_width + query_pos - key_pos
    inside = (offset >= 0) & (offset < window_width)
    bias_grid = toeplitz_grid(per_offset, window_width)
    token_bias = jnp.pad(bias_grid, ((0, 0), (0, 0), (0, vector_rows)))
    is_fresh = fresh_start == 1
    state_now = jnp.where(
        is_fresh[:, None, None], initial_full.astype(jnp.float32)[None], carried_state
    )
    past_key = past_keys[:, :, 0]
    past_value = past_keys[:, :, 1]
    past_ok = jnp.broadcast_to(~is_fresh[:, None], (item_count, window_width))
    gains_token, gains_middle, gains_state = (norm_gains[0], norm_gains[1], norm_gains[2])
    share_pos = state_rank * share_rows + jnp.arange(share_rows)
    square_sums = jnp.zeros((3,), jnp.float32)
    valid_total = jnp.zeros((), jnp.float32)
    kept_values = []
    results = []
    for block_at in range(blocks):
        token_ok = (
            block_at * window_width + jnp.arange(window_width)[None, :] < valid_count[:, None]
        )
        inputs = tokens[:, block_at].astype(jnp.float32)
        normed, state_normed = (
            lax.all_gather(
                rms_norm(inputs, gains_token).astype(jnp.bfloat16), "state", axis=1, tiled=True
            ),
            lax.all_gather(
                rms_norm(state_now, gains_state).astype(jnp.bfloat16), "state", axis=1, tiled=True
            ),
        )
        project = jnp.einsum(
            "iwd,dch->ciwh", normed, qkv_full, preferred_element_type=jnp.float32
        ).astype(jnp.bfloat16)
        state_project = jnp.einsum(
            "ind,dch->cinh", state_normed, sqkv_full, preferred_element_type=jnp.float32
        ).astype(jnp.bfloat16)
        token_keys = jnp.concatenate([past_key, project[1], state_project[1]], axis=1)
        token_values = jnp.concatenate([past_value, project[2], state_project[2]], axis=1)
        window_ok = inside[None] & jnp.concatenate([past_ok, token_ok], axis=1)[:, None, :]
        token_allowed = jnp.concatenate(
            [window_ok, jnp.ones((item_count, window_width, vector_rows), jnp.bool_)], axis=2
        )
        mixed_heads, token_total = attend_forward(
            split_heads(project[0]),
            split_heads(token_keys),
            split_heads(token_values),
            token_bias,
            token_allowed,
        )
        branch = sum_rows(
            jnp.einsum("iwh,dh->iwd", mixed_heads, out_full, preferred_element_type=jnp.float32)
        )
        middle = inputs + branch
        middle_normed = lax.all_gather(
            rms_norm(middle, gains_middle).astype(jnp.bfloat16), "state", axis=1, tiled=True
        )
        up_values = jnp.einsum(
            "iwd,df->iwf", middle_normed, up_full, preferred_element_type=jnp.float32
        )
        hidden = smooth_gelu(up_values).astype(jnp.bfloat16)
        feed_out = sum_rows(
            jnp.einsum("iwf,df->iwd", hidden, down_full, preferred_element_type=jnp.float32)
        )
        result = middle + feed_out
        results.append(result.astype(jnp.bfloat16))
        share_ok = (block_at * window_width + share_pos[None, :] < valid_count[:, None]).astype(
            jnp.float32
        )[:, :, None]
        square_sums = square_sums + jnp.stack(
            [
                jnp.sum(share_ok * result * result),
                jnp.sum(share_ok * branch * branch),
                jnp.sum(share_ok * feed_out * feed_out),
            ]
        )
        valid_total = valid_total + jnp.sum(share_ok)
        state_keys = jnp.concatenate([state_project[1], project[1]], axis=1)
        state_values = jnp.concatenate([state_project[2], project[2]], axis=1)
        state_allowed = jnp.concatenate(
            [
                jnp.ones((item_count, vector_rows, vector_rows), jnp.bool_),
                jnp.broadcast_to(token_ok[:, None, :], (item_count, vector_rows, window_width)),
            ],
            axis=2,
        )
        state_mixed, state_total = attend_forward(
            split_heads(state_project[0]),
            split_heads(state_keys),
            split_heads(state_values),
            None,
            state_allowed,
        )
        gate_source = state_mixed
        gate_values = lax.psum_scatter(
            jnp.einsum(
                "inh,dch->cind", state_mixed, gates_used, preferred_element_type=jnp.float32
            ).astype(jnp.bfloat16),
            "state",
            scatter_dimension=2,
            tiled=True,
        ).astype(jnp.float32)
        kept_values.append(
            (
                inputs,
                normed,
                state_normed,
                project,
                state_project,
                token_keys,
                token_values,
                token_allowed,
                mixed_heads,
                token_total,
                middle,
                middle_normed,
                up_values,
                hidden,
                state_keys,
                state_values,
                state_allowed,
                state_total,
                gate_source,
                gate_values,
                state_now,
            )
        )
        state_now = renew_state(state_now, gate_values)
        past_key, past_value, past_ok = (project[1], project[2], token_ok)
    square_sums, valid_total = lax.psum((square_sums, valid_total), ("dp", "state"))
    rms_stats = jnp.sqrt(square_sums / valid_total)
    qkv_grad = jnp.zeros(qkv_full.shape, jnp.float32)
    out_grad = jnp.zeros(out_full.shape, jnp.float32)
    up_grad = jnp.zeros(up_full.shape, jnp.float32)
    down_grad = jnp.zeros(down_full.shape, jnp.float32)
    sqkv_grad = jnp.zeros(sqkv_full.shape, jnp.float32)
    gate_grad = jnp.zeros(gates_used.shape, jnp.float32)
    bias_grad = jnp.zeros(bias_grid.shape, jnp.float32)
    gain_token_grad = jnp.zeros((model_width,), jnp.float32)
    gain_middle_grad = jnp.zeros((model_width,), jnp.float32)
    gain_state_grad = jnp.zeros((model_width,), jnp.float32)
    state_grad = grad_state
    carried_key_rows = jnp.zeros(past_keys[:, :, 0].shape, jnp.float32)
    carry_value = jnp.zeros(past_keys[:, :, 0].shape, jnp.float32)
    token_grads = [None] * blocks
    for block_at in reversed(range(blocks)):
        (
            inputs,
            normed,
            state_normed,
            project,
            state_project,
            token_keys,
            token_values,
            token_allowed,
            mixed_heads,
            token_total,
            middle,
            middle_normed,
            up_values,
            hidden,
            state_keys,
            state_values,
            state_allowed,
            state_total,
            gate_source,
            gate_values,
            state_before,
        ) = kept_values[block_at]
        direct_grad, gates_grad = jax.vjp(renew_state, state_before, gate_values)[1](state_grad)
        gates_low = gates_grad.astype(jnp.bfloat16)
        gates_rows = lax.all_gather(gates_low, "state", axis=2, tiled=True)
        state_mixed_grad = jnp.einsum(
            "cind,dch->inh", gates_rows, gates_used, preferred_element_type=jnp.float32
        ).astype(jnp.bfloat16)
        gate_grad = gate_grad + jnp.einsum(
            "inh,cind->dch", gate_source, gates_rows, preferred_element_type=jnp.float32
        )
        state_query_gradient, state_keys_gradient, state_values_gradient, discarded_output = (
            attention_backward_pass(
                split_heads(state_project[0]),
                split_heads(state_keys),
                split_heads(state_values),
                None,
                state_allowed,
                state_total,
                split_heads(state_mixed_grad),
            )
        )
        out_share = grad_output[:, block_at]
        out_whole = whole_rows(out_share)
        down_grad = down_grad + jnp.einsum(
            "iwf,iwd->df", hidden, out_whole, preferred_element_type=jnp.float32
        )
        hidden_grad = jnp.einsum(
            "iwd,df->iwf", out_whole, down_full, preferred_element_type=jnp.float32
        )
        up_values_grad = jax.vjp(smooth_gelu, up_values)[1](hidden_grad)[0].astype(jnp.bfloat16)
        up_grad = up_grad + jnp.einsum(
            "iwd,iwf->df", middle_normed, up_values_grad, preferred_element_type=jnp.float32
        )
        middle_normed_grad = lax.psum_scatter(
            jnp.einsum(
                "iwf,df->iwd", up_values_grad, up_full, preferred_element_type=jnp.float32
            ).astype(jnp.bfloat16),
            "state",
            scatter_dimension=1,
            tiled=True,
        ).astype(jnp.float32)
        middle_grad, gain_part = norm_back(middle, gains_middle, middle_normed_grad)
        middle_grad = out_share.astype(jnp.float32) + middle_grad
        gain_middle_grad = gain_middle_grad + gain_part
        branch_whole = whole_rows(middle_grad.astype(jnp.bfloat16))
        out_grad = out_grad + jnp.einsum(
            "iwh,iwd->dh", mixed_heads, branch_whole, preferred_element_type=jnp.float32
        )
        mixed_grad = jnp.einsum(
            "iwd,dh->iwh", branch_whole, out_full, preferred_element_type=jnp.float32
        ).astype(jnp.bfloat16)
        query_grad, token_keys_gradient, tvalues_grad, scores_grad = attention_backward_pass(
            split_heads(project[0]),
            split_heads(token_keys),
            split_heads(token_values),
            token_bias,
            token_allowed,
            token_total,
            split_heads(mixed_grad),
        )
        bias_grad = bias_grad + jnp.sum(
            scores_grad[:, :, :, : 2 * window_width].astype(jnp.float32), axis=0
        )
        key_gradient_rows = (
            token_keys_gradient[:, window_width : 2 * window_width]
            + state_keys_gradient[:, vector_rows:]
            + carried_key_rows
        )
        value_grad = (
            tvalues_grad[:, window_width : 2 * window_width]
            + state_values_gradient[:, vector_rows:]
            + carry_value
        )
        state_key_gradient = (
            token_keys_gradient[:, 2 * window_width :] + state_keys_gradient[:, :vector_rows]
        )
        state_value_gradient = (
            tvalues_grad[:, 2 * window_width :] + state_values_gradient[:, :vector_rows]
        )
        project_grad = jnp.stack([query_grad, key_gradient_rows, value_grad]).astype(jnp.bfloat16)
        state_projection_gradient = jnp.stack(
            [state_query_gradient, state_key_gradient, state_value_gradient]
        ).astype(jnp.bfloat16)
        qkv_grad = qkv_grad + jnp.einsum(
            "iwd,ciwh->dch", normed, project_grad, preferred_element_type=jnp.float32
        )
        sqkv_grad = sqkv_grad + jnp.einsum(
            "ind,cinh->dch",
            state_normed,
            state_projection_gradient,
            preferred_element_type=jnp.float32,
        )
        normed_grad, state_normed_grad = (
            lax.psum_scatter(
                jnp.einsum(
                    "ciwh,dch->iwd", project_grad, qkv_full, preferred_element_type=jnp.float32
                ).astype(jnp.bfloat16),
                "state",
                scatter_dimension=1,
                tiled=True,
            ).astype(jnp.float32),
            lax.psum_scatter(
                jnp.einsum(
                    "cinh,dch->ind",
                    state_projection_gradient,
                    sqkv_full,
                    preferred_element_type=jnp.float32,
                ).astype(jnp.bfloat16),
                "state",
                scatter_dimension=1,
                tiled=True,
            ).astype(jnp.float32),
        )
        input_grad, gain_part = norm_back(inputs, gains_token, normed_grad)
        gain_token_grad = gain_token_grad + gain_part
        token_grads[block_at] = (middle_grad + input_grad).astype(jnp.bfloat16)
        state_norm_grad, gain_part = norm_back(state_before, gains_state, state_normed_grad)
        gain_state_grad = gain_state_grad + gain_part
        state_grad = direct_grad + state_norm_grad
        carried_key_rows = token_keys_gradient[:, :window_width]
        carry_value = tvalues_grad[:, :window_width]
    carried_grad = jnp.where(is_fresh[:, None, None], 0.0, state_grad)
    initial_part = jnp.sum(jnp.where(is_fresh[:, None, None], state_grad, 0.0), axis=0)
    past_grad = jnp.stack([carried_key_rows, carry_value], axis=2)
    table_part = jnp.dot(one_hot.T, diagonal_sums(bias_grad).T, precision=HIGHEST)
    gain_columns = jnp.stack([gain_token_grad, gain_middle_grad, gain_state_grad], axis=1)
    summed = (
        lax.psum_scatter(
            qkv_grad.astype(jnp.bfloat16), "dp", scatter_dimension=0, tiled=True
        ).astype(jnp.float32),
        lax.psum_scatter(
            out_grad.astype(jnp.bfloat16), "dp", scatter_dimension=0, tiled=True
        ).astype(jnp.float32),
        lax.psum_scatter(
            table_part.astype(jnp.bfloat16), "dp", scatter_dimension=0, tiled=True
        ).astype(jnp.float32),
        lax.psum_scatter(
            up_grad.astype(jnp.bfloat16), "dp", scatter_dimension=0, tiled=True
        ).astype(jnp.float32),
        lax.psum_scatter(
            down_grad.astype(jnp.bfloat16), "dp", scatter_dimension=0, tiled=True
        ).astype(jnp.float32),
        lax.psum_scatter(
            sqkv_grad.astype(jnp.bfloat16), "dp", scatter_dimension=0, tiled=True
        ).astype(jnp.float32),
        lax.psum_scatter(
            initial_part.astype(jnp.bfloat16), "dp", scatter_dimension=1, tiled=True
        ).astype(jnp.float32),
        lax.psum_scatter(
            gate_grad.astype(jnp.bfloat16), "dp", scatter_dimension=0, tiled=True
        ).astype(jnp.float32),
        lax.psum_scatter(
            gain_columns.astype(jnp.bfloat16), "dp", scatter_dimension=0, tiled=True
        ).astype(jnp.float32),
    )
    gate_pieces, gain_pieces = (
        lax.all_to_all(
            summed[7][:, :, None, :].astype(jnp.bfloat16),
            "state",
            split_axis=0,
            concat_axis=2,
            tiled=True,
        ).astype(jnp.float32),
        lax.all_to_all(
            summed[8][:, :, None, None].astype(jnp.bfloat16),
            "state",
            split_axis=0,
            concat_axis=2,
            tiled=True,
        ).astype(jnp.float32),
    )
    gains_grad = jnp.sum(gain_pieces, axis=(2, 3)).T
    gates_grad_out = gate_pieces.reshape(
        gate_pieces.shape[0], gate_pieces.shape[1], gate_pieces.shape[2] * gate_pieces.shape[3]
    )
    return (
        jnp.stack(results, axis=1),
        state_now,
        rms_stats,
        jnp.stack(token_grads, axis=1),
        carried_grad,
        past_grad,
        gains_grad,
        summed[0],
        summed[1],
        summed[2],
        summed[3],
        summed[4],
        summed[5],
        gates_grad_out,
        summed[6],
    )


MESH = pl.DeviceIdType.MESH
NN = (((1,), (0,)), ((), ()))
NT = (((1,), (1,)), ((), ()))
TN = (((0,), (0,)), ((), ()))
VMEM_BYTES = 127 * 2**19


class Place:
    def __init__(self):
        chip_core, level = lax.axis_index("dp"), lax.axis_index("state")
        core, low = lax.rem(chip_core, 2), lax.rem(level, 2)
        x, y = lax.rem(chip_core // 2, 2), chip_core // 4
        flip = lambda bit: 1 - 2 * bit
        self.dp, self.core, self.level, self.half = chip_core, core, level, level // 2
        self.rank = 2 * low + core
        self.ranks = [self.rank, 2 * low + 1 - core, 2 * (1 - low) + core, 2 * (1 - low) + 1 - core]
        self.mates = [
            None,
            (chip_core + flip(core), level),
            (chip_core, level + flip(low)),
            (chip_core + flip(core), level + flip(low)),
        ]
        self.planes = [2 * y + x, 2 * y + 1 - x, 2 * (1 - y) + x, 2 * (1 - y) + 1 - x]
        self.plane_mates = [
            None,
            (chip_core + 2 * flip(x), level),
            (chip_core + 4 * flip(y), level),
            (chip_core + 2 * flip(x) + 4 * flip(y), level),
        ]
        first = chip_core - core
        self.there = (first + low, 2 * core + self.half)
        self.across = (first + low, 2 * (1 - core) + self.half)
        self.from_there = (first + self.half, 2 * low + core)
        self.from_across = (first + 1 - self.half, 2 * low + core)
        self.stays = (core == low) & (self.half == core)


def rows_at(start, size, step=128):
    return pl.ds(pl.multiple_of(start, step), size)


def rows_of(ref, start, size, step=128):
    at = rows_at(start, size, step)
    return ref.at[:, at] if len(ref.shape) == 3 else ref.at[at]


class Links:
    def __init__(self, send_sems, recv_sems):
        self.send_sems, self.recv_sems = send_sems, recv_sems
        self.used = 0
        self.open_sends = []
        self.open_turns = []

    def plan(self, source, target, device):
        at = self.used
        self.used += 1
        return pltpu.make_async_remote_copy(
            src_ref=source,
            dst_ref=target,
            send_sem=self.send_sems.at[at],
            recv_sem=self.recv_sems.at[at],
            device_id=device,
            device_id_type=MESH,
        )

    def copy(self, source, target, device):
        moved = self.plan(source, target, device)
        moved.start()
        self.open_sends.append(moved)
        return moved

    def sent(self, moved):
        self.open_sends = [other for other in self.open_sends if other is not moved]
        moved.wait_send()

    def close(self):
        for moved in self.open_sends:
            moved.wait_send()
        for turn in self.open_turns:
            turn.sent()
        self.open_sends, self.open_turns = [], []


def greet(devices, turned=None):
    barrier = pltpu.get_barrier_semaphore()
    for device in devices:
        pl.semaphore_signal(barrier, inc=1, device_id=device, device_id_type=MESH)
    if turned is None:
        pl.semaphore_wait(barrier, len(devices))
    else:
        moves = jnp.logical_not(turned.stays)

        @pl.when(moves)
        def _():
            pl.semaphore_signal(barrier, inc=1, device_id=turned.from_there, device_id_type=MESH)

        pl.semaphore_wait(barrier, len(devices) + moves.astype(jnp.int32))


class Turn:
    def __init__(self, links, here, source, target, device):
        self.stays = here.stays
        self.moved = links.plan(source, target, device)
        self.kept = pltpu.make_async_copy(source, target, links.recv_sems.at[links.used - 1])
        links.open_turns.append(self)

        @pl.when(jnp.logical_not(self.stays))
        def _():
            self.moved.start()

        @pl.when(self.stays)
        def _():
            self.kept.start()

    def arrived(self):
        @pl.when(jnp.logical_not(self.stays))
        def _():
            self.moved.wait_recv()

        @pl.when(self.stays)
        def _():
            self.kept.wait()

    def sent(self):
        @pl.when(jnp.logical_not(self.stays))
        def _():
            self.moved.wait_send()


class WeightGather:
    def __init__(self, links, here, local, full):
        self.links, self.here, self.local, self.full = links, here, local, full
        self.rows = local.shape[-2]

    def enter(self):
        target = rows_of(self.full, self.here.dp * self.rows, self.rows)
        self.turn = Turn(self.links, self.here, self.local, target, self.here.there)
        self.cross = self.links.copy(self.local, target, self.here.across)
        return self

    def block(self, k):
        return rows_of(self.full, self.here.planes[k] * 2 * self.rows, 2 * self.rows)

    def half(self, k, which):
        start = self.here.planes[k] * 2 * self.rows + which * self.rows
        return rows_of(self.full, start, self.rows)

    def spread(self):
        self.turn.arrived()
        self.cross.wait_recv()
        mates = self.here.plane_mates
        self.over_x = self.links.copy(self.block(0), self.block(0), mates[1])
        self.over_y = self.links.copy(self.block(0), self.block(0), mates[2])

    def forward(self):
        mates = self.here.plane_mates
        self.over_x.wait_recv()
        self.corner_0 = self.links.copy(self.half(1, 0), self.half(1, 0), mates[2])
        self.over_y.wait_recv()
        self.corner_1 = self.links.copy(self.half(2, 1), self.half(2, 1), mates[1])

    def finish(self):
        self.corner_0.wait_recv()
        self.corner_1.wait_recv()


class GateGather:
    def __init__(self, links, here, local, full, sem):
        self.links, self.here, self.local, self.full, self.sem = links, here, local, full, sem
        self.rows = local.shape[-2]

    def block(self, k):
        start = (2 * self.here.planes[k] + self.here.core) * self.rows
        return rows_of(self.full, start, self.rows)

    def part(self, k, which):
        size = self.rows // 2
        start = (2 * self.here.planes[k] + self.here.core) * self.rows + which * size
        return rows_of(self.full, start, size, 64)

    def spread(self):
        mates, sibling = self.here.plane_mates, self.here.mates[1]
        self.over_x = self.links.copy(self.local, self.block(0), mates[1])
        self.over_y = self.links.copy(self.local, self.block(0), mates[2])
        self.near = [self.links.copy(self.local, self.block(0), sibling)]
        self.kept = pltpu.make_async_copy(self.local, self.block(0), self.sem)
        self.kept.start()

    def forward(self):
        mates, sibling = self.here.plane_mates, self.here.mates[1]
        self.over_x.wait_recv()
        self.corner_0 = self.links.copy(self.part(1, 0), self.part(1, 0), mates[2])
        self.near.append(self.links.copy(self.block(1), self.block(1), sibling))
        self.over_y.wait_recv()
        self.corner_1 = self.links.copy(self.part(2, 1), self.part(2, 1), mates[1])
        self.near.append(self.links.copy(self.block(2), self.block(2), sibling))

    def last(self):
        self.corner_0.wait_recv()
        self.corner_1.wait_recv()
        self.near.append(self.links.copy(self.block(3), self.block(3), self.here.mates[1]))

    def finish(self):
        self.kept.wait()
        for moved in self.near:
            moved.wait_recv()


class RowGather:
    def __init__(self, links, here, ref, base, rows):
        self.links, self.here, self.ref, self.base, self.rows = links, here, ref, base, rows

    def part(self, k):
        return self.ref.at[rows_at(self.base + self.here.ranks[k] * self.rows, self.rows)]

    def start(self):
        own, mates = self.part(0), self.here.mates
        self.far = self.links.copy(own, own, mates[2])
        self.near = self.links.copy(own, own, mates[1])
        return self

    def ready(self, k):
        if k == 1:
            self.near.wait_recv()
        elif k == 2:
            self.far.wait_recv()
            block = self.part(2)
            self.last = self.links.copy(block, block, self.here.mates[1])
        elif k == 3:
            self.last.wait_recv()

    def sent(self):
        for moved in (self.far, self.near, self.last):
            self.links.sent(moved)


class RowSum:
    def __init__(self, links, here, stage, near_in, far_out, far_in, rows):
        self.links, self.here, self.rows = links, here, rows
        self.stage, self.near_in, self.far_out, self.far_in = stage, near_in, far_out, far_in

    def part(self, k):
        return self.stage.at[rows_at(self.here.ranks[k] * self.rows, self.rows)]

    def fill(self, make_rows):
        sibling = self.here.mates[1]
        for k, slot in ((3, 0), (1, 1)):
            self.part(k)[...] = make_rows(self.here.ranks[k]).astype(jnp.bfloat16)
            moved = self.links.copy(self.part(k), self.near_in.at[slot], sibling)
            if slot == 0:
                self.near_far = moved
            else:
                self.near_own = moved
        for k in (2, 0):
            self.part(k)[...] = make_rows(self.here.ranks[k]).astype(jnp.bfloat16)
        return self

    def forward(self):
        self.near_far.wait_recv()
        summed = self.part(2)[...].astype(jnp.float32) + self.near_in[0].astype(jnp.float32)
        self.far_out[...] = summed.astype(jnp.bfloat16)
        self.far = self.links.copy(self.far_out, self.far_in, self.here.mates[2])
        return self

    def sent(self):
        for moved in (self.near_far, self.near_own, self.far):
            self.links.sent(moved)

    def finish(self):
        self.near_own.wait_recv()
        self.far.wait_recv()
        return (
            self.part(0)[...].astype(jnp.float32)
            + self.near_in[1].astype(jnp.float32)
            + self.far_in[...].astype(jnp.float32)
        )


def row_sum_scratch(rows, width):
    return [
        pltpu.VMEM((4 * rows, width), jnp.bfloat16),
        pltpu.VMEM((2, rows, width), jnp.bfloat16),
        pltpu.VMEM((rows, width), jnp.bfloat16),
        pltpu.VMEM((rows, width), jnp.bfloat16),
    ]


def dot(left, right, dims):
    return lax.dot_general(left, right, dims, preferred_element_type=jnp.float32)


def scale_of(tensor):
    return lax.rsqrt(jnp.mean(tensor * tensor, axis=-1, keepdims=True) + EPS)


def rms_back(tensor, gains_row, cotangent):
    scale = scale_of(tensor)
    weighted = cotangent * gains_row
    inner = jnp.mean(tensor * weighted, axis=-1, keepdims=True)
    straight = scale * weighted - tensor * (scale * scale * scale * inner)
    return straight, jnp.sum(cotangent * tensor * scale, axis=0, keepdims=True)


def row_mask(facts, start, rows):
    place_of = lax.broadcasted_iota(jnp.int32, (rows, 1), 0) + start
    return jnp.where(place_of.astype(jnp.float32) < facts[2:3, 0:1], 1.0, 0.0)


def bias_tiles(lines_ref, tiles_ref, heads, width, scale=1.0):
    for head in range(heads):
        line = lines_ref[head : head + 1, :] * scale
        spread = jnp.broadcast_to(line, (tiles_ref.shape[1], line.shape[1]))
        tiles_ref[head] = pltpu.roll(spread, 0, 1, stride=1, stride_axis=0)[:, :width]


def softmax_pair(first, second):
    top = jnp.maximum(
        jnp.max(first, axis=-1, keepdims=True), jnp.max(second, axis=-1, keepdims=True)
    )
    first, second = jnp.exp(first - top), jnp.exp(second - top)
    total = jnp.sum(first, axis=-1, keepdims=True) + jnp.sum(second, axis=-1, keepdims=True)
    share = 1.0 / total
    return (
        (first * share).astype(jnp.bfloat16),
        (second * share).astype(jnp.bfloat16),
        top + jnp.log(total),
    )


TILE = 256
LOG2E = math.log2(math.e)
ROOT = 1.0 / math.sqrt(DH)


def forward_kernel(
    x_in, carried_in, initial_in, far_past, facts_in, far_gout, gstate_in, gains_ref,
    wst_in, wtok_in, wout_in, gates_in, far_wup, far_wdn,
    far_normed, far_snormed, far_queries, far_keys, far_values, far_state_qkv, far_lse, far_mixed,
    far_wst, far_wtok, far_wout, far_gates, far_x, far_s0, far_s1,
    far_gate_values, far_gstate_here, far_wup_grad, far_wdn_grad,
    smixed_rows, s2_ref, facts, block_out, middle_grad, branch_rows, small_sums,
    normed, snormed, queries, keys, values, state_qkv, lse_ref, mixed,
    wst, wtok, wout, gates, x_ref, s0_ref, s1_ref,
    smixed, tiles, initial_all, normed_send, gstate_send, s0_send, gate_values, wup, wdn, middle,
    middle_normed, gout_rows, gout, slope, hidden, up_grad, grad_stage, *rest,
):
    rs = [rest[4 * k : 4 * k + 4] for k in range(4)]
    links = Links(rest[16], rest[17])
    local_sems, keep_sems = rest[18], rest[19]
    kept = []

    def keep(source, target):
        moved = pltpu.make_async_copy(source, target, keep_sems.at[len(kept)])
        moved.start()
        kept.append(moved)

    here = Place()
    rank, ranks, mates = here.rank, here.ranks, here.mates
    rows = s0_ref.shape[0]
    window = 4 * rows
    width = queries.shape[1]
    heads = width // DH
    ring = [(lax.rem(here.dp + step, 8), here.level) for step in range(1, 8)]
    greet(ring + mates[2:] + [here.from_across], here)

    def turn(source, target):
        return Turn(links, here, source, target, here.there)

    part = initial_in.shape[1]
    own_columns = pl.ds(pl.multiple_of(here.dp * part, part), part)
    initial_moves = [links.copy(initial_in, initial_all.at[:, own_columns], mate) for mate in ring]
    facts_turn = turn(facts_in, facts)
    gather_wst = WeightGather(links, here, wst_in, wst).enter()
    initial_all[:, own_columns] = initial_in[...]
    for moved in initial_moves:
        moved.wait_recv()
    is_fresh = facts_in[3:4, :] > 0.5
    start = jnp.where(is_fresh, initial_all[...].astype(jnp.float32), carried_in[...])
    s0_send[...] = start
    normed_send[...] = (start * scale_of(start) * gains_ref[2:3, :]).astype(jnp.bfloat16)
    normed_turn = turn(normed_send, snormed.at[rows_at(here.level * rows, rows)])
    facts_turn.arrived()
    bias_tiles(facts, tiles, heads, 3 * TILE)
    gather_wst.spread()
    gather_wtok = WeightGather(links, here, wtok_in, wtok).enter()
    normed_turn.arrived()
    gather_s0 = RowGather(links, here, snormed, 0, rows).start()

    def enter_x(block):
        at = pl.ds(block * rows, rows)
        return turn(x_in.at[at], x_ref.at[at])

    def norm_x(block, moved):
        moved.arrived()
        x = x_ref[block * rows : (block + 1) * rows, :].astype(jnp.float32)
        normed[rows_at(block * window + rank * rows, rows), :] = (
            x * scale_of(x) * gains_ref[0:1, :]
        ).astype(jnp.bfloat16)
        return RowGather(links, here, normed, block * window, rows).start()

    x_turn_0 = enter_x(0)
    gather_wst.forward()
    gather_wtok.spread()
    x_turn_1 = enter_x(1)

    def key_mask(start, size):
        place_of = lax.broadcasted_iota(jnp.int32, (1, size), 1).astype(jnp.float32)
        place_of = place_of + float(start - window)
        own = jnp.where(place_of < facts[2:3, 0:size], 0.0, NEGATIVE)
        return jnp.where(place_of < 0.0, facts[3:4, 0:size] * NEGATIVE, own)

    def project_state(block, gather):
        for k in range(4):
            gather.ready(k)
            at = rows_at(block * window + ranks[k] * rows, rows)
            for c in range(3):
                state_qkv[at, c * width : (c + 1) * width] = dot(snormed[at, :], wst[c], NN).astype(
                    jnp.bfloat16
                )

    def project_token(block, gather):
        for k in range(4):
            gather.ready(k)
            at = rows_at(block * window + ranks[k] * rows, rows)
            later = rows_at((block + 1) * window + ranks[k] * rows, rows)
            queries[at, :] = dot(normed[at, :], wtok[0], NN).astype(jnp.bfloat16)
            keys[later, :] = dot(normed[at, :], wtok[1], NN).astype(jnp.bfloat16)
            values[later, :] = dot(normed[at, :], wtok[2], NN).astype(jnp.bfloat16)

    def state_attention(block):
        base = block * window
        own = pl.ds((block + 1) * window, window)
        whole = pl.ds(base, window)
        own_mask = key_mask(base + window, window)
        for head in range(heads):
            at = head * DH
            for tile in range(window // TILE):
                here_rows = pl.ds(base + tile * TILE, TILE)
                query = state_qkv[here_rows, at : at + DH]
                first = dot(query, state_qkv[whole, width + at : width + at + DH], NT) * ROOT
                second = dot(query, keys[own, at : at + DH], NT) * ROOT + own_mask
                first, second, lse = softmax_pair(first, second)
                out = dot(first, state_qkv[whole, 2 * width + at : 2 * width + at + DH], NN)
                out = out + dot(second, values[own, at : at + DH], NN)
                smixed[here_rows, at : at + DH] = out.astype(jnp.bfloat16)
                lse_ref[here_rows, heads + head : heads + head + 1] = lse

    def token_attention(block):
        base = block * window
        whole = pl.ds(base, window)
        for tile in range(window // TILE):
            near_mask = key_mask(base + tile * TILE, 3 * TILE)
            for head in range(heads):
                at = head * DH
                here_rows = pl.ds(base + tile * TILE, TILE)
                near = pl.ds(base + tile * TILE, 3 * TILE)
                query = queries[here_rows, at : at + DH]
                first = dot(query, keys[near, at : at + DH], NT) * ROOT + tiles[head] + near_mask
                second = dot(query, state_qkv[whole, width + at : width + at + DH], NT) * ROOT
                first, second, lse = softmax_pair(first, second)
                out = dot(first, values[near, at : at + DH], NN)
                out = out + dot(second, state_qkv[whole, 2 * width + at : 2 * width + at + DH], NN)
                mixed[here_rows, at : at + DH] = out.astype(jnp.bfloat16)
                lse_ref[here_rows, head : head + 1] = lse

    def spread_state(block, buffer):
        moves = []
        columns = pl.ds(pl.multiple_of(rank * width, width), width)
        for k in (2, 3, 1):
            source = smixed.at[rows_at(block * window + ranks[k] * rows, rows)]
            moves.append(links.copy(source, buffer.at[:, columns], mates[k]))
        buffer[:, columns] = smixed[rows_at(block * window + rank * rows, rows), :]
        return moves

    def renew(block, buffer, state_now):
        size = state_now.shape[1]
        source = buffer[...]
        parts = []
        for c in range(3):
            part = dot(source, gates[c], NT)
            gate_values[:, c * size : (c + 1) * size] = part
            parts.append(part)
        stored = pltpu.make_async_copy(
            gate_values, far_gate_values.at[pl.ds(block * rows, rows)], local_sems.at[0]
        )
        stored.start()
        new_state = state_now * jax.nn.sigmoid(parts[2] + 1.0) + jnp.tanh(parts[0]) * jax.nn.sigmoid(
            parts[1] - 1.0
        )
        return new_state, stored

    def out_rows(block):
        def make(which):
            return dot(mixed[rows_at(block * window + which * rows, rows), :], wout[...], NT)

        return make

    sums = [RowSum(links, here, *rs[block], rows) for block in range(2)]

    def finish_branch(block):
        branch = sums[block].finish()
        at = slice(block * rows, (block + 1) * rows)
        total = x_ref[at, :].astype(jnp.float32) + branch
        middle[at, :] = total
        middle_normed[rows_at(block * window + rank * rows, rows), :] = (
            total * scale_of(total) * gains_ref[1:2, :]
        ).astype(jnp.bfloat16)
        gather = RowGather(links, here, middle_normed, block * window, rows).start()
        share = row_mask(facts, block * window + rank * rows, rows)
        return jnp.sum(branch * branch * share, axis=0, keepdims=True), gather

    def rise(block, gather):
        root = math.sqrt(2.0 / math.pi)
        for k in range(4):
            gather.ready(k)
            at = rows_at(block * window + ranks[k] * rows, rows)
            value = dot(middle_normed[at, :], wup[...], NN)
            square = value * value
            bend = jnp.tanh(root * value * (1.0 + 0.044715 * square))
            half = 0.5 * (1.0 + bend)
            hidden[at, :] = (value * half).astype(jnp.bfloat16)
            slope[at, :] = half + 0.5 * value * (1.0 - bend * bend) * (
                root * (1.0 + 3.0 * 0.044715 * square)
            )

    def feed_sum(block):
        return RowSum(links, here, *rs[block], rows).fill(
            lambda which: dot(hidden[rows_at(block * window + which * rows, rows), :], wdn[...], NT)
        )

    def start_gout(block):
        at = slice(block * rows, (block + 1) * rows)
        gout[rows_at(block * window + rank * rows, rows), :] = gout_rows[at, :]
        return RowGather(links, here, gout, block * window, rows).start()

    def feed_back(block, gather):
        for k in range(4):
            gather.ready(k)
            at = rows_at(block * window + ranks[k] * rows, rows)
            up_grad[at, :] = (dot(gout[at, :], wdn[...], NN) * slope[at, :]).astype(jnp.bfloat16)
        return RowSum(links, here, *rs[2 + block], rows).fill(
            lambda which: dot(up_grad[rows_at(block * window + which * rows, rows), :], wup[...], NT)
        )

    def weight_grad(stage, left, right, target, sem):
        step = 256
        for part in range(stage.shape[0] // step):
            at = slice(part * step, (part + 1) * step)
            stage[at, :] = dot(left[:, at], right[...], TN).astype(jnp.bfloat16)
        stored = pltpu.make_async_copy(stage, target, sem)
        stored.start()
        return stored

    gather_wst.finish()
    keep(wst, far_wst)
    project_state(0, gather_s0)
    gather_x0 = norm_x(0, x_turn_0)
    gather_wtok.forward()
    gather_gates = GateGather(links, here, gates_in, gates, local_sems.at[3])
    gather_gates.spread()
    gather_wout = WeightGather(links, here, wout_in, wout).enter()
    past_turns = [
        turn(far_past.at[0], keys.at[pl.ds(0, window)]),
        turn(far_past.at[1], values.at[pl.ds(0, window)]),
    ]
    gather_x1 = norm_x(1, x_turn_1)
    gather_wtok.finish()
    keep(wtok, far_wtok)
    keep(x_ref, far_x)
    project_token(0, gather_x0)
    state_attention(0)
    a2a_0 = smixed_rows.at[pl.ds(0, rows)]
    a2a_1 = smixed_rows.at[pl.ds(rows, rows)]
    moves_0 = spread_state(0, a2a_0)
    s0_turn = turn(s0_send, s0_ref)
    gather_wout.spread()
    gather_wup = WeightGather(links, here, far_wup, wup).enter()
    project_token(1, gather_x1)
    keep(normed, far_normed)
    keep(queries, far_queries)
    gather_gates.forward()
    for moved in past_turns:
        moved.arrived()
    keep(keys, far_keys)
    keep(values, far_values)
    token_attention(0)
    gather_wout.forward()
    gather_gates.last()
    gather_wdn = WeightGather(links, here, far_wdn, wdn).enter()
    gather_wup.spread()
    gather_wout.finish()
    keep(wout, far_wout)
    sums[0].fill(out_rows(0))
    for moved in moves_0:
        moved.wait_recv()
    gather_gates.finish()
    keep(gates, far_gates)
    s0_turn.arrived()
    keep(s0_ref, far_s0)
    s1, keep_gates = renew(0, a2a_0, s0_ref[...])
    s1_ref[...] = s1
    keep(s1_ref, far_s1)
    snormed[rows_at(window + rank * rows, rows), :] = (s1 * scale_of(s1) * gains_ref[2:3, :]).astype(
        jnp.bfloat16
    )
    gather_s1 = RowGather(links, here, snormed, window, rows).start()
    sums[0].forward()
    gather_wup.forward()
    gather_wdn.spread()
    project_state(1, gather_s1)
    gout_turn = turn(far_gout, gout_rows)
    keep(snormed, far_snormed)
    keep(state_qkv, far_state_qkv)
    branch_total, gather_m0 = finish_branch(0)
    token_attention(1)
    keep(mixed, far_mixed)
    sums[1].fill(out_rows(1))
    gather_wdn.forward()
    state_attention(1)
    keep(lse_ref, far_lse)
    sums[1].forward()
    moves_1 = spread_state(1, a2a_1)
    gather_wup.finish()
    rise(0, gather_m0)
    more, gather_m1 = finish_branch(1)
    branch_total = branch_total + more
    gout_turn.arrived()
    gather_g0 = start_gout(0)
    gather_wdn.finish()
    sums[0].sent()
    feed_0 = feed_sum(0)
    for moved in moves_1:
        moved.wait_recv()
    keep_gates.wait()
    s2, keep_gates = renew(1, a2a_1, s1_ref[...])
    gstate_send[...] = gstate_in[...].astype(jnp.bfloat16)
    gstate_turn = turn(gstate_send, far_gstate_here)
    s2_ref[...] = s2.astype(jnp.bfloat16)
    rise(1, gather_m1)
    gather_g1 = start_gout(1)
    sums[1].sent()
    feed_1 = feed_sum(1)
    feed_0.forward()
    back_0 = feed_back(0, gather_g0)
    back_0.forward()
    back_1 = feed_back(1, gather_g1)
    feed_1.forward()
    keep_down = weight_grad(grad_stage, gout, hidden, far_wdn_grad, local_sems.at[1])
    back_1.forward()
    keep_up = weight_grad(hidden, middle_normed, up_grad, far_wup_grad, local_sems.at[2])
    feed_total, result_total, gain_total = 0.0, 0.0, 0.0
    for block, feed_here in ((0, feed_0), (1, feed_1)):
        at = slice(block * rows, (block + 1) * rows)
        feed = feed_here.finish()
        result = middle[at, :] + feed
        block_out[at, :] = result.astype(jnp.bfloat16)
        share = row_mask(facts, block * window + rank * rows, rows)
        feed_total = feed_total + jnp.sum(feed * feed * share, axis=0, keepdims=True)
        result_total = result_total + jnp.sum(result * result * share, axis=0, keepdims=True)
    for block, back_here in ((1, back_1), (0, back_0)):
        at = slice(block * rows, (block + 1) * rows)
        straight, gain = rms_back(middle[at, :], gains_ref[1:2, :], back_here.finish())
        total = gout_rows[at, :].astype(jnp.float32) + straight
        middle_grad[at, :] = total
        branch_rows[at, :] = total.astype(jnp.bfloat16)
        gain_total = gain_total + gain
    small_sums[...] = jnp.concatenate(
        [gain_total, result_total, branch_total, feed_total]
        + [jnp.zeros((4, gain_total.shape[1]), jnp.float32)],
        axis=0,
    )
    gstate_turn.arrived()
    keep_gates.wait()
    keep_down.wait()
    keep_up.wait()
    for moved in kept:
        moved.wait()
    links.close()


class PlaneSum:
    def __init__(self, links, here, grad, first_in, last_in):
        self.links, self.here, self.grad = links, here, grad
        self.first_in, self.last_in = first_in, last_in
        self.rows = first_in.shape[-2]

    def part(self, k, which):
        start = self.here.planes[k] * 2 * self.rows + which * self.rows
        return rows_of(self.grad, start, self.rows)

    def start(self):
        mates = self.here.plane_mates
        self.firsts = [
            self.links.copy(self.part(k, which), self.first_in.at[slot], mates[mate])
            for slot, (k, which, mate) in enumerate(((1, 0, 1), (3, 0, 1), (2, 1, 2), (3, 1, 2)))
        ]
        return self

    def add(self, k, which, arrived):
        part = self.part(k, which)
        part[...] = (part[...].astype(jnp.float32) + arrived[...].astype(jnp.float32)).astype(part.dtype)

    def forward(self):
        mates = self.here.plane_mates
        self.firsts[1].wait_recv()
        self.add(2, 0, self.first_in.at[1])
        self.last_0 = self.links.copy(self.part(2, 0), self.last_in.at[0], mates[2])
        self.firsts[3].wait_recv()
        self.add(1, 1, self.first_in.at[3])
        self.last_1 = self.links.copy(self.part(1, 1), self.last_in.at[1], mates[1])

    def finish(self):
        self.firsts[0].wait_recv()
        self.add(0, 0, self.first_in.at[0])
        self.firsts[2].wait_recv()
        self.add(0, 1, self.first_in.at[2])
        self.last_0.wait_recv()
        self.add(0, 0, self.last_in.at[0])
        self.last_1.wait_recv()
        self.add(0, 1, self.last_in.at[1])

    def result(self, which):
        return rows_of(self.grad, self.here.planes[0] * 2 * self.rows + which * self.rows, self.rows)


class FarPlaneSum(PlaneSum):
    def __init__(self, links, here, grad, first_in, last_in, held, held_sems):
        super().__init__(links, here, grad, first_in, last_in)
        self.held, self.held_sems = held, held_sems

    def bring(self, *pieces):
        self.brings = [
            pltpu.make_async_copy(self.part(k, which), self.held.at[slot], self.held_sems.at[slot])
            for slot, (k, which) in enumerate(pieces)
        ]
        for moved in self.brings:
            moved.start()

    def start(self):
        super().start()
        self.bring((2, 0), (1, 1))
        return self

    def add_to(self, slot, *arrived):
        total = self.held[slot].astype(jnp.float32)
        for piece in arrived:
            total = total + piece.astype(jnp.float32)
        self.held[slot] = total.astype(jnp.bfloat16)

    def forward(self):
        mates = self.here.plane_mates
        for moved in self.brings:
            moved.wait()
        self.firsts[1].wait_recv()
        self.add_to(0, self.first_in[1])
        self.last_0 = self.links.copy(self.held.at[0], self.last_in.at[0], mates[2])
        self.firsts[3].wait_recv()
        self.add_to(1, self.first_in[3])
        self.last_1 = self.links.copy(self.held.at[1], self.last_in.at[1], mates[1])

    def bring_own(self):
        self.links.sent(self.last_0)
        self.links.sent(self.last_1)
        self.bring((0, 0), (0, 1))

    def finish(self):
        for moved in self.brings:
            moved.wait()
        self.firsts[0].wait_recv()
        self.last_0.wait_recv()
        self.add_to(0, self.first_in[0], self.last_in[0])
        self.firsts[2].wait_recv()
        self.last_1.wait_recv()
        self.add_to(1, self.first_in[2], self.last_in[1])

    def result(self, which):
        return self.held.at[which]


class Settle:
    def __init__(self, links, here, summed, target):
        half = here.half
        self.straight = Turn(links, here, summed.result(half), target.at[0], here.from_there)
        self.crossed = links.copy(summed.result(1 - half), target.at[1], here.from_across)

    def arrived(self):
        self.straight.arrived()
        self.crossed.wait_recv()


def cotangent_kernel(
    far_middle_grad, far_branch_rows, gstate_ref, far_x, s0_ref, s1_ref, far_gate_values, gains_ref, facts, facts_home,
    small_sums,
    far_normed, far_snormed, far_queries, far_keys, far_values, far_state_qkv, far_lse, far_mixed,
    far_smixed, far_wst, far_wtok, far_wout, far_gates, far_wup_grad, far_wdn_grad, far_block_out, far_state_out,
    block_home, state_home, tokens_home, past_home, carried_grad, initial_grad, totals,
    up_home, down_home, wst_home, wtok_home, wout_home, gates_home,
    gates, wout, queries, keys, state_qkv, values, lse_ref, mixed, wst, wtok,
    tiles, tile_grads, branch_grad, mixed_grad, gate_rows, state_mixed_grad, key_grad, value_grad,
    skey_grad, svalue_grad, token_cot, state_cot, gate_values, smixed_pair, sending,
    tokens_send, carried_send, carried_in, initial_send, initial_in,
    wst_grad, wtok_grad, wout_grad, gates_grad,
    wst_first, wtok_first, wout_first, gates_first, wst_last, wtok_last, wout_last, gates_last,
    up_first, down_first, up_last, down_last, up_held, down_held, ring_in, level_in, ring_send, level_send,
    late_in, late_level_in, late_send, late_level_send,
    *rest,
):
    rs = [rest[0:4], rest[4:8], rest[8:12]]
    links = Links(rest[12], rest[13])
    local_sems, held_sems, bring_sems = rest[14], rest[15], rest[16]
    here = Place()
    rank, ranks, mates = here.rank, here.ranks, here.mates
    rows = s0_ref.shape[0]
    window = 4 * rows
    width = queries.shape[1]
    heads = width // DH
    size = s0_ref.shape[1]
    reach = 2 * width
    other_half = pl.ds(pl.multiple_of((1 - here.core) * reach, reach), reach)
    own_half = pl.ds(pl.multiple_of(here.core * reach, reach), reach)

    def pair_rows(block):
        return rows_at((2 * block + here.core) * rows, rows)

    def own_branch(block):
        return branch_grad.at[rows_at(block * window + rank * rows, rows)]

    brings = []
    for source, target in (
        (far_branch_rows.at[pl.ds(rows, rows)], own_branch(1)),
        (far_branch_rows.at[pl.ds(0, rows)], own_branch(0)),
        (far_gates, gates),
        (far_wout, wout),
        (far_queries, queries),
        (far_keys, keys),
        (far_state_qkv, state_qkv),
        (far_values, values),
        (far_lse, lse_ref),
        (far_mixed, mixed),
        (far_wst, wst),
        (far_wtok, wtok),
        (far_x, tokens_send),
        (far_smixed.at[pl.ds(0, rows), own_half], smixed_pair.at[pair_rows(0)]),
        (far_smixed.at[pl.ds(rows, rows), own_half], smixed_pair.at[pair_rows(1)]),
    ):
        brings.append(pltpu.make_async_copy(source, target, bring_sems.at[len(brings)]))
        brings[-1].start()
    ring = [(lax.rem(here.dp + step, 8), here.level) for step in range(1, 8)]
    other = here.dp + 1 - 2 * here.core
    column = [
        (chip, lax.rem(here.level + step, 4)) for step in range(1, 4) for chip in (here.dp, other)
    ]
    bring_gates = pltpu.make_async_copy(
        far_gate_values.at[pl.ds(rows, rows)], gate_values, local_sems.at[0]
    )
    bring_gates.start()
    greet(ring + column)
    def home(source, target):
        return Turn(links, here, source, target, here.from_there)

    def gates_back(block, state, state_grad):
        spot = pair_rows(block)
        keep = jax.nn.sigmoid(gate_values[:, 2 * size : 3 * size] + 1.0)
        fresh = jnp.tanh(gate_values[:, 0:size])
        let_in = jax.nn.sigmoid(gate_values[:, size : 2 * size] - 1.0)
        gate_rows[spot, 0:size] = (state_grad * let_in * (1.0 - fresh * fresh)).astype(jnp.bfloat16)
        gate_rows[spot, size : 2 * size] = (
            state_grad * fresh * let_in * (1.0 - let_in)
        ).astype(jnp.bfloat16)
        gate_rows[spot, 2 * size : 3 * size] = (
            state_grad * state * keep * (1.0 - keep)
        ).astype(jnp.bfloat16)
        out = dot(gate_rows[spot, 0:size], gates[0], NN)
        out = out + dot(gate_rows[spot, size : 2 * size], gates[1], NN)
        out = out + dot(gate_rows[spot, 2 * size : 3 * size], gates[2], NN)
        sending[...] = out.astype(jnp.bfloat16)
        spot = rows_at(block * window + rank * rows, rows)
        moves = []
        for k in (2, 3, 1):
            columns = pl.ds(pl.multiple_of(ranks[k] * width, width), width)
            moves.append(
                links.copy(sending.at[:, columns], state_mixed_grad.at[spot], mates[k])
            )
        columns = pl.ds(pl.multiple_of(rank * width, width), width)
        state_mixed_grad[spot, :] = sending[:, columns]
        pair = gate_rows.at[pair_rows(block)]
        return state_grad * keep, moves, links.copy(pair, pair, mates[1])

    lane = lax.broadcasted_iota(jnp.int32, (1, DH), 1)

    def widen(columns, value):
        high = value.astype(jnp.bfloat16).astype(jnp.float32)
        middle = (value - high).astype(jnp.bfloat16).astype(jnp.float32)
        more = jnp.where(lane == 1, high, jnp.where(lane == 2, middle, value - high - middle))
        more = jnp.where(lane == 0, 1.0, jnp.where(lane < 4, more, 0.0))
        return jnp.concatenate([columns, more.astype(jnp.bfloat16)], axis=1)

    plain = jnp.where((lane > 0) & (lane < 4), 1.0, 0.0)

    def beside(columns, mask=None):
        more = jnp.broadcast_to(plain, (columns.shape[0], DH))
        if mask is not None:
            more = jnp.where(lane == 0, mask, more)
        return jnp.concatenate([columns, more.astype(jnp.bfloat16)], axis=1)

    def key_mask(start, size):
        place_of = lax.broadcasted_iota(jnp.int32, (size, 1), 0).astype(jnp.float32)
        place_of = place_of + float(start - window)
        own = jnp.where(place_of < facts[2:3, 0:1], 0.0, NEGATIVE)
        return jnp.where(place_of < 0.0, facts[3:4, 0:1] * NEGATIVE, own)

    def token_back(block):
        base = block * window
        whole = pl.ds(base, window)
        for tile in range(window // TILE):
            near_mask = key_mask(base + tile * TILE, 3 * TILE)
            for head in range(heads):
                at = head * DH
                lanes = slice(at, at + DH)
                skey_lanes = slice(width + at, width + at + DH)
                svalue_lanes = slice(2 * width + at, 2 * width + at + DH)
                here_rows = pl.ds(base + tile * TILE, TILE)
                near = pl.ds(base + tile * TILE, 3 * TILE)
                query = queries[here_rows, lanes]
                out_grad = mixed_grad[here_rows, lanes]
                wide = widen(query, lse_ref[here_rows, head : head + 1] * (-1.0 / ROOT))
                inner = jnp.sum(
                    out_grad.astype(jnp.float32) * mixed[here_rows, lanes].astype(jnp.float32),
                    axis=-1,
                    keepdims=True,
                )
                wide_grad = widen(out_grad, -inner)
                first = jnp.exp2(
                    dot(wide, beside(keys[near, lanes], near_mask), NT) * (ROOT * LOG2E) + tiles[head]
                )
                second = jnp.exp2(
                    dot(wide, beside(state_qkv[whole, skey_lanes]), NT) * (ROOT * LOG2E)
                )
                first_low, second_low = first.astype(jnp.bfloat16), second.astype(jnp.bfloat16)
                first = first * dot(wide_grad, beside(values[near, lanes]), NT)
                second = second * dot(wide_grad, beside(state_qkv[whole, svalue_lanes]), NT)
                first_grad, second_grad = first.astype(jnp.bfloat16), second.astype(jnp.bfloat16)
                value_grad[near, lanes] += dot(first_low, out_grad, TN)
                svalue_grad[:, lanes] += dot(second_low, out_grad, TN)
                part = dot(first_grad, keys[near, lanes], NN) + dot(
                    second_grad, state_qkv[whole, skey_lanes], NN
                )
                token_cot[here_rows, lanes] = (part * ROOT).astype(jnp.bfloat16)
                key_grad[near, lanes] += dot(first_grad, query, TN) * ROOT
                skey_grad[:, lanes] += dot(second_grad, query, TN) * ROOT
                tile_grads[head] += first

    def state_back(block):
        base = block * window
        whole = pl.ds(base, window)
        own = pl.ds(base + window, window)
        own_mask = key_mask(base + window, window)
        for head in range(heads):
            at = head * DH
            lanes = slice(at, at + DH)
            skey_lanes = slice(width + at, width + at + DH)
            svalue_lanes = slice(2 * width + at, 2 * width + at + DH)
            wide_skeys = beside(state_qkv[whole, skey_lanes])
            wide_keys = beside(keys[own, lanes], own_mask)
            for tile in range(window // TILE):
                here_rows = pl.ds(base + tile * TILE, TILE)
                query = state_qkv[here_rows, lanes]
                out_grad = state_mixed_grad[here_rows, lanes]
                wide = widen(query, lse_ref[here_rows, heads + head : heads + head + 1] * (-1.0 / ROOT))
                first = jnp.exp2(dot(wide, wide_skeys, NT) * (ROOT * LOG2E))
                second = jnp.exp2(dot(wide, wide_keys, NT) * (ROOT * LOG2E))
                first_low, second_low = first.astype(jnp.bfloat16), second.astype(jnp.bfloat16)
                first_grad = dot(out_grad, state_qkv[whole, svalue_lanes], NT)
                second_grad = dot(out_grad, values[own, lanes], NT)
                inner = jnp.sum(first * first_grad, axis=-1, keepdims=True) + jnp.sum(
                    second * second_grad, axis=-1, keepdims=True
                )
                first_grad = (first * (first_grad - inner)).astype(jnp.bfloat16)
                second_grad = (second * (second_grad - inner)).astype(jnp.bfloat16)
                svalue_grad[:, lanes] += dot(first_low, out_grad, TN)
                value_grad[own, lanes] += dot(second_low, out_grad, TN)
                part = dot(first_grad, state_qkv[whole, skey_lanes], NN) + dot(
                    second_grad, keys[own, lanes], NN
                )
                state_cot[here_rows, lanes] = (part * ROOT).astype(jnp.bfloat16)
                skey_grad[:, lanes] += dot(first_grad, query, TN) * ROOT
                key_grad[own, lanes] += dot(second_grad, query, TN) * ROOT

    def gather_cot(block):
        whole = pl.ds(block * window, window)
        own = pl.ds(block * window + window, window)
        token_cot[whole, width : 2 * width] = key_grad[own, :].astype(jnp.bfloat16)
        token_cot[whole, 2 * width : 3 * width] = value_grad[own, :].astype(jnp.bfloat16)
        state_cot[whole, width : 2 * width] = skey_grad[...].astype(jnp.bfloat16)
        state_cot[whole, 2 * width : 3 * width] = svalue_grad[...].astype(jnp.bfloat16)

    def back_rows(cots, weight, block):
        def make(which):
            at = rows_at(block * window + which * rows, rows)
            out = dot(cots[at, 0:width], weight[0], NT)
            for c in (1, 2):
                out = out + dot(cots[at, c * width : (c + 1) * width], weight[c], NT)
            return out

        return make

    def state_sum(block):
        return RowSum(links, here, *rs[0], rows).fill(back_rows(state_cot, wst, block))

    def token_sum(block):
        return RowSum(links, here, *rs[1 + block], rows).fill(back_rows(token_cot, wtok, block))

    def mix_back(block, gather):
        for k in range(4):
            gather.ready(k)
            at = rows_at(block * window + ranks[k] * rows, rows)
            mixed_grad[at, :] = dot(branch_grad[at, :], wout[...], NN).astype(jnp.bfloat16)

    def store_grad(target, at, out):
        if len(target.shape) == 2:
            target[at, :] = out.astype(jnp.bfloat16)
        else:
            for c in range(3):
                target[c, at, :] = out[:, c * width : (c + 1) * width].astype(jnp.bfloat16)

    def weight_grad(target, left, right):
        step = 256
        for part in range(size // step):
            at = slice(part * step, (part + 1) * step)
            store_grad(target, at, dot(left[:, at], right[...], TN))

    def finish_tokens(block, summed):
        at = slice(block * rows, (block + 1) * rows)
        x = tokens_send[at, :].astype(jnp.float32)
        straight, gain = rms_back(x, gains_ref[0:1, :], summed.finish())
        middle_grad = gate_values[:, block * size : (block + 1) * size]
        tokens_send[at, :] = (middle_grad + straight).astype(jnp.bfloat16)
        return gain, home(tokens_send.at[pl.ds(block * rows, rows)], tokens_home.at[pl.ds(block * rows, rows)])

    smixed_moves = []
    for block in range(2):
        smixed_moves.append(
            links.copy(
                far_smixed.at[pl.ds(block * rows, rows), other_half],
                smixed_pair.at[pair_rows(block)],
                mates[1],
            )
        )
    brings[0].wait()
    branch_1 = RowGather(links, here, branch_grad, window, rows).start()
    bring_gates.wait()
    brings[2].wait()
    direct_1, moves_1, pair_1 = gates_back(1, s1_ref[...], gstate_ref[...].astype(jnp.float32))
    up_sum = FarPlaneSum(
        links, here, far_wup_grad, up_first, up_last, up_held, held_sems.at[pl.ds(0, 2)]
    ).start()
    down_sum = FarPlaneSum(
        links, here, far_wdn_grad, down_first, down_last, down_held, held_sems.at[pl.ds(2, 2)]
    ).start()
    bring_gates = pltpu.make_async_copy(far_gate_values.at[pl.ds(0, rows)], gate_values, local_sems.at[0])
    bring_gates.start()
    for ref in (tile_grads, key_grad, value_grad, skey_grad, svalue_grad):
        ref[...] = jnp.zeros(ref.shape, ref.dtype)
    bias_tiles(facts, tiles, heads, 3 * TILE, LOG2E)
    brings[1].wait()
    for moved in brings[3:]:
        moved.wait()
    mix_back(1, branch_1)
    branch_0 = RowGather(links, here, branch_grad, 0, rows).start()
    block_turn = home(far_block_out, block_home)
    state_turn = home(far_state_out, state_home)
    token_back(1)
    for moved in moves_1:
        moved.wait_recv()
    state_back(1)
    gather_cot(1)
    up_sum.forward()
    state_sum_1 = state_sum(1)
    token_sum_1 = token_sum(1)
    state_sum_1.forward()
    down_sum.forward()
    up_sum.bring_own()
    mix_back(0, branch_0)
    for ref in (skey_grad, svalue_grad):
        ref[...] = jnp.zeros(ref.shape, ref.dtype)
    up_sum.finish()
    up_settle = Settle(links, here, up_sum, up_home)
    token_back(0)
    for head in range(heads):
        lines = tile_grads[head, 0:8, :]
        span = lines.shape[1]
        for group in range(1, TILE // 8):
            lines = lines + pltpu.roll(tile_grads[head, 8 * group : 8 * group + 8, :], span - 8 * group, 1)
        total = lines[0:1]
        for line in range(1, 8):
            total = total + pltpu.roll(lines[line : line + 1], span - line, 1)
        for owner in range(4):
            at = 8 + heads * owner + head
            ring_send[at : at + 1, :] = jnp.zeros((1, size), jnp.float32)
            ring_send[at : at + 1, 0:span] = jnp.where(rank == owner, total, 0.0)
    ring_send[1:2, :] = small_sums[0:1, :]
    ring_send[3:6, :] = small_sums[1:4, :]
    counted = jnp.zeros((1, 1), jnp.float32)
    for block in range(2):
        valid_rows = row_mask(facts, block * window + rank * rows, rows)
        counted = counted + jnp.sum(valid_rows, axis=0, keepdims=True)
    ring_send[6:7, :] = jnp.broadcast_to(counted, (1, size))
    for line in (0, 2, 7):
        ring_send[line : line + 1, :] = jnp.zeros((1, size), jnp.float32)
    ring_moves = [
        links.copy(ring_send, ring_in.at[step - 1], ring[step - 1]) for step in range(1, 8)
    ]
    token_sum_1.forward()
    bring_gates.wait()
    state_norm_grad, gain_2 = rms_back(s1_ref[...], gains_ref[2:3, :], state_sum_1.finish())
    for moved in moves_1:
        links.sent(moved)
    direct_0, moves_0, pair_0 = gates_back(0, s0_ref[...], direct_1 + state_norm_grad)
    bring_middle = [
        pltpu.make_async_copy(
            far_middle_grad.at[pl.ds(block * rows, rows)],
            gate_values.at[:, pl.ds(block * size, size)],
            local_sems.at[6 + block],
        )
        for block in range(2)
    ]
    for moved in bring_middle:
        moved.start()
    mixed_grad[0:window, :] = key_grad[0:window, :].astype(jnp.bfloat16)
    mixed_grad[window : 2 * window, :] = value_grad[0:window, :].astype(jnp.bfloat16)
    down_sum.bring_own()
    for moved in smixed_moves + [pair_1, pair_0]:
        moved.wait_recv()
    for c in range(3):
        weight_grad(gates_grad.at[c], gate_rows.at[:, c * size : (c + 1) * size], smixed_pair)
    gates_sum = PlaneSum(links, here, gates_grad, gates_first, gates_last).start()
    weight_grad(wout_grad, branch_grad, mixed)
    wout_sum = PlaneSum(links, here, wout_grad, wout_first, wout_last).start()
    for moved in ring_moves:
        moved.wait_recv()
    total = ring_send[...]
    for step in range(7):
        total = total + ring_in[step]
    level_send[...] = total
    level_moves = [
        links.copy(level_send, level_in.at[step - 1], (here.dp, lax.rem(here.level + step, 4)))
        for step in range(1, 4)
    ]
    down_sum.finish()
    for moved in bring_middle:
        moved.wait()
    gain_1, turn_1 = finish_tokens(1, token_sum_1)
    for moved in moves_0:
        moved.wait_recv()
    past_turn = home(mixed_grad, past_home)
    down_settle = Settle(links, here, down_sum, down_home)
    for gather in (branch_1, branch_0):
        gather.sent()
    bring_snormed = pltpu.make_async_copy(far_snormed, branch_grad, local_sems.at[2])
    bring_snormed.start()
    for moved in (pair_1, pair_0):
        links.sent(moved)
    bring_normed = []
    for block in range(2):
        bring_normed.append(
            pltpu.make_async_copy(
                far_normed.at[pl.ds(block * window, window)],
                gate_rows.at[:, block * size : (block + 1) * size],
                local_sems.at[4 + block],
            )
        )
        bring_normed[block].start()
    state_back(0)
    gather_cot(0)
    bring_snormed.wait()
    weight_grad(wst_grad, branch_grad, state_cot)
    wst_sum = PlaneSum(links, here, wst_grad, wst_first, wst_last).start()
    for block in range(2):
        bring_normed[block].wait()
    for part in range(size // 256):
        at = slice(part * 256, (part + 1) * 256)
        later = slice(size + part * 256, size + (part + 1) * 256)
        summed = dot(gate_rows[:, at], token_cot[0:window, :], TN)
        summed = summed + dot(gate_rows[:, later], token_cot[window : 2 * window, :], TN)
        store_grad(wtok_grad, at, summed)
    wtok_sum = PlaneSum(links, here, wtok_grad, wtok_first, wtok_last).start()
    gates_sum.forward()
    state_sum_1.sent()
    state_sum_0 = state_sum(0)
    token_sum_0 = token_sum(0)
    state_sum_0.forward()
    token_sum_0.forward()
    wst_sum.forward()
    wtok_sum.forward()
    wout_sum.forward()
    state_norm_grad, gain = rms_back(s0_ref[...], gains_ref[2:3, :], state_sum_0.finish())
    carried_send[...] = (direct_0 + state_norm_grad).astype(jnp.bfloat16)
    carried_turn = home(carried_send, carried_in)
    gain_2 = gain_2 + gain
    gates_sum.finish()
    slot = here.level * 2 + here.core
    piece = rows // 4
    gate_moves = []
    for step in range(4):
        to_level = lax.rem(here.level + step, 4)
        for to_core, chip in ((here.core, here.dp), (1 - here.core, other)):
            start = here.planes[0] * 2 * rows + to_core * rows + to_level * piece
            source = rows_of(gates_grad, start, piece, piece)
            if step == 0 and chip is here.dp:
                kept = pltpu.make_async_copy(source, gates_home.at[slot], local_sems.at[3])
                kept.start()
            else:
                gate_moves.append(links.copy(source, gates_home.at[slot], (chip, to_level)))
    wst_sum.finish()
    wst_settle = Settle(links, here, wst_sum, wst_home)
    gain_0, turn_0 = finish_tokens(0, token_sum_0)

    late_send[...] = jnp.concatenate(
        [gain[:, step * 256 : (step + 1) * 256] for gain in (gain_0 + gain_1, gain_2) for step in range(4)],
        axis=0,
    )
    late_moves = [
        links.copy(late_send, late_in.at[step - 1], ring[step - 1]) for step in range(1, 8)
    ]
    wtok_sum.finish()
    wtok_settle = Settle(links, here, wtok_sum, wtok_home)
    wout_sum.finish()
    wout_settle = Settle(links, here, wout_sum, wout_home)
    carried_turn.arrived()
    is_fresh = facts_home[3:4, :] > 0.5
    came = carried_in[...]
    carried_grad[...] = jnp.where(is_fresh, 0.0, came.astype(jnp.float32))
    initial_send[...] = jnp.where(is_fresh, came, jnp.zeros_like(came))
    part = initial_grad.shape[1]
    initial_moves = []
    for step in range(1, 8):
        to = lax.rem(here.dp + step, 8)
        columns = pl.ds(pl.multiple_of(to * part, part), part)
        initial_moves.append(
            links.copy(initial_send.at[:, columns], initial_in.at[step - 1], ring[step - 1])
        )
    for moved in late_moves:
        moved.wait_recv()
    late = late_send[...]
    for step in range(7):
        late = late + late_in[step]
    late_level_send[...] = late
    late_level_moves = [
        links.copy(late_level_send, late_level_in.at[step - 1], (here.dp, lax.rem(here.level + step, 4)))
        for step in range(1, 4)
    ]
    for moved in initial_moves:
        moved.wait_recv()
    own_columns = pl.ds(pl.multiple_of(here.dp * part, part), part)
    initial = initial_send[:, own_columns].astype(jnp.float32)
    for step in range(7):
        initial = initial + initial_in[step].astype(jnp.float32)
    initial_grad[...] = initial
    for moved in level_moves:
        moved.wait_recv()
    total = level_send[...]
    for step in range(3):
        total = total + level_in[step]
    totals[...] = total
    for moved in late_level_moves:
        moved.wait_recv()
    late = late_level_send[...]
    for step in range(3):
        late = late + late_level_in[step]
    for row, first in ((0, 0), (2, 4)):
        for step in range(4):
            totals[row : row + 1, step * 256 : (step + 1) * 256] = late[first + step : first + step + 1, :]
    kept.wait()
    for moved in gate_moves:
        moved.wait_recv()
    for turn in (block_turn, state_turn, past_turn, turn_1, turn_0):
        turn.arrived()
    for settle in (up_settle, down_settle, wout_settle, wst_settle, wtok_settle):
        settle.arrived()
    links.close()


def run_kernel(body, outs, scratch, collective, name, operands, far_in=(), far_out=()):
    vmem = pl.BlockSpec(memory_space=pltpu.VMEM)
    far = pl.BlockSpec(memory_space=pl.ANY)
    return pl.pallas_call(
        body,
        out_shape=outs,
        in_specs=[far if at in far_in else vmem for at in range(len(operands))],
        out_specs=[far if at in far_out else vmem for at in range(len(outs))],
        scratch_shapes=scratch,
        compiler_params=pltpu.CompilerParams(
            collective_id=collective, has_side_effects=True, vmem_limit_bytes=VMEM_BYTES
        ),
        name=name,
    )(*operands)


def sems(count):
    return [pltpu.SemaphoreType.DMA((count,)), pltpu.SemaphoreType.DMA((count,))]


def grouped(
    tokens, carried_state, past_keys, fresh_start, valid_count, bucket_ids, grad_output, grad_state,
    norm_gains, token_qkv, token_out, bias_table, mlp_up, mlp_down, state_qkv, state_gates, initial_state,
):
    dp_size, levels = lax.axis_size("dp"), lax.axis_size("state")
    dp_at, level = lax.axis_index("dp"), lax.axis_index("state")
    _, blocks, rows, size = tokens.shape
    window = rows * levels
    width = token_qkv.shape[2]
    heads = width // DH
    units = mlp_up.shape[1]
    model_rows = token_qkv.shape[0]
    low, full = jnp.bfloat16, jnp.float32

    one_hot = (bucket_ids[:, None] == jnp.arange(bias_table.shape[0])[None, :]).astype(full)
    per_offset = jnp.dot(one_hot, bias_table, precision=HIGHEST)
    lines = jnp.pad(per_offset[::-1].T, ((0, 0), (1, window - 1)), constant_values=NEGATIVE)
    numbers = jnp.stack([valid_count[0], fresh_start[0]]).astype(full)
    facts_in = jnp.concatenate(
        [
            lines,
            jnp.broadcast_to(numbers[:, None], (2, lines.shape[1])),
            jnp.zeros((4, lines.shape[1]), full),
        ]
    )

    stacked = lambda weight: jnp.transpose(weight, (1, 0, 2))
    shape = jax.ShapeDtypeStruct
    vmem = pltpu.VMEM
    rs = row_sum_scratch(rows, size)
    kept = [
        ((2 * window, size), low),
        ((2 * window, size), low),
        ((2 * window, width), low),
        ((3 * window, width), low),
        ((3 * window, width), low),
        ((2 * window, 3 * width), low),
        ((2 * window, 2 * heads), full),
        ((2 * window, width), low),
        ((3, size, width), low),
        ((3, size, width), low),
        ((size, width), low),
        ((3, size, size), low),
        ((2 * rows, size), low),
        ((rows, size), full),
        ((rows, size), full),
    ]
    (
        normed, snormed, queries, keys, values, sqkv, lse, mixed, wst_all, wtok_all, wout_all, gates_all,
        x, s0, s1, gate_values, gstate, wup_grad, wdn_grad, smixed_rows, s2, facts,
        block_out, middle_grad, branch_rows, small_sums,
    ) = run_kernel(
        forward_kernel,
        [shape(*of) for of in kept]
        + [
            shape((2 * rows, 3 * size), full),
            shape((rows, size), low),
            shape((size, units), low),
            shape((size, units), low),
            shape((2 * rows, size), low),
            shape((rows, size), low),
            shape((8, 2 * window), full),
            shape((2 * rows, size), low),
            shape((2 * rows, size), full),
            shape((2 * rows, size), low),
            shape((8, size), full),
        ],
        [vmem(*of) for of in kept]
        + [
            vmem((2 * window, width), low),
            vmem((heads, TILE, 3 * TILE), full),
            vmem((rows, size), low),
            vmem((rows, size), low),
            vmem((rows, size), low),
            vmem((rows, size), full),
            vmem((rows, 3 * size), full),
            vmem((size, units), low),
            vmem((size, units), low),
            vmem((2 * rows, size), full),
            vmem((2 * window, size), low),
            vmem((2 * rows, size), low),
            vmem((2 * window, size), low),
            vmem((2 * window, units), full),
            vmem((2 * window, units), low),
            vmem((2 * window, units), low),
            vmem((size, units), low),
        ]
        + rs * 4
        + sems(128)
        + [pltpu.SemaphoreType.DMA((4,)), pltpu.SemaphoreType.DMA((len(kept),))],
        0,
        "forward",
        [
            tokens[0].reshape(blocks * rows, size),
            carried_state[0],
            initial_state,
            jnp.swapaxes(past_keys[0], 0, 1),
            facts_in,
            grad_output[0].reshape(blocks * rows, size),
            grad_state[0],
            norm_gains,
            stacked(state_qkv),
            stacked(token_qkv),
            token_out,
            stacked(state_gates),
            mlp_up,
            mlp_down,
        ],
        far_in=(3, 5, 12, 13),
        far_out=range(len(kept) + 4),
    )
    grads = [((3,), width), ((3,), width), ((), width), ((3,), 2 * width)]
    (
        block_home, state_home, tokens_home, past_home, carried_grad, initial_grad, totals,
        up_home, down_home, wst_home, wtok_home, wout_home, gates_home,
    ) = run_kernel(
        cotangent_kernel,
        [
            shape((2 * rows, size), low),
            shape((rows, size), low),
            shape((2 * rows, size), low),
            shape((2 * window, width), low),
            shape((rows, size), full),
            shape((rows, size // dp_size), full),
            shape((16, size), full),
            shape((2, rows, units), low),
            shape((2, rows, units), low),
            shape((2, 3, rows, width), low),
            shape((2, 3, rows, width), low),
            shape((2, rows, width), low),
            shape((8, 3, rows // 4, 2 * width), low),
        ],
        [
            vmem((3, size, size), low),
            vmem((size, width), low),
            vmem((2 * window, width), low),
            vmem((3 * window, width), low),
            vmem((2 * window, 3 * width), low),
            vmem((3 * window, width), low),
            vmem((2 * window, 2 * heads), full),
            vmem((2 * window, width), low),
            vmem((3, size, width), low),
            vmem((3, size, width), low),
            vmem((heads, TILE, 3 * TILE), full),
            vmem((heads, TILE, 3 * TILE), full),
            vmem((2 * window, size), low),
            vmem((2 * window, width), low),
            vmem((4 * rows, 3 * size), low),
            vmem((2 * window, width), low),
            vmem((3 * window, width), full),
            vmem((3 * window, width), full),
            vmem((window, width), full),
            vmem((window, width), full),
            vmem((2 * window, 3 * width), low),
            vmem((2 * window, 3 * width), low),
            vmem((rows, 3 * size), full),
            vmem((4 * rows, 2 * width), low),
            vmem((rows, size), low),
            vmem((2 * rows, size), low),
            vmem((rows, size), low),
            vmem((rows, size), low),
            vmem((rows, size), low),
            vmem((dp_size - 1, rows, size // dp_size), low),
        ]
        + [vmem((*stack, size, columns), low) for stack, columns in grads]
        + [vmem((4, *stack, rows, columns), low) for stack, columns in grads]
        + [vmem((2, *stack, rows, columns), low) for stack, columns in grads]
        + [vmem((4, rows, units), low)] * 2
        + [vmem((2, rows, units), low)] * 4
        + [
            vmem((dp_size - 1, 16, size), full),
            vmem((levels - 1, 16, size), full),
            vmem((16, size), full),
            vmem((16, size), full),
            vmem((dp_size - 1, 8, size // 4), full),
            vmem((levels - 1, 8, size // 4), full),
            vmem((8, size // 4), full),
            vmem((8, size // 4), full),
        ]
        + rs * 3
        + sems(128)
        + [pltpu.SemaphoreType.DMA((8,)), pltpu.SemaphoreType.DMA((4,)), pltpu.SemaphoreType.DMA((15,))],
        1,
        "cotangent",
        [
            middle_grad, branch_rows, gstate, x, s0, s1, gate_values, norm_gains, facts, facts_in,
            small_sums,
            normed, snormed, queries, keys, values, sqkv, lse, mixed, smixed_rows,
            wst_all, wtok_all, wout_all, gates_all, wup_grad, wdn_grad, block_out, s2,
        ],
        far_in=(0, 1, 3, 6, *range(11, 28)),
        far_out=(0, 1, 2, 3, 7, 8, 9, 10, 11, 12),
    )
    both = lambda pair: pair[0].astype(full) + pair[1].astype(full)
    gates_out = jnp.sum(gates_home.astype(full).reshape(levels, 2, 3, rows // 4, 2 * width), axis=0)
    gates_out = jnp.transpose(gates_out, (2, 1, 0, 3)).reshape(rows // 4, 3, size)
    line_sums = totals[8 : 8 + levels * heads, 1 : window + 1][:, ::-1]
    table_all = jnp.dot(one_hot.T, line_sums.T, precision=HIGHEST)
    table_rows = table_all.shape[0] // dp_size
    table_out = lax.dynamic_slice(table_all, (dp_at * table_rows, level * heads), (table_rows, heads))
    share = size // (dp_size * levels)
    gains_out = lax.dynamic_slice(totals, (0, (dp_at * levels + level) * share), (3, share))
    rms_stats = jnp.sqrt(jnp.sum(totals[3:6], axis=1) / totals[6, 0])
    return (
        block_home.reshape(1, blocks, rows, size),
        state_home.astype(full)[None],
        rms_stats,
        tokens_home.reshape(1, blocks, rows, size),
        carried_grad[None],
        jnp.swapaxes(past_home.reshape(2, window, width).astype(full), 0, 1)[None],
        gains_out,
        stacked(both(wtok_home)),
        both(wout_home),
        table_out,
        both(up_home),
        both(down_home),
        stacked(both(wst_home)),
        gates_out,
        initial_grad,
    )


def solution(mesh):
    in_specs = (
        P("dp", None, "state", None),
        P("dp", "state", None),
        P("dp", None, None, "state"),
        P("dp"),
        P("dp"),
        P(),
        P("dp", None, "state", None),
        P("dp", "state", None),
        P(),
        P("dp", None, "state"),
        P("dp", "state"),
        P(None, "state"),
        P("dp", "state"),
        P("dp", "state"),
        P("dp", None, "state"),
        P("dp", None, None),
        P("state", "dp"),
    )
    out_specs = (
        P("dp", None, "state", None),
        P("dp", "state", None),
        P(),
        P("dp", None, "state", None),
        P("dp", "state", None),
        P("dp", None, None, "state"),
        P(None, ("dp", "state")),
        P("dp", None, "state"),
        P("dp", "state"),
        P("dp", "state"),
        P("dp", "state"),
        P("dp", "state"),
        P("dp", None, "state"),
        P(("dp", "state"), None, None),
        P("state", "dp"),
    )
    body = grouped if dict(mesh.shape) == {"dp": 8, "state": 4} else shards
    return jax.shard_map(body, mesh=mesh, in_specs=in_specs, out_specs=out_specs, check_vma=False)
```

```python
import math

import jax
import jax.numpy as jnp
from jax import lax
from jax.experimental import pallas as pl
from jax.experimental.pallas import tpu as pltpu
from jax.sharding import PartitionSpec as P

DH = 128


EPS = 1e-06
NEGATIVE = -1e30
HIGHEST = lax.Precision.HIGHEST


def rms_norm(tensor, gains_row):
    return tensor * lax.rsqrt(jnp.mean(tensor * tensor, axis=-1, keepdims=True) + EPS) * gains_row


def norm_back(tensor, gains_row, cotangent):
    return jax.vjp(rms_norm, tensor, gains_row)[1](cotangent)


def smooth_gelu(tensor):
    return jax.nn.gelu(tensor, approximate=True)


def renew_state(state_now, gate_values):
    return state_now * jax.nn.sigmoid(gate_values[2] + 1.0) + jnp.tanh(
        gate_values[0]
    ) * jax.nn.sigmoid(gate_values[1] - 1.0)


def split_heads(tensor):
    return tensor.reshape(tensor.shape[0], tensor.shape[1], tensor.shape[2] // DH, DH)


def merge_heads(tensor):
    return tensor.reshape(tensor.shape[0], tensor.shape[1], tensor.shape[2] * DH)


def score_grid(queries, key_rows, bias_add, allowed):
    scores = jnp.einsum(
        "iqhd,ikhd->ihqk", queries, key_rows, preferred_element_type=jnp.float32
    ) / math.sqrt(DH)
    if bias_add is not None:
        scores = scores + bias_add[None]
    return jnp.where(allowed[:, None], scores, NEGATIVE)


def attend_forward(queries, key_rows, values, bias_add, allowed):
    scores = score_grid(queries, key_rows, bias_add, allowed)
    row_max = jnp.max(scores, axis=-1, keepdims=True)
    weights = jnp.exp(scores - row_max)
    row_total = jnp.sum(weights, axis=-1, keepdims=True)
    attn_probs = (weights / row_total).astype(jnp.bfloat16)
    mixed_heads = jnp.einsum(
        "ihqk,ikhd->iqhd", attn_probs, values, preferred_element_type=jnp.float32
    )
    return (merge_heads(mixed_heads.astype(jnp.bfloat16)), row_max + jnp.log(row_total))


def attention_backward_pass(queries, key_rows, values, bias_add, allowed, log_total, grad_mixed):
    scores = score_grid(queries, key_rows, bias_add, allowed)
    attn_probs = jnp.exp(scores - log_total)
    probs_grad = jnp.einsum(
        "iqhd,ikhd->ihqk", grad_mixed, values, preferred_element_type=jnp.float32
    )
    scores_grad = attn_probs * (
        probs_grad - jnp.sum(attn_probs * probs_grad, axis=-1, keepdims=True)
    )
    scores_grad = scores_grad.astype(jnp.bfloat16)
    values_grad = jnp.einsum(
        "ihqk,iqhd->ikhd",
        attn_probs.astype(jnp.bfloat16),
        grad_mixed,
        preferred_element_type=jnp.float32,
    )
    queries_grad = jnp.einsum(
        "ihqk,ikhd->iqhd", scores_grad, key_rows, preferred_element_type=jnp.float32
    ) / math.sqrt(DH)
    keys_grad = jnp.einsum(
        "ihqk,iqhd->ikhd", scores_grad, queries, preferred_element_type=jnp.float32
    ) / math.sqrt(DH)
    return (
        merge_heads(queries_grad),
        merge_heads(keys_grad),
        merge_heads(values_grad),
        scores_grad,
    )


def diagonal_sums(grid_values):
    num_heads, num_rows, num_cols = grid_values.shape
    flat = grid_values.reshape(num_heads, num_rows * num_cols)
    flat = jnp.pad(flat, ((0, 0), (0, num_rows)))
    sums = jnp.sum(flat.reshape(num_heads, num_rows, num_cols + 1), axis=1)
    return sums[:, num_rows:0:-1]


def toeplitz_grid(per_offset, num_rows):
    num_cols = 2 * num_rows
    line = jnp.pad(per_offset[::-1].T, ((0, 0), (1, num_cols - num_rows)))
    flat = jnp.tile(line, (1, num_rows))[:, : num_rows * num_cols]
    return flat.reshape(-1, num_rows, num_cols)


def sum_rows(partial_value):
    return lax.psum_scatter(
        partial_value.astype(jnp.bfloat16), "state", scatter_dimension=1, tiled=True
    ).astype(jnp.float32)


def whole_rows(partial_value):
    return lax.all_gather(partial_value, "state", axis=1, tiled=True)


def shards(
    tokens,
    carried_state,
    past_keys,
    fresh_start,
    valid_count,
    bucket_ids,
    grad_output,
    grad_state,
    norm_gains,
    token_qkv,
    token_out,
    bias_table,
    mlp_up,
    mlp_down,
    state_qkv,
    state_gates,
    initial_state,
):
    item_count, blocks, share_rows, model_width = tokens.shape
    groups = lax.axis_size("state")
    state_rank = lax.axis_index("state")
    window_width = share_rows * groups
    vector_rows = carried_state.shape[1] * groups
    local_width = token_qkv.shape[2]
    qkv_full, out_full, up_full, down_full, sqkv_full, gates_full, initial_full = (
        lax.all_gather(token_qkv, "dp", axis=0, tiled=True),
        lax.all_gather(token_out, "dp", axis=0, tiled=True),
        lax.all_gather(mlp_up, "dp", axis=0, tiled=True),
        lax.all_gather(mlp_down, "dp", axis=0, tiled=True),
        lax.all_gather(state_qkv, "dp", axis=0, tiled=True),
        lax.all_gather(state_gates, "dp", axis=0, tiled=True),
        lax.all_gather(initial_state, "dp", axis=1, tiled=True),
    )
    gates_used = lax.dynamic_slice_in_dim(gates_full, state_rank * local_width, local_width, 2)
    one_hot = (bucket_ids[:, None] == jnp.arange(bias_table.shape[0])[None, :]).astype(jnp.float32)
    per_offset = jnp.dot(one_hot, bias_table, precision=HIGHEST)
    query_pos = jnp.arange(window_width)[:, None]
    key_pos = jnp.arange(2 * window_width)[None, :]
    offset = window_width + query_pos - key_pos
    inside = (offset >= 0) & (offset < window_width)
    bias_grid = toeplitz_grid(per_offset, window_width)
    token_bias = jnp.pad(bias_grid, ((0, 0), (0, 0), (0, vector_rows)))
    is_fresh = fresh_start == 1
    state_now = jnp.where(
        is_fresh[:, None, None], initial_full.astype(jnp.float32)[None], carried_state
    )
    past_key = past_keys[:, :, 0]
    past_value = past_keys[:, :, 1]
    past_ok = jnp.broadcast_to(~is_fresh[:, None], (item_count, window_width))
    gains_token, gains_middle, gains_state = (norm_gains[0], norm_gains[1], norm_gains[2])
    share_pos = state_rank * share_rows + jnp.arange(share_rows)
    square_sums = jnp.zeros((3,), jnp.float32)
    valid_total = jnp.zeros((), jnp.float32)
    kept_values = []
    results = []
    for block_at in range(blocks):
        token_ok = (
            block_at * window_width + jnp.arange(window_width)[None, :] < valid_count[:, None]
        )
        inputs = tokens[:, block_at].astype(jnp.float32)
        normed, state_normed = (
            lax.all_gather(
                rms_norm(inputs, gains_token).astype(jnp.bfloat16), "state", axis=1, tiled=True
            ),
            lax.all_gather(
                rms_norm(state_now, gains_state).astype(jnp.bfloat16), "state", axis=1, tiled=True
            ),
        )
        project = jnp.einsum(
            "iwd,dch->ciwh", normed, qkv_full, preferred_element_type=jnp.float32
        ).astype(jnp.bfloat16)
        state_project = jnp.einsum(
            "ind,dch->cinh", state_normed, sqkv_full, preferred_element_type=jnp.float32
        ).astype(jnp.bfloat16)
        token_keys = jnp.concatenate([past_key, project[1], state_project[1]], axis=1)
        token_values = jnp.concatenate([past_value, project[2], state_project[2]], axis=1)
        window_ok = inside[None] & jnp.concatenate([past_ok, token_ok], axis=1)[:, None, :]
        token_allowed = jnp.concatenate(
            [window_ok, jnp.ones((item_count, window_width, vector_rows), jnp.bool_)], axis=2
        )
        mixed_heads, token_total = attend_forward(
            split_heads(project[0]),
            split_heads(token_keys),
            split_heads(token_values),
            token_bias,
            token_allowed,
        )
        branch = sum_rows(
            jnp.einsum("iwh,dh->iwd", mixed_heads, out_full, preferred_element_type=jnp.float32)
        )
        middle = inputs + branch
        middle_normed = lax.all_gather(
            rms_norm(middle, gains_middle).astype(jnp.bfloat16), "state", axis=1, tiled=True
        )
        up_values = jnp.einsum(
            "iwd,df->iwf", middle_normed, up_full, preferred_element_type=jnp.float32
        )
        hidden = smooth_gelu(up_values).astype(jnp.bfloat16)
        feed_out = sum_rows(
            jnp.einsum("iwf,df->iwd", hidden, down_full, preferred_element_type=jnp.float32)
        )
        result = middle + feed_out
        results.append(result.astype(jnp.bfloat16))
        share_ok = (block_at * window_width + share_pos[None, :] < valid_count[:, None]).astype(
            jnp.float32
        )[:, :, None]
        square_sums = square_sums + jnp.stack(
            [
                jnp.sum(share_ok * result * result),
                jnp.sum(share_ok * branch * branch),
                jnp.sum(share_ok * feed_out * feed_out),
            ]
        )
        valid_total = valid_total + jnp.sum(share_ok)
        state_keys = jnp.concatenate([state_project[1], project[1]], axis=1)
        state_values = jnp.concatenate([state_project[2], project[2]], axis=1)
        state_allowed = jnp.concatenate(
            [
                jnp.ones((item_count, vector_rows, vector_rows), jnp.bool_),
                jnp.broadcast_to(token_ok[:, None, :], (item_count, vector_rows, window_width)),
            ],
            axis=2,
        )
        state_mixed, state_total = attend_forward(
            split_heads(state_project[0]),
            split_heads(state_keys),
            split_heads(state_values),
            None,
            state_allowed,
        )
        gate_source = state_mixed
        gate_values = lax.psum_scatter(
            jnp.einsum(
                "inh,dch->cind", state_mixed, gates_used, preferred_element_type=jnp.float32
            ).astype(jnp.bfloat16),
            "state",
            scatter_dimension=2,
            tiled=True,
        ).astype(jnp.float32)
        kept_values.append(
            (
                inputs,
                normed,
                state_normed,
                project,
                state_project,
                token_keys,
                token_values,
                token_allowed,
                mixed_heads,
                token_total,
                middle,
                middle_normed,
                up_values,
                hidden,
                state_keys,
                state_values,
                state_allowed,
                state_total,
                gate_source,
                gate_values,
                state_now,
            )
        )
        state_now = renew_state(state_now, gate_values)
        past_key, past_value, past_ok = (project[1], project[2], token_ok)
    square_sums, valid_total = lax.psum((square_sums, valid_total), ("dp", "state"))
    rms_stats = jnp.sqrt(square_sums / valid_total)
    qkv_grad = jnp.zeros(qkv_full.shape, jnp.float32)
    out_grad = jnp.zeros(out_full.shape, jnp.float32)
    up_grad = jnp.zeros(up_full.shape, jnp.float32)
    down_grad = jnp.zeros(down_full.shape, jnp.float32)
    sqkv_grad = jnp.zeros(sqkv_full.shape, jnp.float32)
    gate_grad = jnp.zeros(gates_used.shape, jnp.float32)
    bias_grad = jnp.zeros(bias_grid.shape, jnp.float32)
    gain_token_grad = jnp.zeros((model_width,), jnp.float32)
    gain_middle_grad = jnp.zeros((model_width,), jnp.float32)
    gain_state_grad = jnp.zeros((model_width,), jnp.float32)
    state_grad = grad_state
    carried_key_rows = jnp.zeros(past_keys[:, :, 0].shape, jnp.float32)
    carry_value = jnp.zeros(past_keys[:, :, 0].shape, jnp.float32)
    token_grads = [None] * blocks
    for block_at in reversed(range(blocks)):
        (
            inputs,
            normed,
            state_normed,
            project,
            state_project,
            token_keys,
            token_values,
            token_allowed,
            mixed_heads,
            token_total,
            middle,
            middle_normed,
            up_values,
            hidden,
            state_keys,
            state_values,
            state_allowed,
            state_total,
            gate_source,
            gate_values,
            state_before,
        ) = kept_values[block_at]
        direct_grad, gates_grad = jax.vjp(renew_state, state_before, gate_values)[1](state_grad)
        gates_low = gates_grad.astype(jnp.bfloat16)
        gates_rows = lax.all_gather(gates_low, "state", axis=2, tiled=True)
        state_mixed_grad = jnp.einsum(
            "cind,dch->inh", gates_rows, gates_used, preferred_element_type=jnp.float32
        ).astype(jnp.bfloat16)
        gate_grad = gate_grad + jnp.einsum(
            "inh,cind->dch", gate_source, gates_rows, preferred_element_type=jnp.float32
        )
        state_query_gradient, state_keys_gradient, state_values_gradient, discarded_output = (
            attention_backward_pass(
                split_heads(state_project[0]),
                split_heads(state_keys),
                split_heads(state_values),
                None,
                state_allowed,
                state_total,
                split_heads(state_mixed_grad),
            )
        )
        out_share = grad_output[:, block_at]
        out_whole = whole_rows(out_share)
        down_grad = down_grad + jnp.einsum(
            "iwf,iwd->df", hidden, out_whole, preferred_element_type=jnp.float32
        )
        hidden_grad = jnp.einsum(
            "iwd,df->iwf", out_whole, down_full, preferred_element_type=jnp.float32
        )
        up_values_grad = jax.vjp(smooth_gelu, up_values)[1](hidden_grad)[0].astype(jnp.bfloat16)
        up_grad = up_grad + jnp.einsum(
            "iwd,iwf->df", middle_normed, up_values_grad, preferred_element_type=jnp.float32
        )
        middle_normed_grad = lax.psum_scatter(
            jnp.einsum(
                "iwf,df->iwd", up_values_grad, up_full, preferred_element_type=jnp.float32
            ).astype(jnp.bfloat16),
            "state",
            scatter_dimension=1,
            tiled=True,
        ).astype(jnp.float32)
        middle_grad, gain_part = norm_back(middle, gains_middle, middle_normed_grad)
        middle_grad = out_share.astype(jnp.float32) + middle_grad
        gain_middle_grad = gain_middle_grad + gain_part
        branch_whole = whole_rows(middle_grad.astype(jnp.bfloat16))
        out_grad = out_grad + jnp.einsum(
            "iwh,iwd->dh", mixed_heads, branch_whole, preferred_element_type=jnp.float32
        )
        mixed_grad = jnp.einsum(
            "iwd,dh->iwh", branch_whole, out_full, preferred_element_type=jnp.float32
        ).astype(jnp.bfloat16)
        query_grad, token_keys_gradient, tvalues_grad, scores_grad = attention_backward_pass(
            split_heads(project[0]),
            split_heads(token_keys),
            split_heads(token_values),
            token_bias,
            token_allowed,
            token_total,
            split_heads(mixed_grad),
        )
        bias_grad = bias_grad + jnp.sum(
            scores_grad[:, :, :, : 2 * window_width].astype(jnp.float32), axis=0
        )
        key_gradient_rows = (
            token_keys_gradient[:, window_width : 2 * window_width]
            + state_keys_gradient[:, vector_rows:]
            + carried_key_rows
        )
        value_grad = (
            tvalues_grad[:, window_width : 2 * window_width]
            + state_values_gradient[:, vector_rows:]
            + carry_value
        )
        state_key_gradient = (
            token_keys_gradient[:, 2 * window_width :] + state_keys_gradient[:, :vector_rows]
        )
        state_value_gradient = (
            tvalues_grad[:, 2 * window_width :] + state_values_gradient[:, :vector_rows]
        )
        project_grad = jnp.stack([query_grad, key_gradient_rows, value_grad]).astype(jnp.bfloat16)
        state_projection_gradient = jnp.stack(
            [state_query_gradient, state_key_gradient, state_value_gradient]
        ).astype(jnp.bfloat16)
        qkv_grad = qkv_grad + jnp.einsum(
            "iwd,ciwh->dch", normed, project_grad, preferred_element_type=jnp.float32
        )
        sqkv_grad = sqkv_grad + jnp.einsum(
            "ind,cinh->dch",
            state_normed,
            state_projection_gradient,
            preferred_element_type=jnp.float32,
        )
        normed_grad, state_normed_grad = (
            lax.psum_scatter(
                jnp.einsum(
                    "ciwh,dch->iwd", project_grad, qkv_full, preferred_element_type=jnp.float32
                ).astype(jnp.bfloat16),
                "state",
                scatter_dimension=1,
                tiled=True,
            ).astype(jnp.float32),
            lax.psum_scatter(
                jnp.einsum(
                    "cinh,dch->ind",
                    state_projection_gradient,
                    sqkv_full,
                    preferred_element_type=jnp.float32,
                ).astype(jnp.bfloat16),
                "state",
                scatter_dimension=1,
                tiled=True,
            ).astype(jnp.float32),
        )
        input_grad, gain_part = norm_back(inputs, gains_token, normed_grad)
        gain_token_grad = gain_token_grad + gain_part
        token_grads[block_at] = (middle_grad + input_grad).astype(jnp.bfloat16)
        state_norm_grad, gain_part = norm_back(state_before, gains_state, state_normed_grad)
        gain_state_grad = gain_state_grad + gain_part
        state_grad = direct_grad + state_norm_grad
        carried_key_rows = token_keys_gradient[:, :window_width]
        carry_value = tvalues_grad[:, :window_width]
    carried_grad = jnp.where(is_fresh[:, None, None], 0.0, state_grad)
    initial_part = jnp.sum(jnp.where(is_fresh[:, None, None], state_grad, 0.0), axis=0)
    past_grad = jnp.stack([carried_key_rows, carry_value], axis=2)
    table_part = jnp.dot(one_hot.T, diagonal_sums(bias_grad).T, precision=HIGHEST)
    gain_columns = jnp.stack([gain_token_grad, gain_middle_grad, gain_state_grad], axis=1)
    summed = (
        lax.psum_scatter(
            qkv_grad.astype(jnp.bfloat16), "dp", scatter_dimension=0, tiled=True
        ).astype(jnp.float32),
        lax.psum_scatter(
            out_grad.astype(jnp.bfloat16), "dp", scatter_dimension=0, tiled=True
        ).astype(jnp.float32),
        lax.psum_scatter(
            table_part.astype(jnp.bfloat16), "dp", scatter_dimension=0, tiled=True
        ).astype(jnp.float32),
        lax.psum_scatter(
            up_grad.astype(jnp.bfloat16), "dp", scatter_dimension=0, tiled=True
        ).astype(jnp.float32),
        lax.psum_scatter(
            down_grad.astype(jnp.bfloat16), "dp", scatter_dimension=0, tiled=True
        ).astype(jnp.float32),
        lax.psum_scatter(
            sqkv_grad.astype(jnp.bfloat16), "dp", scatter_dimension=0, tiled=True
        ).astype(jnp.float32),
        lax.psum_scatter(
            initial_part.astype(jnp.bfloat16), "dp", scatter_dimension=1, tiled=True
        ).astype(jnp.float32),
        lax.psum_scatter(
            gate_grad.astype(jnp.bfloat16), "dp", scatter_dimension=0, tiled=True
        ).astype(jnp.float32),
        lax.psum_scatter(
            gain_columns.astype(jnp.bfloat16), "dp", scatter_dimension=0, tiled=True
        ).astype(jnp.float32),
    )
    gate_pieces, gain_pieces = (
        lax.all_to_all(
            summed[7][:, :, None, :].astype(jnp.bfloat16),
            "state",
            split_axis=0,
            concat_axis=2,
            tiled=True,
        ).astype(jnp.float32),
        lax.all_to_all(
            summed[8][:, :, None, None].astype(jnp.bfloat16),
            "state",
            split_axis=0,
            concat_axis=2,
            tiled=True,
        ).astype(jnp.float32),
    )
    gains_grad = jnp.sum(gain_pieces, axis=(2, 3)).T
    gates_grad_out = gate_pieces.reshape(
        gate_pieces.shape[0], gate_pieces.shape[1], gate_pieces.shape[2] * gate_pieces.shape[3]
    )
    return (
        jnp.stack(results, axis=1),
        state_now,
        rms_stats,
        jnp.stack(token_grads, axis=1),
        carried_grad,
        past_grad,
        gains_grad,
        summed[0],
        summed[1],
        summed[2],
        summed[3],
        summed[4],
        summed[5],
        gates_grad_out,
        summed[6],
    )


MESH = pl.DeviceIdType.MESH
NN = (((1,), (0,)), ((), ()))
NT = (((1,), (1,)), ((), ()))
TN = (((0,), (0,)), ((), ()))
VMEM_BYTES = 127 * 2**19


class Place:
    def __init__(self):
        chip_core, level = lax.axis_index("dp"), lax.axis_index("state")
        core, low = lax.rem(chip_core, 2), lax.rem(level, 2)
        x, y = lax.rem(chip_core // 2, 2), chip_core // 4
        flip = lambda bit: 1 - 2 * bit
        self.dp, self.core, self.level, self.half = chip_core, core, level, level // 2
        self.rank = 2 * low + core
        self.ranks = [self.rank, 2 * low + 1 - core, 2 * (1 - low) + core, 2 * (1 - low) + 1 - core]
        self.mates = [
            None,
            (chip_core + flip(core), level),
            (chip_core, level + flip(low)),
            (chip_core + flip(core), level + flip(low)),
        ]
        self.planes = [2 * y + x, 2 * y + 1 - x, 2 * (1 - y) + x, 2 * (1 - y) + 1 - x]
        self.plane_mates = [
            None,
            (chip_core + 2 * flip(x), level),
            (chip_core + 4 * flip(y), level),
            (chip_core + 2 * flip(x) + 4 * flip(y), level),
        ]
        first = chip_core - core
        self.there = (first + low, 2 * core + self.half)
        self.across = (first + low, 2 * (1 - core) + self.half)
        self.from_there = (first + self.half, 2 * low + core)
        self.from_across = (first + 1 - self.half, 2 * low + core)
        self.stays = (core == low) & (self.half == core)


def rows_at(start, size, step=128):
    return pl.ds(pl.multiple_of(start, step), size)


def rows_of(ref, start, size, step=128):
    at = rows_at(start, size, step)
    return ref.at[:, at] if len(ref.shape) == 3 else ref.at[at]


class Links:
    def __init__(self, send_sems, recv_sems):
        self.send_sems, self.recv_sems = send_sems, recv_sems
        self.used = 0
        self.open_sends = []
        self.open_turns = []

    def plan(self, source, target, device):
        at = self.used
        self.used += 1
        return pltpu.make_async_remote_copy(
            src_ref=source,
            dst_ref=target,
            send_sem=self.send_sems.at[at],
            recv_sem=self.recv_sems.at[at],
            device_id=device,
            device_id_type=MESH,
        )

    def copy(self, source, target, device):
        moved = self.plan(source, target, device)
        moved.start()
        self.open_sends.append(moved)
        return moved

    def sent(self, moved):
        self.open_sends = [other for other in self.open_sends if other is not moved]
        moved.wait_send()

    def close(self):
        for moved in self.open_sends:
            moved.wait_send()
        for turn in self.open_turns:
            turn.sent()
        self.open_sends, self.open_turns = [], []


def greet(devices, turned=None):
    barrier = pltpu.get_barrier_semaphore()
    for device in devices:
        pl.semaphore_signal(barrier, inc=1, device_id=device, device_id_type=MESH)
    if turned is None:
        pl.semaphore_wait(barrier, len(devices))
    else:
        moves = jnp.logical_not(turned.stays)

        @pl.when(moves)
        def _():
            pl.semaphore_signal(barrier, inc=1, device_id=turned.from_there, device_id_type=MESH)

        pl.semaphore_wait(barrier, len(devices) + moves.astype(jnp.int32))


class Turn:
    def __init__(self, links, here, source, target, device):
        self.stays = here.stays
        self.moved = links.plan(source, target, device)
        self.kept = pltpu.make_async_copy(source, target, links.recv_sems.at[links.used - 1])
        links.open_turns.append(self)

        @pl.when(jnp.logical_not(self.stays))
        def _():
            self.moved.start()

        @pl.when(self.stays)
        def _():
            self.kept.start()

    def arrived(self):
        @pl.when(jnp.logical_not(self.stays))
        def _():
            self.moved.wait_recv()

        @pl.when(self.stays)
        def _():
            self.kept.wait()

    def sent(self):
        @pl.when(jnp.logical_not(self.stays))
        def _():
            self.moved.wait_send()


class WeightGather:
    def __init__(self, links, here, local, full):
        self.links, self.here, self.local, self.full = links, here, local, full
        self.rows = local.shape[-2]

    def enter(self):
        target = rows_of(self.full, self.here.dp * self.rows, self.rows)
        self.turn = Turn(self.links, self.here, self.local, target, self.here.there)
        self.cross = self.links.copy(self.local, target, self.here.across)
        return self

    def block(self, k):
        return rows_of(self.full, self.here.planes[k] * 2 * self.rows, 2 * self.rows)

    def half(self, k, which):
        start = self.here.planes[k] * 2 * self.rows + which * self.rows
        return rows_of(self.full, start, self.rows)

    def spread(self):
        self.turn.arrived()
        self.cross.wait_recv()
        mates = self.here.plane_mates
        self.over_x = self.links.copy(self.block(0), self.block(0), mates[1])
        self.over_y = self.links.copy(self.block(0), self.block(0), mates[2])

    def forward(self):
        mates = self.here.plane_mates
        self.over_x.wait_recv()
        self.corner_0 = self.links.copy(self.half(1, 0), self.half(1, 0), mates[2])
        self.over_y.wait_recv()
        self.corner_1 = self.links.copy(self.half(2, 1), self.half(2, 1), mates[1])

    def finish(self):
        self.corner_0.wait_recv()
        self.corner_1.wait_recv()


class GateGather:
    def __init__(self, links, here, local, full, sem):
        self.links, self.here, self.local, self.full, self.sem = links, here, local, full, sem
        self.rows = local.shape[-2]

    def block(self, k):
        start = (2 * self.here.planes[k] + self.here.core) * self.rows
        return rows_of(self.full, start, self.rows)

    def part(self, k, which):
        size = self.rows // 2
        start = (2 * self.here.planes[k] + self.here.core) * self.rows + which * size
        return rows_of(self.full, start, size, 64)

    def spread(self):
        mates, sibling = self.here.plane_mates, self.here.mates[1]
        self.over_x = self.links.copy(self.local, self.block(0), mates[1])
        self.over_y = self.links.copy(self.local, self.block(0), mates[2])
        self.near = [self.links.copy(self.local, self.block(0), sibling)]
        self.kept = pltpu.make_async_copy(self.local, self.block(0), self.sem)
        self.kept.start()

    def forward(self):
        mates, sibling = self.here.plane_mates, self.here.mates[1]
        self.over_x.wait_recv()
        self.corner_0 = self.links.copy(self.part(1, 0), self.part(1, 0), mates[2])
        self.near.append(self.links.copy(self.block(1), self.block(1), sibling))
        self.over_y.wait_recv()
        self.corner_1 = self.links.copy(self.part(2, 1), self.part(2, 1), mates[1])
        self.near.append(self.links.copy(self.block(2), self.block(2), sibling))

    def last(self):
        self.corner_0.wait_recv()
        self.corner_1.wait_recv()
        self.near.append(self.links.copy(self.block(3), self.block(3), self.here.mates[1]))

    def finish(self):
        self.kept.wait()
        for moved in self.near:
            moved.wait_recv()


class RowGather:
    def __init__(self, links, here, ref, base, rows):
        self.links, self.here, self.ref, self.base, self.rows = links, here, ref, base, rows

    def part(self, k):
        return self.ref.at[rows_at(self.base + self.here.ranks[k] * self.rows, self.rows)]

    def start(self):
        own, mates = self.part(0), self.here.mates
        self.far = self.links.copy(own, own, mates[2])
        self.near = self.links.copy(own, own, mates[1])
        return self

    def ready(self, k):
        if k == 1:
            self.near.wait_recv()
        elif k == 2:
            self.far.wait_recv()
            block = self.part(2)
            self.last = self.links.copy(block, block, self.here.mates[1])
        elif k == 3:
            self.last.wait_recv()

    def sent(self):
        for moved in (self.far, self.near, self.last):
            self.links.sent(moved)


class RowSum:
    def __init__(self, links, here, stage, near_in, far_out, far_in, rows):
        self.links, self.here, self.rows = links, here, rows
        self.stage, self.near_in, self.far_out, self.far_in = stage, near_in, far_out, far_in

    def part(self, k):
        return self.stage.at[rows_at(self.here.ranks[k] * self.rows, self.rows)]

    def fill(self, make_rows):
        sibling = self.here.mates[1]
        for k, slot in ((3, 0), (1, 1)):
            self.part(k)[...] = make_rows(self.here.ranks[k]).astype(jnp.bfloat16)
            moved = self.links.copy(self.part(k), self.near_in.at[slot], sibling)
            if slot == 0:
                self.near_far = moved
            else:
                self.near_own = moved
        for k in (2, 0):
            self.part(k)[...] = make_rows(self.here.ranks[k]).astype(jnp.bfloat16)
        return self

    def forward(self):
        self.near_far.wait_recv()
        summed = self.part(2)[...].astype(jnp.float32) + self.near_in[0].astype(jnp.float32)
        self.far_out[...] = summed.astype(jnp.bfloat16)
        self.far = self.links.copy(self.far_out, self.far_in, self.here.mates[2])
        return self

    def sent(self):
        for moved in (self.near_far, self.near_own, self.far):
            self.links.sent(moved)

    def finish(self):
        self.near_own.wait_recv()
        self.far.wait_recv()
        return (
            self.part(0)[...].astype(jnp.float32)
            + self.near_in[1].astype(jnp.float32)
            + self.far_in[...].astype(jnp.float32)
        )


def row_sum_scratch(rows, width):
    return [
        pltpu.VMEM((4 * rows, width), jnp.bfloat16),
        pltpu.VMEM((2, rows, width), jnp.bfloat16),
        pltpu.VMEM((rows, width), jnp.bfloat16),
        pltpu.VMEM((rows, width), jnp.bfloat16),
    ]


def dot(left, right, dims):
    return lax.dot_general(left, right, dims, preferred_element_type=jnp.float32)


def scale_of(tensor):
    return lax.rsqrt(jnp.mean(tensor * tensor, axis=-1, keepdims=True) + EPS)


def rms_back(tensor, gains_row, cotangent):
    scale = scale_of(tensor)
    weighted = cotangent * gains_row
    inner = jnp.mean(tensor * weighted, axis=-1, keepdims=True)
    straight = scale * weighted - tensor * (scale * scale * scale * inner)
    return straight, jnp.sum(cotangent * tensor * scale, axis=0, keepdims=True)


def row_mask(facts, start, rows):
    place_of = lax.broadcasted_iota(jnp.int32, (rows, 1), 0) + start
    return jnp.where(place_of.astype(jnp.float32) < facts[2:3, 0:1], 1.0, 0.0)


def bias_tiles(lines_ref, tiles_ref, heads, width, scale=1.0):
    for head in range(heads):
        line = lines_ref[head : head + 1, :] * scale
        spread = jnp.broadcast_to(line, (tiles_ref.shape[1], line.shape[1]))
        tiles_ref[head] = pltpu.roll(spread, 0, 1, stride=1, stride_axis=0)[:, :width]


def softmax_pair(first, second):
    top = jnp.maximum(
        jnp.max(first, axis=-1, keepdims=True), jnp.max(second, axis=-1, keepdims=True)
    )
    first, second = jnp.exp(first - top), jnp.exp(second - top)
    total = jnp.sum(first, axis=-1, keepdims=True) + jnp.sum(second, axis=-1, keepdims=True)
    share = 1.0 / total
    return (
        (first * share).astype(jnp.bfloat16),
        (second * share).astype(jnp.bfloat16),
        top + jnp.log(total),
    )


TILE = 256
LOG2E = math.log2(math.e)
ROOT = 1.0 / math.sqrt(DH)


def forward_kernel(
    x_in, carried_in, initial_in, far_past, facts_in, far_gout, gstate_in, gains_ref,
    wst_in, wtok_in, wout_in, gates_in, far_wup, far_wdn,
    far_normed, far_snormed, far_queries, far_keys, far_values, far_state_qkv, far_lse, far_mixed,
    far_wst, far_wtok, far_wout, far_gates, far_x, far_s0, far_s1,
    far_gate_values, far_gstate_here, far_wup_grad, far_wdn_grad,
    smixed_rows, s2_ref, facts, block_out, middle_grad, branch_rows, small_sums,
    normed, snormed, queries, keys, values, state_qkv, lse_ref, mixed,
    wst, wtok, wout, gates, x_ref, s0_ref, s1_ref,
    smixed, tiles, initial_all, normed_send, gstate_send, s0_send, gate_values, wup, wdn, middle,
    middle_normed, gout_rows, gout, slope, hidden, up_grad, grad_stage, *rest,
):
    rs = [rest[4 * k : 4 * k + 4] for k in range(4)]
    links = Links(rest[16], rest[17])
    local_sems, keep_sems = rest[18], rest[19]
    kept = []

    def keep(source, target):
        moved = pltpu.make_async_copy(source, target, keep_sems.at[len(kept)])
        moved.start()
        kept.append(moved)

    here = Place()
    rank, ranks, mates = here.rank, here.ranks, here.mates
    rows = s0_ref.shape[0]
    window = 4 * rows
    width = queries.shape[1]
    heads = width // DH
    ring = [(lax.rem(here.dp + step, 8), here.level) for step in range(1, 8)]
    greet(ring + mates[2:] + [here.from_across], here)

    def turn(source, target):
        return Turn(links, here, source, target, here.there)

    part = initial_in.shape[1]
    own_columns = pl.ds(pl.multiple_of(here.dp * part, part), part)
    initial_moves = [links.copy(initial_in, initial_all.at[:, own_columns], mate) for mate in ring]
    facts_turn = turn(facts_in, facts)
    gather_wst = WeightGather(links, here, wst_in, wst).enter()
    initial_all[:, own_columns] = initial_in[...]
    for moved in initial_moves:
        moved.wait_recv()
    is_fresh = facts_in[3:4, :] > 0.5
    start = jnp.where(is_fresh, initial_all[...].astype(jnp.float32), carried_in[...])
    s0_send[...] = start
    normed_send[...] = (start * scale_of(start) * gains_ref[2:3, :]).astype(jnp.bfloat16)
    normed_turn = turn(normed_send, snormed.at[rows_at(here.level * rows, rows)])
    facts_turn.arrived()
    bias_tiles(facts, tiles, heads, 3 * TILE)
    gather_wst.spread()
    gather_wtok = WeightGather(links, here, wtok_in, wtok).enter()
    normed_turn.arrived()
    gather_s0 = RowGather(links, here, snormed, 0, rows).start()

    def enter_x(block):
        at = pl.ds(block * rows, rows)
        return turn(x_in.at[at], x_ref.at[at])

    def norm_x(block, moved):
        moved.arrived()
        x = x_ref[block * rows : (block + 1) * rows, :].astype(jnp.float32)
        normed[rows_at(block * window + rank * rows, rows), :] = (
            x * scale_of(x) * gains_ref[0:1, :]
        ).astype(jnp.bfloat16)
        return RowGather(links, here, normed, block * window, rows).start()

    x_turn_0 = enter_x(0)
    gather_wst.forward()
    gather_wtok.spread()
    x_turn_1 = enter_x(1)

    def key_mask(start, size):
        place_of = lax.broadcasted_iota(jnp.int32, (1, size), 1).astype(jnp.float32)
        place_of = place_of + float(start - window)
        own = jnp.where(place_of < facts[2:3, 0:size], 0.0, NEGATIVE)
        return jnp.where(place_of < 0.0, facts[3:4, 0:size] * NEGATIVE, own)

    def project_state(block, gather):
        for k in range(4):
            gather.ready(k)
            at = rows_at(block * window + ranks[k] * rows, rows)
            for c in range(3):
                state_qkv[at, c * width : (c + 1) * width] = dot(snormed[at, :], wst[c], NN).astype(
                    jnp.bfloat16
                )

    def project_token(block, gather):
        for k in range(4):
            gather.ready(k)
            at = rows_at(block * window + ranks[k] * rows, rows)
            later = rows_at((block + 1) * window + ranks[k] * rows, rows)
            queries[at, :] = dot(normed[at, :], wtok[0], NN).astype(jnp.bfloat16)
            keys[later, :] = dot(normed[at, :], wtok[1], NN).astype(jnp.bfloat16)
            values[later, :] = dot(normed[at, :], wtok[2], NN).astype(jnp.bfloat16)

    def state_attention(block):
        base = block * window
        own = pl.ds((block + 1) * window, window)
        whole = pl.ds(base, window)
        own_mask = key_mask(base + window, window)
        for head in range(heads):
            at = head * DH
            for tile in range(window // TILE):
                here_rows = pl.ds(base + tile * TILE, TILE)
                query = state_qkv[here_rows, at : at + DH]
                first = dot(query, state_qkv[whole, width + at : width + at + DH], NT) * ROOT
                second = dot(query, keys[own, at : at + DH], NT) * ROOT + own_mask
                first, second, lse = softmax_pair(first, second)
                out = dot(first, state_qkv[whole, 2 * width + at : 2 * width + at + DH], NN)
                out = out + dot(second, values[own, at : at + DH], NN)
                smixed[here_rows, at : at + DH] = out.astype(jnp.bfloat16)
                lse_ref[here_rows, heads + head : heads + head + 1] = lse

    def token_attention(block):
        base = block * window
        whole = pl.ds(base, window)
        for tile in range(window // TILE):
            near_mask = key_mask(base + tile * TILE, 3 * TILE)
            for head in range(heads):
                at = head * DH
                here_rows = pl.ds(base + tile * TILE, TILE)
                near = pl.ds(base + tile * TILE, 3 * TILE)
                query = queries[here_rows, at : at + DH]
                first = dot(query, keys[near, at : at + DH], NT) * ROOT + tiles[head] + near_mask
                second = dot(query, state_qkv[whole, width + at : width + at + DH], NT) * ROOT
                first, second, lse = softmax_pair(first, second)
                out = dot(first, values[near, at : at + DH], NN)
                out = out + dot(second, state_qkv[whole, 2 * width + at : 2 * width + at + DH], NN)
                mixed[here_rows, at : at + DH] = out.astype(jnp.bfloat16)
                lse_ref[here_rows, head : head + 1] = lse

    def spread_state(block, buffer):
        moves = []
        columns = pl.ds(pl.multiple_of(rank * width, width), width)
        for k in (2, 3, 1):
            source = smixed.at[rows_at(block * window + ranks[k] * rows, rows)]
            moves.append(links.copy(source, buffer.at[:, columns], mates[k]))
        buffer[:, columns] = smixed[rows_at(block * window + rank * rows, rows), :]
        return moves

    def renew(block, buffer, state_now):
        size = state_now.shape[1]
        source = buffer[...]
        parts = []
        for c in range(3):
            part = dot(source, gates[c], NT)
            gate_values[:, c * size : (c + 1) * size] = part
            parts.append(part)
        stored = pltpu.make_async_copy(
            gate_values, far_gate_values.at[pl.ds(block * rows, rows)], local_sems.at[0]
        )
        stored.start()
        new_state = state_now * jax.nn.sigmoid(parts[2] + 1.0) + jnp.tanh(parts[0]) * jax.nn.sigmoid(
            parts[1] - 1.0
        )
        return new_state, stored

    def out_rows(block):
        def make(which):
            return dot(mixed[rows_at(block * window + which * rows, rows), :], wout[...], NT)

        return make

    sums = [RowSum(links, here, *rs[block], rows) for block in range(2)]

    def finish_branch(block):
        branch = sums[block].finish()
        at = slice(block * rows, (block + 1) * rows)
        total = x_ref[at, :].astype(jnp.float32) + branch
        middle[at, :] = total
        middle_normed[rows_at(block * window + rank * rows, rows), :] = (
            total * scale_of(total) * gains_ref[1:2, :]
        ).astype(jnp.bfloat16)
        gather = RowGather(links, here, middle_normed, block * window, rows).start()
        share = row_mask(facts, block * window + rank * rows, rows)
        return jnp.sum(branch * branch * share, axis=0, keepdims=True), gather

    def rise(block, gather):
        root = math.sqrt(2.0 / math.pi)
        for k in range(4):
            gather.ready(k)
            at = rows_at(block * window + ranks[k] * rows, rows)
            value = dot(middle_normed[at, :], wup[...], NN)
            square = value * value
            bend = jnp.tanh(root * value * (1.0 + 0.044715 * square))
            half = 0.5 * (1.0 + bend)
            hidden[at, :] = (value * half).astype(jnp.bfloat16)
            slope[at, :] = half + 0.5 * value * (1.0 - bend * bend) * (
                root * (1.0 + 3.0 * 0.044715 * square)
            )

    def feed_sum(block):
        return RowSum(links, here, *rs[block], rows).fill(
            lambda which: dot(hidden[rows_at(block * window + which * rows, rows), :], wdn[...], NT)
        )

    def start_gout(block):
        at = slice(block * rows, (block + 1) * rows)
        gout[rows_at(block * window + rank * rows, rows), :] = gout_rows[at, :]
        return RowGather(links, here, gout, block * window, rows).start()

    def feed_back(block, gather):
        for k in range(4):
            gather.ready(k)
            at = rows_at(block * window + ranks[k] * rows, rows)
            up_grad[at, :] = (dot(gout[at, :], wdn[...], NN) * slope[at, :]).astype(jnp.bfloat16)
        return RowSum(links, here, *rs[2 + block], rows).fill(
            lambda which: dot(up_grad[rows_at(block * window + which * rows, rows), :], wup[...], NT)
        )

    def weight_grad(stage, left, right, target, sem):
        step = 256
        for part in range(stage.shape[0] // step):
            at = slice(part * step, (part + 1) * step)
            stage[at, :] = dot(left[:, at], right[...], TN).astype(jnp.bfloat16)
        stored = pltpu.make_async_copy(stage, target, sem)
        stored.start()
        return stored

    gather_wst.finish()
    keep(wst, far_wst)
    project_state(0, gather_s0)
    gather_x0 = norm_x(0, x_turn_0)
    gather_wtok.forward()
    gather_gates = GateGather(links, here, gates_in, gates, local_sems.at[3])
    gather_gates.spread()
    gather_wout = WeightGather(links, here, wout_in, wout).enter()
    past_turns = [
        turn(far_past.at[0], keys.at[pl.ds(0, window)]),
        turn(far_past.at[1], values.at[pl.ds(0, window)]),
    ]
    gather_x1 = norm_x(1, x_turn_1)
    gather_wtok.finish()
    keep(wtok, far_wtok)
    keep(x_ref, far_x)
    project_token(0, gather_x0)
    state_attention(0)
    a2a_0 = smixed_rows.at[pl.ds(0, rows)]
    a2a_1 = smixed_rows.at[pl.ds(rows, rows)]
    moves_0 = spread_state(0, a2a_0)
    s0_turn = turn(s0_send, s0_ref)
    gather_wout.spread()
    gather_wup = WeightGather(links, here, far_wup, wup).enter()
    project_token(1, gather_x1)
    keep(normed, far_normed)
    keep(queries, far_queries)
    gather_gates.forward()
    for moved in past_turns:
        moved.arrived()
    keep(keys, far_keys)
    keep(values, far_values)
    token_attention(0)
    gather_wout.forward()
    gather_gates.last()
    gather_wdn = WeightGather(links, here, far_wdn, wdn).enter()
    gather_wup.spread()
    gather_wout.finish()
    keep(wout, far_wout)
    sums[0].fill(out_rows(0))
    for moved in moves_0:
        moved.wait_recv()
    gather_gates.finish()
    keep(gates, far_gates)
    s0_turn.arrived()
    keep(s0_ref, far_s0)
    s1, keep_gates = renew(0, a2a_0, s0_ref[...])
    s1_ref[...] = s1
    keep(s1_ref, far_s1)
    snormed[rows_at(window + rank * rows, rows), :] = (s1 * scale_of(s1) * gains_ref[2:3, :]).astype(
        jnp.bfloat16
    )
    gather_s1 = RowGather(links, here, snormed, window, rows).start()
    sums[0].forward()
    gather_wup.forward()
    gather_wdn.spread()
    project_state(1, gather_s1)
    gout_turn = turn(far_gout, gout_rows)
    keep(snormed, far_snormed)
    keep(state_qkv, far_state_qkv)
    branch_total, gather_m0 = finish_branch(0)
    token_attention(1)
    keep(mixed, far_mixed)
    sums[1].fill(out_rows(1))
    gather_wdn.forward()
    state_attention(1)
    keep(lse_ref, far_lse)
    sums[1].forward()
    moves_1 = spread_state(1, a2a_1)
    gather_wup.finish()
    rise(0, gather_m0)
    more, gather_m1 = finish_branch(1)
    branch_total = branch_total + more
    gout_turn.arrived()
    gather_g0 = start_gout(0)
    gather_wdn.finish()
    sums[0].sent()
    feed_0 = feed_sum(0)
    for moved in moves_1:
        moved.wait_recv()
    keep_gates.wait()
    s2, keep_gates = renew(1, a2a_1, s1_ref[...])
    gstate_send[...] = gstate_in[...].astype(jnp.bfloat16)
    gstate_turn = turn(gstate_send, far_gstate_here)
    s2_ref[...] = s2.astype(jnp.bfloat16)
    rise(1, gather_m1)
    gather_g1 = start_gout(1)
    sums[1].sent()
    feed_1 = feed_sum(1)
    feed_0.forward()
    back_0 = feed_back(0, gather_g0)
    back_0.forward()
    back_1 = feed_back(1, gather_g1)
    feed_1.forward()
    keep_down = weight_grad(grad_stage, gout, hidden, far_wdn_grad, local_sems.at[1])
    back_1.forward()
    keep_up = weight_grad(hidden, middle_normed, up_grad, far_wup_grad, local_sems.at[2])
    feed_total, result_total, gain_total = 0.0, 0.0, 0.0
    for block, feed_here in ((0, feed_0), (1, feed_1)):
        at = slice(block * rows, (block + 1) * rows)
        feed = feed_here.finish()
        result = middle[at, :] + feed
        block_out[at, :] = result.astype(jnp.bfloat16)
        share = row_mask(facts, block * window + rank * rows, rows)
        feed_total = feed_total + jnp.sum(feed * feed * share, axis=0, keepdims=True)
        result_total = result_total + jnp.sum(result * result * share, axis=0, keepdims=True)
    for block, back_here in ((1, back_1), (0, back_0)):
        at = slice(block * rows, (block + 1) * rows)
        straight, gain = rms_back(middle[at, :], gains_ref[1:2, :], back_here.finish())
        total = gout_rows[at, :].astype(jnp.float32) + straight
        middle_grad[at, :] = total
        branch_rows[at, :] = total.astype(jnp.bfloat16)
        gain_total = gain_total + gain
    small_sums[...] = jnp.concatenate(
        [gain_total, result_total, branch_total, feed_total]
        + [jnp.zeros((4, gain_total.shape[1]), jnp.float32)],
        axis=0,
    )
    gstate_turn.arrived()
    keep_gates.wait()
    keep_down.wait()
    keep_up.wait()
    for moved in kept:
        moved.wait()
    links.close()


class PlaneSum:
    def __init__(self, links, here, grad, first_in, last_in):
        self.links, self.here, self.grad = links, here, grad
        self.first_in, self.last_in = first_in, last_in
        self.rows = first_in.shape[-2]

    def part(self, k, which):
        start = self.here.planes[k] * 2 * self.rows + which * self.rows
        return rows_of(self.grad, start, self.rows)

    def start(self):
        mates = self.here.plane_mates
        self.firsts = [
            self.links.copy(self.part(k, which), self.first_in.at[slot], mates[mate])
            for slot, (k, which, mate) in enumerate(((1, 0, 1), (3, 0, 1), (2, 1, 2), (3, 1, 2)))
        ]
        return self

    def add(self, k, which, arrived):
        part = self.part(k, which)
        part[...] = (part[...].astype(jnp.float32) + arrived[...].astype(jnp.float32)).astype(part.dtype)

    def forward(self):
        mates = self.here.plane_mates
        self.firsts[1].wait_recv()
        self.add(2, 0, self.first_in.at[1])
        self.last_0 = self.links.copy(self.part(2, 0), self.last_in.at[0], mates[2])
        self.firsts[3].wait_recv()
        self.add(1, 1, self.first_in.at[3])
        self.last_1 = self.links.copy(self.part(1, 1), self.last_in.at[1], mates[1])

    def finish(self):
        self.firsts[0].wait_recv()
        self.add(0, 0, self.first_in.at[0])
        self.firsts[2].wait_recv()
        self.add(0, 1, self.first_in.at[2])
        self.last_0.wait_recv()
        self.add(0, 0, self.last_in.at[0])
        self.last_1.wait_recv()
        self.add(0, 1, self.last_in.at[1])

    def result(self, which):
        return rows_of(self.grad, self.here.planes[0] * 2 * self.rows + which * self.rows, self.rows)


class FarPlaneSum(PlaneSum):
    def __init__(self, links, here, grad, first_in, last_in, held, held_sems):
        super().__init__(links, here, grad, first_in, last_in)
        self.held, self.held_sems = held, held_sems

    def bring(self, *pieces):
        self.brings = [
            pltpu.make_async_copy(self.part(k, which), self.held.at[slot], self.held_sems.at[slot])
            for slot, (k, which) in enumerate(pieces)
        ]
        for moved in self.brings:
            moved.start()

    def start(self):
        super().start()
        self.bring((2, 0), (1, 1))
        return self

    def add_to(self, slot, *arrived):
        total = self.held[slot].astype(jnp.float32)
        for piece in arrived:
            total = total + piece.astype(jnp.float32)
        self.held[slot] = total.astype(jnp.bfloat16)

    def forward(self):
        mates = self.here.plane_mates
        for moved in self.brings:
            moved.wait()
        self.firsts[1].wait_recv()
        self.add_to(0, self.first_in[1])
        self.last_0 = self.links.copy(self.held.at[0], self.last_in.at[0], mates[2])
        self.firsts[3].wait_recv()
        self.add_to(1, self.first_in[3])
        self.last_1 = self.links.copy(self.held.at[1], self.last_in.at[1], mates[1])

    def bring_own(self):
        self.links.sent(self.last_0)
        self.links.sent(self.last_1)
        self.bring((0, 0), (0, 1))

    def finish(self):
        for moved in self.brings:
            moved.wait()
        self.firsts[0].wait_recv()
        self.last_0.wait_recv()
        self.add_to(0, self.first_in[0], self.last_in[0])
        self.firsts[2].wait_recv()
        self.last_1.wait_recv()
        self.add_to(1, self.first_in[2], self.last_in[1])

    def result(self, which):
        return self.held.at[which]


class Settle:
    def __init__(self, links, here, summed, target):
        half = here.half
        self.straight = Turn(links, here, summed.result(half), target.at[0], here.from_there)
        self.crossed = links.copy(summed.result(1 - half), target.at[1], here.from_across)

    def arrived(self):
        self.straight.arrived()
        self.crossed.wait_recv()


class GateHome:
    def __init__(self, links, here, grad, target, rows):
        self.links, self.here = links, here
        low = lax.rem(here.level, 2)
        piece = rows // 4
        self.slot = target.at[2 * here.half + here.core]
        chip = here.dp - here.core + low
        self.stays = here.core == low
        self.moves = {}
        for step in range(4):
            to_level = lax.rem(here.level + step, 4)
            start = here.planes[0] * 2 * rows + low * rows + to_level * piece
            source = rows_of(grad, start, piece, piece)
            for core in range(2):
                moved = links.plan(source, self.slot, (chip, to_level))
                self.moves[step, core] = moved
                sends = here.core == core
                if step == 0:
                    kept = pltpu.make_async_copy(source, self.slot, links.recv_sems.at[links.used - 1])
                    self.moves[core] = kept

                    @pl.when(sends & self.stays)
                    def _(kept=kept):
                        kept.start()

                    sends = sends & jnp.logical_not(self.stays)

                @pl.when(sends)
                def _(moved=moved):
                    moved.start()

    def arrived(self):
        for step in range(4):
            comes = lax.rem(self.here.level + step, 2) == self.here.core
            for core in range(2):
                own = self.here.core == core
                if step == 0:

                    @pl.when(comes & own)
                    def _(kept=self.moves[core]):
                        kept.wait()

                    comes_here = comes & jnp.logical_not(own)
                else:
                    comes_here = comes

                @pl.when(comes_here)
                def _(moved=self.moves[step, core]):
                    moved.wait_recv()

                sent = own & jnp.logical_not(self.stays) if step == 0 else own

                @pl.when(sent)
                def _(moved=self.moves[step, core]):
                    moved.wait_send()


def cotangent_kernel(
    far_middle_grad, far_branch_rows, gstate_ref, far_x, s0_ref, s1_ref, far_gate_values, gains_ref, facts, facts_home,
    small_sums,
    far_normed, far_snormed, far_queries, far_keys, far_values, far_state_qkv, far_lse, far_mixed,
    far_smixed, far_wst, far_wtok, far_wout, far_gates, far_wup_grad, far_wdn_grad, far_block_out, far_state_out,
    block_home, state_home, tokens_home, past_home, carried_grad, initial_grad, totals,
    up_home, down_home, wst_home, wtok_home, wout_home, gates_home,
    gates, wout, queries, keys, state_qkv, values, lse_ref, mixed, wst, wtok,
    tiles, tile_grads, branch_grad, mixed_grad, gate_rows, state_mixed_grad, key_grad, value_grad,
    skey_grad, svalue_grad, token_cot, state_cot, gate_values, smixed_pair, sending,
    tokens_send, carried_send, carried_in, initial_send, initial_in,
    wst_grad, wtok_grad, wout_grad, gates_grad,
    wst_first, wtok_first, wout_first, gates_first, wst_last, wtok_last, wout_last, gates_last,
    up_first, down_first, up_last, down_last, up_held, down_held, ring_in, level_in, ring_send, level_send,
    late_in, late_level_in, late_send, late_level_send, gate_pair_in,
    *rest,
):
    rs = [rest[0:4], rest[4:8], rest[8:12]]
    links = Links(rest[12], rest[13])
    local_sems, held_sems, bring_sems = rest[14], rest[15], rest[16]
    here = Place()
    rank, ranks, mates = here.rank, here.ranks, here.mates
    rows = s0_ref.shape[0]
    window = 4 * rows
    width = queries.shape[1]
    heads = width // DH
    size = s0_ref.shape[1]
    reach = 2 * width
    other_half = pl.ds(pl.multiple_of((1 - here.core) * reach, reach), reach)
    own_half = pl.ds(pl.multiple_of(here.core * reach, reach), reach)

    def pair_rows(block):
        return rows_at((2 * block + here.core) * rows, rows)

    def own_branch(block):
        return branch_grad.at[rows_at(block * window + rank * rows, rows)]

    brings = []
    for source, target in (
        (far_branch_rows.at[pl.ds(rows, rows)], own_branch(1)),
        (far_branch_rows.at[pl.ds(0, rows)], own_branch(0)),
        (far_gates, gates),
        (far_wout, wout),
        (far_queries, queries),
        (far_keys, keys),
        (far_state_qkv, state_qkv),
        (far_values, values),
        (far_lse, lse_ref),
        (far_mixed, mixed),
        (far_wst, wst),
        (far_wtok, wtok),
        (far_x, tokens_send),
        (far_smixed.at[pl.ds(0, rows), own_half], smixed_pair.at[pair_rows(0)]),
        (far_smixed.at[pl.ds(rows, rows), own_half], smixed_pair.at[pair_rows(1)]),
    ):
        brings.append(pltpu.make_async_copy(source, target, bring_sems.at[len(brings)]))
        brings[-1].start()
    ring = [(lax.rem(here.dp + step, 8), here.level) for step in range(1, 8)]
    other = here.dp + 1 - 2 * here.core
    column = [
        (chip, lax.rem(here.level + step, 4)) for step in range(1, 4) for chip in (here.dp, other)
    ]
    bring_gates = pltpu.make_async_copy(
        far_gate_values.at[pl.ds(rows, rows)], gate_values, local_sems.at[0]
    )
    bring_gates.start()
    greet(ring + column)
    def home(source, target):
        return Turn(links, here, source, target, here.from_there)

    def gates_back(block, state, state_grad):
        spot = pair_rows(block)
        keep = jax.nn.sigmoid(gate_values[:, 2 * size : 3 * size] + 1.0)
        fresh = jnp.tanh(gate_values[:, 0:size])
        let_in = jax.nn.sigmoid(gate_values[:, size : 2 * size] - 1.0)
        gate_rows[spot, 0:size] = (state_grad * let_in * (1.0 - fresh * fresh)).astype(jnp.bfloat16)
        gate_rows[spot, size : 2 * size] = (
            state_grad * fresh * let_in * (1.0 - let_in)
        ).astype(jnp.bfloat16)
        gate_rows[spot, 2 * size : 3 * size] = (
            state_grad * state * keep * (1.0 - keep)
        ).astype(jnp.bfloat16)
        out = dot(gate_rows[spot, 0:size], gates[0], NN)
        out = out + dot(gate_rows[spot, size : 2 * size], gates[1], NN)
        out = out + dot(gate_rows[spot, 2 * size : 3 * size], gates[2], NN)
        sending[...] = out.astype(jnp.bfloat16)
        spot = rows_at(block * window + rank * rows, rows)
        moves = []
        for k in (2, 3, 1):
            columns = pl.ds(pl.multiple_of(ranks[k] * width, width), width)
            moves.append(
                links.copy(sending.at[:, columns], state_mixed_grad.at[spot], mates[k])
            )
        columns = pl.ds(pl.multiple_of(rank * width, width), width)
        state_mixed_grad[spot, :] = sending[:, columns]
        pair = gate_rows.at[pair_rows(block)]
        return state_grad * keep, moves, links.copy(pair, pair, mates[1])

    lane = lax.broadcasted_iota(jnp.int32, (1, DH), 1)

    def widen(columns, value):
        high = value.astype(jnp.bfloat16).astype(jnp.float32)
        middle = (value - high).astype(jnp.bfloat16).astype(jnp.float32)
        more = jnp.where(lane == 1, high, jnp.where(lane == 2, middle, value - high - middle))
        more = jnp.where(lane == 0, 1.0, jnp.where(lane < 4, more, 0.0))
        return jnp.concatenate([columns, more.astype(jnp.bfloat16)], axis=1)

    plain = jnp.where((lane > 0) & (lane < 4), 1.0, 0.0)

    def beside(columns, mask=None):
        more = jnp.broadcast_to(plain, (columns.shape[0], DH))
        if mask is not None:
            more = jnp.where(lane == 0, mask, more)
        return jnp.concatenate([columns, more.astype(jnp.bfloat16)], axis=1)

    def key_mask(start, size):
        place_of = lax.broadcasted_iota(jnp.int32, (size, 1), 0).astype(jnp.float32)
        place_of = place_of + float(start - window)
        own = jnp.where(place_of < facts[2:3, 0:1], 0.0, NEGATIVE)
        return jnp.where(place_of < 0.0, facts[3:4, 0:1] * NEGATIVE, own)

    def token_back(block):
        base = block * window
        whole = pl.ds(base, window)
        for tile in range(window // TILE):
            near_mask = key_mask(base + tile * TILE, 3 * TILE)
            for head in range(heads):
                at = head * DH
                lanes = slice(at, at + DH)
                skey_lanes = slice(width + at, width + at + DH)
                svalue_lanes = slice(2 * width + at, 2 * width + at + DH)
                here_rows = pl.ds(base + tile * TILE, TILE)
                near = pl.ds(base + tile * TILE, 3 * TILE)
                query = queries[here_rows, lanes]
                out_grad = mixed_grad[here_rows, lanes]
                wide = widen(query, lse_ref[here_rows, head : head + 1] * (-1.0 / ROOT))
                inner = jnp.sum(
                    out_grad.astype(jnp.float32) * mixed[here_rows, lanes].astype(jnp.float32),
                    axis=-1,
                    keepdims=True,
                )
                wide_grad = widen(out_grad, -inner)
                first = jnp.exp2(
                    dot(wide, beside(keys[near, lanes], near_mask), NT) * (ROOT * LOG2E) + tiles[head]
                )
                second = jnp.exp2(
                    dot(wide, beside(state_qkv[whole, skey_lanes]), NT) * (ROOT * LOG2E)
                )
                first_low, second_low = first.astype(jnp.bfloat16), second.astype(jnp.bfloat16)
                first = first * dot(wide_grad, beside(values[near, lanes]), NT)
                second = second * dot(wide_grad, beside(state_qkv[whole, svalue_lanes]), NT)
                first_grad, second_grad = first.astype(jnp.bfloat16), second.astype(jnp.bfloat16)
                value_grad[near, lanes] += dot(first_low, out_grad, TN)
                svalue_grad[:, lanes] += dot(second_low, out_grad, TN)
                part = dot(first_grad, keys[near, lanes], NN) + dot(
                    second_grad, state_qkv[whole, skey_lanes], NN
                )
                token_cot[here_rows, lanes] = (part * ROOT).astype(jnp.bfloat16)
                key_grad[near, lanes] += dot(first_grad, query, TN) * ROOT
                skey_grad[:, lanes] += dot(second_grad, query, TN) * ROOT
                tile_grads[head] += first

    def state_back(block):
        base = block * window
        whole = pl.ds(base, window)
        own = pl.ds(base + window, window)
        own_mask = key_mask(base + window, window)
        for head in range(heads):
            at = head * DH
            lanes = slice(at, at + DH)
            skey_lanes = slice(width + at, width + at + DH)
            svalue_lanes = slice(2 * width + at, 2 * width + at + DH)
            wide_skeys = beside(state_qkv[whole, skey_lanes])
            wide_keys = beside(keys[own, lanes], own_mask)
            for tile in range(window // TILE):
                here_rows = pl.ds(base + tile * TILE, TILE)
                query = state_qkv[here_rows, lanes]
                out_grad = state_mixed_grad[here_rows, lanes]
                wide = widen(query, lse_ref[here_rows, heads + head : heads + head + 1] * (-1.0 / ROOT))
                first = jnp.exp2(dot(wide, wide_skeys, NT) * (ROOT * LOG2E))
                second = jnp.exp2(dot(wide, wide_keys, NT) * (ROOT * LOG2E))
                first_low, second_low = first.astype(jnp.bfloat16), second.astype(jnp.bfloat16)
                first_grad = dot(out_grad, state_qkv[whole, svalue_lanes], NT)
                second_grad = dot(out_grad, values[own, lanes], NT)
                inner = jnp.sum(first * first_grad, axis=-1, keepdims=True) + jnp.sum(
                    second * second_grad, axis=-1, keepdims=True
                )
                first_grad = (first * (first_grad - inner)).astype(jnp.bfloat16)
                second_grad = (second * (second_grad - inner)).astype(jnp.bfloat16)
                svalue_grad[:, lanes] += dot(first_low, out_grad, TN)
                value_grad[own, lanes] += dot(second_low, out_grad, TN)
                part = dot(first_grad, state_qkv[whole, skey_lanes], NN) + dot(
                    second_grad, keys[own, lanes], NN
                )
                state_cot[here_rows, lanes] = (part * ROOT).astype(jnp.bfloat16)
                skey_grad[:, lanes] += dot(first_grad, query, TN) * ROOT
                key_grad[own, lanes] += dot(second_grad, query, TN) * ROOT

    def gather_cot(block):
        whole = pl.ds(block * window, window)
        own = pl.ds(block * window + window, window)
        token_cot[whole, width : 2 * width] = key_grad[own, :].astype(jnp.bfloat16)
        token_cot[whole, 2 * width : 3 * width] = value_grad[own, :].astype(jnp.bfloat16)
        state_cot[whole, width : 2 * width] = skey_grad[...].astype(jnp.bfloat16)
        state_cot[whole, 2 * width : 3 * width] = svalue_grad[...].astype(jnp.bfloat16)

    def back_rows(cots, weight, block):
        def make(which):
            at = rows_at(block * window + which * rows, rows)
            out = dot(cots[at, 0:width], weight[0], NT)
            for c in (1, 2):
                out = out + dot(cots[at, c * width : (c + 1) * width], weight[c], NT)
            return out

        return make

    def state_sum(block):
        return RowSum(links, here, *rs[0], rows).fill(back_rows(state_cot, wst, block))

    def token_sum(block):
        return RowSum(links, here, *rs[1 + block], rows).fill(back_rows(token_cot, wtok, block))

    def mix_back(block, gather):
        for k in range(4):
            gather.ready(k)
            at = rows_at(block * window + ranks[k] * rows, rows)
            mixed_grad[at, :] = dot(branch_grad[at, :], wout[...], NN).astype(jnp.bfloat16)

    def store_grad(target, at, out):
        if len(target.shape) == 2:
            target[at, :] = out.astype(jnp.bfloat16)
        else:
            for c in range(3):
                target[c, at, :] = out[:, c * width : (c + 1) * width].astype(jnp.bfloat16)

    def weight_grad(target, left, right):
        step = 256
        for part in range(size // step):
            at = slice(part * step, (part + 1) * step)
            store_grad(target, at, dot(left[:, at], right[...], TN))

    def finish_tokens(block, summed):
        at = slice(block * rows, (block + 1) * rows)
        x = tokens_send[at, :].astype(jnp.float32)
        straight, gain = rms_back(x, gains_ref[0:1, :], summed.finish())
        middle_grad = gate_values[:, block * size : (block + 1) * size]
        tokens_send[at, :] = (middle_grad + straight).astype(jnp.bfloat16)
        return gain, home(tokens_send.at[pl.ds(block * rows, rows)], tokens_home.at[pl.ds(block * rows, rows)])

    smixed_moves = []
    for block in range(2):
        smixed_moves.append(
            links.copy(
                far_smixed.at[pl.ds(block * rows, rows), other_half],
                smixed_pair.at[pair_rows(block)],
                mates[1],
            )
        )
    brings[0].wait()
    branch_1 = RowGather(links, here, branch_grad, window, rows).start()
    bring_gates.wait()
    brings[2].wait()
    direct_1, moves_1, pair_1 = gates_back(1, s1_ref[...], gstate_ref[...].astype(jnp.float32))
    up_sum = FarPlaneSum(
        links, here, far_wup_grad, up_first, up_last, up_held, held_sems.at[pl.ds(0, 2)]
    ).start()
    down_sum = FarPlaneSum(
        links, here, far_wdn_grad, down_first, down_last, down_held, held_sems.at[pl.ds(2, 2)]
    ).start()
    bring_gates = pltpu.make_async_copy(far_gate_values.at[pl.ds(0, rows)], gate_values, local_sems.at[0])
    bring_gates.start()
    for ref in (tile_grads, key_grad, value_grad, skey_grad, svalue_grad):
        ref[...] = jnp.zeros(ref.shape, ref.dtype)
    bias_tiles(facts, tiles, heads, 3 * TILE, LOG2E)
    brings[1].wait()
    for moved in brings[3:]:
        moved.wait()
    mix_back(1, branch_1)
    branch_0 = RowGather(links, here, branch_grad, 0, rows).start()
    block_turn = home(far_block_out, block_home)
    state_turn = home(far_state_out, state_home)
    token_back(1)
    for moved in moves_1:
        moved.wait_recv()
    state_back(1)
    gather_cot(1)
    up_sum.forward()
    state_sum_1 = state_sum(1)
    token_sum_1 = token_sum(1)
    state_sum_1.forward()
    down_sum.forward()
    up_sum.bring_own()
    mix_back(0, branch_0)
    for ref in (skey_grad, svalue_grad):
        ref[...] = jnp.zeros(ref.shape, ref.dtype)
    up_sum.finish()
    up_settle = Settle(links, here, up_sum, up_home)
    token_back(0)
    for head in range(heads):
        lines = tile_grads[head, 0:8, :]
        span = lines.shape[1]
        for group in range(1, TILE // 8):
            lines = lines + pltpu.roll(tile_grads[head, 8 * group : 8 * group + 8, :], span - 8 * group, 1)
        total = lines[0:1]
        for line in range(1, 8):
            total = total + pltpu.roll(lines[line : line + 1], span - line, 1)
        for owner in range(4):
            at = 8 + heads * owner + head
            ring_send[at : at + 1, :] = jnp.zeros((1, size), jnp.float32)
            ring_send[at : at + 1, 0:span] = jnp.where(rank == owner, total, 0.0)
    ring_send[1:2, :] = small_sums[0:1, :]
    ring_send[3:6, :] = small_sums[1:4, :]
    counted = jnp.zeros((1, 1), jnp.float32)
    for block in range(2):
        valid_rows = row_mask(facts, block * window + rank * rows, rows)
        counted = counted + jnp.sum(valid_rows, axis=0, keepdims=True)
    ring_send[6:7, :] = jnp.broadcast_to(counted, (1, size))
    for line in (0, 2, 7):
        ring_send[line : line + 1, :] = jnp.zeros((1, size), jnp.float32)
    ring_moves = [
        links.copy(ring_send, ring_in.at[step - 1], ring[step - 1]) for step in range(1, 8)
    ]
    token_sum_1.forward()
    bring_gates.wait()
    state_norm_grad, gain_2 = rms_back(s1_ref[...], gains_ref[2:3, :], state_sum_1.finish())
    for moved in moves_1:
        links.sent(moved)
    direct_0, moves_0, pair_0 = gates_back(0, s0_ref[...], direct_1 + state_norm_grad)
    bring_middle = [
        pltpu.make_async_copy(
            far_middle_grad.at[pl.ds(block * rows, rows)],
            gate_values.at[:, pl.ds(block * size, size)],
            local_sems.at[6 + block],
        )
        for block in range(2)
    ]
    for moved in bring_middle:
        moved.start()
    mixed_grad[0:window, :] = key_grad[0:window, :].astype(jnp.bfloat16)
    mixed_grad[window : 2 * window, :] = value_grad[0:window, :].astype(jnp.bfloat16)
    down_sum.bring_own()
    for moved in smixed_moves + [pair_1, pair_0]:
        moved.wait_recv()
    for c in range(3):
        weight_grad(gates_grad.at[c], gate_rows.at[:, c * size : (c + 1) * size], smixed_pair)
    gates_sum = PlaneSum(links, here, gates_grad, gates_first, gates_last).start()
    weight_grad(wout_grad, branch_grad, mixed)
    wout_sum = PlaneSum(links, here, wout_grad, wout_first, wout_last).start()
    for moved in ring_moves:
        moved.wait_recv()
    total = ring_send[...]
    for step in range(7):
        total = total + ring_in[step]
    level_send[...] = total
    level_moves = [
        links.copy(level_send, level_in.at[step - 1], (here.dp, lax.rem(here.level + step, 4)))
        for step in range(1, 4)
    ]
    down_sum.finish()
    for moved in bring_middle:
        moved.wait()
    gain_1, turn_1 = finish_tokens(1, token_sum_1)
    for moved in moves_0:
        moved.wait_recv()
    past_turn = home(mixed_grad, past_home)
    down_settle = Settle(links, here, down_sum, down_home)
    for gather in (branch_1, branch_0):
        gather.sent()
    bring_snormed = pltpu.make_async_copy(far_snormed, branch_grad, local_sems.at[2])
    bring_snormed.start()
    for moved in (pair_1, pair_0):
        links.sent(moved)
    bring_normed = []
    for block in range(2):
        bring_normed.append(
            pltpu.make_async_copy(
                far_normed.at[pl.ds(block * window, window)],
                gate_rows.at[:, block * size : (block + 1) * size],
                local_sems.at[4 + block],
            )
        )
        bring_normed[block].start()
    state_back(0)
    gather_cot(0)
    bring_snormed.wait()
    weight_grad(wst_grad, branch_grad, state_cot)
    wst_sum = PlaneSum(links, here, wst_grad, wst_first, wst_last).start()
    for block in range(2):
        bring_normed[block].wait()
    for part in range(size // 256):
        at = slice(part * 256, (part + 1) * 256)
        later = slice(size + part * 256, size + (part + 1) * 256)
        summed = dot(gate_rows[:, at], token_cot[0:window, :], TN)
        summed = summed + dot(gate_rows[:, later], token_cot[window : 2 * window, :], TN)
        store_grad(wtok_grad, at, summed)
    wtok_sum = PlaneSum(links, here, wtok_grad, wtok_first, wtok_last).start()
    gates_sum.forward()
    state_sum_1.sent()
    state_sum_0 = state_sum(0)
    token_sum_0 = token_sum(0)
    state_sum_0.forward()
    token_sum_0.forward()
    wst_sum.forward()
    wtok_sum.forward()
    wout_sum.forward()
    state_norm_grad, gain = rms_back(s0_ref[...], gains_ref[2:3, :], state_sum_0.finish())
    carried_send[...] = (direct_0 + state_norm_grad).astype(jnp.bfloat16)
    carried_turn = home(carried_send, carried_in)
    gain_2 = gain_2 + gain
    gates_sum.finish()
    low = lax.rem(here.level, 2)
    gates_pair = links.copy(gates_sum.result(1 - low), gate_pair_in, mates[2])
    wst_sum.finish()
    wst_settle = Settle(links, here, wst_sum, wst_home)
    gain_0, turn_0 = finish_tokens(0, token_sum_0)

    late_send[...] = jnp.concatenate(
        [gain[:, step * 256 : (step + 1) * 256] for gain in (gain_0 + gain_1, gain_2) for step in range(4)],
        axis=0,
    )
    late_moves = [
        links.copy(late_send, late_in.at[step - 1], ring[step - 1]) for step in range(1, 8)
    ]
    gates_pair.wait_recv()
    gates_part = gates_sum.result(low)
    gates_part[...] = (
        gates_part[...].astype(jnp.float32) + gate_pair_in[...].astype(jnp.float32)
    ).astype(jnp.bfloat16)
    gate_moves = GateHome(links, here, gates_grad, gates_home, rows)
    wtok_sum.finish()
    wtok_settle = Settle(links, here, wtok_sum, wtok_home)
    wout_sum.finish()
    wout_settle = Settle(links, here, wout_sum, wout_home)
    carried_turn.arrived()
    is_fresh = facts_home[3:4, :] > 0.5
    came = carried_in[...]
    carried_grad[...] = jnp.where(is_fresh, 0.0, came.astype(jnp.float32))
    initial_send[...] = jnp.where(is_fresh, came, jnp.zeros_like(came))
    part = initial_grad.shape[1]
    initial_moves = []
    for step in range(1, 8):
        to = lax.rem(here.dp + step, 8)
        columns = pl.ds(pl.multiple_of(to * part, part), part)
        initial_moves.append(
            links.copy(initial_send.at[:, columns], initial_in.at[step - 1], ring[step - 1])
        )
    for moved in late_moves:
        moved.wait_recv()
    late = late_send[...]
    for step in range(7):
        late = late + late_in[step]
    late_level_send[...] = late
    late_level_moves = [
        links.copy(late_level_send, late_level_in.at[step - 1], (here.dp, lax.rem(here.level + step, 4)))
        for step in range(1, 4)
    ]
    for moved in initial_moves:
        moved.wait_recv()
    own_columns = pl.ds(pl.multiple_of(here.dp * part, part), part)
    initial = initial_send[:, own_columns].astype(jnp.float32)
    for step in range(7):
        initial = initial + initial_in[step].astype(jnp.float32)
    initial_grad[...] = initial
    for moved in level_moves:
        moved.wait_recv()
    total = level_send[...]
    for step in range(3):
        total = total + level_in[step]
    totals[...] = total
    for moved in late_level_moves:
        moved.wait_recv()
    late = late_level_send[...]
    for step in range(3):
        late = late + late_level_in[step]
    for row, first in ((0, 0), (2, 4)):
        for step in range(4):
            totals[row : row + 1, step * 256 : (step + 1) * 256] = late[first + step : first + step + 1, :]
    gate_moves.arrived()
    for turn in (block_turn, state_turn, past_turn, turn_1, turn_0):
        turn.arrived()
    for settle in (up_settle, down_settle, wout_settle, wst_settle, wtok_settle):
        settle.arrived()
    links.close()


def run_kernel(body, outs, scratch, collective, name, operands, far_in=(), far_out=()):
    vmem = pl.BlockSpec(memory_space=pltpu.VMEM)
    far = pl.BlockSpec(memory_space=pl.ANY)
    return pl.pallas_call(
        body,
        out_shape=outs,
        in_specs=[far if at in far_in else vmem for at in range(len(operands))],
        out_specs=[far if at in far_out else vmem for at in range(len(outs))],
        scratch_shapes=scratch,
        compiler_params=pltpu.CompilerParams(
            collective_id=collective, has_side_effects=True, vmem_limit_bytes=VMEM_BYTES
        ),
        name=name,
    )(*operands)


def sems(count):
    return [pltpu.SemaphoreType.DMA((count,)), pltpu.SemaphoreType.DMA((count,))]


def grouped(
    tokens, carried_state, past_keys, fresh_start, valid_count, bucket_ids, grad_output, grad_state,
    norm_gains, token_qkv, token_out, bias_table, mlp_up, mlp_down, state_qkv, state_gates, initial_state,
):
    dp_size, levels = lax.axis_size("dp"), lax.axis_size("state")
    dp_at, level = lax.axis_index("dp"), lax.axis_index("state")
    _, blocks, rows, size = tokens.shape
    window = rows * levels
    width = token_qkv.shape[2]
    heads = width // DH
    units = mlp_up.shape[1]
    model_rows = token_qkv.shape[0]
    low, full = jnp.bfloat16, jnp.float32

    one_hot = (bucket_ids[:, None] == jnp.arange(bias_table.shape[0])[None, :]).astype(full)
    per_offset = jnp.dot(one_hot, bias_table, precision=HIGHEST)
    lines = jnp.pad(per_offset[::-1].T, ((0, 0), (1, window - 1)), constant_values=NEGATIVE)
    numbers = jnp.stack([valid_count[0], fresh_start[0]]).astype(full)
    facts_in = jnp.concatenate(
        [
            lines,
            jnp.broadcast_to(numbers[:, None], (2, lines.shape[1])),
            jnp.zeros((4, lines.shape[1]), full),
        ]
    )

    stacked = lambda weight: jnp.transpose(weight, (1, 0, 2))
    shape = jax.ShapeDtypeStruct
    vmem = pltpu.VMEM
    rs = row_sum_scratch(rows, size)
    kept = [
        ((2 * window, size), low),
        ((2 * window, size), low),
        ((2 * window, width), low),
        ((3 * window, width), low),
        ((3 * window, width), low),
        ((2 * window, 3 * width), low),
        ((2 * window, 2 * heads), full),
        ((2 * window, width), low),
        ((3, size, width), low),
        ((3, size, width), low),
        ((size, width), low),
        ((3, size, size), low),
        ((2 * rows, size), low),
        ((rows, size), full),
        ((rows, size), full),
    ]
    (
        normed, snormed, queries, keys, values, sqkv, lse, mixed, wst_all, wtok_all, wout_all, gates_all,
        x, s0, s1, gate_values, gstate, wup_grad, wdn_grad, smixed_rows, s2, facts,
        block_out, middle_grad, branch_rows, small_sums,
    ) = run_kernel(
        forward_kernel,
        [shape(*of) for of in kept]
        + [
            shape((2 * rows, 3 * size), full),
            shape((rows, size), low),
            shape((size, units), low),
            shape((size, units), low),
            shape((2 * rows, size), low),
            shape((rows, size), low),
            shape((8, 2 * window), full),
            shape((2 * rows, size), low),
            shape((2 * rows, size), full),
            shape((2 * rows, size), low),
            shape((8, size), full),
        ],
        [vmem(*of) for of in kept]
        + [
            vmem((2 * window, width), low),
            vmem((heads, TILE, 3 * TILE), full),
            vmem((rows, size), low),
            vmem((rows, size), low),
            vmem((rows, size), low),
            vmem((rows, size), full),
            vmem((rows, 3 * size), full),
            vmem((size, units), low),
            vmem((size, units), low),
            vmem((2 * rows, size), full),
            vmem((2 * window, size), low),
            vmem((2 * rows, size), low),
            vmem((2 * window, size), low),
            vmem((2 * window, units), full),
            vmem((2 * window, units), low),
            vmem((2 * window, units), low),
            vmem((size, units), low),
        ]
        + rs * 4
        + sems(128)
        + [pltpu.SemaphoreType.DMA((4,)), pltpu.SemaphoreType.DMA((len(kept),))],
        0,
        "forward",
        [
            tokens[0].reshape(blocks * rows, size),
            carried_state[0],
            initial_state,
            jnp.swapaxes(past_keys[0], 0, 1),
            facts_in,
            grad_output[0].reshape(blocks * rows, size),
            grad_state[0],
            norm_gains,
            stacked(state_qkv),
            stacked(token_qkv),
            token_out,
            stacked(state_gates),
            mlp_up,
            mlp_down,
        ],
        far_in=(3, 5, 12, 13),
        far_out=range(len(kept) + 4),
    )
    grads = [((3,), width), ((3,), width), ((), width), ((3,), 2 * width)]
    (
        block_home, state_home, tokens_home, past_home, carried_grad, initial_grad, totals,
        up_home, down_home, wst_home, wtok_home, wout_home, gates_home,
    ) = run_kernel(
        cotangent_kernel,
        [
            shape((2 * rows, size), low),
            shape((rows, size), low),
            shape((2 * rows, size), low),
            shape((2 * window, width), low),
            shape((rows, size), full),
            shape((rows, size // dp_size), full),
            shape((16, size), full),
            shape((2, rows, units), low),
            shape((2, rows, units), low),
            shape((2, 3, rows, width), low),
            shape((2, 3, rows, width), low),
            shape((2, rows, width), low),
            shape((4, 3, rows // 4, 2 * width), low),
        ],
        [
            vmem((3, size, size), low),
            vmem((size, width), low),
            vmem((2 * window, width), low),
            vmem((3 * window, width), low),
            vmem((2 * window, 3 * width), low),
            vmem((3 * window, width), low),
            vmem((2 * window, 2 * heads), full),
            vmem((2 * window, width), low),
            vmem((3, size, width), low),
            vmem((3, size, width), low),
            vmem((heads, TILE, 3 * TILE), full),
            vmem((heads, TILE, 3 * TILE), full),
            vmem((2 * window, size), low),
            vmem((2 * window, width), low),
            vmem((4 * rows, 3 * size), low),
            vmem((2 * window, width), low),
            vmem((3 * window, width), full),
            vmem((3 * window, width), full),
            vmem((window, width), full),
            vmem((window, width), full),
            vmem((2 * window, 3 * width), low),
            vmem((2 * window, 3 * width), low),
            vmem((rows, 3 * size), full),
            vmem((4 * rows, 2 * width), low),
            vmem((rows, size), low),
            vmem((2 * rows, size), low),
            vmem((rows, size), low),
            vmem((rows, size), low),
            vmem((rows, size), low),
            vmem((dp_size - 1, rows, size // dp_size), low),
        ]
        + [vmem((*stack, size, columns), low) for stack, columns in grads]
        + [vmem((4, *stack, rows, columns), low) for stack, columns in grads]
        + [vmem((2, *stack, rows, columns), low) for stack, columns in grads]
        + [vmem((4, rows, units), low)] * 2
        + [vmem((2, rows, units), low)] * 4
        + [
            vmem((dp_size - 1, 16, size), full),
            vmem((levels - 1, 16, size), full),
            vmem((16, size), full),
            vmem((16, size), full),
            vmem((dp_size - 1, 8, size // 4), full),
            vmem((levels - 1, 8, size // 4), full),
            vmem((8, size // 4), full),
            vmem((8, size // 4), full),
            vmem((3, rows, 2 * width), low),
        ]
        + rs * 3
        + sems(128)
        + [pltpu.SemaphoreType.DMA((8,)), pltpu.SemaphoreType.DMA((4,)), pltpu.SemaphoreType.DMA((15,))],
        1,
        "cotangent",
        [
            middle_grad, branch_rows, gstate, x, s0, s1, gate_values, norm_gains, facts, facts_in,
            small_sums,
            normed, snormed, queries, keys, values, sqkv, lse, mixed, smixed_rows,
            wst_all, wtok_all, wout_all, gates_all, wup_grad, wdn_grad, block_out, s2,
        ],
        far_in=(0, 1, 3, 6, *range(11, 28)),
        far_out=(0, 1, 2, 3, 7, 8, 9, 10, 11, 12),
    )
    both = lambda pair: pair[0].astype(full) + pair[1].astype(full)
    gates_out = jnp.sum(gates_home.astype(full).reshape(2, 2, 3, rows // 4, 2 * width), axis=0)
    gates_out = jnp.transpose(gates_out, (2, 1, 0, 3)).reshape(rows // 4, 3, size)
    line_sums = totals[8 : 8 + levels * heads, 1 : window + 1][:, ::-1]
    table_all = jnp.dot(one_hot.T, line_sums.T, precision=HIGHEST)
    table_rows = table_all.shape[0] // dp_size
    table_out = lax.dynamic_slice(table_all, (dp_at * table_rows, level * heads), (table_rows, heads))
    share = size // (dp_size * levels)
    gains_out = lax.dynamic_slice(totals, (0, (dp_at * levels + level) * share), (3, share))
    rms_stats = jnp.sqrt(jnp.sum(totals[3:6], axis=1) / totals[6, 0])
    return (
        block_home.reshape(1, blocks, rows, size),
        state_home.astype(full)[None],
        rms_stats,
        tokens_home.reshape(1, blocks, rows, size),
        carried_grad[None],
        jnp.swapaxes(past_home.reshape(2, window, width).astype(full), 0, 1)[None],
        gains_out,
        stacked(both(wtok_home)),
        both(wout_home),
        table_out,
        both(up_home),
        both(down_home),
        stacked(both(wst_home)),
        gates_out,
        initial_grad,
    )


def solution(mesh):
    in_specs = (
        P("dp", None, "state", None),
        P("dp", "state", None),
        P("dp", None, None, "state"),
        P("dp"),
        P("dp"),
        P(),
        P("dp", None, "state", None),
        P("dp", "state", None),
        P(),
        P("dp", None, "state"),
        P("dp", "state"),
        P(None, "state"),
        P("dp", "state"),
        P("dp", "state"),
        P("dp", None, "state"),
        P("dp", None, None),
        P("state", "dp"),
    )
    out_specs = (
        P("dp", None, "state", None),
        P("dp", "state", None),
        P(),
        P("dp", None, "state", None),
        P("dp", "state", None),
        P("dp", None, None, "state"),
        P(None, ("dp", "state")),
        P("dp", None, "state"),
        P("dp", "state"),
        P("dp", "state"),
        P("dp", "state"),
        P("dp", "state"),
        P("dp", None, "state"),
        P(("dp", "state"), None, None),
        P("state", "dp"),
    )
    body = grouped if dict(mesh.shape) == {"dp": 8, "state": 4} else shards
    return jax.shard_map(body, mesh=mesh, in_specs=in_specs, out_specs=out_specs, check_vma=False)
```

```python
import math

import jax
import jax.numpy as jnp
from jax import lax
from jax.experimental import pallas as pl
from jax.experimental.pallas import tpu as pltpu
from jax.sharding import PartitionSpec as P

DH = 128


EPS = 1e-06
NEGATIVE = -1e30
HIGHEST = lax.Precision.HIGHEST


def rms_norm(tensor, gains_row):
    return tensor * lax.rsqrt(jnp.mean(tensor * tensor, axis=-1, keepdims=True) + EPS) * gains_row


def norm_back(tensor, gains_row, cotangent):
    return jax.vjp(rms_norm, tensor, gains_row)[1](cotangent)


def smooth_gelu(tensor):
    return jax.nn.gelu(tensor, approximate=True)


def renew_state(state_now, gate_values):
    return state_now * jax.nn.sigmoid(gate_values[2] + 1.0) + jnp.tanh(
        gate_values[0]
    ) * jax.nn.sigmoid(gate_values[1] - 1.0)


def split_heads(tensor):
    return tensor.reshape(tensor.shape[0], tensor.shape[1], tensor.shape[2] // DH, DH)


def merge_heads(tensor):
    return tensor.reshape(tensor.shape[0], tensor.shape[1], tensor.shape[2] * DH)


def score_grid(queries, key_rows, bias_add, allowed):
    scores = jnp.einsum(
        "iqhd,ikhd->ihqk", queries, key_rows, preferred_element_type=jnp.float32
    ) / math.sqrt(DH)
    if bias_add is not None:
        scores = scores + bias_add[None]
    return jnp.where(allowed[:, None], scores, NEGATIVE)


def attend_forward(queries, key_rows, values, bias_add, allowed):
    scores = score_grid(queries, key_rows, bias_add, allowed)
    row_max = jnp.max(scores, axis=-1, keepdims=True)
    weights = jnp.exp(scores - row_max)
    row_total = jnp.sum(weights, axis=-1, keepdims=True)
    attn_probs = (weights / row_total).astype(jnp.bfloat16)
    mixed_heads = jnp.einsum(
        "ihqk,ikhd->iqhd", attn_probs, values, preferred_element_type=jnp.float32
    )
    return (merge_heads(mixed_heads.astype(jnp.bfloat16)), row_max + jnp.log(row_total))


def attention_backward_pass(queries, key_rows, values, bias_add, allowed, log_total, grad_mixed):
    scores = score_grid(queries, key_rows, bias_add, allowed)
    attn_probs = jnp.exp(scores - log_total)
    probs_grad = jnp.einsum(
        "iqhd,ikhd->ihqk", grad_mixed, values, preferred_element_type=jnp.float32
    )
    scores_grad = attn_probs * (
        probs_grad - jnp.sum(attn_probs * probs_grad, axis=-1, keepdims=True)
    )
    scores_grad = scores_grad.astype(jnp.bfloat16)
    values_grad = jnp.einsum(
        "ihqk,iqhd->ikhd",
        attn_probs.astype(jnp.bfloat16),
        grad_mixed,
        preferred_element_type=jnp.float32,
    )
    queries_grad = jnp.einsum(
        "ihqk,ikhd->iqhd", scores_grad, key_rows, preferred_element_type=jnp.float32
    ) / math.sqrt(DH)
    keys_grad = jnp.einsum(
        "ihqk,iqhd->ikhd", scores_grad, queries, preferred_element_type=jnp.float32
    ) / math.sqrt(DH)
    return (
        merge_heads(queries_grad),
        merge_heads(keys_grad),
        merge_heads(values_grad),
        scores_grad,
    )


def diagonal_sums(grid_values):
    num_heads, num_rows, num_cols = grid_values.shape
    flat = grid_values.reshape(num_heads, num_rows * num_cols)
    flat = jnp.pad(flat, ((0, 0), (0, num_rows)))
    sums = jnp.sum(flat.reshape(num_heads, num_rows, num_cols + 1), axis=1)
    return sums[:, num_rows:0:-1]


def toeplitz_grid(per_offset, num_rows):
    num_cols = 2 * num_rows
    line = jnp.pad(per_offset[::-1].T, ((0, 0), (1, num_cols - num_rows)))
    flat = jnp.tile(line, (1, num_rows))[:, : num_rows * num_cols]
    return flat.reshape(-1, num_rows, num_cols)


def sum_rows(partial_value):
    return lax.psum_scatter(
        partial_value.astype(jnp.bfloat16), "state", scatter_dimension=1, tiled=True
    ).astype(jnp.float32)


def whole_rows(partial_value):
    return lax.all_gather(partial_value, "state", axis=1, tiled=True)


def shards(
    tokens,
    carried_state,
    past_keys,
    fresh_start,
    valid_count,
    bucket_ids,
    grad_output,
    grad_state,
    norm_gains,
    token_qkv,
    token_out,
    bias_table,
    mlp_up,
    mlp_down,
    state_qkv,
    state_gates,
    initial_state,
):
    item_count, blocks, share_rows, model_width = tokens.shape
    groups = lax.axis_size("state")
    state_rank = lax.axis_index("state")
    window_width = share_rows * groups
    vector_rows = carried_state.shape[1] * groups
    local_width = token_qkv.shape[2]
    qkv_full, out_full, up_full, down_full, sqkv_full, gates_full, initial_full = (
        lax.all_gather(token_qkv, "dp", axis=0, tiled=True),
        lax.all_gather(token_out, "dp", axis=0, tiled=True),
        lax.all_gather(mlp_up, "dp", axis=0, tiled=True),
        lax.all_gather(mlp_down, "dp", axis=0, tiled=True),
        lax.all_gather(state_qkv, "dp", axis=0, tiled=True),
        lax.all_gather(state_gates, "dp", axis=0, tiled=True),
        lax.all_gather(initial_state, "dp", axis=1, tiled=True),
    )
    gates_used = lax.dynamic_slice_in_dim(gates_full, state_rank * local_width, local_width, 2)
    one_hot = (bucket_ids[:, None] == jnp.arange(bias_table.shape[0])[None, :]).astype(jnp.float32)
    per_offset = jnp.dot(one_hot, bias_table, precision=HIGHEST)
    query_pos = jnp.arange(window_width)[:, None]
    key_pos = jnp.arange(2 * window_width)[None, :]
    offset = window_width + query_pos - key_pos
    inside = (offset >= 0) & (offset < window_width)
    bias_grid = toeplitz_grid(per_offset, window_width)
    token_bias = jnp.pad(bias_grid, ((0, 0), (0, 0), (0, vector_rows)))
    is_fresh = fresh_start == 1
    state_now = jnp.where(
        is_fresh[:, None, None], initial_full.astype(jnp.float32)[None], carried_state
    )
    past_key = past_keys[:, :, 0]
    past_value = past_keys[:, :, 1]
    past_ok = jnp.broadcast_to(~is_fresh[:, None], (item_count, window_width))
    gains_token, gains_middle, gains_state = (norm_gains[0], norm_gains[1], norm_gains[2])
    share_pos = state_rank * share_rows + jnp.arange(share_rows)
    square_sums = jnp.zeros((3,), jnp.float32)
    valid_total = jnp.zeros((), jnp.float32)
    kept_values = []
    results = []
    for block_at in range(blocks):
        token_ok = (
            block_at * window_width + jnp.arange(window_width)[None, :] < valid_count[:, None]
        )
        inputs = tokens[:, block_at].astype(jnp.float32)
        normed, state_normed = (
            lax.all_gather(
                rms_norm(inputs, gains_token).astype(jnp.bfloat16), "state", axis=1, tiled=True
            ),
            lax.all_gather(
                rms_norm(state_now, gains_state).astype(jnp.bfloat16), "state", axis=1, tiled=True
            ),
        )
        project = jnp.einsum(
            "iwd,dch->ciwh", normed, qkv_full, preferred_element_type=jnp.float32
        ).astype(jnp.bfloat16)
        state_project = jnp.einsum(
            "ind,dch->cinh", state_normed, sqkv_full, preferred_element_type=jnp.float32
        ).astype(jnp.bfloat16)
        token_keys = jnp.concatenate([past_key, project[1], state_project[1]], axis=1)
        token_values = jnp.concatenate([past_value, project[2], state_project[2]], axis=1)
        window_ok = inside[None] & jnp.concatenate([past_ok, token_ok], axis=1)[:, None, :]
        token_allowed = jnp.concatenate(
            [window_ok, jnp.ones((item_count, window_width, vector_rows), jnp.bool_)], axis=2
        )
        mixed_heads, token_total = attend_forward(
            split_heads(project[0]),
            split_heads(token_keys),
            split_heads(token_values),
            token_bias,
            token_allowed,
        )
        branch = sum_rows(
            jnp.einsum("iwh,dh->iwd", mixed_heads, out_full, preferred_element_type=jnp.float32)
        )
        middle = inputs + branch
        middle_normed = lax.all_gather(
            rms_norm(middle, gains_middle).astype(jnp.bfloat16), "state", axis=1, tiled=True
        )
        up_values = jnp.einsum(
            "iwd,df->iwf", middle_normed, up_full, preferred_element_type=jnp.float32
        )
        hidden = smooth_gelu(up_values).astype(jnp.bfloat16)
        feed_out = sum_rows(
            jnp.einsum("iwf,df->iwd", hidden, down_full, preferred_element_type=jnp.float32)
        )
        result = middle + feed_out
        results.append(result.astype(jnp.bfloat16))
        share_ok = (block_at * window_width + share_pos[None, :] < valid_count[:, None]).astype(
            jnp.float32
        )[:, :, None]
        square_sums = square_sums + jnp.stack(
            [
                jnp.sum(share_ok * result * result),
                jnp.sum(share_ok * branch * branch),
                jnp.sum(share_ok * feed_out * feed_out),
            ]
        )
        valid_total = valid_total + jnp.sum(share_ok)
        state_keys = jnp.concatenate([state_project[1], project[1]], axis=1)
        state_values = jnp.concatenate([state_project[2], project[2]], axis=1)
        state_allowed = jnp.concatenate(
            [
                jnp.ones((item_count, vector_rows, vector_rows), jnp.bool_),
                jnp.broadcast_to(token_ok[:, None, :], (item_count, vector_rows, window_width)),
            ],
            axis=2,
        )
        state_mixed, state_total = attend_forward(
            split_heads(state_project[0]),
            split_heads(state_keys),
            split_heads(state_values),
            None,
            state_allowed,
        )
        gate_source = state_mixed
        gate_values = lax.psum_scatter(
            jnp.einsum(
                "inh,dch->cind", state_mixed, gates_used, preferred_element_type=jnp.float32
            ).astype(jnp.bfloat16),
            "state",
            scatter_dimension=2,
            tiled=True,
        ).astype(jnp.float32)
        kept_values.append(
            (
                inputs,
                normed,
                state_normed,
                project,
                state_project,
                token_keys,
                token_values,
                token_allowed,
                mixed_heads,
                token_total,
                middle,
                middle_normed,
                up_values,
                hidden,
                state_keys,
                state_values,
                state_allowed,
                state_total,
                gate_source,
                gate_values,
                state_now,
            )
        )
        state_now = renew_state(state_now, gate_values)
        past_key, past_value, past_ok = (project[1], project[2], token_ok)
    square_sums, valid_total = lax.psum((square_sums, valid_total), ("dp", "state"))
    rms_stats = jnp.sqrt(square_sums / valid_total)
    qkv_grad = jnp.zeros(qkv_full.shape, jnp.float32)
    out_grad = jnp.zeros(out_full.shape, jnp.float32)
    up_grad = jnp.zeros(up_full.shape, jnp.float32)
    down_grad = jnp.zeros(down_full.shape, jnp.float32)
    sqkv_grad = jnp.zeros(sqkv_full.shape, jnp.float32)
    gate_grad = jnp.zeros(gates_used.shape, jnp.float32)
    bias_grad = jnp.zeros(bias_grid.shape, jnp.float32)
    gain_token_grad = jnp.zeros((model_width,), jnp.float32)
    gain_middle_grad = jnp.zeros((model_width,), jnp.float32)
    gain_state_grad = jnp.zeros((model_width,), jnp.float32)
    state_grad = grad_state
    carried_key_rows = jnp.zeros(past_keys[:, :, 0].shape, jnp.float32)
    carry_value = jnp.zeros(past_keys[:, :, 0].shape, jnp.float32)
    token_grads = [None] * blocks
    for block_at in reversed(range(blocks)):
        (
            inputs,
            normed,
            state_normed,
            project,
            state_project,
            token_keys,
            token_values,
            token_allowed,
            mixed_heads,
            token_total,
            middle,
            middle_normed,
            up_values,
            hidden,
            state_keys,
            state_values,
            state_allowed,
            state_total,
            gate_source,
            gate_values,
            state_before,
        ) = kept_values[block_at]
        direct_grad, gates_grad = jax.vjp(renew_state, state_before, gate_values)[1](state_grad)
        gates_low = gates_grad.astype(jnp.bfloat16)
        gates_rows = lax.all_gather(gates_low, "state", axis=2, tiled=True)
        state_mixed_grad = jnp.einsum(
            "cind,dch->inh", gates_rows, gates_used, preferred_element_type=jnp.float32
        ).astype(jnp.bfloat16)
        gate_grad = gate_grad + jnp.einsum(
            "inh,cind->dch", gate_source, gates_rows, preferred_element_type=jnp.float32
        )
        state_query_gradient, state_keys_gradient, state_values_gradient, discarded_output = (
            attention_backward_pass(
                split_heads(state_project[0]),
                split_heads(state_keys),
                split_heads(state_values),
                None,
                state_allowed,
                state_total,
                split_heads(state_mixed_grad),
            )
        )
        out_share = grad_output[:, block_at]
        out_whole = whole_rows(out_share)
        down_grad = down_grad + jnp.einsum(
            "iwf,iwd->df", hidden, out_whole, preferred_element_type=jnp.float32
        )
        hidden_grad = jnp.einsum(
            "iwd,df->iwf", out_whole, down_full, preferred_element_type=jnp.float32
        )
        up_values_grad = jax.vjp(smooth_gelu, up_values)[1](hidden_grad)[0].astype(jnp.bfloat16)
        up_grad = up_grad + jnp.einsum(
            "iwd,iwf->df", middle_normed, up_values_grad, preferred_element_type=jnp.float32
        )
        middle_normed_grad = lax.psum_scatter(
            jnp.einsum(
                "iwf,df->iwd", up_values_grad, up_full, preferred_element_type=jnp.float32
            ).astype(jnp.bfloat16),
            "state",
            scatter_dimension=1,
            tiled=True,
        ).astype(jnp.float32)
        middle_grad, gain_part = norm_back(middle, gains_middle, middle_normed_grad)
        middle_grad = out_share.astype(jnp.float32) + middle_grad
        gain_middle_grad = gain_middle_grad + gain_part
        branch_whole = whole_rows(middle_grad.astype(jnp.bfloat16))
        out_grad = out_grad + jnp.einsum(
            "iwh,iwd->dh", mixed_heads, branch_whole, preferred_element_type=jnp.float32
        )
        mixed_grad = jnp.einsum(
            "iwd,dh->iwh", branch_whole, out_full, preferred_element_type=jnp.float32
        ).astype(jnp.bfloat16)
        query_grad, token_keys_gradient, tvalues_grad, scores_grad = attention_backward_pass(
            split_heads(project[0]),
            split_heads(token_keys),
            split_heads(token_values),
            token_bias,
            token_allowed,
            token_total,
            split_heads(mixed_grad),
        )
        bias_grad = bias_grad + jnp.sum(
            scores_grad[:, :, :, : 2 * window_width].astype(jnp.float32), axis=0
        )
        key_gradient_rows = (
            token_keys_gradient[:, window_width : 2 * window_width]
            + state_keys_gradient[:, vector_rows:]
            + carried_key_rows
        )
        value_grad = (
            tvalues_grad[:, window_width : 2 * window_width]
            + state_values_gradient[:, vector_rows:]
            + carry_value
        )
        state_key_gradient = (
            token_keys_gradient[:, 2 * window_width :] + state_keys_gradient[:, :vector_rows]
        )
        state_value_gradient = (
            tvalues_grad[:, 2 * window_width :] + state_values_gradient[:, :vector_rows]
        )
        project_grad = jnp.stack([query_grad, key_gradient_rows, value_grad]).astype(jnp.bfloat16)
        state_projection_gradient = jnp.stack(
            [state_query_gradient, state_key_gradient, state_value_gradient]
        ).astype(jnp.bfloat16)
        qkv_grad = qkv_grad + jnp.einsum(
            "iwd,ciwh->dch", normed, project_grad, preferred_element_type=jnp.float32
        )
        sqkv_grad = sqkv_grad + jnp.einsum(
            "ind,cinh->dch",
            state_normed,
            state_projection_gradient,
            preferred_element_type=jnp.float32,
        )
        normed_grad, state_normed_grad = (
            lax.psum_scatter(
                jnp.einsum(
                    "ciwh,dch->iwd", project_grad, qkv_full, preferred_element_type=jnp.float32
                ).astype(jnp.bfloat16),
                "state",
                scatter_dimension=1,
                tiled=True,
            ).astype(jnp.float32),
            lax.psum_scatter(
                jnp.einsum(
                    "cinh,dch->ind",
                    state_projection_gradient,
                    sqkv_full,
                    preferred_element_type=jnp.float32,
                ).astype(jnp.bfloat16),
                "state",
                scatter_dimension=1,
                tiled=True,
            ).astype(jnp.float32),
        )
        input_grad, gain_part = norm_back(inputs, gains_token, normed_grad)
        gain_token_grad = gain_token_grad + gain_part
        token_grads[block_at] = (middle_grad + input_grad).astype(jnp.bfloat16)
        state_norm_grad, gain_part = norm_back(state_before, gains_state, state_normed_grad)
        gain_state_grad = gain_state_grad + gain_part
        state_grad = direct_grad + state_norm_grad
        carried_key_rows = token_keys_gradient[:, :window_width]
        carry_value = tvalues_grad[:, :window_width]
    carried_grad = jnp.where(is_fresh[:, None, None], 0.0, state_grad)
    initial_part = jnp.sum(jnp.where(is_fresh[:, None, None], state_grad, 0.0), axis=0)
    past_grad = jnp.stack([carried_key_rows, carry_value], axis=2)
    table_part = jnp.dot(one_hot.T, diagonal_sums(bias_grad).T, precision=HIGHEST)
    gain_columns = jnp.stack([gain_token_grad, gain_middle_grad, gain_state_grad], axis=1)
    summed = (
        lax.psum_scatter(
            qkv_grad.astype(jnp.bfloat16), "dp", scatter_dimension=0, tiled=True
        ).astype(jnp.float32),
        lax.psum_scatter(
            out_grad.astype(jnp.bfloat16), "dp", scatter_dimension=0, tiled=True
        ).astype(jnp.float32),
        lax.psum_scatter(
            table_part.astype(jnp.bfloat16), "dp", scatter_dimension=0, tiled=True
        ).astype(jnp.float32),
        lax.psum_scatter(
            up_grad.astype(jnp.bfloat16), "dp", scatter_dimension=0, tiled=True
        ).astype(jnp.float32),
        lax.psum_scatter(
            down_grad.astype(jnp.bfloat16), "dp", scatter_dimension=0, tiled=True
        ).astype(jnp.float32),
        lax.psum_scatter(
            sqkv_grad.astype(jnp.bfloat16), "dp", scatter_dimension=0, tiled=True
        ).astype(jnp.float32),
        lax.psum_scatter(
            initial_part.astype(jnp.bfloat16), "dp", scatter_dimension=1, tiled=True
        ).astype(jnp.float32),
        lax.psum_scatter(
            gate_grad.astype(jnp.bfloat16), "dp", scatter_dimension=0, tiled=True
        ).astype(jnp.float32),
        lax.psum_scatter(
            gain_columns.astype(jnp.bfloat16), "dp", scatter_dimension=0, tiled=True
        ).astype(jnp.float32),
    )
    gate_pieces, gain_pieces = (
        lax.all_to_all(
            summed[7][:, :, None, :].astype(jnp.bfloat16),
            "state",
            split_axis=0,
            concat_axis=2,
            tiled=True,
        ).astype(jnp.float32),
        lax.all_to_all(
            summed[8][:, :, None, None].astype(jnp.bfloat16),
            "state",
            split_axis=0,
            concat_axis=2,
            tiled=True,
        ).astype(jnp.float32),
    )
    gains_grad = jnp.sum(gain_pieces, axis=(2, 3)).T
    gates_grad_out = gate_pieces.reshape(
        gate_pieces.shape[0], gate_pieces.shape[1], gate_pieces.shape[2] * gate_pieces.shape[3]
    )
    return (
        jnp.stack(results, axis=1),
        state_now,
        rms_stats,
        jnp.stack(token_grads, axis=1),
        carried_grad,
        past_grad,
        gains_grad,
        summed[0],
        summed[1],
        summed[2],
        summed[3],
        summed[4],
        summed[5],
        gates_grad_out,
        summed[6],
    )


MESH = pl.DeviceIdType.MESH
NN = (((1,), (0,)), ((), ()))
NT = (((1,), (1,)), ((), ()))
TN = (((0,), (0,)), ((), ()))
VMEM_BYTES = 127 * 2**19


class Place:
    def __init__(self):
        chip_core, level = lax.axis_index("dp"), lax.axis_index("state")
        core, low = lax.rem(chip_core, 2), lax.rem(level, 2)
        x, y = lax.rem(chip_core // 2, 2), chip_core // 4
        flip = lambda bit: 1 - 2 * bit
        self.dp, self.core, self.level, self.half = chip_core, core, level, level // 2
        self.rank = 2 * low + core
        self.ranks = [self.rank, 2 * low + 1 - core, 2 * (1 - low) + core, 2 * (1 - low) + 1 - core]
        self.mates = [
            None,
            (chip_core + flip(core), level),
            (chip_core, level + flip(low)),
            (chip_core + flip(core), level + flip(low)),
        ]
        self.planes = [2 * y + x, 2 * y + 1 - x, 2 * (1 - y) + x, 2 * (1 - y) + 1 - x]
        self.plane_mates = [
            None,
            (chip_core + 2 * flip(x), level),
            (chip_core + 4 * flip(y), level),
            (chip_core + 2 * flip(x) + 4 * flip(y), level),
        ]
        first = chip_core - core
        self.there = (first + low, 2 * core + self.half)
        self.across = (first + low, 2 * (1 - core) + self.half)
        self.from_there = (first + self.half, 2 * low + core)
        self.from_across = (first + 1 - self.half, 2 * low + core)
        self.stays = (core == low) & (self.half == core)


def rows_at(start, size, step=128):
    return pl.ds(pl.multiple_of(start, step), size)


def rows_of(ref, start, size, step=128):
    at = rows_at(start, size, step)
    return ref.at[:, at] if len(ref.shape) == 3 else ref.at[at]


class Links:
    def __init__(self, send_sems, recv_sems):
        self.send_sems, self.recv_sems = send_sems, recv_sems
        self.used = 0
        self.open_sends = []
        self.open_turns = []

    def plan(self, source, target, device):
        at = self.used
        self.used += 1
        return pltpu.make_async_remote_copy(
            src_ref=source,
            dst_ref=target,
            send_sem=self.send_sems.at[at],
            recv_sem=self.recv_sems.at[at],
            device_id=device,
            device_id_type=MESH,
        )

    def copy(self, source, target, device):
        moved = self.plan(source, target, device)
        moved.start()
        self.open_sends.append(moved)
        return moved

    def sent(self, moved):
        self.open_sends = [other for other in self.open_sends if other is not moved]
        moved.wait_send()

    def close(self):
        for moved in self.open_sends:
            moved.wait_send()
        for turn in self.open_turns:
            turn.sent()
        self.open_sends, self.open_turns = [], []


def greet(devices, turned=None):
    barrier = pltpu.get_barrier_semaphore()
    for device in devices:
        pl.semaphore_signal(barrier, inc=1, device_id=device, device_id_type=MESH)
    if turned is None:
        pl.semaphore_wait(barrier, len(devices))
    else:
        moves = jnp.logical_not(turned.stays)

        @pl.when(moves)
        def _():
            pl.semaphore_signal(barrier, inc=1, device_id=turned.from_there, device_id_type=MESH)

        pl.semaphore_wait(barrier, len(devices) + moves.astype(jnp.int32))


class Turn:
    def __init__(self, links, here, source, target, device):
        self.stays = here.stays
        self.moved = links.plan(source, target, device)
        self.kept = pltpu.make_async_copy(source, target, links.recv_sems.at[links.used - 1])
        links.open_turns.append(self)

        @pl.when(jnp.logical_not(self.stays))
        def _():
            self.moved.start()

        @pl.when(self.stays)
        def _():
            self.kept.start()

    def arrived(self):
        @pl.when(jnp.logical_not(self.stays))
        def _():
            self.moved.wait_recv()

        @pl.when(self.stays)
        def _():
            self.kept.wait()

    def sent(self):
        @pl.when(jnp.logical_not(self.stays))
        def _():
            self.moved.wait_send()


class WeightGather:
    def __init__(self, links, here, local, full):
        self.links, self.here, self.local, self.full = links, here, local, full
        self.rows = local.shape[-2]

    def enter(self):
        target = rows_of(self.full, self.here.dp * self.rows, self.rows)
        self.turn = Turn(self.links, self.here, self.local, target, self.here.there)
        self.cross = self.links.copy(self.local, target, self.here.across)
        return self

    def block(self, k):
        return rows_of(self.full, self.here.planes[k] * 2 * self.rows, 2 * self.rows)

    def half(self, k, which):
        start = self.here.planes[k] * 2 * self.rows + which * self.rows
        return rows_of(self.full, start, self.rows)

    def spread(self):
        self.turn.arrived()
        self.cross.wait_recv()
        mates = self.here.plane_mates
        self.over_x = self.links.copy(self.block(0), self.block(0), mates[1])
        self.over_y = self.links.copy(self.block(0), self.block(0), mates[2])

    def forward(self):
        mates = self.here.plane_mates
        self.over_x.wait_recv()
        self.corner_0 = self.links.copy(self.half(1, 0), self.half(1, 0), mates[2])
        self.over_y.wait_recv()
        self.corner_1 = self.links.copy(self.half(2, 1), self.half(2, 1), mates[1])

    def finish(self):
        self.corner_0.wait_recv()
        self.corner_1.wait_recv()


class GateGather:
    def __init__(self, links, here, local, full, sem):
        self.links, self.here, self.local, self.full, self.sem = links, here, local, full, sem
        self.rows = local.shape[-2]

    def block(self, k):
        start = (2 * self.here.planes[k] + self.here.core) * self.rows
        return rows_of(self.full, start, self.rows)

    def part(self, k, which):
        size = self.rows // 2
        start = (2 * self.here.planes[k] + self.here.core) * self.rows + which * size
        return rows_of(self.full, start, size, 64)

    def spread(self):
        mates, sibling = self.here.plane_mates, self.here.mates[1]
        self.over_x = self.links.copy(self.local, self.block(0), mates[1])
        self.over_y = self.links.copy(self.local, self.block(0), mates[2])
        self.near = [self.links.copy(self.local, self.block(0), sibling)]
        self.kept = pltpu.make_async_copy(self.local, self.block(0), self.sem)
        self.kept.start()

    def forward(self):
        mates, sibling = self.here.plane_mates, self.here.mates[1]
        self.over_x.wait_recv()
        self.corner_0 = self.links.copy(self.part(1, 0), self.part(1, 0), mates[2])
        self.near.append(self.links.copy(self.block(1), self.block(1), sibling))
        self.over_y.wait_recv()
        self.corner_1 = self.links.copy(self.part(2, 1), self.part(2, 1), mates[1])
        self.near.append(self.links.copy(self.block(2), self.block(2), sibling))

    def last(self):
        self.corner_0.wait_recv()
        self.corner_1.wait_recv()
        self.near.append(self.links.copy(self.block(3), self.block(3), self.here.mates[1]))

    def finish(self):
        self.kept.wait()
        for moved in self.near:
            moved.wait_recv()


class RowGather:
    def __init__(self, links, here, ref, base, rows):
        self.links, self.here, self.ref, self.base, self.rows = links, here, ref, base, rows

    def part(self, k):
        return self.ref.at[rows_at(self.base + self.here.ranks[k] * self.rows, self.rows)]

    def start(self):
        own, mates = self.part(0), self.here.mates
        self.far = self.links.copy(own, own, mates[2])
        self.near = self.links.copy(own, own, mates[1])
        return self

    def ready(self, k):
        if k == 1:
            self.near.wait_recv()
        elif k == 2:
            self.far.wait_recv()
            block = self.part(2)
            self.last = self.links.copy(block, block, self.here.mates[1])
        elif k == 3:
            self.last.wait_recv()

    def sent(self):
        for moved in (self.far, self.near, self.last):
            self.links.sent(moved)


class RowSum:
    def __init__(self, links, here, stage, near_in, far_out, far_in, rows):
        self.links, self.here, self.rows = links, here, rows
        self.stage, self.near_in, self.far_out, self.far_in = stage, near_in, far_out, far_in

    def part(self, k):
        return self.stage.at[rows_at(self.here.ranks[k] * self.rows, self.rows)]

    def fill(self, make_rows):
        sibling = self.here.mates[1]
        for k, slot in ((3, 0), (1, 1)):
            self.part(k)[...] = make_rows(self.here.ranks[k]).astype(jnp.bfloat16)
            moved = self.links.copy(self.part(k), self.near_in.at[slot], sibling)
            if slot == 0:
                self.near_far = moved
            else:
                self.near_own = moved
        for k in (2, 0):
            self.part(k)[...] = make_rows(self.here.ranks[k]).astype(jnp.bfloat16)
        return self

    def forward(self):
        self.near_far.wait_recv()
        summed = self.part(2)[...].astype(jnp.float32) + self.near_in[0].astype(jnp.float32)
        self.far_out[...] = summed.astype(jnp.bfloat16)
        self.far = self.links.copy(self.far_out, self.far_in, self.here.mates[2])
        return self

    def sent(self):
        for moved in (self.near_far, self.near_own, self.far):
            self.links.sent(moved)

    def split(self):
        self.near_far.wait_recv()
        summed = self.part(2)[...].astype(jnp.float32) + self.near_in[0].astype(jnp.float32)
        self.near_own.wait_recv()
        own = self.part(0)[...].astype(jnp.float32) + self.near_in[1].astype(jnp.float32)
        return summed.astype(jnp.bfloat16), own

    def finish(self):
        self.near_own.wait_recv()
        self.far.wait_recv()
        return (
            self.part(0)[...].astype(jnp.float32)
            + self.near_in[1].astype(jnp.float32)
            + self.far_in[...].astype(jnp.float32)
        )


def row_sum_scratch(rows, width):
    return [
        pltpu.VMEM((4 * rows, width), jnp.bfloat16),
        pltpu.VMEM((2, rows, width), jnp.bfloat16),
        pltpu.VMEM((rows, width), jnp.bfloat16),
        pltpu.VMEM((rows, width), jnp.bfloat16),
    ]


def dot(left, right, dims):
    return lax.dot_general(left, right, dims, preferred_element_type=jnp.float32)


def scale_of(tensor):
    return lax.rsqrt(jnp.mean(tensor * tensor, axis=-1, keepdims=True) + EPS)


def rms_back(tensor, gains_row, cotangent):
    scale = scale_of(tensor)
    weighted = cotangent * gains_row
    inner = jnp.mean(tensor * weighted, axis=-1, keepdims=True)
    straight = scale * weighted - tensor * (scale * scale * scale * inner)
    return straight, jnp.sum(cotangent * tensor * scale, axis=0, keepdims=True)


def row_mask(facts, start, rows):
    place_of = lax.broadcasted_iota(jnp.int32, (rows, 1), 0) + start
    return jnp.where(place_of.astype(jnp.float32) < facts[2:3, 0:1], 1.0, 0.0)


def bias_tiles(lines_ref, tiles_ref, heads, width, scale=1.0):
    for head in range(heads):
        line = lines_ref[head : head + 1, :] * scale
        spread = jnp.broadcast_to(line, (tiles_ref.shape[1], line.shape[1]))
        tiles_ref[head] = pltpu.roll(spread, 0, 1, stride=1, stride_axis=0)[:, :width]


def softmax_pair(first, second):
    top = jnp.maximum(
        jnp.max(first, axis=-1, keepdims=True), jnp.max(second, axis=-1, keepdims=True)
    )
    first, second = jnp.exp(first - top), jnp.exp(second - top)
    total = jnp.sum(first, axis=-1, keepdims=True) + jnp.sum(second, axis=-1, keepdims=True)
    share = 1.0 / total
    return (
        (first * share).astype(jnp.bfloat16),
        (second * share).astype(jnp.bfloat16),
        top + jnp.log(total),
    )


TILE = 256
LOG2E = math.log2(math.e)
ROOT = 1.0 / math.sqrt(DH)


def forward_kernel(
    x_in, carried_in, initial_in, far_past, facts_in, far_gout, gstate_in, gains_ref,
    wst_in, wtok_in, wout_in, gates_in, far_wup, far_wdn,
    far_normed, far_snormed, far_queries, far_keys, far_values, far_state_qkv, far_lse, far_mixed,
    far_wst, far_wtok, far_wout, far_gates, far_x, far_s0, far_s1,
    far_gate_values, far_gstate_here, far_wup_grad, far_wdn_grad,
    smixed_rows, s2_ref, facts, feed_far, feed_own, result_own, middle_grad, branch_rows, small_sums,
    normed, snormed, queries, keys, values, state_qkv, lse_ref, mixed,
    wst, wtok, wout, gates, x_ref, s0_ref, s1_ref,
    smixed, tiles, initial_all, normed_send, gstate_send, s0_send, gate_values, wup, wdn, middle,
    middle_normed, gout_rows, gout, slope, hidden, up_grad, grad_stage, *rest,
):
    rs = [rest[4 * k : 4 * k + 4] for k in range(4)]
    links = Links(rest[16], rest[17])
    local_sems, keep_sems = rest[18], rest[19]
    kept = []

    def keep(source, target):
        moved = pltpu.make_async_copy(source, target, keep_sems.at[len(kept)])
        moved.start()
        kept.append(moved)

    here = Place()
    rank, ranks, mates = here.rank, here.ranks, here.mates
    rows = s0_ref.shape[0]
    window = 4 * rows
    width = queries.shape[1]
    heads = width // DH
    ring = [(lax.rem(here.dp + step, 8), here.level) for step in range(1, 8)]
    greet(ring + mates[2:] + [here.from_across], here)

    def turn(source, target):
        return Turn(links, here, source, target, here.there)

    part = initial_in.shape[1]
    own_columns = pl.ds(pl.multiple_of(here.dp * part, part), part)
    initial_moves = [links.copy(initial_in, initial_all.at[:, own_columns], mate) for mate in ring]
    facts_turn = turn(facts_in, facts)
    gather_wst = WeightGather(links, here, wst_in, wst).enter()
    initial_all[:, own_columns] = initial_in[...]
    for moved in initial_moves:
        moved.wait_recv()
    is_fresh = facts_in[3:4, :] > 0.5
    start = jnp.where(is_fresh, initial_all[...].astype(jnp.float32), carried_in[...])
    s0_send[...] = start
    normed_send[...] = (start * scale_of(start) * gains_ref[2:3, :]).astype(jnp.bfloat16)
    normed_turn = turn(normed_send, snormed.at[rows_at(here.level * rows, rows)])
    facts_turn.arrived()
    bias_tiles(facts, tiles, heads, 3 * TILE)
    gather_wst.spread()
    gather_wtok = WeightGather(links, here, wtok_in, wtok).enter()
    normed_turn.arrived()
    gather_s0 = RowGather(links, here, snormed, 0, rows).start()

    def enter_x(block):
        at = pl.ds(block * rows, rows)
        return turn(x_in.at[at], x_ref.at[at])

    def norm_x(block, moved):
        moved.arrived()
        x = x_ref[block * rows : (block + 1) * rows, :].astype(jnp.float32)
        normed[rows_at(block * window + rank * rows, rows), :] = (
            x * scale_of(x) * gains_ref[0:1, :]
        ).astype(jnp.bfloat16)
        return RowGather(links, here, normed, block * window, rows).start()

    x_turn_0 = enter_x(0)
    gather_wst.forward()
    gather_wtok.spread()
    x_turn_1 = enter_x(1)

    def key_mask(start, size):
        place_of = lax.broadcasted_iota(jnp.int32, (1, size), 1).astype(jnp.float32)
        place_of = place_of + float(start - window)
        own = jnp.where(place_of < facts[2:3, 0:size], 0.0, NEGATIVE)
        return jnp.where(place_of < 0.0, facts[3:4, 0:size] * NEGATIVE, own)

    def project_state(block, gather):
        for k in range(4):
            gather.ready(k)
            at = rows_at(block * window + ranks[k] * rows, rows)
            for c in range(3):
                state_qkv[at, c * width : (c + 1) * width] = dot(snormed[at, :], wst[c], NN).astype(
                    jnp.bfloat16
                )

    def project_token(block, gather):
        for k in range(4):
            gather.ready(k)
            at = rows_at(block * window + ranks[k] * rows, rows)
            later = rows_at((block + 1) * window + ranks[k] * rows, rows)
            queries[at, :] = dot(normed[at, :], wtok[0], NN).astype(jnp.bfloat16)
            keys[later, :] = dot(normed[at, :], wtok[1], NN).astype(jnp.bfloat16)
            values[later, :] = dot(normed[at, :], wtok[2], NN).astype(jnp.bfloat16)

    def state_attention(block):
        base = block * window
        own = pl.ds((block + 1) * window, window)
        whole = pl.ds(base, window)
        own_mask = key_mask(base + window, window)
        for head in range(heads):
            at = head * DH
            for tile in range(window // TILE):
                here_rows = pl.ds(base + tile * TILE, TILE)
                query = state_qkv[here_rows, at : at + DH]
                first = dot(query, state_qkv[whole, width + at : width + at + DH], NT) * ROOT
                second = dot(query, keys[own, at : at + DH], NT) * ROOT + own_mask
                first, second, lse = softmax_pair(first, second)
                out = dot(first, state_qkv[whole, 2 * width + at : 2 * width + at + DH], NN)
                out = out + dot(second, values[own, at : at + DH], NN)
                smixed[here_rows, at : at + DH] = out.astype(jnp.bfloat16)
                lse_ref[here_rows, heads + head : heads + head + 1] = lse

    def token_attention(block):
        base = block * window
        whole = pl.ds(base, window)
        for tile in range(window // TILE):
            near_mask = key_mask(base + tile * TILE, 3 * TILE)
            for head in range(heads):
                at = head * DH
                here_rows = pl.ds(base + tile * TILE, TILE)
                near = pl.ds(base + tile * TILE, 3 * TILE)
                query = queries[here_rows, at : at + DH]
                first = dot(query, keys[near, at : at + DH], NT) * ROOT + tiles[head] + near_mask
                second = dot(query, state_qkv[whole, width + at : width + at + DH], NT) * ROOT
                first, second, lse = softmax_pair(first, second)
                out = dot(first, values[near, at : at + DH], NN)
                out = out + dot(second, state_qkv[whole, 2 * width + at : 2 * width + at + DH], NN)
                mixed[here_rows, at : at + DH] = out.astype(jnp.bfloat16)
                lse_ref[here_rows, head : head + 1] = lse

    def spread_state(block, buffer):
        moves = []
        columns = pl.ds(pl.multiple_of(rank * width, width), width)
        for k in (2, 3, 1):
            source = smixed.at[rows_at(block * window + ranks[k] * rows, rows)]
            moves.append(links.copy(source, buffer.at[:, columns], mates[k]))
        buffer[:, columns] = smixed[rows_at(block * window + rank * rows, rows), :]
        return moves

    def renew(block, buffer, state_now):
        size = state_now.shape[1]
        source = buffer[...]
        parts = []
        for c in range(3):
            part = dot(source, gates[c], NT)
            gate_values[:, c * size : (c + 1) * size] = part
            parts.append(part)
        stored = pltpu.make_async_copy(
            gate_values, far_gate_values.at[pl.ds(block * rows, rows)], local_sems.at[0]
        )
        stored.start()
        new_state = state_now * jax.nn.sigmoid(parts[2] + 1.0) + jnp.tanh(parts[0]) * jax.nn.sigmoid(
            parts[1] - 1.0
        )
        return new_state, stored

    def out_rows(block):
        def make(which):
            return dot(mixed[rows_at(block * window + which * rows, rows), :], wout[...], NT)

        return make

    sums = [RowSum(links, here, *rs[block], rows) for block in range(2)]

    def finish_branch(block):
        branch = sums[block].finish()
        at = slice(block * rows, (block + 1) * rows)
        total = x_ref[at, :].astype(jnp.float32) + branch
        middle[at, :] = total
        middle_normed[rows_at(block * window + rank * rows, rows), :] = (
            total * scale_of(total) * gains_ref[1:2, :]
        ).astype(jnp.bfloat16)
        gather = RowGather(links, here, middle_normed, block * window, rows).start()
        share = row_mask(facts, block * window + rank * rows, rows)
        return jnp.sum(branch * branch * share, axis=0, keepdims=True), gather

    def rise(block, gather):
        root = math.sqrt(2.0 / math.pi)
        for k in range(4):
            gather.ready(k)
            at = rows_at(block * window + ranks[k] * rows, rows)
            value = dot(middle_normed[at, :], wup[...], NN)
            square = value * value
            bend = jnp.tanh(root * value * (1.0 + 0.044715 * square))
            half = 0.5 * (1.0 + bend)
            hidden[at, :] = (value * half).astype(jnp.bfloat16)
            slope[at, :] = half + 0.5 * value * (1.0 - bend * bend) * (
                root * (1.0 + 3.0 * 0.044715 * square)
            )

    def feed_sum(block):
        return RowSum(links, here, *rs[block], rows).fill(
            lambda which: dot(hidden[rows_at(block * window + which * rows, rows), :], wdn[...], NT)
        )

    def store_feed(block, summed):
        at = slice(block * rows, (block + 1) * rows)
        feed_far[block], own = summed.split()
        feed_own[at, :] = own.astype(jnp.bfloat16)
        result_own[at, :] = middle[at, :] + own

    def start_gout(block):
        at = slice(block * rows, (block + 1) * rows)
        gout[rows_at(block * window + rank * rows, rows), :] = gout_rows[at, :]
        return RowGather(links, here, gout, block * window, rows).start()

    def feed_back(block, gather):
        for k in range(4):
            gather.ready(k)
            at = rows_at(block * window + ranks[k] * rows, rows)
            up_grad[at, :] = (dot(gout[at, :], wdn[...], NN) * slope[at, :]).astype(jnp.bfloat16)
        return RowSum(links, here, *rs[2 + block], rows).fill(
            lambda which: dot(up_grad[rows_at(block * window + which * rows, rows), :], wup[...], NT)
        )

    def weight_grad(stage, left, right, target, sem):
        step = 256
        for part in range(stage.shape[0] // step):
            at = slice(part * step, (part + 1) * step)
            stage[at, :] = dot(left[:, at], right[...], TN).astype(jnp.bfloat16)
        stored = pltpu.make_async_copy(stage, target, sem)
        stored.start()
        return stored

    gather_wst.finish()
    keep(wst, far_wst)
    project_state(0, gather_s0)
    gather_x0 = norm_x(0, x_turn_0)
    gather_wtok.forward()
    gather_gates = GateGather(links, here, gates_in, gates, local_sems.at[3])
    gather_gates.spread()
    gather_wout = WeightGather(links, here, wout_in, wout).enter()
    past_turns = [
        turn(far_past.at[0], keys.at[pl.ds(0, window)]),
        turn(far_past.at[1], values.at[pl.ds(0, window)]),
    ]
    gather_x1 = norm_x(1, x_turn_1)
    gather_wtok.finish()
    keep(wtok, far_wtok)
    keep(x_ref, far_x)
    project_token(0, gather_x0)
    state_attention(0)
    a2a_0 = smixed_rows.at[pl.ds(0, rows)]
    a2a_1 = smixed_rows.at[pl.ds(rows, rows)]
    moves_0 = spread_state(0, a2a_0)
    s0_turn = turn(s0_send, s0_ref)
    gather_wout.spread()
    gather_wup = WeightGather(links, here, far_wup, wup).enter()
    project_token(1, gather_x1)
    keep(normed, far_normed)
    keep(queries, far_queries)
    gather_gates.forward()
    for moved in past_turns:
        moved.arrived()
    keep(keys, far_keys)
    keep(values, far_values)
    token_attention(0)
    gather_wout.forward()
    gather_gates.last()
    gather_wdn = WeightGather(links, here, far_wdn, wdn).enter()
    gather_wup.spread()
    gather_wout.finish()
    keep(wout, far_wout)
    sums[0].fill(out_rows(0))
    for moved in moves_0:
        moved.wait_recv()
    gather_gates.finish()
    keep(gates, far_gates)
    s0_turn.arrived()
    keep(s0_ref, far_s0)
    s1, keep_gates = renew(0, a2a_0, s0_ref[...])
    s1_ref[...] = s1
    keep(s1_ref, far_s1)
    snormed[rows_at(window + rank * rows, rows), :] = (s1 * scale_of(s1) * gains_ref[2:3, :]).astype(
        jnp.bfloat16
    )
    gather_s1 = RowGather(links, here, snormed, window, rows).start()
    sums[0].forward()
    gather_wup.forward()
    gather_wdn.spread()
    project_state(1, gather_s1)
    gout_turn = turn(far_gout, gout_rows)
    keep(snormed, far_snormed)
    keep(state_qkv, far_state_qkv)
    branch_total, gather_m0 = finish_branch(0)
    token_attention(1)
    keep(mixed, far_mixed)
    sums[1].fill(out_rows(1))
    gather_wdn.forward()
    state_attention(1)
    keep(lse_ref, far_lse)
    sums[1].forward()
    moves_1 = spread_state(1, a2a_1)
    gather_wup.finish()
    rise(0, gather_m0)
    more, gather_m1 = finish_branch(1)
    branch_total = branch_total + more
    gout_turn.arrived()
    gather_g0 = start_gout(0)
    gather_wdn.finish()
    sums[0].sent()
    feed_0 = feed_sum(0)
    for moved in moves_1:
        moved.wait_recv()
    keep_gates.wait()
    s2, keep_gates = renew(1, a2a_1, s1_ref[...])
    gstate_send[...] = gstate_in[...].astype(jnp.bfloat16)
    gstate_turn = turn(gstate_send, far_gstate_here)
    s2_ref[...] = s2.astype(jnp.bfloat16)
    rise(1, gather_m1)
    gather_g1 = start_gout(1)
    sums[1].sent()
    feed_1 = feed_sum(1)
    store_feed(0, feed_0)
    back_0 = feed_back(0, gather_g0)
    back_0.forward()
    back_1 = feed_back(1, gather_g1)
    store_feed(1, feed_1)
    keep_down = weight_grad(grad_stage, gout, hidden, far_wdn_grad, local_sems.at[1])
    back_1.forward()
    keep_up = weight_grad(hidden, middle_normed, up_grad, far_wup_grad, local_sems.at[2])
    gain_total = 0.0
    for block, back_here in ((1, back_1), (0, back_0)):
        at = slice(block * rows, (block + 1) * rows)
        straight, gain = rms_back(middle[at, :], gains_ref[1:2, :], back_here.finish())
        total = gout_rows[at, :].astype(jnp.float32) + straight
        middle_grad[at, :] = total
        branch_rows[at, :] = total.astype(jnp.bfloat16)
        gain_total = gain_total + gain
    small_sums[...] = jnp.concatenate(
        [gain_total, branch_total, jnp.zeros((6, gain_total.shape[1]), jnp.float32)],
        axis=0,
    )
    gstate_turn.arrived()
    keep_gates.wait()
    keep_down.wait()
    keep_up.wait()
    for moved in kept:
        moved.wait()
    links.close()


class PlaneSum:
    def __init__(self, links, here, grad, first_in, last_in):
        self.links, self.here, self.grad = links, here, grad
        self.first_in, self.last_in = first_in, last_in
        self.rows = first_in.shape[-2]

    def part(self, k, which):
        start = self.here.planes[k] * 2 * self.rows + which * self.rows
        return rows_of(self.grad, start, self.rows)

    def start(self):
        mates = self.here.plane_mates
        self.firsts = [
            self.links.copy(self.part(k, which), self.first_in.at[slot], mates[mate])
            for slot, (k, which, mate) in enumerate(((1, 0, 1), (3, 0, 1), (2, 1, 2), (3, 1, 2)))
        ]
        return self

    def add(self, k, which, arrived):
        part = self.part(k, which)
        part[...] = (part[...].astype(jnp.float32) + arrived[...].astype(jnp.float32)).astype(part.dtype)

    def forward(self):
        mates = self.here.plane_mates
        self.firsts[1].wait_recv()
        self.add(2, 0, self.first_in.at[1])
        self.last_0 = self.links.copy(self.part(2, 0), self.last_in.at[0], mates[2])
        self.firsts[3].wait_recv()
        self.add(1, 1, self.first_in.at[3])
        self.last_1 = self.links.copy(self.part(1, 1), self.last_in.at[1], mates[1])

    def finish(self):
        self.firsts[0].wait_recv()
        self.add(0, 0, self.first_in.at[0])
        self.firsts[2].wait_recv()
        self.add(0, 1, self.first_in.at[2])
        self.last_0.wait_recv()
        self.add(0, 0, self.last_in.at[0])
        self.last_1.wait_recv()
        self.add(0, 1, self.last_in.at[1])

    def result(self, which):
        return rows_of(self.grad, self.here.planes[0] * 2 * self.rows + which * self.rows, self.rows)


class FarPlaneSum(PlaneSum):
    def __init__(self, links, here, grad, first_in, last_in, held, held_sems):
        super().__init__(links, here, grad, first_in, last_in)
        self.held, self.held_sems = held, held_sems

    def bring(self, *pieces):
        self.brings = [
            pltpu.make_async_copy(self.part(k, which), self.held.at[slot], self.held_sems.at[slot])
            for slot, (k, which) in enumerate(pieces)
        ]
        for moved in self.brings:
            moved.start()

    def start(self):
        super().start()
        self.bring((2, 0), (1, 1))
        return self

    def add_to(self, slot, *arrived):
        total = self.held[slot].astype(jnp.float32)
        for piece in arrived:
            total = total + piece.astype(jnp.float32)
        self.held[slot] = total.astype(jnp.bfloat16)

    def forward(self):
        mates = self.here.plane_mates
        for moved in self.brings:
            moved.wait()
        self.firsts[1].wait_recv()
        self.add_to(0, self.first_in[1])
        self.last_0 = self.links.copy(self.held.at[0], self.last_in.at[0], mates[2])
        self.firsts[3].wait_recv()
        self.add_to(1, self.first_in[3])
        self.last_1 = self.links.copy(self.held.at[1], self.last_in.at[1], mates[1])

    def bring_own(self):
        self.links.sent(self.last_0)
        self.links.sent(self.last_1)
        self.bring((0, 0), (0, 1))

    def finish(self):
        for moved in self.brings:
            moved.wait()
        self.firsts[0].wait_recv()
        self.last_0.wait_recv()
        self.add_to(0, self.first_in[0], self.last_in[0])
        self.firsts[2].wait_recv()
        self.last_1.wait_recv()
        self.add_to(1, self.first_in[2], self.last_in[1])

    def result(self, which):
        return self.held.at[which]


class Settle:
    def __init__(self, links, here, summed, target):
        half = here.half
        self.straight = Turn(links, here, summed.result(half), target.at[0], here.from_there)
        self.crossed = links.copy(summed.result(1 - half), target.at[1], here.from_across)

    def arrived(self):
        self.straight.arrived()
        self.crossed.wait_recv()


class GateHome:
    def __init__(self, links, here, grad, target, rows):
        self.links, self.here = links, here
        low = lax.rem(here.level, 2)
        piece = rows // 4
        self.slot = target.at[2 * here.half + here.core]
        chip = here.dp - here.core + low
        self.stays = here.core == low
        self.moves = {}
        for step in range(4):
            to_level = lax.rem(here.level + step, 4)
            start = here.planes[0] * 2 * rows + low * rows + to_level * piece
            source = rows_of(grad, start, piece, piece)
            for core in range(2):
                moved = links.plan(source, self.slot, (chip, to_level))
                self.moves[step, core] = moved
                sends = here.core == core
                if step == 0:
                    kept = pltpu.make_async_copy(source, self.slot, links.recv_sems.at[links.used - 1])
                    self.moves[core] = kept

                    @pl.when(sends & self.stays)
                    def _(kept=kept):
                        kept.start()

                    sends = sends & jnp.logical_not(self.stays)

                @pl.when(sends)
                def _(moved=moved):
                    moved.start()

    def arrived(self):
        for step in range(4):
            comes = lax.rem(self.here.level + step, 2) == self.here.core
            for core in range(2):
                own = self.here.core == core
                if step == 0:

                    @pl.when(comes & own)
                    def _(kept=self.moves[core]):
                        kept.wait()

                    comes_here = comes & jnp.logical_not(own)
                else:
                    comes_here = comes

                @pl.when(comes_here)
                def _(moved=self.moves[step, core]):
                    moved.wait_recv()

                sent = own & jnp.logical_not(self.stays) if step == 0 else own

                @pl.when(sent)
                def _(moved=self.moves[step, core]):
                    moved.wait_send()


def cotangent_kernel(
    far_middle_grad, far_branch_rows, gstate_ref, far_x, s0_ref, s1_ref, far_gate_values, gains_ref, facts, facts_home,
    small_sums,
    far_normed, far_snormed, far_queries, far_keys, far_values, far_state_qkv, far_lse, far_mixed,
    far_smixed, far_wst, far_wtok, far_wout, far_gates, far_wup_grad, far_wdn_grad, far_feed, far_feed_own, far_result_own,
    far_state_out,
    block_home, state_home, tokens_home, past_home, carried_grad, initial_grad, totals,
    up_home, down_home, wst_home, wtok_home, wout_home, gates_home,
    gates, wout, queries, keys, state_qkv, values, lse_ref, mixed, wst, wtok,
    tiles, tile_grads, branch_grad, mixed_grad, gate_rows, state_mixed_grad, key_grad, value_grad,
    skey_grad, svalue_grad, token_cot, state_cot, gate_values, smixed_pair, sending,
    tokens_send, carried_send, carried_in, initial_send, initial_in,
    wst_grad, wtok_grad, wout_grad, gates_grad,
    wst_first, wtok_first, wout_first, gates_first, wst_last, wtok_last, wout_last, gates_last,
    up_first, down_first, up_last, down_last, up_held, down_held, ring_in, level_in, ring_send, level_send,
    late_in, late_level_in, late_send, late_level_send, gate_pair_in,
    feed_in, feed_own,
    *rest,
):
    rs = [rest[0:4], rest[4:8], rest[8:12]]
    links = Links(rest[12], rest[13])
    local_sems, held_sems, bring_sems = rest[14], rest[15], rest[16]
    here = Place()
    rank, ranks, mates = here.rank, here.ranks, here.mates
    rows = s0_ref.shape[0]
    window = 4 * rows
    width = queries.shape[1]
    heads = width // DH
    size = s0_ref.shape[1]
    reach = 2 * width
    other_half = pl.ds(pl.multiple_of((1 - here.core) * reach, reach), reach)
    own_half = pl.ds(pl.multiple_of(here.core * reach, reach), reach)

    def pair_rows(block):
        return rows_at((2 * block + here.core) * rows, rows)

    def own_branch(block):
        return branch_grad.at[rows_at(block * window + rank * rows, rows)]

    brings = []
    for source, target in (
        (far_branch_rows.at[pl.ds(rows, rows)], own_branch(1)),
        (far_branch_rows.at[pl.ds(0, rows)], own_branch(0)),
        (far_gates, gates),
        (far_wout, wout),
        (far_queries, queries),
        (far_keys, keys),
        (far_state_qkv, state_qkv),
        (far_values, values),
        (far_lse, lse_ref),
        (far_mixed, mixed),
        (far_wst, wst),
        (far_wtok, wtok),
        (far_x, tokens_send),
        (far_feed_own, feed_own),
        (far_smixed.at[pl.ds(0, rows), own_half], smixed_pair.at[pair_rows(0)]),
        (far_smixed.at[pl.ds(rows, rows), own_half], smixed_pair.at[pair_rows(1)]),
    ):
        brings.append(pltpu.make_async_copy(source, target, bring_sems.at[len(brings)]))
        brings[-1].start()
    ring = [(lax.rem(here.dp + step, 8), here.level) for step in range(1, 8)]
    other = here.dp + 1 - 2 * here.core
    column = [
        (chip, lax.rem(here.level + step, 4)) for step in range(1, 4) for chip in (here.dp, other)
    ]
    bring_gates = pltpu.make_async_copy(
        far_gate_values.at[pl.ds(rows, rows)], gate_values, local_sems.at[0]
    )
    bring_gates.start()
    greet(ring + column)
    def home(source, target):
        return Turn(links, here, source, target, here.from_there)

    def gates_back(block, state, state_grad):
        spot = pair_rows(block)
        keep = jax.nn.sigmoid(gate_values[:, 2 * size : 3 * size] + 1.0)
        fresh = jnp.tanh(gate_values[:, 0:size])
        let_in = jax.nn.sigmoid(gate_values[:, size : 2 * size] - 1.0)
        gate_rows[spot, 0:size] = (state_grad * let_in * (1.0 - fresh * fresh)).astype(jnp.bfloat16)
        gate_rows[spot, size : 2 * size] = (
            state_grad * fresh * let_in * (1.0 - let_in)
        ).astype(jnp.bfloat16)
        gate_rows[spot, 2 * size : 3 * size] = (
            state_grad * state * keep * (1.0 - keep)
        ).astype(jnp.bfloat16)
        out = dot(gate_rows[spot, 0:size], gates[0], NN)
        out = out + dot(gate_rows[spot, size : 2 * size], gates[1], NN)
        out = out + dot(gate_rows[spot, 2 * size : 3 * size], gates[2], NN)
        sending[...] = out.astype(jnp.bfloat16)
        spot = rows_at(block * window + rank * rows, rows)
        moves = []
        for k in (2, 3, 1):
            columns = pl.ds(pl.multiple_of(ranks[k] * width, width), width)
            moves.append(
                links.copy(sending.at[:, columns], state_mixed_grad.at[spot], mates[k])
            )
        columns = pl.ds(pl.multiple_of(rank * width, width), width)
        state_mixed_grad[spot, :] = sending[:, columns]
        pair = gate_rows.at[pair_rows(block)]
        return state_grad * keep, moves, links.copy(pair, pair, mates[1])

    lane = lax.broadcasted_iota(jnp.int32, (1, DH), 1)

    def widen(columns, value):
        high = value.astype(jnp.bfloat16).astype(jnp.float32)
        middle = (value - high).astype(jnp.bfloat16).astype(jnp.float32)
        more = jnp.where(lane == 1, high, jnp.where(lane == 2, middle, value - high - middle))
        more = jnp.where(lane == 0, 1.0, jnp.where(lane < 4, more, 0.0))
        return jnp.concatenate([columns, more.astype(jnp.bfloat16)], axis=1)

    plain = jnp.where((lane > 0) & (lane < 4), 1.0, 0.0)

    def beside(columns, mask=None):
        more = jnp.broadcast_to(plain, (columns.shape[0], DH))
        if mask is not None:
            more = jnp.where(lane == 0, mask, more)
        return jnp.concatenate([columns, more.astype(jnp.bfloat16)], axis=1)

    def key_mask(start, size):
        place_of = lax.broadcasted_iota(jnp.int32, (size, 1), 0).astype(jnp.float32)
        place_of = place_of + float(start - window)
        own = jnp.where(place_of < facts[2:3, 0:1], 0.0, NEGATIVE)
        return jnp.where(place_of < 0.0, facts[3:4, 0:1] * NEGATIVE, own)

    def token_back(block):
        base = block * window
        whole = pl.ds(base, window)
        for tile in range(window // TILE):
            near_mask = key_mask(base + tile * TILE, 3 * TILE)
            for head in range(heads):
                at = head * DH
                lanes = slice(at, at + DH)
                skey_lanes = slice(width + at, width + at + DH)
                svalue_lanes = slice(2 * width + at, 2 * width + at + DH)
                here_rows = pl.ds(base + tile * TILE, TILE)
                near = pl.ds(base + tile * TILE, 3 * TILE)
                query = queries[here_rows, lanes]
                out_grad = mixed_grad[here_rows, lanes]
                wide = widen(query, lse_ref[here_rows, head : head + 1] * (-1.0 / ROOT))
                inner = jnp.sum(
                    out_grad.astype(jnp.float32) * mixed[here_rows, lanes].astype(jnp.float32),
                    axis=-1,
                    keepdims=True,
                )
                wide_grad = widen(out_grad, -inner)
                first = jnp.exp2(
                    dot(wide, beside(keys[near, lanes], near_mask), NT) * (ROOT * LOG2E) + tiles[head]
                )
                second = jnp.exp2(
                    dot(wide, beside(state_qkv[whole, skey_lanes]), NT) * (ROOT * LOG2E)
                )
                first_low, second_low = first.astype(jnp.bfloat16), second.astype(jnp.bfloat16)
                first = first * dot(wide_grad, beside(values[near, lanes]), NT)
                second = second * dot(wide_grad, beside(state_qkv[whole, svalue_lanes]), NT)
                first_grad, second_grad = first.astype(jnp.bfloat16), second.astype(jnp.bfloat16)
                value_grad[near, lanes] += dot(first_low, out_grad, TN)
                svalue_grad[:, lanes] += dot(second_low, out_grad, TN)
                part = dot(first_grad, keys[near, lanes], NN) + dot(
                    second_grad, state_qkv[whole, skey_lanes], NN
                )
                token_cot[here_rows, lanes] = (part * ROOT).astype(jnp.bfloat16)
                key_grad[near, lanes] += dot(first_grad, query, TN) * ROOT
                skey_grad[:, lanes] += dot(second_grad, query, TN) * ROOT
                tile_grads[head] += first

    def state_back(block):
        base = block * window
        whole = pl.ds(base, window)
        own = pl.ds(base + window, window)
        own_mask = key_mask(base + window, window)
        for head in range(heads):
            at = head * DH
            lanes = slice(at, at + DH)
            skey_lanes = slice(width + at, width + at + DH)
            svalue_lanes = slice(2 * width + at, 2 * width + at + DH)
            wide_skeys = beside(state_qkv[whole, skey_lanes])
            wide_keys = beside(keys[own, lanes], own_mask)
            for tile in range(window // TILE):
                here_rows = pl.ds(base + tile * TILE, TILE)
                query = state_qkv[here_rows, lanes]
                out_grad = state_mixed_grad[here_rows, lanes]
                wide = widen(query, lse_ref[here_rows, heads + head : heads + head + 1] * (-1.0 / ROOT))
                first = jnp.exp2(dot(wide, wide_skeys, NT) * (ROOT * LOG2E))
                second = jnp.exp2(dot(wide, wide_keys, NT) * (ROOT * LOG2E))
                first_low, second_low = first.astype(jnp.bfloat16), second.astype(jnp.bfloat16)
                first_grad = dot(out_grad, state_qkv[whole, svalue_lanes], NT)
                second_grad = dot(out_grad, values[own, lanes], NT)
                inner = jnp.sum(first * first_grad, axis=-1, keepdims=True) + jnp.sum(
                    second * second_grad, axis=-1, keepdims=True
                )
                first_grad = (first * (first_grad - inner)).astype(jnp.bfloat16)
                second_grad = (second * (second_grad - inner)).astype(jnp.bfloat16)
                svalue_grad[:, lanes] += dot(first_low, out_grad, TN)
                value_grad[own, lanes] += dot(second_low, out_grad, TN)
                part = dot(first_grad, state_qkv[whole, skey_lanes], NN) + dot(
                    second_grad, keys[own, lanes], NN
                )
                state_cot[here_rows, lanes] = (part * ROOT).astype(jnp.bfloat16)
                skey_grad[:, lanes] += dot(first_grad, query, TN) * ROOT
                key_grad[own, lanes] += dot(second_grad, query, TN) * ROOT

    def gather_cot(block):
        whole = pl.ds(block * window, window)
        own = pl.ds(block * window + window, window)
        token_cot[whole, width : 2 * width] = key_grad[own, :].astype(jnp.bfloat16)
        token_cot[whole, 2 * width : 3 * width] = value_grad[own, :].astype(jnp.bfloat16)
        state_cot[whole, width : 2 * width] = skey_grad[...].astype(jnp.bfloat16)
        state_cot[whole, 2 * width : 3 * width] = svalue_grad[...].astype(jnp.bfloat16)

    def back_rows(cots, weight, block):
        def make(which):
            at = rows_at(block * window + which * rows, rows)
            out = dot(cots[at, 0:width], weight[0], NT)
            for c in (1, 2):
                out = out + dot(cots[at, c * width : (c + 1) * width], weight[c], NT)
            return out

        return make

    def state_sum(block):
        return RowSum(links, here, *rs[0], rows).fill(back_rows(state_cot, wst, block))

    def token_sum(block):
        return RowSum(links, here, *rs[1 + block], rows).fill(back_rows(token_cot, wtok, block))

    def mix_back(block, gather):
        for k in range(4):
            gather.ready(k)
            at = rows_at(block * window + ranks[k] * rows, rows)
            mixed_grad[at, :] = dot(branch_grad[at, :], wout[...], NN).astype(jnp.bfloat16)

    def store_grad(target, at, out):
        if len(target.shape) == 2:
            target[at, :] = out.astype(jnp.bfloat16)
        else:
            for c in range(3):
                target[c, at, :] = out[:, c * width : (c + 1) * width].astype(jnp.bfloat16)

    def weight_grad(target, left, right):
        step = 256
        for part in range(size // step):
            at = slice(part * step, (part + 1) * step)
            store_grad(target, at, dot(left[:, at], right[...], TN))

    def finish_tokens(block, summed):
        at = slice(block * rows, (block + 1) * rows)
        x = tokens_send[at, :].astype(jnp.float32)
        straight, gain = rms_back(x, gains_ref[0:1, :], summed.finish())
        middle_grad = gate_values[:, block * size : (block + 1) * size]
        tokens_send[at, :] = (middle_grad + straight).astype(jnp.bfloat16)
        return gain, home(tokens_send.at[pl.ds(block * rows, rows)], tokens_home.at[pl.ds(block * rows, rows)])

    smixed_moves = []
    for block in range(2):
        smixed_moves.append(
            links.copy(
                far_smixed.at[pl.ds(block * rows, rows), other_half],
                smixed_pair.at[pair_rows(block)],
                mates[1],
            )
        )
    brings[0].wait()
    branch_1 = RowGather(links, here, branch_grad, window, rows).start()
    bring_gates.wait()
    brings[2].wait()
    direct_1, moves_1, pair_1 = gates_back(1, s1_ref[...], gstate_ref[...].astype(jnp.float32))
    up_sum = FarPlaneSum(
        links, here, far_wup_grad, up_first, up_last, up_held, held_sems.at[pl.ds(0, 2)]
    ).start()
    down_sum = FarPlaneSum(
        links, here, far_wdn_grad, down_first, down_last, down_held, held_sems.at[pl.ds(2, 2)]
    ).start()
    bring_result = [
        pltpu.make_async_copy(
            far_result_own.at[pl.ds(block * rows, rows)],
            gate_values.at[:, pl.ds(block * size, size)],
            local_sems.at[6 + block],
        )
        for block in range(2)
    ]
    for moved in bring_result:
        moved.start()
    for ref in (tile_grads, key_grad, value_grad, skey_grad, svalue_grad):
        ref[...] = jnp.zeros(ref.shape, ref.dtype)
    bias_tiles(facts, tiles, heads, 3 * TILE, LOG2E)
    brings[1].wait()
    for moved in brings[3:]:
        moved.wait()
    mix_back(1, branch_1)
    branch_0 = RowGather(links, here, branch_grad, 0, rows).start()
    feed_moves = [links.copy(far_feed.at[block], feed_in.at[block], mates[2]) for block in range(2)]
    state_turn = home(far_state_out, state_home)
    token_back(1)
    for moved in moves_1:
        moved.wait_recv()
    state_back(1)
    gather_cot(1)
    result_total, feed_total = 0.0, 0.0
    for block in range(2):
        at = slice(block * rows, (block + 1) * rows)
        feed_moves[block].wait_recv()
        bring_result[block].wait()
        came = feed_in[block].astype(jnp.float32)
        feed = feed_own[at, :].astype(jnp.float32) + came
        result = gate_values[:, block * size : (block + 1) * size] + came
        feed_in[block] = result.astype(jnp.bfloat16)
        share = row_mask(facts, block * window + rank * rows, rows)
        feed_total = feed_total + jnp.sum(feed * feed * share, axis=0, keepdims=True)
        result_total = result_total + jnp.sum(result * result * share, axis=0, keepdims=True)
    block_turns = [
        home(feed_in.at[block], block_home.at[pl.ds(block * rows, rows)]) for block in range(2)
    ]
    bring_gates = pltpu.make_async_copy(far_gate_values.at[pl.ds(0, rows)], gate_values, local_sems.at[0])
    bring_gates.start()
    up_sum.forward()
    state_sum_1 = state_sum(1)
    token_sum_1 = token_sum(1)
    state_sum_1.forward()
    down_sum.forward()
    up_sum.bring_own()
    mix_back(0, branch_0)
    for ref in (skey_grad, svalue_grad):
        ref[...] = jnp.zeros(ref.shape, ref.dtype)
    up_sum.finish()
    up_settle = Settle(links, here, up_sum, up_home)
    token_back(0)
    for head in range(heads):
        lines = tile_grads[head, 0:8, :]
        span = lines.shape[1]
        for group in range(1, TILE // 8):
            lines = lines + pltpu.roll(tile_grads[head, 8 * group : 8 * group + 8, :], span - 8 * group, 1)
        total = lines[0:1]
        for line in range(1, 8):
            total = total + pltpu.roll(lines[line : line + 1], span - line, 1)
        for owner in range(4):
            at = 8 + heads * owner + head
            ring_send[at : at + 1, :] = jnp.zeros((1, size), jnp.float32)
            ring_send[at : at + 1, 0:span] = jnp.where(rank == owner, total, 0.0)
    ring_send[1:2, :] = small_sums[0:1, :]
    ring_send[3:4, :] = result_total
    ring_send[4:5, :] = small_sums[1:2, :]
    ring_send[5:6, :] = feed_total
    counted = jnp.zeros((1, 1), jnp.float32)
    for block in range(2):
        valid_rows = row_mask(facts, block * window + rank * rows, rows)
        counted = counted + jnp.sum(valid_rows, axis=0, keepdims=True)
    ring_send[6:7, :] = jnp.broadcast_to(counted, (1, size))
    for line in (0, 2, 7):
        ring_send[line : line + 1, :] = jnp.zeros((1, size), jnp.float32)
    ring_moves = [
        links.copy(ring_send, ring_in.at[step - 1], ring[step - 1]) for step in range(1, 8)
    ]
    token_sum_1.forward()
    bring_gates.wait()
    state_norm_grad, gain_2 = rms_back(s1_ref[...], gains_ref[2:3, :], state_sum_1.finish())
    for moved in moves_1:
        links.sent(moved)
    direct_0, moves_0, pair_0 = gates_back(0, s0_ref[...], direct_1 + state_norm_grad)
    bring_middle = [
        pltpu.make_async_copy(
            far_middle_grad.at[pl.ds(block * rows, rows)],
            gate_values.at[:, pl.ds(block * size, size)],
            local_sems.at[6 + block],
        )
        for block in range(2)
    ]
    for moved in bring_middle:
        moved.start()
    mixed_grad[0:window, :] = key_grad[0:window, :].astype(jnp.bfloat16)
    mixed_grad[window : 2 * window, :] = value_grad[0:window, :].astype(jnp.bfloat16)
    down_sum.bring_own()
    for moved in smixed_moves + [pair_1, pair_0]:
        moved.wait_recv()
    for c in range(3):
        weight_grad(gates_grad.at[c], gate_rows.at[:, c * size : (c + 1) * size], smixed_pair)
    gates_sum = PlaneSum(links, here, gates_grad, gates_first, gates_last).start()
    weight_grad(wout_grad, branch_grad, mixed)
    wout_sum = PlaneSum(links, here, wout_grad, wout_first, wout_last).start()
    for moved in ring_moves:
        moved.wait_recv()
    total = ring_send[...]
    for step in range(7):
        total = total + ring_in[step]
    level_send[...] = total
    level_moves = [
        links.copy(level_send, level_in.at[step - 1], (here.dp, lax.rem(here.level + step, 4)))
        for step in range(1, 4)
    ]
    down_sum.finish()
    for moved in bring_middle:
        moved.wait()
    gain_1, turn_1 = finish_tokens(1, token_sum_1)
    for moved in moves_0:
        moved.wait_recv()
    past_turn = home(mixed_grad, past_home)
    down_settle = Settle(links, here, down_sum, down_home)
    for gather in (branch_1, branch_0):
        gather.sent()
    bring_snormed = pltpu.make_async_copy(far_snormed, branch_grad, local_sems.at[2])
    bring_snormed.start()
    for moved in (pair_1, pair_0):
        links.sent(moved)
    bring_normed = []
    for block in range(2):
        bring_normed.append(
            pltpu.make_async_copy(
                far_normed.at[pl.ds(block * window, window)],
                gate_rows.at[:, block * size : (block + 1) * size],
                local_sems.at[4 + block],
            )
        )
        bring_normed[block].start()
    state_back(0)
    gather_cot(0)
    bring_snormed.wait()
    weight_grad(wst_grad, branch_grad, state_cot)
    wst_sum = PlaneSum(links, here, wst_grad, wst_first, wst_last).start()
    for block in range(2):
        bring_normed[block].wait()
    for part in range(size // 256):
        at = slice(part * 256, (part + 1) * 256)
        later = slice(size + part * 256, size + (part + 1) * 256)
        summed = dot(gate_rows[:, at], token_cot[0:window, :], TN)
        summed = summed + dot(gate_rows[:, later], token_cot[window : 2 * window, :], TN)
        store_grad(wtok_grad, at, summed)
    wtok_sum = PlaneSum(links, here, wtok_grad, wtok_first, wtok_last).start()
    gates_sum.forward()
    state_sum_1.sent()
    state_sum_0 = state_sum(0)
    token_sum_0 = token_sum(0)
    state_sum_0.forward()
    token_sum_0.forward()
    wst_sum.forward()
    wtok_sum.forward()
    wout_sum.forward()
    state_norm_grad, gain = rms_back(s0_ref[...], gains_ref[2:3, :], state_sum_0.finish())
    carried_send[...] = (direct_0 + state_norm_grad).astype(jnp.bfloat16)
    carried_turn = home(carried_send, carried_in)
    gain_2 = gain_2 + gain
    gates_sum.finish()
    low = lax.rem(here.level, 2)
    gates_pair = links.copy(gates_sum.result(1 - low), gate_pair_in, mates[2])
    wst_sum.finish()
    wst_settle = Settle(links, here, wst_sum, wst_home)
    gain_0, turn_0 = finish_tokens(0, token_sum_0)

    late_send[...] = jnp.concatenate(
        [gain[:, step * 256 : (step + 1) * 256] for gain in (gain_0 + gain_1, gain_2) for step in range(4)],
        axis=0,
    )
    late_moves = [
        links.copy(late_send, late_in.at[step - 1], ring[step - 1]) for step in range(1, 8)
    ]
    gates_pair.wait_recv()
    gates_part = gates_sum.result(low)
    gates_part[...] = (
        gates_part[...].astype(jnp.float32) + gate_pair_in[...].astype(jnp.float32)
    ).astype(jnp.bfloat16)
    gate_moves = GateHome(links, here, gates_grad, gates_home, rows)
    wtok_sum.finish()
    wtok_settle = Settle(links, here, wtok_sum, wtok_home)
    wout_sum.finish()
    wout_settle = Settle(links, here, wout_sum, wout_home)
    carried_turn.arrived()
    is_fresh = facts_home[3:4, :] > 0.5
    came = carried_in[...]
    carried_grad[...] = jnp.where(is_fresh, 0.0, came.astype(jnp.float32))
    initial_send[...] = jnp.where(is_fresh, came, jnp.zeros_like(came))
    part = initial_grad.shape[1]
    initial_moves = []
    for step in range(1, 8):
        to = lax.rem(here.dp + step, 8)
        columns = pl.ds(pl.multiple_of(to * part, part), part)
        initial_moves.append(
            links.copy(initial_send.at[:, columns], initial_in.at[step - 1], ring[step - 1])
        )
    for moved in late_moves:
        moved.wait_recv()
    late = late_send[...]
    for step in range(7):
        late = late + late_in[step]
    late_level_send[...] = late
    late_level_moves = [
        links.copy(late_level_send, late_level_in.at[step - 1], (here.dp, lax.rem(here.level + step, 4)))
        for step in range(1, 4)
    ]
    for moved in initial_moves:
        moved.wait_recv()
    own_columns = pl.ds(pl.multiple_of(here.dp * part, part), part)
    initial = initial_send[:, own_columns].astype(jnp.float32)
    for step in range(7):
        initial = initial + initial_in[step].astype(jnp.float32)
    initial_grad[...] = initial
    for moved in level_moves:
        moved.wait_recv()
    total = level_send[...]
    for step in range(3):
        total = total + level_in[step]
    totals[...] = total
    for moved in late_level_moves:
        moved.wait_recv()
    late = late_level_send[...]
    for step in range(3):
        late = late + late_level_in[step]
    for row, first in ((0, 0), (2, 4)):
        for step in range(4):
            totals[row : row + 1, step * 256 : (step + 1) * 256] = late[first + step : first + step + 1, :]
    gate_moves.arrived()
    for turn in (*block_turns, state_turn, past_turn, turn_1, turn_0):
        turn.arrived()
    for settle in (up_settle, down_settle, wout_settle, wst_settle, wtok_settle):
        settle.arrived()
    links.close()


def run_kernel(body, outs, scratch, collective, name, operands, far_in=(), far_out=()):
    vmem = pl.BlockSpec(memory_space=pltpu.VMEM)
    far = pl.BlockSpec(memory_space=pl.ANY)
    return pl.pallas_call(
        body,
        out_shape=outs,
        in_specs=[far if at in far_in else vmem for at in range(len(operands))],
        out_specs=[far if at in far_out else vmem for at in range(len(outs))],
        scratch_shapes=scratch,
        compiler_params=pltpu.CompilerParams(
            collective_id=collective, has_side_effects=True, vmem_limit_bytes=VMEM_BYTES
        ),
        name=name,
    )(*operands)


def sems(count):
    return [pltpu.SemaphoreType.DMA((count,)), pltpu.SemaphoreType.DMA((count,))]


def grouped(
    tokens, carried_state, past_keys, fresh_start, valid_count, bucket_ids, grad_output, grad_state,
    norm_gains, token_qkv, token_out, bias_table, mlp_up, mlp_down, state_qkv, state_gates, initial_state,
):
    dp_size, levels = lax.axis_size("dp"), lax.axis_size("state")
    dp_at, level = lax.axis_index("dp"), lax.axis_index("state")
    _, blocks, rows, size = tokens.shape
    window = rows * levels
    width = token_qkv.shape[2]
    heads = width // DH
    units = mlp_up.shape[1]
    model_rows = token_qkv.shape[0]
    low, full = jnp.bfloat16, jnp.float32

    one_hot = (bucket_ids[:, None] == jnp.arange(bias_table.shape[0])[None, :]).astype(full)
    per_offset = jnp.dot(one_hot, bias_table, precision=HIGHEST)
    lines = jnp.pad(per_offset[::-1].T, ((0, 0), (1, window - 1)), constant_values=NEGATIVE)
    numbers = jnp.stack([valid_count[0], fresh_start[0]]).astype(full)
    facts_in = jnp.concatenate(
        [
            lines,
            jnp.broadcast_to(numbers[:, None], (2, lines.shape[1])),
            jnp.zeros((4, lines.shape[1]), full),
        ]
    )

    stacked = lambda weight: jnp.transpose(weight, (1, 0, 2))
    shape = jax.ShapeDtypeStruct
    vmem = pltpu.VMEM
    rs = row_sum_scratch(rows, size)
    kept = [
        ((2 * window, size), low),
        ((2 * window, size), low),
        ((2 * window, width), low),
        ((3 * window, width), low),
        ((3 * window, width), low),
        ((2 * window, 3 * width), low),
        ((2 * window, 2 * heads), full),
        ((2 * window, width), low),
        ((3, size, width), low),
        ((3, size, width), low),
        ((size, width), low),
        ((3, size, size), low),
        ((2 * rows, size), low),
        ((rows, size), full),
        ((rows, size), full),
    ]
    (
        normed, snormed, queries, keys, values, sqkv, lse, mixed, wst_all, wtok_all, wout_all, gates_all,
        x, s0, s1, gate_values, gstate, wup_grad, wdn_grad, smixed_rows, s2, facts,
        feed_far, feed_own, result_own, middle_grad, branch_rows, small_sums,
    ) = run_kernel(
        forward_kernel,
        [shape(*of) for of in kept]
        + [
            shape((2 * rows, 3 * size), full),
            shape((rows, size), low),
            shape((size, units), low),
            shape((size, units), low),
            shape((2 * rows, size), low),
            shape((rows, size), low),
            shape((8, 2 * window), full),
            shape((2, rows, size), low),
            shape((2 * rows, size), low),
            shape((2 * rows, size), full),
            shape((2 * rows, size), full),
            shape((2 * rows, size), low),
            shape((8, size), full),
        ],
        [vmem(*of) for of in kept]
        + [
            vmem((2 * window, width), low),
            vmem((heads, TILE, 3 * TILE), full),
            vmem((rows, size), low),
            vmem((rows, size), low),
            vmem((rows, size), low),
            vmem((rows, size), full),
            vmem((rows, 3 * size), full),
            vmem((size, units), low),
            vmem((size, units), low),
            vmem((2 * rows, size), full),
            vmem((2 * window, size), low),
            vmem((2 * rows, size), low),
            vmem((2 * window, size), low),
            vmem((2 * window, units), full),
            vmem((2 * window, units), low),
            vmem((2 * window, units), low),
            vmem((size, units), low),
        ]
        + rs * 4
        + sems(128)
        + [pltpu.SemaphoreType.DMA((4,)), pltpu.SemaphoreType.DMA((len(kept),))],
        0,
        "forward",
        [
            tokens[0].reshape(blocks * rows, size),
            carried_state[0],
            initial_state,
            jnp.swapaxes(past_keys[0], 0, 1),
            facts_in,
            grad_output[0].reshape(blocks * rows, size),
            grad_state[0],
            norm_gains,
            stacked(state_qkv),
            stacked(token_qkv),
            token_out,
            stacked(state_gates),
            mlp_up,
            mlp_down,
        ],
        far_in=(3, 5, 12, 13),
        far_out=range(len(kept) + 4),
    )
    grads = [((3,), width), ((3,), width), ((), width), ((3,), 2 * width)]
    (
        block_home, state_home, tokens_home, past_home, carried_grad, initial_grad, totals,
        up_home, down_home, wst_home, wtok_home, wout_home, gates_home,
    ) = run_kernel(
        cotangent_kernel,
        [
            shape((2 * rows, size), low),
            shape((rows, size), low),
            shape((2 * rows, size), low),
            shape((2 * window, width), low),
            shape((rows, size), full),
            shape((rows, size // dp_size), full),
            shape((16, size), full),
            shape((2, rows, units), low),
            shape((2, rows, units), low),
            shape((2, 3, rows, width), low),
            shape((2, 3, rows, width), low),
            shape((2, rows, width), low),
            shape((4, 3, rows // 4, 2 * width), low),
        ],
        [
            vmem((3, size, size), low),
            vmem((size, width), low),
            vmem((2 * window, width), low),
            vmem((3 * window, width), low),
            vmem((2 * window, 3 * width), low),
            vmem((3 * window, width), low),
            vmem((2 * window, 2 * heads), full),
            vmem((2 * window, width), low),
            vmem((3, size, width), low),
            vmem((3, size, width), low),
            vmem((heads, TILE, 3 * TILE), full),
            vmem((heads, TILE, 3 * TILE), full),
            vmem((2 * window, size), low),
            vmem((2 * window, width), low),
            vmem((4 * rows, 3 * size), low),
            vmem((2 * window, width), low),
            vmem((3 * window, width), full),
            vmem((3 * window, width), full),
            vmem((window, width), full),
            vmem((window, width), full),
            vmem((2 * window, 3 * width), low),
            vmem((2 * window, 3 * width), low),
            vmem((rows, 3 * size), full),
            vmem((4 * rows, 2 * width), low),
            vmem((rows, size), low),
            vmem((2 * rows, size), low),
            vmem((rows, size), low),
            vmem((rows, size), low),
            vmem((rows, size), low),
            vmem((dp_size - 1, rows, size // dp_size), low),
        ]
        + [vmem((*stack, size, columns), low) for stack, columns in grads]
        + [vmem((4, *stack, rows, columns), low) for stack, columns in grads]
        + [vmem((2, *stack, rows, columns), low) for stack, columns in grads]
        + [vmem((4, rows, units), low)] * 2
        + [vmem((2, rows, units), low)] * 4
        + [
            vmem((dp_size - 1, 16, size), full),
            vmem((levels - 1, 16, size), full),
            vmem((16, size), full),
            vmem((16, size), full),
            vmem((dp_size - 1, 8, size // 4), full),
            vmem((levels - 1, 8, size // 4), full),
            vmem((8, size // 4), full),
            vmem((8, size // 4), full),
            vmem((3, rows, 2 * width), low),
            vmem((2, rows, size), low),
            vmem((2 * rows, size), low),
        ]
        + rs * 3
        + sems(128)
        + [pltpu.SemaphoreType.DMA((8,)), pltpu.SemaphoreType.DMA((4,)), pltpu.SemaphoreType.DMA((16,))],
        1,
        "cotangent",
        [
            middle_grad, branch_rows, gstate, x, s0, s1, gate_values, norm_gains, facts, facts_in,
            small_sums,
            normed, snormed, queries, keys, values, sqkv, lse, mixed, smixed_rows,
            wst_all, wtok_all, wout_all, gates_all, wup_grad, wdn_grad, feed_far, feed_own, result_own, s2,
        ],
        far_in=(0, 1, 3, 6, *range(11, 30)),
        far_out=(0, 1, 2, 3, 7, 8, 9, 10, 11, 12),
    )
    both = lambda pair: pair[0].astype(full) + pair[1].astype(full)
    gates_out = jnp.sum(gates_home.astype(full).reshape(2, 2, 3, rows // 4, 2 * width), axis=0)
    gates_out = jnp.transpose(gates_out, (2, 1, 0, 3)).reshape(rows // 4, 3, size)
    line_sums = totals[8 : 8 + levels * heads, 1 : window + 1][:, ::-1]
    table_all = jnp.dot(one_hot.T, line_sums.T, precision=HIGHEST)
    table_rows = table_all.shape[0] // dp_size
    table_out = lax.dynamic_slice(table_all, (dp_at * table_rows, level * heads), (table_rows, heads))
    share = size // (dp_size * levels)
    gains_out = lax.dynamic_slice(totals, (0, (dp_at * levels + level) * share), (3, share))
    rms_stats = jnp.sqrt(jnp.sum(totals[3:6], axis=1) / totals[6, 0])
    return (
        block_home.reshape(1, blocks, rows, size),
        state_home.astype(full)[None],
        rms_stats,
        tokens_home.reshape(1, blocks, rows, size),
        carried_grad[None],
        jnp.swapaxes(past_home.reshape(2, window, width).astype(full), 0, 1)[None],
        gains_out,
        stacked(both(wtok_home)),
        both(wout_home),
        table_out,
        both(up_home),
        both(down_home),
        stacked(both(wst_home)),
        gates_out,
        initial_grad,
    )


def solution(mesh):
    in_specs = (
        P("dp", None, "state", None),
        P("dp", "state", None),
        P("dp", None, None, "state"),
        P("dp"),
        P("dp"),
        P(),
        P("dp", None, "state", None),
        P("dp", "state", None),
        P(),
        P("dp", None, "state"),
        P("dp", "state"),
        P(None, "state"),
        P("dp", "state"),
        P("dp", "state"),
        P("dp", None, "state"),
        P("dp", None, None),
        P("state", "dp"),
    )
    out_specs = (
        P("dp", None, "state", None),
        P("dp", "state", None),
        P(),
        P("dp", None, "state", None),
        P("dp", "state", None),
        P("dp", None, None, "state"),
        P(None, ("dp", "state")),
        P("dp", None, "state"),
        P("dp", "state"),
        P("dp", "state"),
        P("dp", "state"),
        P("dp", "state"),
        P("dp", None, "state"),
        P(("dp", "state"), None, None),
        P("state", "dp"),
    )
    body = grouped if dict(mesh.shape) == {"dp": 8, "state": 4} else shards
    return jax.shard_map(body, mesh=mesh, in_specs=in_specs, out_specs=out_specs, check_vma=False)
```

```python
import math

import jax
import jax.numpy as jnp
from jax import lax
from jax.experimental import pallas as pl
from jax.experimental.pallas import tpu as pltpu
from jax.sharding import PartitionSpec as P

DH = 128


EPS = 1e-06
NEGATIVE = -1e30
HIGHEST = lax.Precision.HIGHEST


def rms_norm(tensor, gains_row):
    return tensor * lax.rsqrt(jnp.mean(tensor * tensor, axis=-1, keepdims=True) + EPS) * gains_row


def norm_back(tensor, gains_row, cotangent):
    return jax.vjp(rms_norm, tensor, gains_row)[1](cotangent)


def smooth_gelu(tensor):
    return jax.nn.gelu(tensor, approximate=True)


def renew_state(state_now, gate_values):
    return state_now * jax.nn.sigmoid(gate_values[2] + 1.0) + jnp.tanh(
        gate_values[0]
    ) * jax.nn.sigmoid(gate_values[1] - 1.0)


def split_heads(tensor):
    return tensor.reshape(tensor.shape[0], tensor.shape[1], tensor.shape[2] // DH, DH)


def merge_heads(tensor):
    return tensor.reshape(tensor.shape[0], tensor.shape[1], tensor.shape[2] * DH)


def score_grid(queries, key_rows, bias_add, allowed):
    scores = jnp.einsum(
        "iqhd,ikhd->ihqk", queries, key_rows, preferred_element_type=jnp.float32
    ) / math.sqrt(DH)
    if bias_add is not None:
        scores = scores + bias_add[None]
    return jnp.where(allowed[:, None], scores, NEGATIVE)


def attend_forward(queries, key_rows, values, bias_add, allowed):
    scores = score_grid(queries, key_rows, bias_add, allowed)
    row_max = jnp.max(scores, axis=-1, keepdims=True)
    weights = jnp.exp(scores - row_max)
    row_total = jnp.sum(weights, axis=-1, keepdims=True)
    attn_probs = (weights / row_total).astype(jnp.bfloat16)
    mixed_heads = jnp.einsum(
        "ihqk,ikhd->iqhd", attn_probs, values, preferred_element_type=jnp.float32
    )
    return (merge_heads(mixed_heads.astype(jnp.bfloat16)), row_max + jnp.log(row_total))


def attention_backward_pass(queries, key_rows, values, bias_add, allowed, log_total, grad_mixed):
    scores = score_grid(queries, key_rows, bias_add, allowed)
    attn_probs = jnp.exp(scores - log_total)
    probs_grad = jnp.einsum(
        "iqhd,ikhd->ihqk", grad_mixed, values, preferred_element_type=jnp.float32
    )
    scores_grad = attn_probs * (
        probs_grad - jnp.sum(attn_probs * probs_grad, axis=-1, keepdims=True)
    )
    scores_grad = scores_grad.astype(jnp.bfloat16)
    values_grad = jnp.einsum(
        "ihqk,iqhd->ikhd",
        attn_probs.astype(jnp.bfloat16),
        grad_mixed,
        preferred_element_type=jnp.float32,
    )
    queries_grad = jnp.einsum(
        "ihqk,ikhd->iqhd", scores_grad, key_rows, preferred_element_type=jnp.float32
    ) / math.sqrt(DH)
    keys_grad = jnp.einsum(
        "ihqk,iqhd->ikhd", scores_grad, queries, preferred_element_type=jnp.float32
    ) / math.sqrt(DH)
    return (
        merge_heads(queries_grad),
        merge_heads(keys_grad),
        merge_heads(values_grad),
        scores_grad,
    )


def diagonal_sums(grid_values):
    num_heads, num_rows, num_cols = grid_values.shape
    flat = grid_values.reshape(num_heads, num_rows * num_cols)
    flat = jnp.pad(flat, ((0, 0), (0, num_rows)))
    sums = jnp.sum(flat.reshape(num_heads, num_rows, num_cols + 1), axis=1)
    return sums[:, num_rows:0:-1]


def toeplitz_grid(per_offset, num_rows):
    num_cols = 2 * num_rows
    line = jnp.pad(per_offset[::-1].T, ((0, 0), (1, num_cols - num_rows)))
    flat = jnp.tile(line, (1, num_rows))[:, : num_rows * num_cols]
    return flat.reshape(-1, num_rows, num_cols)


def sum_rows(partial_value):
    return lax.psum_scatter(
        partial_value.astype(jnp.bfloat16), "state", scatter_dimension=1, tiled=True
    ).astype(jnp.float32)


def whole_rows(partial_value):
    return lax.all_gather(partial_value, "state", axis=1, tiled=True)


def shards(
    tokens,
    carried_state,
    past_keys,
    fresh_start,
    valid_count,
    bucket_ids,
    grad_output,
    grad_state,
    norm_gains,
    token_qkv,
    token_out,
    bias_table,
    mlp_up,
    mlp_down,
    state_qkv,
    state_gates,
    initial_state,
):
    item_count, blocks, share_rows, model_width = tokens.shape
    groups = lax.axis_size("state")
    state_rank = lax.axis_index("state")
    window_width = share_rows * groups
    vector_rows = carried_state.shape[1] * groups
    local_width = token_qkv.shape[2]
    qkv_full, out_full, up_full, down_full, sqkv_full, gates_full, initial_full = (
        lax.all_gather(token_qkv, "dp", axis=0, tiled=True),
        lax.all_gather(token_out, "dp", axis=0, tiled=True),
        lax.all_gather(mlp_up, "dp", axis=0, tiled=True),
        lax.all_gather(mlp_down, "dp", axis=0, tiled=True),
        lax.all_gather(state_qkv, "dp", axis=0, tiled=True),
        lax.all_gather(state_gates, "dp", axis=0, tiled=True),
        lax.all_gather(initial_state, "dp", axis=1, tiled=True),
    )
    gates_used = lax.dynamic_slice_in_dim(gates_full, state_rank * local_width, local_width, 2)
    one_hot = (bucket_ids[:, None] == jnp.arange(bias_table.shape[0])[None, :]).astype(jnp.float32)
    per_offset = jnp.dot(one_hot, bias_table, precision=HIGHEST)
    query_pos = jnp.arange(window_width)[:, None]
    key_pos = jnp.arange(2 * window_width)[None, :]
    offset = window_width + query_pos - key_pos
    inside = (offset >= 0) & (offset < window_width)
    bias_grid = toeplitz_grid(per_offset, window_width)
    token_bias = jnp.pad(bias_grid, ((0, 0), (0, 0), (0, vector_rows)))
    is_fresh = fresh_start == 1
    state_now = jnp.where(
        is_fresh[:, None, None], initial_full.astype(jnp.float32)[None], carried_state
    )
    past_key = past_keys[:, :, 0]
    past_value = past_keys[:, :, 1]
    past_ok = jnp.broadcast_to(~is_fresh[:, None], (item_count, window_width))
    gains_token, gains_middle, gains_state = (norm_gains[0], norm_gains[1], norm_gains[2])
    share_pos = state_rank * share_rows + jnp.arange(share_rows)
    square_sums = jnp.zeros((3,), jnp.float32)
    valid_total = jnp.zeros((), jnp.float32)
    kept_values = []
    results = []
    for block_at in range(blocks):
        token_ok = (
            block_at * window_width + jnp.arange(window_width)[None, :] < valid_count[:, None]
        )
        inputs = tokens[:, block_at].astype(jnp.float32)
        normed, state_normed = (
            lax.all_gather(
                rms_norm(inputs, gains_token).astype(jnp.bfloat16), "state", axis=1, tiled=True
            ),
            lax.all_gather(
                rms_norm(state_now, gains_state).astype(jnp.bfloat16), "state", axis=1, tiled=True
            ),
        )
        project = jnp.einsum(
            "iwd,dch->ciwh", normed, qkv_full, preferred_element_type=jnp.float32
        ).astype(jnp.bfloat16)
        state_project = jnp.einsum(
            "ind,dch->cinh", state_normed, sqkv_full, preferred_element_type=jnp.float32
        ).astype(jnp.bfloat16)
        token_keys = jnp.concatenate([past_key, project[1], state_project[1]], axis=1)
        token_values = jnp.concatenate([past_value, project[2], state_project[2]], axis=1)
        window_ok = inside[None] & jnp.concatenate([past_ok, token_ok], axis=1)[:, None, :]
        token_allowed = jnp.concatenate(
            [window_ok, jnp.ones((item_count, window_width, vector_rows), jnp.bool_)], axis=2
        )
        mixed_heads, token_total = attend_forward(
            split_heads(project[0]),
            split_heads(token_keys),
            split_heads(token_values),
            token_bias,
            token_allowed,
        )
        branch = sum_rows(
            jnp.einsum("iwh,dh->iwd", mixed_heads, out_full, preferred_element_type=jnp.float32)
        )
        middle = inputs + branch
        middle_normed = lax.all_gather(
            rms_norm(middle, gains_middle).astype(jnp.bfloat16), "state", axis=1, tiled=True
        )
        up_values = jnp.einsum(
            "iwd,df->iwf", middle_normed, up_full, preferred_element_type=jnp.float32
        )
        hidden = smooth_gelu(up_values).astype(jnp.bfloat16)
        feed_out = sum_rows(
            jnp.einsum("iwf,df->iwd", hidden, down_full, preferred_element_type=jnp.float32)
        )
        result = middle + feed_out
        results.append(result.astype(jnp.bfloat16))
        share_ok = (block_at * window_width + share_pos[None, :] < valid_count[:, None]).astype(
            jnp.float32
        )[:, :, None]
        square_sums = square_sums + jnp.stack(
            [
                jnp.sum(share_ok * result * result),
                jnp.sum(share_ok * branch * branch),
                jnp.sum(share_ok * feed_out * feed_out),
            ]
        )
        valid_total = valid_total + jnp.sum(share_ok)
        state_keys = jnp.concatenate([state_project[1], project[1]], axis=1)
        state_values = jnp.concatenate([state_project[2], project[2]], axis=1)
        state_allowed = jnp.concatenate(
            [
                jnp.ones((item_count, vector_rows, vector_rows), jnp.bool_),
                jnp.broadcast_to(token_ok[:, None, :], (item_count, vector_rows, window_width)),
            ],
            axis=2,
        )
        state_mixed, state_total = attend_forward(
            split_heads(state_project[0]),
            split_heads(state_keys),
            split_heads(state_values),
            None,
            state_allowed,
        )
        gate_source = state_mixed
        gate_values = lax.psum_scatter(
            jnp.einsum(
                "inh,dch->cind", state_mixed, gates_used, preferred_element_type=jnp.float32
            ).astype(jnp.bfloat16),
            "state",
            scatter_dimension=2,
            tiled=True,
        ).astype(jnp.float32)
        kept_values.append(
            (
                inputs,
                normed,
                state_normed,
                project,
                state_project,
                token_keys,
                token_values,
                token_allowed,
                mixed_heads,
                token_total,
                middle,
                middle_normed,
                up_values,
                hidden,
                state_keys,
                state_values,
                state_allowed,
                state_total,
                gate_source,
                gate_values,
                state_now,
            )
        )
        state_now = renew_state(state_now, gate_values)
        past_key, past_value, past_ok = (project[1], project[2], token_ok)
    square_sums, valid_total = lax.psum((square_sums, valid_total), ("dp", "state"))
    rms_stats = jnp.sqrt(square_sums / valid_total)
    qkv_grad = jnp.zeros(qkv_full.shape, jnp.float32)
    out_grad = jnp.zeros(out_full.shape, jnp.float32)
    up_grad = jnp.zeros(up_full.shape, jnp.float32)
    down_grad = jnp.zeros(down_full.shape, jnp.float32)
    sqkv_grad = jnp.zeros(sqkv_full.shape, jnp.float32)
    gate_grad = jnp.zeros(gates_used.shape, jnp.float32)
    bias_grad = jnp.zeros(bias_grid.shape, jnp.float32)
    gain_token_grad = jnp.zeros((model_width,), jnp.float32)
    gain_middle_grad = jnp.zeros((model_width,), jnp.float32)
    gain_state_grad = jnp.zeros((model_width,), jnp.float32)
    state_grad = grad_state
    carried_key_rows = jnp.zeros(past_keys[:, :, 0].shape, jnp.float32)
    carry_value = jnp.zeros(past_keys[:, :, 0].shape, jnp.float32)
    token_grads = [None] * blocks
    for block_at in reversed(range(blocks)):
        (
            inputs,
            normed,
            state_normed,
            project,
            state_project,
            token_keys,
            token_values,
            token_allowed,
            mixed_heads,
            token_total,
            middle,
            middle_normed,
            up_values,
            hidden,
            state_keys,
            state_values,
            state_allowed,
            state_total,
            gate_source,
            gate_values,
            state_before,
        ) = kept_values[block_at]
        direct_grad, gates_grad = jax.vjp(renew_state, state_before, gate_values)[1](state_grad)
        gates_low = gates_grad.astype(jnp.bfloat16)
        gates_rows = lax.all_gather(gates_low, "state", axis=2, tiled=True)
        state_mixed_grad = jnp.einsum(
            "cind,dch->inh", gates_rows, gates_used, preferred_element_type=jnp.float32
        ).astype(jnp.bfloat16)
        gate_grad = gate_grad + jnp.einsum(
            "inh,cind->dch", gate_source, gates_rows, preferred_element_type=jnp.float32
        )
        state_query_gradient, state_keys_gradient, state_values_gradient, discarded_output = (
            attention_backward_pass(
                split_heads(state_project[0]),
                split_heads(state_keys),
                split_heads(state_values),
                None,
                state_allowed,
                state_total,
                split_heads(state_mixed_grad),
            )
        )
        out_share = grad_output[:, block_at]
        out_whole = whole_rows(out_share)
        down_grad = down_grad + jnp.einsum(
            "iwf,iwd->df", hidden, out_whole, preferred_element_type=jnp.float32
        )
        hidden_grad = jnp.einsum(
            "iwd,df->iwf", out_whole, down_full, preferred_element_type=jnp.float32
        )
        up_values_grad = jax.vjp(smooth_gelu, up_values)[1](hidden_grad)[0].astype(jnp.bfloat16)
        up_grad = up_grad + jnp.einsum(
            "iwd,iwf->df", middle_normed, up_values_grad, preferred_element_type=jnp.float32
        )
        middle_normed_grad = lax.psum_scatter(
            jnp.einsum(
                "iwf,df->iwd", up_values_grad, up_full, preferred_element_type=jnp.float32
            ).astype(jnp.bfloat16),
            "state",
            scatter_dimension=1,
            tiled=True,
        ).astype(jnp.float32)
        middle_grad, gain_part = norm_back(middle, gains_middle, middle_normed_grad)
        middle_grad = out_share.astype(jnp.float32) + middle_grad
        gain_middle_grad = gain_middle_grad + gain_part
        branch_whole = whole_rows(middle_grad.astype(jnp.bfloat16))
        out_grad = out_grad + jnp.einsum(
            "iwh,iwd->dh", mixed_heads, branch_whole, preferred_element_type=jnp.float32
        )
        mixed_grad = jnp.einsum(
            "iwd,dh->iwh", branch_whole, out_full, preferred_element_type=jnp.float32
        ).astype(jnp.bfloat16)
        query_grad, token_keys_gradient, tvalues_grad, scores_grad = attention_backward_pass(
            split_heads(project[0]),
            split_heads(token_keys),
            split_heads(token_values),
            token_bias,
            token_allowed,
            token_total,
            split_heads(mixed_grad),
        )
        bias_grad = bias_grad + jnp.sum(
            scores_grad[:, :, :, : 2 * window_width].astype(jnp.float32), axis=0
        )
        key_gradient_rows = (
            token_keys_gradient[:, window_width : 2 * window_width]
            + state_keys_gradient[:, vector_rows:]
            + carried_key_rows
        )
        value_grad = (
            tvalues_grad[:, window_width : 2 * window_width]
            + state_values_gradient[:, vector_rows:]
            + carry_value
        )
        state_key_gradient = (
            token_keys_gradient[:, 2 * window_width :] + state_keys_gradient[:, :vector_rows]
        )
        state_value_gradient = (
            tvalues_grad[:, 2 * window_width :] + state_values_gradient[:, :vector_rows]
        )
        project_grad = jnp.stack([query_grad, key_gradient_rows, value_grad]).astype(jnp.bfloat16)
        state_projection_gradient = jnp.stack(
            [state_query_gradient, state_key_gradient, state_value_gradient]
        ).astype(jnp.bfloat16)
        qkv_grad = qkv_grad + jnp.einsum(
            "iwd,ciwh->dch", normed, project_grad, preferred_element_type=jnp.float32
        )
        sqkv_grad = sqkv_grad + jnp.einsum(
            "ind,cinh->dch",
            state_normed,
            state_projection_gradient,
            preferred_element_type=jnp.float32,
        )
        normed_grad, state_normed_grad = (
            lax.psum_scatter(
                jnp.einsum(
                    "ciwh,dch->iwd", project_grad, qkv_full, preferred_element_type=jnp.float32
                ).astype(jnp.bfloat16),
                "state",
                scatter_dimension=1,
                tiled=True,
            ).astype(jnp.float32),
            lax.psum_scatter(
                jnp.einsum(
                    "cinh,dch->ind",
                    state_projection_gradient,
                    sqkv_full,
                    preferred_element_type=jnp.float32,
                ).astype(jnp.bfloat16),
                "state",
                scatter_dimension=1,
                tiled=True,
            ).astype(jnp.float32),
        )
        input_grad, gain_part = norm_back(inputs, gains_token, normed_grad)
        gain_token_grad = gain_token_grad + gain_part
        token_grads[block_at] = (middle_grad + input_grad).astype(jnp.bfloat16)
        state_norm_grad, gain_part = norm_back(state_before, gains_state, state_normed_grad)
        gain_state_grad = gain_state_grad + gain_part
        state_grad = direct_grad + state_norm_grad
        carried_key_rows = token_keys_gradient[:, :window_width]
        carry_value = tvalues_grad[:, :window_width]
    carried_grad = jnp.where(is_fresh[:, None, None], 0.0, state_grad)
    initial_part = jnp.sum(jnp.where(is_fresh[:, None, None], state_grad, 0.0), axis=0)
    past_grad = jnp.stack([carried_key_rows, carry_value], axis=2)
    table_part = jnp.dot(one_hot.T, diagonal_sums(bias_grad).T, precision=HIGHEST)
    gain_columns = jnp.stack([gain_token_grad, gain_middle_grad, gain_state_grad], axis=1)
    summed = (
        lax.psum_scatter(
            qkv_grad.astype(jnp.bfloat16), "dp", scatter_dimension=0, tiled=True
        ).astype(jnp.float32),
        lax.psum_scatter(
            out_grad.astype(jnp.bfloat16), "dp", scatter_dimension=0, tiled=True
        ).astype(jnp.float32),
        lax.psum_scatter(
            table_part.astype(jnp.bfloat16), "dp", scatter_dimension=0, tiled=True
        ).astype(jnp.float32),
        lax.psum_scatter(
            up_grad.astype(jnp.bfloat16), "dp", scatter_dimension=0, tiled=True
        ).astype(jnp.float32),
        lax.psum_scatter(
            down_grad.astype(jnp.bfloat16), "dp", scatter_dimension=0, tiled=True
        ).astype(jnp.float32),
        lax.psum_scatter(
            sqkv_grad.astype(jnp.bfloat16), "dp", scatter_dimension=0, tiled=True
        ).astype(jnp.float32),
        lax.psum_scatter(
            initial_part.astype(jnp.bfloat16), "dp", scatter_dimension=1, tiled=True
        ).astype(jnp.float32),
        lax.psum_scatter(
            gate_grad.astype(jnp.bfloat16), "dp", scatter_dimension=0, tiled=True
        ).astype(jnp.float32),
        lax.psum_scatter(
            gain_columns.astype(jnp.bfloat16), "dp", scatter_dimension=0, tiled=True
        ).astype(jnp.float32),
    )
    gate_pieces, gain_pieces = (
        lax.all_to_all(
            summed[7][:, :, None, :].astype(jnp.bfloat16),
            "state",
            split_axis=0,
            concat_axis=2,
            tiled=True,
        ).astype(jnp.float32),
        lax.all_to_all(
            summed[8][:, :, None, None].astype(jnp.bfloat16),
            "state",
            split_axis=0,
            concat_axis=2,
            tiled=True,
        ).astype(jnp.float32),
    )
    gains_grad = jnp.sum(gain_pieces, axis=(2, 3)).T
    gates_grad_out = gate_pieces.reshape(
        gate_pieces.shape[0], gate_pieces.shape[1], gate_pieces.shape[2] * gate_pieces.shape[3]
    )
    return (
        jnp.stack(results, axis=1),
        state_now,
        rms_stats,
        jnp.stack(token_grads, axis=1),
        carried_grad,
        past_grad,
        gains_grad,
        summed[0],
        summed[1],
        summed[2],
        summed[3],
        summed[4],
        summed[5],
        gates_grad_out,
        summed[6],
    )


MESH = pl.DeviceIdType.MESH
NN = (((1,), (0,)), ((), ()))
NT = (((1,), (1,)), ((), ()))
TN = (((0,), (0,)), ((), ()))
VMEM_BYTES = 127 * 2**19


class Place:
    def __init__(self):
        chip_core, level = lax.axis_index("dp"), lax.axis_index("state")
        core, low = lax.rem(chip_core, 2), lax.rem(level, 2)
        x, y = lax.rem(chip_core // 2, 2), chip_core // 4
        flip = lambda bit: 1 - 2 * bit
        self.dp, self.core, self.level, self.half = chip_core, core, level, level // 2
        self.rank = 2 * low + core
        self.ranks = [self.rank, 2 * low + 1 - core, 2 * (1 - low) + core, 2 * (1 - low) + 1 - core]
        self.mates = [
            None,
            (chip_core + flip(core), level),
            (chip_core, level + flip(low)),
            (chip_core + flip(core), level + flip(low)),
        ]
        self.planes = [2 * y + x, 2 * y + 1 - x, 2 * (1 - y) + x, 2 * (1 - y) + 1 - x]
        self.plane_mates = [
            None,
            (chip_core + 2 * flip(x), level),
            (chip_core + 4 * flip(y), level),
            (chip_core + 2 * flip(x) + 4 * flip(y), level),
        ]
        first = chip_core - core
        self.there = (first + low, 2 * core + self.half)
        self.across = (first + low, 2 * (1 - core) + self.half)
        self.from_there = (first + self.half, 2 * low + core)
        self.from_across = (first + 1 - self.half, 2 * low + core)
        self.stays = (core == low) & (self.half == core)


def rows_at(start, size, step=128):
    return pl.ds(pl.multiple_of(start, step), size)


def rows_of(ref, start, size, step=128):
    at = rows_at(start, size, step)
    return ref.at[:, at] if len(ref.shape) == 3 else ref.at[at]


class Links:
    def __init__(self, send_sems, recv_sems):
        self.send_sems, self.recv_sems = send_sems, recv_sems
        self.used = 0
        self.open_sends = []
        self.open_turns = []

    def plan(self, source, target, device):
        at = self.used
        self.used += 1
        return pltpu.make_async_remote_copy(
            src_ref=source,
            dst_ref=target,
            send_sem=self.send_sems.at[at],
            recv_sem=self.recv_sems.at[at],
            device_id=device,
            device_id_type=MESH,
        )

    def copy(self, source, target, device):
        moved = self.plan(source, target, device)
        moved.start()
        self.open_sends.append(moved)
        return moved

    def sent(self, moved):
        self.open_sends = [other for other in self.open_sends if other is not moved]
        moved.wait_send()

    def close(self):
        for moved in self.open_sends:
            moved.wait_send()
        for turn in self.open_turns:
            turn.sent()
        self.open_sends, self.open_turns = [], []


def greet(devices, turned=None):
    barrier = pltpu.get_barrier_semaphore()
    for device in devices:
        pl.semaphore_signal(barrier, inc=1, device_id=device, device_id_type=MESH)
    if turned is None:
        pl.semaphore_wait(barrier, len(devices))
    else:
        moves = jnp.logical_not(turned.stays)

        @pl.when(moves)
        def _():
            pl.semaphore_signal(barrier, inc=1, device_id=turned.from_there, device_id_type=MESH)

        pl.semaphore_wait(barrier, len(devices) + moves.astype(jnp.int32))


class Turn:
    def __init__(self, links, here, source, target, device):
        self.stays = here.stays
        self.moved = links.plan(source, target, device)
        self.kept = pltpu.make_async_copy(source, target, links.recv_sems.at[links.used - 1])
        links.open_turns.append(self)

        @pl.when(jnp.logical_not(self.stays))
        def _():
            self.moved.start()

        @pl.when(self.stays)
        def _():
            self.kept.start()

    def arrived(self):
        @pl.when(jnp.logical_not(self.stays))
        def _():
            self.moved.wait_recv()

        @pl.when(self.stays)
        def _():
            self.kept.wait()

    def sent(self):
        @pl.when(jnp.logical_not(self.stays))
        def _():
            self.moved.wait_send()


class WeightGather:
    def __init__(self, links, here, local, full):
        self.links, self.here, self.local, self.full = links, here, local, full
        self.rows = local.shape[-2]

    def enter(self):
        target = rows_of(self.full, self.here.dp * self.rows, self.rows)
        self.turn = Turn(self.links, self.here, self.local, target, self.here.there)
        self.cross = self.links.copy(self.local, target, self.here.across)
        return self

    def block(self, k):
        return rows_of(self.full, self.here.planes[k] * 2 * self.rows, 2 * self.rows)

    def half(self, k, which):
        start = self.here.planes[k] * 2 * self.rows + which * self.rows
        return rows_of(self.full, start, self.rows)

    def spread(self):
        self.turn.arrived()
        self.cross.wait_recv()
        mates = self.here.plane_mates
        self.over_x = self.links.copy(self.block(0), self.block(0), mates[1])
        self.over_y = self.links.copy(self.block(0), self.block(0), mates[2])

    def forward(self):
        mates = self.here.plane_mates
        self.over_x.wait_recv()
        self.corner_0 = self.links.copy(self.half(1, 0), self.half(1, 0), mates[2])
        self.over_y.wait_recv()
        self.corner_1 = self.links.copy(self.half(2, 1), self.half(2, 1), mates[1])

    def finish(self):
        self.corner_0.wait_recv()
        self.corner_1.wait_recv()


class GateGather:
    def __init__(self, links, here, local, full, sem):
        self.links, self.here, self.local, self.full, self.sem = links, here, local, full, sem
        self.rows = local.shape[-2]

    def block(self, k):
        start = (2 * self.here.planes[k] + self.here.core) * self.rows
        return rows_of(self.full, start, self.rows)

    def part(self, k, which):
        size = self.rows // 2
        start = (2 * self.here.planes[k] + self.here.core) * self.rows + which * size
        return rows_of(self.full, start, size, 64)

    def spread(self):
        mates, sibling = self.here.plane_mates, self.here.mates[1]
        self.over_x = self.links.copy(self.local, self.block(0), mates[1])
        self.over_y = self.links.copy(self.local, self.block(0), mates[2])
        self.near = [self.links.copy(self.local, self.block(0), sibling)]
        self.kept = pltpu.make_async_copy(self.local, self.block(0), self.sem)
        self.kept.start()

    def forward(self):
        mates, sibling = self.here.plane_mates, self.here.mates[1]
        self.over_x.wait_recv()
        self.corner_0 = self.links.copy(self.part(1, 0), self.part(1, 0), mates[2])
        self.near.append(self.links.copy(self.block(1), self.block(1), sibling))
        self.over_y.wait_recv()
        self.corner_1 = self.links.copy(self.part(2, 1), self.part(2, 1), mates[1])
        self.near.append(self.links.copy(self.block(2), self.block(2), sibling))

    def last(self):
        self.corner_0.wait_recv()
        self.corner_1.wait_recv()
        self.near.append(self.links.copy(self.block(3), self.block(3), self.here.mates[1]))

    def finish(self):
        self.kept.wait()
        for moved in self.near:
            moved.wait_recv()


class RowGather:
    def __init__(self, links, here, ref, base, rows):
        self.links, self.here, self.ref, self.base, self.rows = links, here, ref, base, rows

    def part(self, k):
        return self.ref.at[rows_at(self.base + self.here.ranks[k] * self.rows, self.rows)]

    def start(self):
        own, mates = self.part(0), self.here.mates
        self.far = self.links.copy(own, own, mates[2])
        self.near = self.links.copy(own, own, mates[1])
        return self

    def ready(self, k):
        if k == 1:
            self.near.wait_recv()
        elif k == 2:
            self.far.wait_recv()
            block = self.part(2)
            self.last = self.links.copy(block, block, self.here.mates[1])
        elif k == 3:
            self.last.wait_recv()

    def sent(self):
        for moved in (self.far, self.near, self.last):
            self.links.sent(moved)


class RowSum:
    def __init__(self, links, here, stage, near_in, far_out, far_in, rows):
        self.links, self.here, self.rows = links, here, rows
        self.stage, self.near_in, self.far_out, self.far_in = stage, near_in, far_out, far_in

    def part(self, k):
        return self.stage.at[rows_at(self.here.ranks[k] * self.rows, self.rows)]

    def fill(self, make_rows):
        sibling = self.here.mates[1]
        for k, slot in ((3, 0), (1, 1)):
            self.part(k)[...] = make_rows(self.here.ranks[k]).astype(jnp.bfloat16)
            moved = self.links.copy(self.part(k), self.near_in.at[slot], sibling)
            if slot == 0:
                self.near_far = moved
            else:
                self.near_own = moved
        for k in (2, 0):
            self.part(k)[...] = make_rows(self.here.ranks[k]).astype(jnp.bfloat16)
        return self

    def forward(self):
        self.near_far.wait_recv()
        summed = self.part(2)[...].astype(jnp.float32) + self.near_in[0].astype(jnp.float32)
        self.far_out[...] = summed.astype(jnp.bfloat16)
        self.far = self.links.copy(self.far_out, self.far_in, self.here.mates[2])
        return self

    def sent(self):
        for moved in (self.near_far, self.near_own, self.far):
            self.links.sent(moved)

    def split(self):
        self.near_far.wait_recv()
        summed = self.part(2)[...].astype(jnp.float32) + self.near_in[0].astype(jnp.float32)
        self.near_own.wait_recv()
        own = self.part(0)[...].astype(jnp.float32) + self.near_in[1].astype(jnp.float32)
        return summed.astype(jnp.bfloat16), own

    def finish(self):
        self.near_own.wait_recv()
        self.far.wait_recv()
        return (
            self.part(0)[...].astype(jnp.float32)
            + self.near_in[1].astype(jnp.float32)
            + self.far_in[...].astype(jnp.float32)
        )


def row_sum_scratch(rows, width):
    return [
        pltpu.VMEM((4 * rows, width), jnp.bfloat16),
        pltpu.VMEM((2, rows, width), jnp.bfloat16),
        pltpu.VMEM((rows, width), jnp.bfloat16),
        pltpu.VMEM((rows, width), jnp.bfloat16),
    ]


def dot(left, right, dims):
    return lax.dot_general(left, right, dims, preferred_element_type=jnp.float32)


def scale_of(tensor):
    return lax.rsqrt(jnp.mean(tensor * tensor, axis=-1, keepdims=True) + EPS)


def rms_back(tensor, gains_row, cotangent):
    scale = scale_of(tensor)
    weighted = cotangent * gains_row
    inner = jnp.mean(tensor * weighted, axis=-1, keepdims=True)
    straight = scale * weighted - tensor * (scale * scale * scale * inner)
    return straight, jnp.sum(cotangent * tensor * scale, axis=0, keepdims=True)


def row_mask(facts, start, rows):
    place_of = lax.broadcasted_iota(jnp.int32, (rows, 1), 0) + start
    return jnp.where(place_of.astype(jnp.float32) < facts[2:3, 0:1], 1.0, 0.0)


def bias_tiles(lines_ref, tiles_ref, heads, width, scale=1.0):
    for head in range(heads):
        line = lines_ref[head : head + 1, :] * scale
        spread = jnp.broadcast_to(line, (tiles_ref.shape[1], line.shape[1]))
        tiles_ref[head] = pltpu.roll(spread, 0, 1, stride=1, stride_axis=0)[:, :width]


def softmax_pair(first, second):
    top = jnp.maximum(
        jnp.max(first, axis=-1, keepdims=True), jnp.max(second, axis=-1, keepdims=True)
    )
    first, second = jnp.exp(first - top), jnp.exp(second - top)
    total = jnp.sum(first, axis=-1, keepdims=True) + jnp.sum(second, axis=-1, keepdims=True)
    share = 1.0 / total
    return (
        (first * share).astype(jnp.bfloat16),
        (second * share).astype(jnp.bfloat16),
        top + jnp.log(total),
    )


TILE = 256
LOG2E = math.log2(math.e)
ROOT = 1.0 / math.sqrt(DH)


def forward_kernel(
    x_in, carried_in, initial_in, far_past, facts_in, far_gout, gstate_in, gains_ref,
    wst_in, wtok_in, wout_in, gates_in, far_wup, far_wdn,
    far_normed, far_snormed, far_queries, far_keys, far_values, far_state_qkv, far_lse, far_mixed,
    far_wst, far_wtok, far_wout, far_gates, far_x, far_s0, far_s1,
    far_gate_values, far_gstate_here, far_wup_grad, far_wdn_grad,
    smixed_rows, s2_ref, facts, feed_far, feed_own, result_own, middle_grad, branch_rows, small_sums,
    normed, snormed, queries, keys, values, state_qkv, lse_ref, mixed,
    wst, wtok, wout, gates, x_ref, s0_ref, s1_ref,
    smixed, tiles, initial_all, normed_send, gstate_send, s0_send, gate_values, wup, wdn, middle,
    middle_normed, gout_rows, gout, slope, hidden, up_grad, grad_stage, *rest,
):
    rs = [rest[4 * k : 4 * k + 4] for k in range(4)]
    links = Links(rest[16], rest[17])
    local_sems, keep_sems = rest[18], rest[19]
    kept = []

    def keep(source, target):
        moved = pltpu.make_async_copy(source, target, keep_sems.at[len(kept)])
        moved.start()
        kept.append(moved)

    here = Place()
    rank, ranks, mates = here.rank, here.ranks, here.mates
    rows = s0_ref.shape[0]
    window = 4 * rows
    width = queries.shape[1]
    heads = width // DH
    ring = [(lax.rem(here.dp + step, 8), here.level) for step in range(1, 8)]
    greet(ring + mates[2:] + [here.from_across], here)

    def turn(source, target):
        return Turn(links, here, source, target, here.there)

    part = initial_in.shape[1]
    own_columns = pl.ds(pl.multiple_of(here.dp * part, part), part)
    initial_moves = [links.copy(initial_in, initial_all.at[:, own_columns], mate) for mate in ring]
    facts_turn = turn(facts_in, facts)
    gather_wst = WeightGather(links, here, wst_in, wst).enter()
    initial_all[:, own_columns] = initial_in[...]
    for moved in initial_moves:
        moved.wait_recv()
    is_fresh = facts_in[3:4, :] > 0.5
    start = jnp.where(is_fresh, initial_all[...].astype(jnp.float32), carried_in[...])
    s0_send[...] = start
    normed_send[...] = (start * scale_of(start) * gains_ref[2:3, :]).astype(jnp.bfloat16)
    normed_turn = turn(normed_send, snormed.at[rows_at(here.level * rows, rows)])
    facts_turn.arrived()
    bias_tiles(facts, tiles, heads, 3 * TILE)
    gather_wst.spread()
    gather_wtok = WeightGather(links, here, wtok_in, wtok).enter()
    normed_turn.arrived()
    gather_s0 = RowGather(links, here, snormed, 0, rows).start()

    def enter_x(block):
        at = pl.ds(block * rows, rows)
        return turn(x_in.at[at], x_ref.at[at])

    def norm_x(block, moved):
        moved.arrived()
        x = x_ref[block * rows : (block + 1) * rows, :].astype(jnp.float32)
        normed[rows_at(block * window + rank * rows, rows), :] = (
            x * scale_of(x) * gains_ref[0:1, :]
        ).astype(jnp.bfloat16)
        return RowGather(links, here, normed, block * window, rows).start()

    x_turn_0 = enter_x(0)
    gather_wst.forward()
    gather_wtok.spread()
    x_turn_1 = enter_x(1)

    def key_mask(start, size):
        place_of = lax.broadcasted_iota(jnp.int32, (1, size), 1).astype(jnp.float32)
        place_of = place_of + float(start - window)
        own = jnp.where(place_of < facts[2:3, 0:size], 0.0, NEGATIVE)
        return jnp.where(place_of < 0.0, facts[3:4, 0:size] * NEGATIVE, own)

    def project_state(block, gather):
        for k in range(4):
            gather.ready(k)
            at = rows_at(block * window + ranks[k] * rows, rows)
            for c in range(3):
                state_qkv[at, c * width : (c + 1) * width] = dot(snormed[at, :], wst[c], NN).astype(
                    jnp.bfloat16
                )

    def project_token(block, gather):
        for k in range(4):
            gather.ready(k)
            at = rows_at(block * window + ranks[k] * rows, rows)
            later = rows_at((block + 1) * window + ranks[k] * rows, rows)
            queries[at, :] = dot(normed[at, :], wtok[0], NN).astype(jnp.bfloat16)
            keys[later, :] = dot(normed[at, :], wtok[1], NN).astype(jnp.bfloat16)
            values[later, :] = dot(normed[at, :], wtok[2], NN).astype(jnp.bfloat16)

    def state_attention(block):
        base = block * window
        own = pl.ds((block + 1) * window, window)
        whole = pl.ds(base, window)
        own_mask = key_mask(base + window, window)
        for head in range(heads):
            at = head * DH
            for tile in range(window // TILE):
                here_rows = pl.ds(base + tile * TILE, TILE)
                query = state_qkv[here_rows, at : at + DH]
                first = dot(query, state_qkv[whole, width + at : width + at + DH], NT) * ROOT
                second = dot(query, keys[own, at : at + DH], NT) * ROOT + own_mask
                first, second, lse = softmax_pair(first, second)
                out = dot(first, state_qkv[whole, 2 * width + at : 2 * width + at + DH], NN)
                out = out + dot(second, values[own, at : at + DH], NN)
                smixed[here_rows, at : at + DH] = out.astype(jnp.bfloat16)
                lse_ref[here_rows, heads + head : heads + head + 1] = lse

    def token_attention(block):
        base = block * window
        whole = pl.ds(base, window)
        for tile in range(window // TILE):
            near_mask = key_mask(base + tile * TILE, 3 * TILE)
            for head in range(heads):
                at = head * DH
                here_rows = pl.ds(base + tile * TILE, TILE)
                near = pl.ds(base + tile * TILE, 3 * TILE)
                query = queries[here_rows, at : at + DH]
                first = dot(query, keys[near, at : at + DH], NT) * ROOT + tiles[head] + near_mask
                second = dot(query, state_qkv[whole, width + at : width + at + DH], NT) * ROOT
                first, second, lse = softmax_pair(first, second)
                out = dot(first, values[near, at : at + DH], NN)
                out = out + dot(second, state_qkv[whole, 2 * width + at : 2 * width + at + DH], NN)
                mixed[here_rows, at : at + DH] = out.astype(jnp.bfloat16)
                lse_ref[here_rows, head : head + 1] = lse

    def spread_state(block, buffer):
        moves = []
        columns = pl.ds(pl.multiple_of(rank * width, width), width)
        for k in (2, 3, 1):
            source = smixed.at[rows_at(block * window + ranks[k] * rows, rows)]
            moves.append(links.copy(source, buffer.at[:, columns], mates[k]))
        buffer[:, columns] = smixed[rows_at(block * window + rank * rows, rows), :]
        return moves

    def renew(block, buffer, state_now):
        size = state_now.shape[1]
        source = buffer[...]
        parts = []
        for c in range(3):
            part = dot(source, gates[c], NT)
            gate_values[:, c * size : (c + 1) * size] = part
            parts.append(part)
        stored = pltpu.make_async_copy(
            gate_values, far_gate_values.at[pl.ds(block * rows, rows)], local_sems.at[0]
        )
        stored.start()
        new_state = state_now * jax.nn.sigmoid(parts[2] + 1.0) + jnp.tanh(parts[0]) * jax.nn.sigmoid(
            parts[1] - 1.0
        )
        return new_state, stored

    def out_rows(block):
        def make(which):
            return dot(mixed[rows_at(block * window + which * rows, rows), :], wout[...], NT)

        return make

    sums = [RowSum(links, here, *rs[block], rows) for block in range(2)]

    def finish_branch(block):
        branch = sums[block].finish()
        at = slice(block * rows, (block + 1) * rows)
        total = x_ref[at, :].astype(jnp.float32) + branch
        middle[at, :] = total
        middle_normed[rows_at(block * window + rank * rows, rows), :] = (
            total * scale_of(total) * gains_ref[1:2, :]
        ).astype(jnp.bfloat16)
        gather = RowGather(links, here, middle_normed, block * window, rows).start()
        share = row_mask(facts, block * window + rank * rows, rows)
        return jnp.sum(branch * branch * share, axis=0, keepdims=True), gather

    def rise(block, gather):
        root = math.sqrt(2.0 / math.pi)
        for k in range(4):
            gather.ready(k)
            at = rows_at(block * window + ranks[k] * rows, rows)
            value = dot(middle_normed[at, :], wup[...], NN)
            square = value * value
            bend = jnp.tanh(root * value * (1.0 + 0.044715 * square))
            half = 0.5 * (1.0 + bend)
            hidden[at, :] = (value * half).astype(jnp.bfloat16)
            slope[at, :] = half + 0.5 * value * (1.0 - bend * bend) * (
                root * (1.0 + 3.0 * 0.044715 * square)
            )

    def feed_sum(block):
        return RowSum(links, here, *rs[block], rows).fill(
            lambda which: dot(hidden[rows_at(block * window + which * rows, rows), :], wdn[...], NT)
        )

    def store_feed(block, summed):
        at = slice(block * rows, (block + 1) * rows)
        feed_far[block], own = summed.split()
        feed_own[at, :] = own.astype(jnp.bfloat16)
        result_own[at, :] = middle[at, :] + own

    def start_gout(block):
        at = slice(block * rows, (block + 1) * rows)
        gout[rows_at(block * window + rank * rows, rows), :] = gout_rows[at, :]
        return RowGather(links, here, gout, block * window, rows).start()

    def feed_back(block, gather):
        for k in range(4):
            gather.ready(k)
            at = rows_at(block * window + ranks[k] * rows, rows)
            up_grad[at, :] = (dot(gout[at, :], wdn[...], NN) * slope[at, :]).astype(jnp.bfloat16)
        return RowSum(links, here, *rs[2 + block], rows).fill(
            lambda which: dot(up_grad[rows_at(block * window + which * rows, rows), :], wup[...], NT)
        )

    def weight_grad(stage, left, right, target, sem):
        step = 256
        for part in range(stage.shape[0] // step):
            at = slice(part * step, (part + 1) * step)
            stage[at, :] = dot(left[:, at], right[...], TN).astype(jnp.bfloat16)
        stored = pltpu.make_async_copy(stage, target, sem)
        stored.start()
        return stored

    gather_wst.finish()
    keep(wst, far_wst)
    project_state(0, gather_s0)
    gather_x0 = norm_x(0, x_turn_0)
    gather_wtok.forward()
    gather_gates = GateGather(links, here, gates_in, gates, local_sems.at[3])
    gather_gates.spread()
    gather_wout = WeightGather(links, here, wout_in, wout).enter()
    past_turns = [
        turn(far_past.at[0], keys.at[pl.ds(0, window)]),
        turn(far_past.at[1], values.at[pl.ds(0, window)]),
    ]
    gather_x1 = norm_x(1, x_turn_1)
    gather_wtok.finish()
    keep(wtok, far_wtok)
    keep(x_ref, far_x)
    project_token(0, gather_x0)
    state_attention(0)
    a2a_0 = smixed_rows.at[pl.ds(0, rows)]
    a2a_1 = smixed_rows.at[pl.ds(rows, rows)]
    moves_0 = spread_state(0, a2a_0)
    s0_turn = turn(s0_send, s0_ref)
    gather_wout.spread()
    gather_wup = WeightGather(links, here, far_wup, wup).enter()
    project_token(1, gather_x1)
    keep(normed, far_normed)
    keep(queries, far_queries)
    gather_gates.forward()
    for moved in past_turns:
        moved.arrived()
    keep(keys, far_keys)
    keep(values, far_values)
    token_attention(0)
    gather_wout.forward()
    gather_gates.last()
    gather_wdn = WeightGather(links, here, far_wdn, wdn).enter()
    gather_wup.spread()
    gather_wout.finish()
    keep(wout, far_wout)
    sums[0].fill(out_rows(0))
    for moved in moves_0:
        moved.wait_recv()
    gather_gates.finish()
    keep(gates, far_gates)
    s0_turn.arrived()
    keep(s0_ref, far_s0)
    s1, keep_gates = renew(0, a2a_0, s0_ref[...])
    s1_ref[...] = s1
    keep(s1_ref, far_s1)
    snormed[rows_at(window + rank * rows, rows), :] = (s1 * scale_of(s1) * gains_ref[2:3, :]).astype(
        jnp.bfloat16
    )
    gather_s1 = RowGather(links, here, snormed, window, rows).start()
    sums[0].forward()
    gather_wup.forward()
    gather_wdn.spread()
    project_state(1, gather_s1)
    gout_turn = turn(far_gout, gout_rows)
    keep(snormed, far_snormed)
    keep(state_qkv, far_state_qkv)
    branch_total, gather_m0 = finish_branch(0)
    token_attention(1)
    keep(mixed, far_mixed)
    sums[1].fill(out_rows(1))
    gather_wdn.forward()
    state_attention(1)
    keep(lse_ref, far_lse)
    sums[1].forward()
    moves_1 = spread_state(1, a2a_1)
    gather_wup.finish()
    rise(0, gather_m0)
    more, gather_m1 = finish_branch(1)
    branch_total = branch_total + more
    gout_turn.arrived()
    gather_g0 = start_gout(0)
    gather_wdn.finish()
    sums[0].sent()
    feed_0 = feed_sum(0)
    for moved in moves_1:
        moved.wait_recv()
    keep_gates.wait()
    s2, keep_gates = renew(1, a2a_1, s1_ref[...])
    gstate_send[...] = gstate_in[...].astype(jnp.bfloat16)
    gstate_turn = turn(gstate_send, far_gstate_here)
    s2_ref[...] = s2.astype(jnp.bfloat16)
    rise(1, gather_m1)
    gather_g1 = start_gout(1)
    sums[1].sent()
    feed_1 = feed_sum(1)
    store_feed(0, feed_0)
    back_0 = feed_back(0, gather_g0)
    back_0.forward()
    back_1 = feed_back(1, gather_g1)
    store_feed(1, feed_1)
    keep_down = weight_grad(grad_stage, gout, hidden, far_wdn_grad, local_sems.at[1])
    back_1.forward()
    keep_up = weight_grad(hidden, middle_normed, up_grad, far_wup_grad, local_sems.at[2])
    gain_total = 0.0
    for block, back_here in ((1, back_1), (0, back_0)):
        at = slice(block * rows, (block + 1) * rows)
        straight, gain = rms_back(middle[at, :], gains_ref[1:2, :], back_here.finish())
        total = gout_rows[at, :].astype(jnp.float32) + straight
        middle_grad[at, :] = total
        branch_rows[at, :] = total.astype(jnp.bfloat16)
        gain_total = gain_total + gain
    small_sums[...] = jnp.concatenate(
        [gain_total, branch_total, jnp.zeros((6, gain_total.shape[1]), jnp.float32)],
        axis=0,
    )
    gstate_turn.arrived()
    keep_gates.wait()
    keep_down.wait()
    keep_up.wait()
    for moved in kept:
        moved.wait()
    links.close()


class PlaneSum:
    def __init__(self, links, here, grad, first_in, last_in):
        self.links, self.here, self.grad = links, here, grad
        self.first_in, self.last_in = first_in, last_in
        self.rows = first_in.shape[-2]

    def part(self, k, which):
        start = self.here.planes[k] * 2 * self.rows + which * self.rows
        return rows_of(self.grad, start, self.rows)

    def start(self):
        mates = self.here.plane_mates
        self.firsts = [
            self.links.copy(self.part(k, which), self.first_in.at[slot], mates[mate])
            for slot, (k, which, mate) in enumerate(((1, 0, 1), (3, 0, 1), (2, 1, 2), (3, 1, 2)))
        ]
        return self

    def add(self, k, which, arrived):
        part = self.part(k, which)
        part[...] = (part[...].astype(jnp.float32) + arrived[...].astype(jnp.float32)).astype(part.dtype)

    def forward(self):
        mates = self.here.plane_mates
        self.firsts[1].wait_recv()
        self.add(2, 0, self.first_in.at[1])
        self.last_0 = self.links.copy(self.part(2, 0), self.last_in.at[0], mates[2])
        self.firsts[3].wait_recv()
        self.add(1, 1, self.first_in.at[3])
        self.last_1 = self.links.copy(self.part(1, 1), self.last_in.at[1], mates[1])

    def finish(self):
        self.firsts[0].wait_recv()
        self.add(0, 0, self.first_in.at[0])
        self.firsts[2].wait_recv()
        self.add(0, 1, self.first_in.at[2])
        self.last_0.wait_recv()
        self.add(0, 0, self.last_in.at[0])
        self.last_1.wait_recv()
        self.add(0, 1, self.last_in.at[1])

    def result(self, which):
        return rows_of(self.grad, self.here.planes[0] * 2 * self.rows + which * self.rows, self.rows)


class FarPlaneSum(PlaneSum):
    def __init__(self, links, here, grad, first_in, last_in, held, held_sems):
        super().__init__(links, here, grad, first_in, last_in)
        self.held, self.held_sems = held, held_sems

    def bring(self, *pieces):
        self.brings = [
            pltpu.make_async_copy(self.part(k, which), self.held.at[slot], self.held_sems.at[slot])
            for slot, (k, which) in enumerate(pieces)
        ]
        for moved in self.brings:
            moved.start()

    def start(self):
        super().start()
        self.bring((2, 0), (1, 1))
        return self

    def add_to(self, slot, *arrived):
        total = self.held[slot].astype(jnp.float32)
        for piece in arrived:
            total = total + piece.astype(jnp.float32)
        self.held[slot] = total.astype(jnp.bfloat16)

    def forward(self):
        mates = self.here.plane_mates
        for moved in self.brings:
            moved.wait()
        self.firsts[1].wait_recv()
        self.add_to(0, self.first_in[1])
        self.last_0 = self.links.copy(self.held.at[0], self.last_in.at[0], mates[2])
        self.firsts[3].wait_recv()
        self.add_to(1, self.first_in[3])
        self.last_1 = self.links.copy(self.held.at[1], self.last_in.at[1], mates[1])

    def bring_own(self):
        self.links.sent(self.last_0)
        self.links.sent(self.last_1)
        self.bring((0, 0), (0, 1))

    def finish(self):
        for moved in self.brings:
            moved.wait()
        self.firsts[0].wait_recv()
        self.last_0.wait_recv()
        self.add_to(0, self.first_in[0], self.last_in[0])
        self.firsts[2].wait_recv()
        self.last_1.wait_recv()
        self.add_to(1, self.first_in[2], self.last_in[1])

    def result(self, which):
        return self.held.at[which]


class Settle:
    def __init__(self, links, here, summed, target):
        half = here.half
        self.straight = Turn(links, here, summed.result(half), target.at[0], here.from_there)
        self.crossed = links.copy(summed.result(1 - half), target.at[1], here.from_across)

    def arrived(self):
        self.straight.arrived()
        self.crossed.wait_recv()


class GateHome:
    def __init__(self, links, here, grad, target, rows):
        self.links, self.here = links, here
        low = lax.rem(here.level, 2)
        piece = rows // 4
        self.slot = target.at[2 * here.half + here.core]
        chip = here.dp - here.core + low
        self.stays = here.core == low
        self.moves = {}
        for step in range(4):
            to_level = lax.rem(here.level + step, 4)
            start = here.planes[0] * 2 * rows + low * rows + to_level * piece
            source = rows_of(grad, start, piece, piece)
            for core in range(2):
                moved = links.plan(source, self.slot, (chip, to_level))
                self.moves[step, core] = moved
                sends = here.core == core
                if step == 0:
                    kept = pltpu.make_async_copy(source, self.slot, links.recv_sems.at[links.used - 1])
                    self.moves[core] = kept

                    @pl.when(sends & self.stays)
                    def _(kept=kept):
                        kept.start()

                    sends = sends & jnp.logical_not(self.stays)

                @pl.when(sends)
                def _(moved=moved):
                    moved.start()

    def arrived(self):
        for step in range(4):
            comes = lax.rem(self.here.level + step, 2) == self.here.core
            for core in range(2):
                own = self.here.core == core
                if step == 0:

                    @pl.when(comes & own)
                    def _(kept=self.moves[core]):
                        kept.wait()

                    comes_here = comes & jnp.logical_not(own)
                else:
                    comes_here = comes

                @pl.when(comes_here)
                def _(moved=self.moves[step, core]):
                    moved.wait_recv()

                sent = own & jnp.logical_not(self.stays) if step == 0 else own

                @pl.when(sent)
                def _(moved=self.moves[step, core]):
                    moved.wait_send()


def cotangent_kernel(
    far_middle_grad, far_branch_rows, gstate_ref, far_x, s0_ref, s1_ref, far_gate_values, gains_ref, facts, facts_home,
    small_sums,
    far_normed, far_snormed, far_queries, far_keys, far_values, far_state_qkv, far_lse, far_mixed,
    far_smixed, far_wst, far_wtok, far_wout, far_gates, far_wup_grad, far_wdn_grad, far_feed, far_feed_own, far_result_own,
    far_state_out,
    block_home, state_home, tokens_home, past_home, carried_grad, initial_grad, totals,
    up_home, down_home, wst_home, wtok_home, wout_home, gates_home,
    gates, wout, queries, keys, state_qkv, values, lse_ref, mixed, wst, wtok,
    tiles, tile_grads, branch_grad, mixed_grad, gate_rows, state_mixed_grad, key_grad, value_grad,
    skey_grad, svalue_grad, token_cot, state_cot, gate_values, smixed_pair, sending,
    tokens_send, carried_send, carried_in, initial_send, initial_in,
    wst_grad, wtok_grad, wout_grad, gates_grad,
    wst_first, wtok_first, wout_first, gates_first, wst_last, wtok_last, wout_last, gates_last,
    up_first, down_first, up_last, down_last, up_held, down_held, ring_in, level_in, ring_send, level_send,
    late_in, late_level_in, late_send, late_level_send, gate_pair_in,
    feed_in, feed_own,
    *rest,
):
    rs = [rest[0:4], rest[4:8], rest[8:12]]
    links = Links(rest[12], rest[13])
    local_sems, held_sems, bring_sems = rest[14], rest[15], rest[16]
    here = Place()
    rank, ranks, mates = here.rank, here.ranks, here.mates
    rows = s0_ref.shape[0]
    window = 4 * rows
    width = queries.shape[1]
    heads = width // DH
    size = s0_ref.shape[1]
    reach = 2 * width
    other_half = pl.ds(pl.multiple_of((1 - here.core) * reach, reach), reach)
    own_half = pl.ds(pl.multiple_of(here.core * reach, reach), reach)

    def pair_rows(block):
        return rows_at((2 * block + here.core) * rows, rows)

    def own_branch(block):
        return branch_grad.at[rows_at(block * window + rank * rows, rows)]

    brings = []
    for source, target in (
        (far_branch_rows.at[pl.ds(rows, rows)], own_branch(1)),
        (far_branch_rows.at[pl.ds(0, rows)], own_branch(0)),
        (far_gates, gates),
        (far_wout, wout),
        (far_queries, queries),
        (far_keys, keys),
        (far_state_qkv, state_qkv),
        (far_values, values),
        (far_lse, lse_ref),
        (far_mixed, mixed),
        (far_wst, wst),
        (far_wtok, wtok),
        (far_x, tokens_send),
        (far_feed_own, feed_own),
        (far_smixed.at[pl.ds(0, rows), own_half], smixed_pair.at[pair_rows(0)]),
        (far_smixed.at[pl.ds(rows, rows), own_half], smixed_pair.at[pair_rows(1)]),
    ):
        brings.append(pltpu.make_async_copy(source, target, bring_sems.at[len(brings)]))
        brings[-1].start()
    ring = [(lax.rem(here.dp + step, 8), here.level) for step in range(1, 8)]
    other = here.dp + 1 - 2 * here.core
    column = [
        (chip, lax.rem(here.level + step, 4)) for step in range(1, 4) for chip in (here.dp, other)
    ]
    bring_gates = pltpu.make_async_copy(
        far_gate_values.at[pl.ds(rows, rows)], gate_values, local_sems.at[0]
    )
    bring_gates.start()
    greet(ring + column)
    def home(source, target):
        return Turn(links, here, source, target, here.from_there)

    def gates_back(block, state, state_grad):
        spot = pair_rows(block)
        keep = jax.nn.sigmoid(gate_values[:, 2 * size : 3 * size] + 1.0)
        fresh = jnp.tanh(gate_values[:, 0:size])
        let_in = jax.nn.sigmoid(gate_values[:, size : 2 * size] - 1.0)
        gate_rows[spot, 0:size] = (state_grad * let_in * (1.0 - fresh * fresh)).astype(jnp.bfloat16)
        gate_rows[spot, size : 2 * size] = (
            state_grad * fresh * let_in * (1.0 - let_in)
        ).astype(jnp.bfloat16)
        gate_rows[spot, 2 * size : 3 * size] = (
            state_grad * state * keep * (1.0 - keep)
        ).astype(jnp.bfloat16)
        out = dot(gate_rows[spot, 0:size], gates[0], NN)
        out = out + dot(gate_rows[spot, size : 2 * size], gates[1], NN)
        out = out + dot(gate_rows[spot, 2 * size : 3 * size], gates[2], NN)
        sending[...] = out.astype(jnp.bfloat16)
        spot = rows_at(block * window + rank * rows, rows)
        moves = []
        for k in (2, 3, 1):
            columns = pl.ds(pl.multiple_of(ranks[k] * width, width), width)
            moves.append(
                links.copy(sending.at[:, columns], state_mixed_grad.at[spot], mates[k])
            )
        columns = pl.ds(pl.multiple_of(rank * width, width), width)
        state_mixed_grad[spot, :] = sending[:, columns]
        pair = gate_rows.at[pair_rows(block)]
        return state_grad * keep, moves, links.copy(pair, pair, mates[1])

    lane = lax.broadcasted_iota(jnp.int32, (1, DH), 1)

    def widen(columns, value):
        high = value.astype(jnp.bfloat16).astype(jnp.float32)
        middle = (value - high).astype(jnp.bfloat16).astype(jnp.float32)
        more = jnp.where(lane == 1, high, jnp.where(lane == 2, middle, value - high - middle))
        more = jnp.where(lane == 0, 1.0, jnp.where(lane < 4, more, 0.0))
        return jnp.concatenate([columns, more.astype(jnp.bfloat16)], axis=1)

    plain = jnp.where((lane > 0) & (lane < 4), 1.0, 0.0)

    def beside(columns, mask=None):
        more = jnp.broadcast_to(plain, (columns.shape[0], DH))
        if mask is not None:
            more = jnp.where(lane == 0, mask, more)
        return jnp.concatenate([columns, more.astype(jnp.bfloat16)], axis=1)

    def key_mask(start, size):
        place_of = lax.broadcasted_iota(jnp.int32, (size, 1), 0).astype(jnp.float32)
        place_of = place_of + float(start - window)
        own = jnp.where(place_of < facts[2:3, 0:1], 0.0, NEGATIVE)
        return jnp.where(place_of < 0.0, facts[3:4, 0:1] * NEGATIVE, own)

    def token_back(block):
        base = block * window
        whole = pl.ds(base, window)
        for tile in range(window // TILE):
            near_mask = key_mask(base + tile * TILE, 3 * TILE)
            for head in range(heads):
                at = head * DH
                lanes = slice(at, at + DH)
                skey_lanes = slice(width + at, width + at + DH)
                svalue_lanes = slice(2 * width + at, 2 * width + at + DH)
                here_rows = pl.ds(base + tile * TILE, TILE)
                near = pl.ds(base + tile * TILE, 3 * TILE)
                query = queries[here_rows, lanes]
                out_grad = mixed_grad[here_rows, lanes]
                wide = widen(query, lse_ref[here_rows, head : head + 1] * (-1.0 / ROOT))
                inner = jnp.sum(
                    out_grad.astype(jnp.float32) * mixed[here_rows, lanes].astype(jnp.float32),
                    axis=-1,
                    keepdims=True,
                )
                wide_grad = widen(out_grad, -inner)
                first = jnp.exp2(
                    dot(wide, beside(keys[near, lanes], near_mask), NT) * (ROOT * LOG2E) + tiles[head]
                )
                second = jnp.exp2(
                    dot(wide, beside(state_qkv[whole, skey_lanes]), NT) * (ROOT * LOG2E)
                )
                first_low, second_low = first.astype(jnp.bfloat16), second.astype(jnp.bfloat16)
                first = first * dot(wide_grad, beside(values[near, lanes]), NT)
                second = second * dot(wide_grad, beside(state_qkv[whole, svalue_lanes]), NT)
                first_grad, second_grad = first.astype(jnp.bfloat16), second.astype(jnp.bfloat16)
                value_grad[near, lanes] += dot(first_low, out_grad, TN)
                svalue_grad[:, lanes] += dot(second_low, out_grad, TN)
                part = dot(first_grad, keys[near, lanes], NN) + dot(
                    second_grad, state_qkv[whole, skey_lanes], NN
                )
                token_cot[here_rows, lanes] = (part * ROOT).astype(jnp.bfloat16)
                key_grad[near, lanes] += dot(first_grad, query, TN) * ROOT
                skey_grad[:, lanes] += dot(second_grad, query, TN) * ROOT
                tile_grads[head] += first

    def state_back(block):
        base = block * window
        whole = pl.ds(base, window)
        own = pl.ds(base + window, window)
        own_mask = key_mask(base + window, window)
        for head in range(heads):
            at = head * DH
            lanes = slice(at, at + DH)
            skey_lanes = slice(width + at, width + at + DH)
            svalue_lanes = slice(2 * width + at, 2 * width + at + DH)
            wide_skeys = beside(state_qkv[whole, skey_lanes])
            wide_keys = beside(keys[own, lanes], own_mask)
            for tile in range(window // TILE):
                here_rows = pl.ds(base + tile * TILE, TILE)
                query = state_qkv[here_rows, lanes]
                out_grad = state_mixed_grad[here_rows, lanes]
                wide = widen(query, lse_ref[here_rows, heads + head : heads + head + 1] * (-1.0 / ROOT))
                first = jnp.exp2(dot(wide, wide_skeys, NT) * (ROOT * LOG2E))
                second = jnp.exp2(dot(wide, wide_keys, NT) * (ROOT * LOG2E))
                first_low, second_low = first.astype(jnp.bfloat16), second.astype(jnp.bfloat16)
                first_grad = dot(out_grad, state_qkv[whole, svalue_lanes], NT)
                second_grad = dot(out_grad, values[own, lanes], NT)
                inner = jnp.sum(first * first_grad, axis=-1, keepdims=True) + jnp.sum(
                    second * second_grad, axis=-1, keepdims=True
                )
                first_grad = (first * (first_grad - inner)).astype(jnp.bfloat16)
                second_grad = (second * (second_grad - inner)).astype(jnp.bfloat16)
                svalue_grad[:, lanes] += dot(first_low, out_grad, TN)
                value_grad[own, lanes] += dot(second_low, out_grad, TN)
                part = dot(first_grad, state_qkv[whole, skey_lanes], NN) + dot(
                    second_grad, keys[own, lanes], NN
                )
                state_cot[here_rows, lanes] = (part * ROOT).astype(jnp.bfloat16)
                skey_grad[:, lanes] += dot(first_grad, query, TN) * ROOT
                key_grad[own, lanes] += dot(second_grad, query, TN) * ROOT

    def gather_cot(block):
        whole = pl.ds(block * window, window)
        own = pl.ds(block * window + window, window)
        token_cot[whole, width : 2 * width] = key_grad[own, :].astype(jnp.bfloat16)
        token_cot[whole, 2 * width : 3 * width] = value_grad[own, :].astype(jnp.bfloat16)
        state_cot[whole, width : 2 * width] = skey_grad[...].astype(jnp.bfloat16)
        state_cot[whole, 2 * width : 3 * width] = svalue_grad[...].astype(jnp.bfloat16)

    def back_rows(cots, weight, block):
        def make(which):
            at = rows_at(block * window + which * rows, rows)
            out = dot(cots[at, 0:width], weight[0], NT)
            for c in (1, 2):
                out = out + dot(cots[at, c * width : (c + 1) * width], weight[c], NT)
            return out

        return make

    def state_sum(block):
        return RowSum(links, here, *rs[0], rows).fill(back_rows(state_cot, wst, block))

    def token_sum(block):
        return RowSum(links, here, *rs[1 + block], rows).fill(back_rows(token_cot, wtok, block))

    def mix_back(block, gather):
        for k in range(4):
            gather.ready(k)
            at = rows_at(block * window + ranks[k] * rows, rows)
            mixed_grad[at, :] = dot(branch_grad[at, :], wout[...], NN).astype(jnp.bfloat16)

    def store_grad(target, at, out):
        if len(target.shape) == 2:
            target[at, :] = out.astype(jnp.bfloat16)
        else:
            for c in range(3):
                target[c, at, :] = out[:, c * width : (c + 1) * width].astype(jnp.bfloat16)

    def weight_grad(target, left, right):
        step = 256
        for part in range(size // step):
            at = slice(part * step, (part + 1) * step)
            store_grad(target, at, dot(left[:, at], right[...], TN))

    def finish_tokens(block, summed):
        at = slice(block * rows, (block + 1) * rows)
        x = tokens_send[at, :].astype(jnp.float32)
        straight, gain = rms_back(x, gains_ref[0:1, :], summed.finish())
        middle_grad = gate_values[:, block * size : (block + 1) * size]
        tokens_send[at, :] = (middle_grad + straight).astype(jnp.bfloat16)
        return gain, home(tokens_send.at[pl.ds(block * rows, rows)], tokens_home.at[pl.ds(block * rows, rows)])

    smixed_moves = []
    for block in range(2):
        smixed_moves.append(
            links.copy(
                far_smixed.at[pl.ds(block * rows, rows), other_half],
                smixed_pair.at[pair_rows(block)],
                mates[1],
            )
        )
    brings[0].wait()
    branch_1 = RowGather(links, here, branch_grad, window, rows).start()
    bring_gates.wait()
    brings[2].wait()
    direct_1, moves_1, pair_1 = gates_back(1, s1_ref[...], gstate_ref[...].astype(jnp.float32))
    up_sum = FarPlaneSum(
        links, here, far_wup_grad, up_first, up_last, up_held, held_sems.at[pl.ds(0, 2)]
    ).start()
    down_sum = FarPlaneSum(
        links, here, far_wdn_grad, down_first, down_last, down_held, held_sems.at[pl.ds(2, 2)]
    ).start()
    bring_result = [
        pltpu.make_async_copy(
            far_result_own.at[pl.ds(block * rows, rows)],
            gate_values.at[:, pl.ds(block * size, size)],
            local_sems.at[6 + block],
        )
        for block in range(2)
    ]
    for moved in bring_result:
        moved.start()
    for ref in (tile_grads, key_grad, value_grad, skey_grad, svalue_grad):
        ref[...] = jnp.zeros(ref.shape, ref.dtype)
    bias_tiles(facts, tiles, heads, 3 * TILE, LOG2E)
    brings[1].wait()
    for moved in brings[3:]:
        moved.wait()
    mix_back(1, branch_1)
    branch_0 = RowGather(links, here, branch_grad, 0, rows).start()
    feed_moves = [links.copy(far_feed.at[block], feed_in.at[block], mates[2]) for block in range(2)]
    state_turn = home(far_state_out, state_home)
    token_back(1)
    for moved in moves_1:
        moved.wait_recv()
    state_back(1)
    gather_cot(1)
    result_total, feed_total = 0.0, 0.0
    for block in range(2):
        at = slice(block * rows, (block + 1) * rows)
        feed_moves[block].wait_recv()
        bring_result[block].wait()
        came = feed_in[block].astype(jnp.float32)
        feed = feed_own[at, :].astype(jnp.float32) + came
        result = gate_values[:, block * size : (block + 1) * size] + came
        feed_in[block] = result.astype(jnp.bfloat16)
        share = row_mask(facts, block * window + rank * rows, rows)
        feed_total = feed_total + jnp.sum(feed * feed * share, axis=0, keepdims=True)
        result_total = result_total + jnp.sum(result * result * share, axis=0, keepdims=True)
    block_turns = [
        home(feed_in.at[block], block_home.at[pl.ds(block * rows, rows)]) for block in range(2)
    ]
    bring_gates = pltpu.make_async_copy(far_gate_values.at[pl.ds(0, rows)], gate_values, local_sems.at[0])
    bring_gates.start()
    up_sum.forward()
    state_sum_1 = state_sum(1)
    token_sum_1 = token_sum(1)
    state_sum_1.forward()
    down_sum.forward()
    up_sum.bring_own()
    mix_back(0, branch_0)
    for ref in (skey_grad, svalue_grad):
        ref[...] = jnp.zeros(ref.shape, ref.dtype)
    up_sum.finish()
    up_settle = Settle(links, here, up_sum, up_home)
    token_back(0)
    for head in range(heads):
        lines = tile_grads[head, 0:8, :]
        span = lines.shape[1]
        for group in range(1, TILE // 8):
            lines = lines + pltpu.roll(tile_grads[head, 8 * group : 8 * group + 8, :], span - 8 * group, 1)
        total = lines[0:1]
        for line in range(1, 8):
            total = total + pltpu.roll(lines[line : line + 1], span - line, 1)
        for owner in range(4):
            at = 8 + heads * owner + head
            ring_send[at : at + 1, :] = jnp.zeros((1, size), jnp.float32)
            ring_send[at : at + 1, 0:span] = jnp.where(rank == owner, total, 0.0)
    ring_send[1:2, :] = small_sums[0:1, :]
    ring_send[3:4, :] = result_total
    ring_send[4:5, :] = small_sums[1:2, :]
    ring_send[5:6, :] = feed_total
    counted = jnp.zeros((1, 1), jnp.float32)
    for block in range(2):
        valid_rows = row_mask(facts, block * window + rank * rows, rows)
        counted = counted + jnp.sum(valid_rows, axis=0, keepdims=True)
    ring_send[6:7, :] = jnp.broadcast_to(counted, (1, size))
    for line in (0, 2, 7):
        ring_send[line : line + 1, :] = jnp.zeros((1, size), jnp.float32)
    ring_moves = [
        links.copy(ring_send, ring_in.at[step - 1], ring[step - 1]) for step in range(1, 8)
    ]
    token_sum_1.forward()
    bring_gates.wait()
    state_norm_grad, gain_2 = rms_back(s1_ref[...], gains_ref[2:3, :], state_sum_1.finish())
    for moved in moves_1:
        links.sent(moved)
    direct_0, moves_0, pair_0 = gates_back(0, s0_ref[...], direct_1 + state_norm_grad)
    bring_middle = [
        pltpu.make_async_copy(
            far_middle_grad.at[pl.ds(block * rows, rows)],
            gate_values.at[:, pl.ds(block * size, size)],
            local_sems.at[6 + block],
        )
        for block in range(2)
    ]
    for moved in bring_middle:
        moved.start()
    mixed_grad[0:window, :] = key_grad[0:window, :].astype(jnp.bfloat16)
    mixed_grad[window : 2 * window, :] = value_grad[0:window, :].astype(jnp.bfloat16)
    down_sum.bring_own()
    for moved in smixed_moves + [pair_1, pair_0]:
        moved.wait_recv()
    for c in range(3):
        weight_grad(gates_grad.at[c], gate_rows.at[:, c * size : (c + 1) * size], smixed_pair)
    gates_sum = PlaneSum(links, here, gates_grad, gates_first, gates_last).start()
    weight_grad(wout_grad, branch_grad, mixed)
    wout_sum = PlaneSum(links, here, wout_grad, wout_first, wout_last).start()
    for moved in ring_moves:
        moved.wait_recv()
    total = ring_send[...]
    for step in range(7):
        total = total + ring_in[step]
    level_send[...] = total
    level_moves = [
        links.copy(level_send, level_in.at[step - 1], (here.dp, lax.rem(here.level + step, 4)))
        for step in range(1, 4)
    ]
    down_sum.finish()
    for moved in bring_middle:
        moved.wait()
    gain_1, turn_1 = finish_tokens(1, token_sum_1)
    for moved in moves_0:
        moved.wait_recv()
    past_turn = home(mixed_grad, past_home)
    down_settle = Settle(links, here, down_sum, down_home)
    for gather in (branch_1, branch_0):
        gather.sent()
    bring_snormed = pltpu.make_async_copy(far_snormed, branch_grad, local_sems.at[2])
    bring_snormed.start()
    for moved in (pair_1, pair_0):
        links.sent(moved)
    bring_normed = []
    for block in range(2):
        bring_normed.append(
            pltpu.make_async_copy(
                far_normed.at[pl.ds(block * window, window)],
                gate_rows.at[:, block * size : (block + 1) * size],
                local_sems.at[4 + block],
            )
        )
        bring_normed[block].start()
    state_back(0)
    gather_cot(0)
    bring_snormed.wait()
    weight_grad(wst_grad, branch_grad, state_cot)
    wst_sum = PlaneSum(links, here, wst_grad, wst_first, wst_last).start()
    for block in range(2):
        bring_normed[block].wait()
    for part in range(size // 256):
        at = slice(part * 256, (part + 1) * 256)
        later = slice(size + part * 256, size + (part + 1) * 256)
        summed = dot(gate_rows[:, at], token_cot[0:window, :], TN)
        summed = summed + dot(gate_rows[:, later], token_cot[window : 2 * window, :], TN)
        store_grad(wtok_grad, at, summed)
    wtok_sum = PlaneSum(links, here, wtok_grad, wtok_first, wtok_last).start()
    gates_sum.forward()
    state_sum_1.sent()
    state_sum_0 = state_sum(0)
    token_sum_0 = token_sum(0)
    state_sum_0.forward()
    token_sum_0.forward()
    wst_sum.forward()
    wtok_sum.forward()
    wout_sum.forward()
    state_norm_grad, gain = rms_back(s0_ref[...], gains_ref[2:3, :], state_sum_0.finish())
    carried_send[...] = (direct_0 + state_norm_grad).astype(jnp.bfloat16)
    carried_turn = home(carried_send, carried_in)
    gain_2 = gain_2 + gain
    gates_sum.finish()
    low = lax.rem(here.level, 2)
    gates_pair = links.copy(gates_sum.result(1 - low), gate_pair_in, mates[2])
    wst_sum.finish()
    wst_settle = Settle(links, here, wst_sum, wst_home)
    gain_0, turn_0 = finish_tokens(0, token_sum_0)

    late_send[...] = jnp.concatenate(
        [gain[:, step * 256 : (step + 1) * 256] for gain in (gain_0 + gain_1, gain_2) for step in range(4)],
        axis=0,
    )
    late_moves = [
        links.copy(late_send, late_in.at[step - 1], ring[step - 1]) for step in range(1, 8)
    ]
    gates_pair.wait_recv()
    gates_part = gates_sum.result(low)
    gates_part[...] = (
        gates_part[...].astype(jnp.float32) + gate_pair_in[...].astype(jnp.float32)
    ).astype(jnp.bfloat16)
    gate_moves = GateHome(links, here, gates_grad, gates_home, rows)
    wtok_sum.finish()
    wtok_settle = Settle(links, here, wtok_sum, wtok_home)
    wout_sum.finish()
    wout_settle = Settle(links, here, wout_sum, wout_home)
    carried_turn.arrived()
    is_fresh = facts_home[3:4, :] > 0.5
    came = carried_in[...]
    carried_grad[...] = jnp.where(is_fresh, 0.0, came.astype(jnp.float32))
    initial_send[...] = jnp.where(is_fresh, came, jnp.zeros_like(came))
    part = initial_grad.shape[1]
    initial_moves = []
    for step in range(1, 8):
        to = lax.rem(here.dp + step, 8)
        columns = pl.ds(pl.multiple_of(to * part, part), part)
        initial_moves.append(
            links.copy(initial_send.at[:, columns], initial_in.at[step - 1], ring[step - 1])
        )
    for moved in late_moves:
        moved.wait_recv()
    late = late_send[...]
    for step in range(7):
        late = late + late_in[step]
    late_level_send[...] = late
    late_level_moves = [
        links.copy(late_level_send, late_level_in.at[step - 1], (here.dp, lax.rem(here.level + step, 4)))
        for step in range(1, 4)
    ]
    for moved in initial_moves:
        moved.wait_recv()
    own_columns = pl.ds(pl.multiple_of(here.dp * part, part), part)
    initial = initial_send[:, own_columns].astype(jnp.float32)
    for step in range(7):
        initial = initial + initial_in[step].astype(jnp.float32)
    initial_grad[...] = initial
    for moved in level_moves:
        moved.wait_recv()
    total = level_send[...]
    for step in range(3):
        total = total + level_in[step]
    totals[...] = total
    for moved in late_level_moves:
        moved.wait_recv()
    late = late_level_send[...]
    for step in range(3):
        late = late + late_level_in[step]
    for row, first in ((0, 0), (2, 4)):
        for step in range(4):
            totals[row : row + 1, step * 256 : (step + 1) * 256] = late[first + step : first + step + 1, :]
    gate_moves.arrived()
    for turn in (*block_turns, state_turn, past_turn, turn_1, turn_0):
        turn.arrived()
    for settle in (up_settle, down_settle, wout_settle, wst_settle, wtok_settle):
        settle.arrived()
    links.close()


def run_kernel(body, outs, scratch, collective, name, operands, far_in=(), far_out=()):
    vmem = pl.BlockSpec(memory_space=pltpu.VMEM)
    far = pl.BlockSpec(memory_space=pl.ANY)
    return pl.pallas_call(
        body,
        out_shape=outs,
        in_specs=[far if at in far_in else vmem for at in range(len(operands))],
        out_specs=[far if at in far_out else vmem for at in range(len(outs))],
        scratch_shapes=scratch,
        compiler_params=pltpu.CompilerParams(
            collective_id=collective, has_side_effects=True, vmem_limit_bytes=VMEM_BYTES
        ),
        name=name,
    )(*operands)


def sems(count):
    return [pltpu.SemaphoreType.DMA((count,)), pltpu.SemaphoreType.DMA((count,))]


def grouped(
    tokens, carried_state, past_keys, fresh_start, valid_count, bucket_ids, grad_output, grad_state,
    norm_gains, token_qkv, token_out, bias_table, mlp_up, mlp_down, state_qkv, state_gates, initial_state,
):
    dp_size, levels = lax.axis_size("dp"), lax.axis_size("state")
    dp_at, level = lax.axis_index("dp"), lax.axis_index("state")
    _, blocks, rows, size = tokens.shape
    window = rows * levels
    width = token_qkv.shape[2]
    heads = width // DH
    units = mlp_up.shape[1]
    model_rows = token_qkv.shape[0]
    low, full = jnp.bfloat16, jnp.float32

    line_ids = jnp.pad(bucket_ids[::-1], (1, window - 1), constant_values=-1)[None, :]
    one_hot = (jnp.arange(bias_table.shape[0])[:, None] == line_ids).astype(full)
    lines = jnp.dot(bias_table.T, one_hot, precision=HIGHEST) + jnp.where(line_ids < 0, NEGATIVE, 0.0)
    numbers = jnp.stack([valid_count[0], fresh_start[0]]).astype(full)
    facts_in = jnp.concatenate(
        [
            lines,
            jnp.broadcast_to(numbers[:, None], (2, lines.shape[1])),
            jnp.zeros((4, lines.shape[1]), full),
        ]
    )

    stacked = lambda weight: jnp.transpose(weight, (1, 0, 2))
    shape = jax.ShapeDtypeStruct
    vmem = pltpu.VMEM
    rs = row_sum_scratch(rows, size)
    kept = [
        ((2 * window, size), low),
        ((2 * window, size), low),
        ((2 * window, width), low),
        ((3 * window, width), low),
        ((3 * window, width), low),
        ((2 * window, 3 * width), low),
        ((2 * window, 2 * heads), full),
        ((2 * window, width), low),
        ((3, size, width), low),
        ((3, size, width), low),
        ((size, width), low),
        ((3, size, size), low),
        ((2 * rows, size), low),
        ((rows, size), full),
        ((rows, size), full),
    ]
    (
        normed, snormed, queries, keys, values, sqkv, lse, mixed, wst_all, wtok_all, wout_all, gates_all,
        x, s0, s1, gate_values, gstate, wup_grad, wdn_grad, smixed_rows, s2, facts,
        feed_far, feed_own, result_own, middle_grad, branch_rows, small_sums,
    ) = run_kernel(
        forward_kernel,
        [shape(*of) for of in kept]
        + [
            shape((2 * rows, 3 * size), full),
            shape((rows, size), low),
            shape((size, units), low),
            shape((size, units), low),
            shape((2 * rows, size), low),
            shape((rows, size), low),
            shape((8, 2 * window), full),
            shape((2, rows, size), low),
            shape((2 * rows, size), low),
            shape((2 * rows, size), full),
            shape((2 * rows, size), full),
            shape((2 * rows, size), low),
            shape((8, size), full),
        ],
        [vmem(*of) for of in kept]
        + [
            vmem((2 * window, width), low),
            vmem((heads, TILE, 3 * TILE), full),
            vmem((rows, size), low),
            vmem((rows, size), low),
            vmem((rows, size), low),
            vmem((rows, size), full),
            vmem((rows, 3 * size), full),
            vmem((size, units), low),
            vmem((size, units), low),
            vmem((2 * rows, size), full),
            vmem((2 * window, size), low),
            vmem((2 * rows, size), low),
            vmem((2 * window, size), low),
            vmem((2 * window, units), full),
            vmem((2 * window, units), low),
            vmem((2 * window, units), low),
            vmem((size, units), low),
        ]
        + rs * 4
        + sems(128)
        + [pltpu.SemaphoreType.DMA((4,)), pltpu.SemaphoreType.DMA((len(kept),))],
        0,
        "forward",
        [
            tokens[0].reshape(blocks * rows, size),
            carried_state[0],
            initial_state,
            jnp.swapaxes(past_keys[0], 0, 1),
            facts_in,
            grad_output[0].reshape(blocks * rows, size),
            grad_state[0],
            norm_gains,
            stacked(state_qkv),
            stacked(token_qkv),
            token_out,
            stacked(state_gates),
            mlp_up,
            mlp_down,
        ],
        far_in=(3, 5, 12, 13),
        far_out=range(len(kept) + 4),
    )
    grads = [((3,), width), ((3,), width), ((), width), ((3,), 2 * width)]
    (
        block_home, state_home, tokens_home, past_home, carried_grad, initial_grad, totals,
        up_home, down_home, wst_home, wtok_home, wout_home, gates_home,
    ) = run_kernel(
        cotangent_kernel,
        [
            shape((2 * rows, size), low),
            shape((rows, size), low),
            shape((2 * rows, size), low),
            shape((2 * window, width), low),
            shape((rows, size), full),
            shape((rows, size // dp_size), full),
            shape((16, size), full),
            shape((2, rows, units), low),
            shape((2, rows, units), low),
            shape((2, 3, rows, width), low),
            shape((2, 3, rows, width), low),
            shape((2, rows, width), low),
            shape((4, 3, rows // 4, 2 * width), low),
        ],
        [
            vmem((3, size, size), low),
            vmem((size, width), low),
            vmem((2 * window, width), low),
            vmem((3 * window, width), low),
            vmem((2 * window, 3 * width), low),
            vmem((3 * window, width), low),
            vmem((2 * window, 2 * heads), full),
            vmem((2 * window, width), low),
            vmem((3, size, width), low),
            vmem((3, size, width), low),
            vmem((heads, TILE, 3 * TILE), full),
            vmem((heads, TILE, 3 * TILE), full),
            vmem((2 * window, size), low),
            vmem((2 * window, width), low),
            vmem((4 * rows, 3 * size), low),
            vmem((2 * window, width), low),
            vmem((3 * window, width), full),
            vmem((3 * window, width), full),
            vmem((window, width), full),
            vmem((window, width), full),
            vmem((2 * window, 3 * width), low),
            vmem((2 * window, 3 * width), low),
            vmem((rows, 3 * size), full),
            vmem((4 * rows, 2 * width), low),
            vmem((rows, size), low),
            vmem((2 * rows, size), low),
            vmem((rows, size), low),
            vmem((rows, size), low),
            vmem((rows, size), low),
            vmem((dp_size - 1, rows, size // dp_size), low),
        ]
        + [vmem((*stack, size, columns), low) for stack, columns in grads]
        + [vmem((4, *stack, rows, columns), low) for stack, columns in grads]
        + [vmem((2, *stack, rows, columns), low) for stack, columns in grads]
        + [vmem((4, rows, units), low)] * 2
        + [vmem((2, rows, units), low)] * 4
        + [
            vmem((dp_size - 1, 16, size), full),
            vmem((levels - 1, 16, size), full),
            vmem((16, size), full),
            vmem((16, size), full),
            vmem((dp_size - 1, 8, size // 4), full),
            vmem((levels - 1, 8, size // 4), full),
            vmem((8, size // 4), full),
            vmem((8, size // 4), full),
            vmem((3, rows, 2 * width), low),
            vmem((2, rows, size), low),
            vmem((2 * rows, size), low),
        ]
        + rs * 3
        + sems(128)
        + [pltpu.SemaphoreType.DMA((8,)), pltpu.SemaphoreType.DMA((4,)), pltpu.SemaphoreType.DMA((16,))],
        1,
        "cotangent",
        [
            middle_grad, branch_rows, gstate, x, s0, s1, gate_values, norm_gains, facts, facts_in,
            small_sums,
            normed, snormed, queries, keys, values, sqkv, lse, mixed, smixed_rows,
            wst_all, wtok_all, wout_all, gates_all, wup_grad, wdn_grad, feed_far, feed_own, result_own, s2,
        ],
        far_in=(0, 1, 3, 6, *range(11, 30)),
        far_out=(0, 1, 2, 3, 7, 8, 9, 10, 11, 12),
    )
    both = lambda pair: pair[0].astype(full) + pair[1].astype(full)
    gates_out = jnp.sum(gates_home.astype(full).reshape(2, 2, 3, rows // 4, 2 * width), axis=0)
    gates_out = jnp.transpose(gates_out, (2, 1, 0, 3)).reshape(rows // 4, 3, size)
    table_rows = bias_table.shape[0] // dp_size
    own_ids = dp_at * table_rows + jnp.arange(table_rows)
    own_lines = lax.dynamic_slice(totals, (8 + level * heads, 0), (heads, 2 * window))
    table_out = jnp.dot(
        (own_ids[:, None] == line_ids).astype(full), own_lines.T, precision=HIGHEST
    )
    share = size // (dp_size * levels)
    gains_out = lax.dynamic_slice(totals, (0, (dp_at * levels + level) * share), (3, share))
    stat_sums = jnp.sum(totals[3:7], axis=1)
    rms_stats = jnp.sqrt(stat_sums[:3] / (stat_sums[3] / size))
    return (
        block_home.reshape(1, blocks, rows, size),
        state_home.astype(full)[None],
        rms_stats,
        tokens_home.reshape(1, blocks, rows, size),
        carried_grad[None],
        jnp.swapaxes(past_home.reshape(2, window, width).astype(full), 0, 1)[None],
        gains_out,
        stacked(both(wtok_home)),
        both(wout_home),
        table_out,
        both(up_home),
        both(down_home),
        stacked(both(wst_home)),
        gates_out,
        initial_grad,
    )


def solution(mesh):
    in_specs = (
        P("dp", None, "state", None),
        P("dp", "state", None),
        P("dp", None, None, "state"),
        P("dp"),
        P("dp"),
        P(),
        P("dp", None, "state", None),
        P("dp", "state", None),
        P(),
        P("dp", None, "state"),
        P("dp", "state"),
        P(None, "state"),
        P("dp", "state"),
        P("dp", "state"),
        P("dp", None, "state"),
        P("dp", None, None),
        P("state", "dp"),
    )
    out_specs = (
        P("dp", None, "state", None),
        P("dp", "state", None),
        P(),
        P("dp", None, "state", None),
        P("dp", "state", None),
        P("dp", None, None, "state"),
        P(None, ("dp", "state")),
        P("dp", None, "state"),
        P("dp", "state"),
        P("dp", "state"),
        P("dp", "state"),
        P("dp", "state"),
        P("dp", None, "state"),
        P(("dp", "state"), None, None),
        P("state", "dp"),
    )
    body = grouped if dict(mesh.shape) == {"dp": 8, "state": 4} else shards
    return jax.shard_map(body, mesh=mesh, in_specs=in_specs, out_specs=out_specs, check_vma=False)
```
